32 devices in a mesh: dp: 4 (over z), wide: 2 (over x), narrow: 4 (over y, core).
Axes of the slice: x: 2, y: 2, z: 4, core: 2. Of those that a mesh axis runs over, the one named last changes fastest.
Arguments:
- tokens: bfloat16 [32768, 1024], P(('dp', 'narrow'), 'wide'), may hold values from -6 to 6
- memory: bfloat16 [32768, 1024], P(('dp', 'narrow'), 'wide'), may hold values from -6 to 6
- dec_segments: int32 [16, 2048], P(('dp', 'narrow')), may hold values from 0 to 3, never falling along the last dimension, each value on 1 to 1024 neighbouring positions
- mem_segments: int32 [16, 2048], P(('dp', 'narrow')), may hold values from 0 to 3, never falling along the last dimension, each value on 1 to 1024 neighbouring positions
- self_qkv: bfloat16 [3, 1024, 1024], P(None, None, 'wide'), may hold values from -0.1875 to 0.1875
- self_out: bfloat16 [1024, 1024], P('wide'), may hold values from -1.5 to 1.5
- cross_q: bfloat16 [1024, 1024], P(None, 'wide'), may hold values from -0.1875 to 0.1875
- cross_kv: bfloat16 [2, 1024, 1024], P(None, None, 'wide'), may hold values from -0.1875 to 0.1875
- cross_out: bfloat16 [1024, 1024], P('wide'), may hold values from -1.5 to 1.5
- ffn_in: bfloat16 [1024, 4096], P(None, 'wide'), may hold values from -0.1875 to 0.1875
- ffn_out: bfloat16 [4096, 1024], P('wide'), may hold values from -0.09375 to 0.09375
- adapter_down: bfloat16 [1024, 512], P(None, 'narrow'), may hold values from -0.1875 to 0.1875
- adapter_up: bfloat16 [512, 1024], P('narrow'), may hold values from -0.125 to 0.125
- self_prefix: bfloat16 [2, 30, 1024], P(None, None, 'wide'), may hold values from -6 to 6
- cross_prefix: bfloat16 [2, 30, 1024], P(None, None, 'wide'), may hold values from -6 to 6
- gains: float32 [3, 1024], replicated, may hold values from 0.1 to 1.9
- cotangent: bfloat16 [32768, 1024], P(('dp', 'narrow'), 'wide'), may hold values from -6 to 6
Outputs:
- output: bfloat16 [32768, 1024], P(('dp', 'narrow'), 'wide')
- grad_tokens: float32 [32768, 1024], P(('dp', 'narrow'), 'wide')
- grad_memory: float32 [32768, 1024], P(('dp', 'narrow'), 'wide')
- grad_self_prefix: float32 [2, 30, 1024], P(None, None, 'wide')
- grad_cross_prefix: float32 [2, 30, 1024], P(None, None, 'wide')
- grad_adapter_down: float32 [1024, 512], P(None, 'narrow')
- grad_adapter_up: float32 [512, 1024], P('narrow')
The draws below stay inside these ranges and needn't reach their ends.
Inputs may be any that keep to these rules, and one draw needn't show every extreme that they name: `dec_segments`: within each row, document numbers never fall and every number 0 to 3 occurs. `mem_segments`: within each row, document numbers never fall and every number 0 to 3 occurs.
All inputs are finite; a program needn't handle non-finite values.
Results may differ from the reference program's by a relative error of at most 0.025.
Values may be sent and summed in bfloat16 or wider, within the bound.
A program may use at most 320 MiB of HBM per device.

```python
import math
from functools import partial
import jax
import jax.numpy as jnp
import numpy as np
from jax import lax

D = 1024
HEADS = 16
HEAD_DIM = 64
FF = 4096
BOT = 512
PREFIX = 30
SEQ = 2048
MEM = 2048
DOCS = 4
DOC_MOST = 1024
MEM_MOST = 1024
ROWS_ALL = 16
TOKENS = 32768
MEM_ROWS = 32768


def block_scale(rng, shape, cuts, low, top_value):
    factor_of = 1.0
    for axis_at, parts in cuts:
        draws = jax.random.uniform(jax.random.fold_in(jax.random.fold_in(rng, 6), axis_at), (parts,), jnp.float32, low / len(cuts), top_value / len(cuts))
        factor_of = factor_of * jnp.repeat(jnp.exp(draws), shape[axis_at] // parts).reshape((-1,) + (1,) * (len(shape) - 1 - axis_at))
    return factor_of


def split_up(number_of, total, most, slope):
    loads = [(1 << 20) // math.isqrt(rank ** slope) + 1 for rank in range(2, number_of + 1)]
    surplus, holding = total - most - (number_of - 1), [1] * (number_of - 1)
    while surplus > 0:
        candidates = [i for i in range(number_of - 1) if holding[i] < most]
        whole, budget = sum([loads[i] for i in candidates]), surplus
        for i in candidates:
            addition = min(most - holding[i], max(1, budget * loads[i] // whole), surplus)
            holding[i] = holding[i] + addition
            surplus = surplus - addition
    return np.array([most] + holding)


def ragged_sizes(own_key, count, total, limit, lean):
    if count == 2:
        one = jax.random.randint(own_key, (), max(1, total - limit), min(limit, total - 1) + 1)
        return jnp.stack([one, total - one])
    tallies = jnp.asarray(split_up(count, total, limit, lean), jnp.int32)
    pairs = (count - 1) // 2
    donor, receiver = tallies[1:1 + 2 * pairs:2], tallies[2:2 + 2 * pairs:2]
    room = jnp.minimum(donor - 1, limit - receiver)
    shifted = jax.random.randint(jax.random.fold_in(own_key, 1), (pairs,), 0, 1 << 20) % (room + 1)
    tallies = tallies.at[1:1 + 2 * pairs:2].set(donor - shifted).at[2:2 + 2 * pairs:2].set(receiver + shifted)
    return tallies[jax.random.permutation(jax.random.fold_in(own_key, 2), count)]


def scatter_about(stream_key, dims, spread, limit, shards=(), held_as=jnp.bfloat16):
    array = spread * jax.random.normal(stream_key, dims, jnp.float32)
    if shards:
        array = array * block_scale(stream_key, dims, shards, -0.22, 0.18)
    return jnp.clip(array, -limit, limit).astype(held_as)


def setup_inputs(seed: int = 0) -> dict:
    key_list = jax.random.split(jax.random.key(seed), 18)
    return {
        "tokens": scatter_about(key_list[0], (TOKENS, D), 1.0, 6.0, ((0, 16), (1, 2))),
        "memory": scatter_about(key_list[1], (MEM_ROWS, D), 1.0, 6.0, ((0, 16), (1, 2))),
        "dec_segments": jax.vmap(lambda own: jnp.searchsorted(jnp.cumsum(ragged_sizes(own, DOCS, SEQ, DOC_MOST, 1)), jnp.arange(SEQ), side="right"))(jax.random.split(key_list[2], ROWS_ALL)).reshape((ROWS_ALL, SEQ)).astype(jnp.int32),
        "mem_segments": jax.vmap(lambda own: jnp.searchsorted(jnp.cumsum(ragged_sizes(own, DOCS, MEM, MEM_MOST, 1)), jnp.arange(MEM), side="right"))(jax.random.split(key_list[3], ROWS_ALL)).reshape((ROWS_ALL, MEM)).astype(jnp.int32),
        "self_qkv": scatter_about(key_list[4], (3, D, D), D ** -0.5, 0.1875, ((2, 2),)),
        "self_out": scatter_about(key_list[5], (D, D), (D // 64) ** -0.5, 1.5, ((0, 2),)),
        "cross_q": scatter_about(key_list[6], (D, D), D ** -0.5, 0.1875, ((1, 2),)),
        "cross_kv": scatter_about(key_list[7], (2, D, D), D ** -0.5, 0.1875, ((2, 2),)),
        "cross_out": scatter_about(key_list[8], (D, D), (D // 64) ** -0.5, 1.5, ((0, 2),)),
        "ffn_in": scatter_about(key_list[9], (D, FF), D ** -0.5, 0.1875, ((1, 2),)),
        "ffn_out": scatter_about(key_list[10], (FF, D), FF ** -0.5, 0.09375, ((0, 2),)),
        "adapter_down": scatter_about(key_list[11], (D, BOT), D ** -0.5, 0.1875, ((1, 4),)),
        "adapter_up": scatter_about(key_list[12], (BOT, D), (4 * BOT) ** -0.5, 0.125, ((0, 4),)),
        "self_prefix": scatter_about(key_list[13], (2, PREFIX, D), 1.0, 6.0, ((2, 2),)),
        "cross_prefix": scatter_about(key_list[14], (2, PREFIX, D), 1.0, 6.0, ((2, 2),)),
        "gains": jnp.clip(1.0 + 0.18 * jax.random.normal(key_list[15], (3, D), jnp.float32), 0.1, 1.9),
        "cotangent": scatter_about(key_list[16], (TOKENS, D), 1.0, 6.0, ((0, 16), (1, 2))),
    }


@jax.custom_vjp
def low(v):
    return lax.optimization_barrier(v.astype(jnp.bfloat16)).astype(jnp.float32)

@jax.custom_vjp
def low_back(v):
    return v

def low_keep(v):
    return (low(v), None)

def low_pass(kept, grad):
    return (grad,)

def back_keep(v):
    return (v, None)

def back_low(kept, grad):
    return (low(grad),)
low.defvjp(low_keep, low_pass)
low_back.defvjp(back_keep, back_low)
precise = lax.Precision.HIGHEST

def matmul(left, right):
    return jnp.dot(left, right, precision=precise, preferred_element_type=jnp.float32)

def both_ways(features):
    return low(low_back(features))

def layer_norm(features, norm_gain):
    average = lax.optimization_barrier(jnp.mean(features, axis=-1, keepdims=True))
    centered = features - average
    variance = lax.optimization_barrier(jnp.mean(centered * centered, axis=-1, keepdims=True))
    return centered * lax.rsqrt(variance + 1e-05) * norm_gain

def attention(query, keys, values, prefix, query_seg, key_seg, causal):
    length = query.shape[0]
    key_count = keys.shape[0]
    block_rows = min(512, length)
    block_count = length // block_rows
    score_scale = HEAD_DIM ** (-0.5)
    key_heads = keys.reshape(key_count, HEADS, HEAD_DIM)
    value_heads = values.reshape(key_count, HEADS, HEAD_DIM)
    prefix_keys = prefix[0].reshape(PREFIX, HEADS, HEAD_DIM)
    prefix_values = prefix[1].reshape(PREFIX, HEADS, HEAD_DIM)
    key_places = jnp.arange(key_count, dtype=jnp.int32)

    def one_block(pieces):
        query_rows, query_segs, block_start = pieces
        query_heads = query_rows.reshape(block_rows, HEADS, HEAD_DIM)
        scores = low_back(jnp.einsum('qhd,khd->hqk', query_heads, key_heads, precision=precise) * score_scale)
        prefix_scores = low_back(jnp.einsum('qhd,phd->hqp', query_heads, prefix_keys, precision=precise) * score_scale)
        allowed = query_segs[:, None] == key_seg[None, :]
        if causal:
            positions = block_start + jnp.arange(block_rows, dtype=jnp.int32)
            allowed = jnp.logical_and(allowed, key_places[None, :] <= positions[:, None])
        scores = jnp.where(allowed[None], scores, -1e+30)
        largest = jnp.maximum(lax.optimization_barrier(jnp.max(scores, axis=-1)), lax.optimization_barrier(jnp.max(prefix_scores, axis=-1)))
        denominator = lax.optimization_barrier(jnp.sum(jnp.exp(scores - largest[..., None]), axis=-1)) + lax.optimization_barrier(jnp.sum(jnp.exp(prefix_scores - largest[..., None]), axis=-1))
        log_total = largest + jnp.log(denominator)
        chances = low(jnp.exp(scores - log_total[..., None]))
        prefix_chances = low(jnp.exp(prefix_scores - log_total[..., None]))
        attended = jnp.einsum('hqk,khd->qhd', chances, value_heads, precision=precise)
        attended = attended + jnp.einsum('hqp,phd->qhd', prefix_chances, prefix_values, precision=precise)
        return attended.reshape(block_rows, HEADS * HEAD_DIM)
    starts = jnp.arange(block_count, dtype=jnp.int32) * block_rows
    blocks = lax.map(jax.checkpoint(one_block), (query.reshape(block_count, block_rows, HEADS * HEAD_DIM), query_seg.reshape(block_count, block_rows), starts))
    return blocks.reshape(length, HEADS * HEAD_DIM)

def one_row(frozen, trainable, row):
    self_qkv, self_out, cross_q, cross_kv, cross_out, ffn_in, ffn_out, gains = frozen
    self_prefix, cross_prefix, adapter_down, adapter_up = trainable
    token_rows, memory_rows, dec_seg, mem_seg = row
    self_query = both_ways(matmul(token_rows, self_qkv[0]))
    self_key = both_ways(matmul(token_rows, self_qkv[1]))
    self_value = both_ways(matmul(token_rows, self_qkv[2]))
    self_heads = both_ways(attention(self_query, self_key, self_value, self_prefix, dec_seg, dec_seg, True))
    first_sum = low(token_rows + low_back(matmul(self_heads, self_out)))
    normed_one = low_back(layer_norm(first_sum, gains[0]))
    cross_query = both_ways(matmul(low(normed_one), cross_q))
    cross_key = both_ways(matmul(memory_rows, cross_kv[0]))
    cross_value = both_ways(matmul(memory_rows, cross_kv[1]))
    cross_heads = both_ways(attention(cross_query, cross_key, cross_value, cross_prefix, dec_seg, mem_seg, False))
    second_sum = low(normed_one + low_back(matmul(cross_heads, cross_out)))
    normed_two = low_back(layer_norm(second_sum, gains[1]))
    normed_low = low(normed_two)
    pre_act = low_back(matmul(normed_low, ffn_in))
    hidden = low(jax.nn.gelu(pre_act, approximate=False))
    bottle_pre = low_back(matmul(normed_low, adapter_down))
    bottle = low(jax.nn.gelu(bottle_pre, approximate=False))
    branch = low_back(matmul(hidden, ffn_out) + 4.0 * matmul(bottle, adapter_up))
    third_sum = low(normed_two + branch)
    return layer_norm(third_sum, gains[2])

def reference(tokens, memory, dec_segments, mem_segments, self_qkv, self_out, cross_q, cross_kv, cross_out, ffn_in, ffn_out, adapter_down, adapter_up, self_prefix, cross_prefix, gains, cotangent):
    frozen = tuple((weight.astype(jnp.float32) for weight in (self_qkv, self_out, cross_q, cross_kv, cross_out, ffn_in, ffn_out, gains)))
    trainable = tuple((weight.astype(jnp.float32) for weight in (self_prefix, cross_prefix, adapter_down, adapter_up)))
    inputs = (tokens.astype(jnp.float32), memory.astype(jnp.float32))

    def forward(trainable_now, inputs_now):
        token_rows = inputs_now[0].reshape(ROWS_ALL, SEQ, D)
        memory_rows = inputs_now[1].reshape(ROWS_ALL, MEM, D)
        per_row = jax.checkpoint(partial(one_row, frozen, trainable_now))
        results = lax.map(per_row, (token_rows, memory_rows, dec_segments, mem_segments))
        return results.reshape(TOKENS, D)
    result, pullback = jax.vjp(forward, trainable, inputs)
    grad_trainable, grad_inputs = pullback(cotangent.astype(jnp.float32))
    return (result.astype(jnp.bfloat16), grad_inputs[0], grad_inputs[1], grad_trainable[0], grad_trainable[1], grad_trainable[2], grad_trainable[3])
```

```python
import functools
import math
from functools import partial

import jax
import jax.numpy as jnp
from jax import lax
from jax.experimental import pallas as pl
from jax.experimental.pallas import tpu as pltpu
from jax.sharding import Mesh
from jax.sharding import PartitionSpec as P

HEAD_DIM = 64
DOCS = 4
NEG = -1e30
BQ = 256
BK = 256
PP = 32
BT = 256
HEADS_FWD = 8
HEADS_BWD = 4
SWAP = [(0, 1), (1, 0)]
MIB = 2**20


def mm(a, b):
    return jnp.dot(a, b, preferred_element_type=jnp.float32)


def mm_nt(a, b):
    return lax.dot_general(a, b, (((1,), (1,)), ((), ())), preferred_element_type=jnp.float32)


def mm_tn(a, b):
    return lax.dot_general(a, b, (((0,), (0,)), ((), ())), preferred_element_type=jnp.float32)


def pair_rows(t):
    zero = jnp.zeros((HEAD_DIM, t.shape[1]), t.dtype)
    return [
        jnp.concatenate([t[:HEAD_DIM], zero], axis=0),
        jnp.concatenate([zero, t[HEAD_DIM:]], axis=0),
    ]


def part_offsets(n_parts, part_len):
    if n_parts == 1:
        return [0]
    core = lax.axis_index("c")
    return [pl.multiple_of(core * part_len, part_len), pl.multiple_of((1 - core) * part_len, part_len)]


def fwd_kernel(causal, n_parts, lo_ref, hi_ref, *refs):
    q_parts, k_parts, v_parts = refs[:n_parts], refs[n_parts:2 * n_parts], refs[2 * n_parts:3 * n_parts]
    ek_ref, eq_ref, pre_ref, ep_ref = refs[3 * n_parts:3 * n_parts + 4]
    o_parts = refs[3 * n_parts + 4:4 * n_parts + 4]
    ot_ref, lt_ref, qt, vt, ke = refs[4 * n_parts + 4:]
    seq = qt.shape[1]
    q_len, m_len = q_parts[0].shape[0], k_parts[0].shape[0]
    width = q_parts[0].shape[1]
    n_pairs = width // 128
    heads_here = width // HEAD_DIM
    n_q = seq // BQ

    for q_ref, at in zip(q_parts, part_offsets(n_parts, q_len)):
        qt[:, pl.ds(at, q_len)] = (q_ref[...] * jnp.bfloat16(0.125)).T
    for k_ref, v_ref, at in zip(k_parts, v_parts, part_offsets(n_parts, m_len)):
        vt[:, pl.ds(at, m_len)] = v_ref[...].T
        for p in range(n_pairs):
            ke[p, pl.ds(at, m_len), :128] = k_ref[:, p * 128:(p + 1) * 128]
    for p in range(n_pairs):
        ke[p, :, 128:] = ek_ref[...]
    vpt = pre_ref[1].T
    ones = jnp.ones((16, BK), jnp.bfloat16)

    def q_step(i, _):
        qs = pl.ds(pl.multiple_of(i * BQ, BQ), BQ)
        eq = eq_ref[:, qs]
        heads = []
        for p in range(n_pairs):
            heads += [jnp.concatenate([r, eq], axis=0) for r in pair_rows(qt[p * 128:(p + 1) * 128, qs])]

        def block(j, carry, diag):
            ks = pl.ds(pl.multiple_of(j * BK, BK), BK)
            out = []
            scores = [mm(ke[h // 2, ks, :], heads[h]) for h in range(heads_here)]
            for h in range(heads_here):
                m, acc = carry[h]
                s = scores[h]
                if diag:
                    kk = lax.broadcasted_iota(jnp.int32, (BK, BQ), 0)
                    qq = lax.broadcasted_iota(jnp.int32, (BK, BQ), 1)
                    s = jnp.where(kk <= qq, s, NEG)
                m_new = jnp.maximum(m, jnp.max(s, axis=0, keepdims=True))
                p = jnp.exp(s - m_new).astype(jnp.bfloat16)
                vb = jnp.concatenate([vt[h * HEAD_DIM:(h + 1) * HEAD_DIM, ks], ones], axis=0)
                acc = acc * jnp.exp(m - m_new) + mm(vb, p)
                out.append((m_new, acc))
            return tuple(out)

        carry = []
        for h in range(heads_here):
            kp = jnp.concatenate([pre_ref[0, :, (h // 2) * 128:(h // 2 + 1) * 128], ep_ref[...]], axis=1)
            s = mm(kp, heads[h])
            m = jnp.max(s, axis=0, keepdims=True)
            p = jnp.exp(s - m).astype(jnp.bfloat16)
            vb = jnp.concatenate([vpt[h * HEAD_DIM:(h + 1) * HEAD_DIM], ones[:, :PP]], axis=0)
            carry.append((m, mm(vb, p)))
        carry = tuple(carry)
        if causal:
            carry = block(i, carry, True)
        carry = lax.fori_loop(lo_ref[i], hi_ref[i], lambda j, c: block(j, c, False), carry)
        outs = []
        for h in range(heads_here):
            m, acc = carry[h]
            total = acc[HEAD_DIM:HEAD_DIM + 1]
            lt_ref[h // 2, h % 2:h % 2 + 1, qs] = m + jnp.log(total)
            outs.append(acc[:HEAD_DIM] / total)
        ot = jnp.concatenate(outs, axis=0)
        ot_ref[:, qs] = ot.astype(jnp.bfloat16)
        o = ot.T.astype(jnp.bfloat16)
        store_part(o_parts, i, o)
        return 0

    lax.fori_loop(0, n_q, q_step, 0)


def store_part(parts, i, value):
    per_part = parts[0].shape[0] // BQ
    at = pl.ds(pl.multiple_of((i % per_part) * BQ, BQ), BQ)
    if len(parts) == 1:
        parts[0][at, :] = value
        return
    own = i // per_part == lax.axis_index("c")

    @pl.when(own)
    def _():
        parts[0][at, :] = value

    @pl.when(jnp.logical_not(own))
    def _():
        parts[1][at, :] = value


def attend_fwd(qs, ks, vs, cols, masks, prefix, lo, hi, causal):
    ek, eq, ep = masks
    n = len(qs)
    q_len, m_len = qs[0][0].shape[0], ks[0][0].shape[0]
    seq, mem = q_len * n, m_len * n
    wd = min(HEAD_DIM * HEADS_FWD, cols)
    steps = cols // wd
    in_specs, operands = [], []
    for group, length in ((qs, q_len), (ks, m_len), (vs, m_len)):
        for array, at in group:
            in_specs.append(pl.BlockSpec((length, wd), partial(lambda at, p, *_: (0, at * steps + p), at)))
            operands.append(array)
    in_specs += [
        pl.BlockSpec((mem, 128), lambda p, *_: (0, 0)),
        pl.BlockSpec((128, seq), lambda p, *_: (0, 0)),
        pl.BlockSpec((2, PP, wd), lambda p, *_: (0, 0, p)),
        pl.BlockSpec((PP, 128), lambda p, *_: (0, 0)),
    ]
    grid_spec = pltpu.PrefetchScalarGridSpec(
        num_scalar_prefetch=2,
        grid=(steps,),
        in_specs=in_specs,
        out_specs=[pl.BlockSpec((q_len, wd), lambda p, *_: (0, p))] * n
        + [
            pl.BlockSpec((wd, seq), lambda p, *_: (p, 0)),
            pl.BlockSpec((wd // 128, 2, seq), lambda p, *_: (p, 0, 0)),
        ],
        scratch_shapes=[
            pltpu.VMEM((wd, seq), jnp.bfloat16),
            pltpu.VMEM((wd, mem), jnp.bfloat16),
            pltpu.VMEM((wd // 128, mem, 256), jnp.bfloat16),
        ],
    )
    result = pl.pallas_call(
        functools.partial(fwd_kernel, causal, n),
        grid_spec=grid_spec,
        out_shape=[jax.ShapeDtypeStruct((q_len, cols), jnp.bfloat16)] * n
        + [
            jax.ShapeDtypeStruct((cols, seq), jnp.bfloat16),
            jax.ShapeDtypeStruct((cols // 128, 2, seq), jnp.float32),
        ],
        compiler_params=pltpu.CompilerParams(vmem_limit_bytes=56 * MIB),
        cost_estimate=pl.CostEstimate(
            flops=8 * seq * mem * cols, bytes_accessed=12 * MIB, transcendentals=seq * mem * cols // 256
        ),
        name="attend_fwd_self" if causal else "attend_fwd_cross",
    )(lo, hi, *operands, ek, eq, prefix, ep)
    return result[:n], result[n], result[n + 1]


def bwd_kernel(causal, n_parts, lo_ref, hi_ref, *refs):
    q_parts, k_parts, v_parts, g_parts = (refs[t * n_parts:(t + 1) * n_parts] for t in range(4))
    ot_ref, lt_ref, ek_ref, eq_ref, pre_ref, ep_ref = refs[4 * n_parts:4 * n_parts + 6]
    dq_parts = refs[4 * n_parts + 6:5 * n_parts + 6]
    dkv_parts = refs[5 * n_parts + 6:6 * n_parts + 6]
    dp_ref, qt, gt, kt, ke, vv, qm, gm, dk, dv, delta = refs[6 * n_parts + 6:]
    seq = qt.shape[1]
    q_len, m_len = q_parts[0].shape[0], k_parts[0].shape[0]
    width = q_parts[0].shape[1]
    n_pairs = width // 128
    heads_here = width // HEAD_DIM
    n_q = seq // BQ
    lane = lax.broadcasted_iota(jnp.int32, (1, width), 1)
    first = lane % 128 < HEAD_DIM
    zero = jnp.zeros((), jnp.bfloat16)

    for q_ref, g_ref, at in zip(q_parts, g_parts, part_offsets(n_parts, q_len)):
        here = pl.ds(at, q_len)
        q_all = q_ref[...] * jnp.bfloat16(0.125)
        g_all = g_ref[...]
        qt[:, here] = q_all.T
        g_turned = g_all.T
        gt[:, here] = g_turned
        qm[0, here, :] = jnp.where(first, q_all, zero)
        qm[1, here, :] = jnp.where(first, zero, q_all)
        gm[0, here, :] = jnp.where(first, g_all, zero)
        gm[1, here, :] = jnp.where(first, zero, g_all)
        prod = g_turned.astype(jnp.float32) * ot_ref[:, here].astype(jnp.float32)
        for h in range(heads_here):
            delta[h:h + 1, here] = jnp.sum(prod[h * HEAD_DIM:(h + 1) * HEAD_DIM], axis=0, keepdims=True)
    for k_ref, v_ref, at in zip(k_parts, v_parts, part_offsets(n_parts, m_len)):
        here = pl.ds(at, m_len)
        kt[:, here] = k_ref[...].T
        vv[here, :] = v_ref[...]
        for p in range(n_pairs):
            ke[p, here, :128] = k_ref[:, p * 128:(p + 1) * 128]
    for p in range(n_pairs):
        ke[p, :, 128:] = ek_ref[...]
    dk[...] = jnp.zeros_like(dk)
    dv[...] = jnp.zeros_like(dv)
    dp_ref[...] = jnp.zeros_like(dp_ref)
    kpt = pre_ref[0].T

    def q_step(i, _):
        qs = pl.ds(pl.multiple_of(i * BQ, BQ), BQ)
        eq = eq_ref[:, qs]
        q_heads, g_heads = [], []
        for p in range(n_pairs):
            q_heads += [jnp.concatenate([r, eq], axis=0) for r in pair_rows(qt[p * 128:(p + 1) * 128, qs])]
            g_heads += pair_rows(gt[p * 128:(p + 1) * 128, qs])
        lts = [lt_ref[h // 2, h % 2:h % 2 + 1, qs] for h in range(heads_here)]
        dls = [delta[h:h + 1, qs] for h in range(heads_here)]

        def grads(s, dp, h, diag):
            if diag:
                kk = lax.broadcasted_iota(jnp.int32, s.shape, 0)
                qq = lax.broadcasted_iota(jnp.int32, s.shape, 1)
                s = jnp.where(kk <= qq, s, NEG)
            p = jnp.exp(s - lts[h])
            ds = (p * (dp - dls[h])).astype(jnp.bfloat16)
            return p.astype(jnp.bfloat16), ds

        def block(j, carry, diag):
            ks = pl.ds(pl.multiple_of(j * BK, BK), BK)
            out, both = [], []
            for h in range(heads_here):
                c = (h // 2) * 128
                both.append((mm(ke[h // 2, ks, :], q_heads[h]), mm(vv[ks, c:c + 128], g_heads[h])))
            for pr in range(n_pairs):
                c = pr * 128
                dkb = dk[ks, c:c + 128]
                dvb = dv[ks, c:c + 128]
                for h in (2 * pr, 2 * pr + 1):
                    p, ds = grads(*both[h], h, diag)
                    dvb += mm(p, gm[h % 2, qs, c:c + 128])
                    dkb += mm(ds, qm[h % 2, qs, c:c + 128])
                    out.append(carry[h] + mm(kt[h * HEAD_DIM:(h + 1) * HEAD_DIM, ks], ds))
                dk[ks, c:c + 128] = dkb
                dv[ks, c:c + 128] = dvb
            return tuple(out)

        carry = []
        for h in range(heads_here):
            c = (h // 2) * 128
            kp = jnp.concatenate([pre_ref[0, :, c:c + 128], ep_ref[...]], axis=1)
            p, ds = grads(mm(kp, q_heads[h]), mm(pre_ref[1, :, c:c + 128], g_heads[h]), h, False)
            dp_ref[0, :, c:c + 128] += mm(ds, qm[h % 2, qs, c:c + 128])
            dp_ref[1, :, c:c + 128] += mm(p, gm[h % 2, qs, c:c + 128])
            carry.append(mm(kpt[h * HEAD_DIM:(h + 1) * HEAD_DIM], ds))
        carry = tuple(carry)
        if causal:
            carry = block(i, carry, True)
        carry = lax.fori_loop(lo_ref[i], hi_ref[i], lambda j, c: block(j, c, False), carry)
        dq = jnp.concatenate(carry, axis=0) * 0.125
        store_part(dq_parts, i, dq.T.astype(jnp.bfloat16))
        return 0

    lax.fori_loop(0, n_q, q_step, 0)
    for dkv_ref, at in zip(dkv_parts, part_offsets(n_parts, m_len)):
        here = pl.ds(at, m_len)
        dkv_ref[0] = dk[here, :].astype(jnp.bfloat16)
        dkv_ref[1] = dv[here, :].astype(jnp.bfloat16)


def attend_bwd(qs, ks, vs, gs, cols, ot, lt, masks, prefix, lo, hi, causal):
    ek, eq, ep = masks
    n = len(qs)
    q_len, m_len = qs[0][0].shape[0], ks[0][0].shape[0]
    seq, mem = q_len * n, m_len * n
    wd = min(HEAD_DIM * HEADS_BWD, cols)
    steps = cols // wd
    in_specs, operands = [], []
    for group, length in ((qs, q_len), (ks, m_len), (vs, m_len), (gs, q_len)):
        for array, at in group:
            in_specs.append(pl.BlockSpec((length, wd), partial(lambda at, p, *_: (0, at * steps + p), at)))
            operands.append(array)
    in_specs += [
        pl.BlockSpec((wd, seq), lambda p, *_: (p, 0)),
        pl.BlockSpec((wd // 128, 2, seq), lambda p, *_: (p, 0, 0)),
        pl.BlockSpec((mem, 128), lambda p, *_: (0, 0)),
        pl.BlockSpec((128, seq), lambda p, *_: (0, 0)),
        pl.BlockSpec((2, PP, wd), lambda p, *_: (0, 0, p)),
        pl.BlockSpec((PP, 128), lambda p, *_: (0, 0)),
    ]
    grid_spec = pltpu.PrefetchScalarGridSpec(
        num_scalar_prefetch=2,
        grid=(steps,),
        in_specs=in_specs,
        out_specs=[pl.BlockSpec((q_len, wd), lambda p, *_: (0, p))] * n
        + [pl.BlockSpec((2, m_len, wd), lambda p, *_: (0, 0, p))] * n
        + [pl.BlockSpec((2, PP, wd), lambda p, *_: (0, 0, p))],
        scratch_shapes=[
            pltpu.VMEM((wd, seq), jnp.bfloat16),
            pltpu.VMEM((wd, seq), jnp.bfloat16),
            pltpu.VMEM((wd, mem), jnp.bfloat16),
            pltpu.VMEM((wd // 128, mem, 256), jnp.bfloat16),
            pltpu.VMEM((mem, wd), jnp.bfloat16),
            pltpu.VMEM((2, seq, wd), jnp.bfloat16),
            pltpu.VMEM((2, seq, wd), jnp.bfloat16),
            pltpu.VMEM((mem, wd), jnp.float32),
            pltpu.VMEM((mem, wd), jnp.float32),
            pltpu.VMEM((8, seq), jnp.float32),
        ],
    )
    result = pl.pallas_call(
        functools.partial(bwd_kernel, causal, n),
        grid_spec=grid_spec,
        out_shape=[jax.ShapeDtypeStruct((q_len, cols), jnp.bfloat16)] * n
        + [jax.ShapeDtypeStruct((2, m_len, cols), jnp.bfloat16)] * n
        + [jax.ShapeDtypeStruct((2, PP, cols), jnp.float32)],
        compiler_params=pltpu.CompilerParams(vmem_limit_bytes=56 * MIB),
        cost_estimate=pl.CostEstimate(
            flops=12 * seq * mem * cols, bytes_accessed=20 * MIB, transcendentals=seq * mem * cols // 256
        ),
        name="attend_bwd_self" if causal else "attend_bwd_cross",
    )(lo, hi, *operands, ot, lt, ek, eq, prefix, ep)
    return result[:n], result[n:2 * n], result[2 * n]


def ranges(dec_seg, mem_seg, causal):
    seq = dec_seg.shape[0]
    blocks = dec_seg.reshape(seq // BQ, BQ)
    low, high = blocks[:, 0], blocks[:, -1]
    lo = jnp.sum((mem_seg[None, :] < low[:, None]).astype(jnp.int32), axis=1) // BK
    if causal:
        hi = jnp.arange(seq // BQ, dtype=jnp.int32)
    else:
        hi = (jnp.sum((mem_seg[None, :] <= high[:, None]).astype(jnp.int32), axis=1) + BK - 1) // BK
    return lo, hi


def mask_columns(dec_seg, mem_seg, prefix_count):
    lane = jnp.arange(128, dtype=jnp.int32)
    row = lane[:, None]
    ek = (mem_seg[:, None] == lane[None, :]).astype(jnp.bfloat16)
    differ = jnp.logical_and(row < DOCS, row != dec_seg[None, :])
    eq = jnp.where(jnp.logical_or(differ, row == DOCS), NEG, 0.0).astype(jnp.bfloat16)
    padding = jnp.arange(PP, dtype=jnp.int32)[:, None] >= prefix_count
    ep = jnp.logical_and(padding, lane[None, :] == DOCS).astype(jnp.bfloat16)
    return ek, eq, ep


def normalize(v):
    centered = v - jnp.mean(v, axis=-1, keepdims=True)
    r = lax.rsqrt(jnp.mean(centered * centered, axis=-1, keepdims=True) + 1e-05)
    return centered * r, r


def norm_back(n, r, gain, upstream):
    u = upstream * gain
    return r * (u - jnp.mean(u, axis=-1, keepdims=True) - n * jnp.mean(u * n, axis=-1, keepdims=True))


def gelu_parts(v):
    chance = 0.5 * (1.0 + lax.erf(v * math.sqrt(0.5)))
    slope = chance + v * (jnp.exp(-0.5 * v * v) * (1.0 / math.sqrt(2.0 * math.pi)))
    return v * chance, slope


def low(v):
    return v.astype(jnp.bfloat16)


def place_halves(own, other, held, sems, at):
    x = lax.axis_index("x")
    return [
        pltpu.make_async_copy(own, held.at[x], sems.at[at]),
        pltpu.make_async_copy(other, held.at[1 - x], sems.at[at + 1]),
    ]


def on_first(copies, act):
    @pl.when(pl.program_id(0) == 0)
    def _():
        for copy in copies:
            getattr(copy, act)()


def after_self_kernel(own_ref, par_ref, tok_ref, gains_ref, so_own, so_oth, cq_own, cq_oth,
                      first_ref, q_own_ref, q_par_ref, so, cq, sems):
    core = lax.axis_index("c")
    so_copies = place_halves(so_own, so_oth, so, sems, 0)
    cq_copies = place_halves(cq_own, cq_oth, cq, sems, 2)
    on_first(so_copies + cq_copies, "start")
    on_first(so_copies, "wait")
    total = tok_ref[...].astype(jnp.float32) + (mm(own_ref[...], so[core]) + mm(par_ref[...], so[1 - core]))
    first = low(total)
    first_ref[...] = first
    n, _ = normalize(first.astype(jnp.float32))
    normed = low(n * gains_ref[0:1, :])
    on_first(cq_copies, "wait")
    q_own_ref[...] = low(mm(normed, cq[core]))
    q_par_ref[...] = low(mm(normed, cq[1 - core]))


def rows_spec(width):
    return pl.BlockSpec((BT, width), lambda i: (i, 0))


ANY = pl.BlockSpec(memory_space=pl.ANY)


def after_self(own, par, tokens, gains, so_own, so_oth, cq_own, cq_oth):
    rows, d = tokens.shape
    half = d // 2
    return pl.pallas_call(
        after_self_kernel,
        grid=(rows // BT,),
        in_specs=[rows_spec(half), rows_spec(half), rows_spec(d), pl.BlockSpec((3, d), lambda i: (0, 0)), ANY, ANY, ANY, ANY],
        out_specs=[rows_spec(d), rows_spec(half), rows_spec(half)],
        out_shape=[
            jax.ShapeDtypeStruct((rows, d), jnp.bfloat16),
            jax.ShapeDtypeStruct((rows, half), jnp.bfloat16),
            jax.ShapeDtypeStruct((rows, half), jnp.bfloat16),
        ],
        scratch_shapes=[
            pltpu.VMEM((2, half, d), jnp.bfloat16),
            pltpu.VMEM((2, d, half), jnp.bfloat16),
            pltpu.SemaphoreType.DMA((4,)),
        ],
        compiler_params=pltpu.CompilerParams(vmem_limit_bytes=40 * MIB),
        cost_estimate=pl.CostEstimate(flops=4 * rows * d * d, bytes_accessed=12 * MIB, transcendentals=0),
        name="after_self",
    )(own, par, tokens, gains, so_own, so_oth, cq_own, cq_oth)


CHUNK = 512


def ffn_kernel(own_ref, par_ref, first_ref, cot_ref, gains_ref, down_ref, up_ref,
               co_own, co_oth, in_own, in_oth, out_own, out_oth,
               keep_ref, send_ref, gsec_ref, g_own_ref, g_par_ref, adapt_ref,
               co, w_in, w_out, slopes, acc, full, sems):
    core = lax.axis_index("c")
    x = lax.axis_index("x")
    half = keep_ref.shape[1]
    hidden_half = w_in.shape[2]
    chunks = 2 * hidden_half // CHUNK
    co_copies = place_halves(co_own, co_oth, co, sems, 0)
    in_copies = place_halves(in_own, in_oth, w_in, sems, 2)
    out_copies = place_halves(out_own, out_oth, w_out, sems, 4)
    on_first(co_copies + in_copies + out_copies, "start")

    @pl.when(pl.program_id(0) == 0)
    def _():
        adapt_ref[...] = jnp.zeros_like(adapt_ref)

    n_one, _ = normalize(first_ref[...].astype(jnp.float32))
    on_first(co_copies, "wait")
    cross = mm(own_ref[...], co[core]) + mm(par_ref[...], co[1 - core])
    second = low(n_one * gains_ref[0:1, :] + cross)
    n_two, r_two = normalize(second.astype(jnp.float32))
    normed_two = n_two * gains_ref[1:2, :]
    normed_low = low(normed_two)
    bottle_pre = mm(normed_low, down_ref[...])
    bottle, bottle_slope = gelu_parts(bottle_pre)
    bottle = low(bottle)
    acc[...] = normed_two + 4.0 * mm(bottle, up_ref[...])
    on_first(in_copies, "wait")
    on_first(out_copies, "wait")

    def up_step(t, _):
        which = t // (hidden_half // CHUNK)
        at = pl.ds(pl.multiple_of((t % (hidden_half // CHUNK)) * CHUNK, CHUNK), CHUNK)
        pre = mm(normed_low, w_in[which, :, at])
        hidden, slope = gelu_parts(pre)
        slopes[t] = slope
        acc[...] += mm(low(hidden), w_out[which, at, :])
        return 0

    lax.fori_loop(0, chunks, up_step, 0, unroll=2)
    third = low(acc[...])
    n_three, r_three = normalize(third.astype(jnp.float32))
    gain_three = gains_ref[2:3, :]
    full[...] = low(n_three * gain_three)
    keep_ref[...] = full[:, pl.ds(pl.multiple_of(x * half, half), half)]
    send_ref[...] = full[:, pl.ds(pl.multiple_of((1 - x) * half, half), half)]

    grad_three = norm_back(n_three, r_three, gain_three, cot_ref[...].astype(jnp.float32))
    branch = low(grad_three)
    adapted = low(4.0 * branch.astype(jnp.float32))
    bottle_grad = low(mm_nt(adapted, up_ref[...]) * bottle_slope)
    adapt_ref[0] += mm_tn(bottle_grad, normed_low)
    adapt_ref[1] += mm_tn(bottle, adapted)
    acc[...] = grad_three + mm_nt(bottle_grad, down_ref[...])

    def down_step(t, _):
        which = t // (hidden_half // CHUNK)
        at = pl.ds(pl.multiple_of((t % (hidden_half // CHUNK)) * CHUNK, CHUNK), CHUNK)
        grad_pre = low(mm_nt(branch, w_out[which, at, :]) * slopes[t])
        acc[...] += mm_nt(grad_pre, w_in[which, :, at])
        return 0

    lax.fori_loop(0, chunks, down_step, 0, unroll=2)
    grad_two = low(acc[...]).astype(jnp.float32)
    grad_second = norm_back(n_two, r_two, gains_ref[1:2, :], grad_two)
    gsec_ref[...] = grad_second
    second_low = low(grad_second)
    g_own_ref[...] = low(mm_nt(second_low, co[core]))
    g_par_ref[...] = low(mm_nt(second_low, co[1 - core]))


def ffn_both_ways(own, par, first, cot, gains, down, up, co_own, co_oth, in_own, in_oth, out_own, out_oth):
    rows, d = first.shape
    half = d // 2
    hidden_half = in_own.shape[1]
    bottleneck = down.shape[1]
    whole = lambda shape: pl.BlockSpec(shape, lambda i: (0,) * len(shape))
    flops = 2 * rows * d * (8 * hidden_half + 6 * bottleneck + 2 * d)
    return pl.pallas_call(
        ffn_kernel,
        grid=(rows // BT,),
        in_specs=[
            rows_spec(half), rows_spec(half), rows_spec(d), rows_spec(d),
            whole((3, d)), whole((d, bottleneck)), whole((bottleneck, d)),
            ANY, ANY, ANY, ANY, ANY, ANY,
        ],
        out_specs=[
            rows_spec(half), rows_spec(half), rows_spec(d), rows_spec(half), rows_spec(half),
            whole((2, bottleneck, d)),
        ],
        out_shape=[
            jax.ShapeDtypeStruct((rows, half), jnp.bfloat16),
            jax.ShapeDtypeStruct((rows, half), jnp.bfloat16),
            jax.ShapeDtypeStruct((rows, d), jnp.float32),
            jax.ShapeDtypeStruct((rows, half), jnp.bfloat16),
            jax.ShapeDtypeStruct((rows, half), jnp.bfloat16),
            jax.ShapeDtypeStruct((2, bottleneck, d), jnp.float32),
        ],
        scratch_shapes=[
            pltpu.VMEM((2, half, d), jnp.bfloat16),
            pltpu.VMEM((2, d, hidden_half), jnp.bfloat16),
            pltpu.VMEM((2, hidden_half, d), jnp.bfloat16),
            pltpu.VMEM((2 * hidden_half // CHUNK, BT, CHUNK), jnp.float32),
            pltpu.VMEM((BT, d), jnp.float32),
            pltpu.VMEM((BT, d), jnp.bfloat16),
            pltpu.SemaphoreType.DMA((6,)),
        ],
        compiler_params=pltpu.CompilerParams(vmem_limit_bytes=58 * MIB),
        cost_estimate=pl.CostEstimate(flops=flops, bytes_accessed=48 * MIB, transcendentals=0),
        name="ffn_both_ways",
    )(own, par, first, cot, gains, down, up, co_own, co_oth, in_own, in_oth, out_own, out_oth)


def before_self_kernel(gsec_ref, own_ref, par_ref, first_ref, gains_ref, so_own, so_oth, cq_own, cq_oth,
                       gfirst_ref, g_own_ref, g_par_ref, so, cq, sems):
    core = lax.axis_index("c")
    so_copies = place_halves(so_own, so_oth, so, sems, 0)
    cq_copies = place_halves(cq_own, cq_oth, cq, sems, 2)
    on_first(cq_copies + so_copies, "start")
    on_first(cq_copies, "wait")
    grad_one = low(gsec_ref[...] + (mm_nt(own_ref[...], cq[core]) + mm_nt(par_ref[...], cq[1 - core])))
    n, r = normalize(first_ref[...].astype(jnp.float32))
    grad_first = norm_back(n, r, gains_ref[0:1, :], grad_one.astype(jnp.float32))
    gfirst_ref[...] = grad_first
    first_low = low(grad_first)
    on_first(so_copies, "wait")
    g_own_ref[...] = low(mm_nt(first_low, so[core]))
    g_par_ref[...] = low(mm_nt(first_low, so[1 - core]))


def before_self(gsec, own, par, first, gains, so_own, so_oth, cq_own, cq_oth):
    rows, d = first.shape
    half = d // 2
    return pl.pallas_call(
        before_self_kernel,
        grid=(rows // BT,),
        in_specs=[
            rows_spec(d), rows_spec(half), rows_spec(half), rows_spec(d), pl.BlockSpec((3, d), lambda i: (0, 0)),
            ANY, ANY, ANY, ANY,
        ],
        out_specs=[rows_spec(d), rows_spec(half), rows_spec(half)],
        out_shape=[
            jax.ShapeDtypeStruct((rows, d), jnp.float32),
            jax.ShapeDtypeStruct((rows, half), jnp.bfloat16),
            jax.ShapeDtypeStruct((rows, half), jnp.bfloat16),
        ],
        scratch_shapes=[
            pltpu.VMEM((2, half, d), jnp.bfloat16),
            pltpu.VMEM((2, d, half), jnp.bfloat16),
            pltpu.SemaphoreType.DMA((4,)),
        ],
        compiler_params=pltpu.CompilerParams(vmem_limit_bytes=40 * MIB),
        cost_estimate=pl.CostEstimate(flops=4 * rows * d * d, bytes_accessed=16 * MIB, transcendentals=0),
        name="before_self",
    )(gsec, own, par, first, gains, so_own, so_oth, cq_own, cq_oth)


def swap(value, axis):
    return lax.ppermute(value, axis, SWAP)


def after(value, *others):
    return lax.optimization_barrier((value, *others))[0]


def other_half(weight):
    group = ("zl", "y", "c")
    count = math.prod(lax.axis_size(name) for name in group)
    piece = weight.shape[0] // count
    mine = lax.dynamic_slice_in_dim(weight, lax.axis_index(group) * piece, piece, 0)
    return swap(mine, "x")


def gather_half(piece):
    return lax.all_gather(piece, ("zl", "y", "c"), axis=0, tiled=True)


def bring_in(rows, agree):
    half = rows.shape[0] // 2
    core = lax.axis_index("c")
    keep = lax.dynamic_slice_in_dim(rows, core * half, half, 0)
    got = swap(lax.dynamic_slice_in_dim(rows, (1 - core) * half, half, 0), "c")
    return jnp.where(agree, keep, got), jnp.where(agree, got, keep)


def in_order(first_here, mine, others, axis):
    left = jnp.where(first_here, mine, others)
    right = jnp.where(first_here, others, mine)
    return jnp.concatenate([left, right], axis=axis)


def send_out(keep, send, agree):
    got = swap(send, "x")
    mine = jnp.where(agree, keep, got)
    passed = swap(jnp.where(agree, got, keep), "c")
    return in_order(lax.axis_index("c") == 0, mine, passed, 0)


def feature_halves(value):
    half = value.shape[1] // 2
    x = lax.axis_index("x")
    return lax.dynamic_slice_in_dim(value, x * half, half, 1), lax.dynamic_slice_in_dim(value, (1 - x) * half, half, 1)


def sum_over(value, axes):
    for name in axes:
        if lax.axis_size(name) == 2:
            value = value + swap(value, name)
        elif lax.axis_size(name) > 2:
            value = lax.psum(value, name)
    return value


def paired_device(
    tokens, memory, dec_segments, mem_segments, self_qkv, self_out, cross_q, cross_kv, cross_out, ffn_in, ffn_out,
    adapter_down, adapter_up, self_prefix, cross_prefix, gains, cotangent,
):
    x, core = lax.axis_index("x"), lax.axis_index("c")
    agree = x == core
    columns = tokens.shape[1]
    prefix_count = self_prefix.shape[1]

    qkv_flat = self_qkv.reshape(-1, columns)
    qkv_piece = other_half(qkv_flat)
    tok_mine, tok_send = bring_in(tokens, agree)
    mem_mine, mem_send = bring_in(memory, agree)
    cot_mine, cot_send = bring_in(cotangent, agree)
    segs = jnp.concatenate([dec_segments, mem_segments], axis=0)
    segs = jnp.where(agree, segs, swap(segs, "c"))
    dec_seg, mem_seg = segs[0], segs[1]
    prefixes = jnp.concatenate([self_prefix, cross_prefix], axis=0)
    prefixes = jnp.where(agree, prefixes, swap(prefixes, "x"))
    prefixes = jnp.pad(prefixes, ((0, 0), (0, PP - prefix_count), (0, 0)))
    self_pre, cross_pre = prefixes[:2], prefixes[2:]

    tok_got = swap(tok_send, "x")
    rows_own = in_order(x == 0, tok_mine, tok_got, 1)
    rows_par = swap(rows_own, "c")
    qkv_other = gather_half(qkv_piece)

    gate = tok_got
    mem_got = swap(after(mem_send, gate), "x")
    ckv_flat = cross_kv.reshape(-1, columns)
    ckv_other = gather_half(other_half(after(ckv_flat, gate)))
    so_other = gather_half(other_half(after(self_out, gate)))
    cq_other = gather_half(other_half(after(cross_q, gate)))
    co_other = gather_half(other_half(after(cross_out, gate)))

    self_masks = mask_columns(dec_seg, dec_seg, prefix_count)
    self_lo, self_hi = ranges(dec_seg, dec_seg, True)
    cross_masks = mask_columns(dec_seg, mem_seg, prefix_count)
    cross_lo, cross_hi = ranges(dec_seg, mem_seg, False)

    qkv_here = jnp.where(agree, qkv_flat, qkv_other).reshape(self_qkv.shape)
    qkv_there = jnp.where(agree, qkv_other, qkv_flat).reshape(self_qkv.shape)

    def project(rows, weights):
        return [low(mm(rows, weights[t])) for t in range(weights.shape[0])]

    own = project(rows_own, qkv_here)
    par = project(rows_par, qkv_here)
    self_q, self_k, self_v = ([(own[t], 0), (par[t], 0)] for t in range(3))
    self_o, self_ot, self_lt = attend_fwd(
        self_q, self_k, self_v, columns, self_masks, self_pre, self_lo, self_hi, True
    )
    heads_got = swap(self_o[1], "c")

    gate = (mem_got, heads_got)
    in_other = gather_half(other_half(after(ffn_in, *gate)))
    out_other = gather_half(other_half(after(ffn_out, *gate)))
    cot_got = swap(after(cot_send, *gate), "x")
    down_full = lax.all_gather(adapter_down.T, ("y", "c"), axis=0, tiled=True).T
    up_full = lax.all_gather(adapter_up, ("y", "c"), axis=0, tiled=True)

    mem_own = in_order(x == 0, mem_mine, mem_got, 1)
    mem_par = swap(mem_own, "c")
    ckv_here = jnp.where(agree, ckv_flat, ckv_other).reshape(cross_kv.shape)
    ckv_there = jnp.where(agree, ckv_other, ckv_flat).reshape(cross_kv.shape)
    first_sum, cq_own, cq_send = after_self(
        self_o[0], heads_got, rows_own, gains, self_out, so_other, cross_q, cq_other
    )
    cq_par = swap(cq_send, "c")
    own = project(mem_own, ckv_here)
    par = project(mem_par, ckv_here)
    cross_qp = [(cq_own, 0), (cq_par, 0)]
    cross_k, cross_v = ([(own[t], 0), (par[t], 0)] for t in range(2))
    cross_o, cross_ot, cross_lt = attend_fwd(
        cross_qp, cross_k, cross_v, columns, cross_masks, cross_pre, cross_lo, cross_hi, False
    )
    cross_got = swap(cross_o[1], "c")
    cot_own = in_order(x == 0, cot_mine, cot_got, 1)
    out_keep, out_send, grad_second, g_own, g_send, grad_adapt = ffn_both_ways(
        cross_o[0], cross_got, first_sum, cot_own, gains, down_full, up_full,
        cross_out, co_other, ffn_in, in_other, ffn_out, out_other,
    )
    g_par = swap(g_send, "c")
    output = send_out(out_keep, out_send, agree)

    n_y = lax.axis_size("y")
    block = grad_adapt.shape[1] // (2 * n_y)
    blocks = grad_adapt.reshape(2, n_y, 2, block, -1)
    part = lax.dynamic_index_in_dim(blocks, core, 2, False) + swap(
        lax.dynamic_index_in_dim(blocks, 1 - core, 2, False), "c"
    )
    if n_y == 2:
        y = lax.axis_index("y")
        part = lax.dynamic_index_in_dim(part, y, 1, False) + swap(
            low(lax.dynamic_index_in_dim(part, 1 - y, 1, False)), "y"
        ).astype(jnp.float32)
    else:
        part = lax.psum_scatter(part, "y", scatter_dimension=1, tiled=False)
    for name in ("zl", "zh", "x"):
        if lax.axis_size(name) == 2:
            part = low(part)
            part = part.astype(jnp.float32) + swap(part, name).astype(jnp.float32)
        elif lax.axis_size(name) > 2:
            part = lax.psum(part, name)
    grad_down, grad_up = part[0].T, part[1]

    cdq, cdkv, cross_dp = attend_bwd(
        cross_qp, cross_k, cross_v, [(g_own, 0), (g_par, 0)], columns, cross_ot, cross_lt,
        cross_masks, cross_pre, cross_lo, cross_hi, False,
    )
    cdq_got = swap(cdq[1], "c")
    cdkv_got = swap(cdkv[1], "c")
    grad_first, g_own, g_send = before_self(
        grad_second, cdq[0], cdq_got, first_sum, gains, self_out, so_other, cross_q, cq_other
    )
    g_par = swap(g_send, "c")

    def back(own, got, here, there):
        total = None
        for t in range(here.shape[0]):
            for rows, weight in ((own[t], here[t]), (got[t], there[t])):
                term = mm_nt(rows, weight)
                total = term if total is None else total + term
        return total

    grad_mem = low(back(cdkv[0], cdkv_got, ckv_here, ckv_there))
    mem_keep, mem_out = feature_halves(grad_mem)
    grad_memory = send_out(mem_keep, mem_out, agree).astype(jnp.float32)

    sdq, sdkv, self_dp = attend_bwd(
        self_q, self_k, self_v, [(g_own, 0), (g_par, 0)], columns, self_ot, self_lt,
        self_masks, self_pre, self_lo, self_hi, True,
    )
    sdq_got = swap(sdq[1], "c")
    sdkv_got = swap(sdkv[1], "c")
    grad_rows = low(
        grad_first
        + back(
            [sdq[0], sdkv[0][0], sdkv[0][1]], [sdq_got, sdkv_got[0], sdkv_got[1]], qkv_here, qkv_there
        )
    )
    tok_keep, tok_out = feature_halves(grad_rows)
    grad_tokens = send_out(tok_keep, tok_out, agree).astype(jnp.float32)

    def prefix_total(value):
        value = sum_over(value, ("zl", "y", "zh", "x"))
        return jnp.where(agree, value, swap(value, "c"))[:, :prefix_count]

    return (
        output, grad_tokens, grad_memory, prefix_total(self_dp), prefix_total(cross_dp), grad_down, grad_up,
    )


def norm_grad(gathered, gain, upstream):
    n, r = normalize(gathered.astype(jnp.float32))
    return norm_back(n, r, gain, upstream)


def wide_device(
    tokens, memory, dec_segments, mem_segments, self_qkv, self_out, cross_q, cross_kv, cross_out, ffn_in, ffn_out,
    adapter_down, adapter_up, self_prefix, cross_prefix, gains, cotangent,
):
    n_wide = lax.axis_size("wide")
    row_count, columns = tokens.shape
    own_start = lax.axis_index("wide") * columns
    block_size = row_count // n_wide
    block_start = lax.axis_index("wide") * block_size
    prefix_count = self_prefix.shape[1]
    dec_seg, mem_seg = dec_segments[0], mem_segments[0]

    def collect(values):
        return lax.all_gather(values, "wide", axis=1, tiled=True)

    def spread(term):
        return lax.psum_scatter(term, "wide", scatter_dimension=1, tiled=True)

    def own_columns(values):
        return lax.dynamic_slice_in_dim(values, own_start, columns, 1)

    def padded(prefix):
        return jnp.pad(prefix, ((0, 0), (0, PP - prefix_count), (0, 0)))

    self_masks = mask_columns(dec_seg, dec_seg, prefix_count)
    self_lo, self_hi = ranges(dec_seg, dec_seg, True)
    cross_masks = mask_columns(dec_seg, mem_seg, prefix_count)
    cross_lo, cross_hi = ranges(dec_seg, mem_seg, False)
    self_pre, cross_pre = padded(self_prefix), padded(cross_prefix)

    all_tokens, all_memory = collect(tokens), collect(memory)
    self_q, self_k, self_v = ([(low(mm(all_tokens, self_qkv[t])), 0)] for t in range(3))
    (self_heads,), self_ot, self_lt = attend_fwd(
        self_q, self_k, self_v, columns, self_masks, self_pre, self_lo, self_hi, True
    )
    first_sum = low(tokens.astype(jnp.float32) + spread(mm(self_heads, self_out)))
    gathered_one = collect(first_sum)
    normed_one = normalize(gathered_one.astype(jnp.float32))[0] * gains[0]
    cross_qp = [(low(mm(low(normed_one), cross_q)), 0)]
    cross_k, cross_v = ([(low(mm(all_memory, cross_kv[t])), 0)] for t in range(2))
    (cross_heads,), cross_ot, cross_lt = attend_fwd(
        cross_qp, cross_k, cross_v, columns, cross_masks, cross_pre, cross_lo, cross_hi, False
    )
    second_sum = low(own_columns(normed_one) + spread(mm(cross_heads, cross_out)))
    gathered_two = collect(second_sum)
    normed_two = normalize(gathered_two.astype(jnp.float32))[0] * gains[1]
    normed_low = low(normed_two)
    adapter_in = lax.dynamic_slice_in_dim(normed_low, block_start, block_size, 0)
    adapter_rows = lax.all_gather(adapter_in, "narrow", axis=0, tiled=True)
    bottle, bottle_slope = gelu_parts(mm(adapter_rows, adapter_down))
    bottle = low(bottle)
    adapted = lax.psum_scatter(low(mm(bottle, adapter_up)), "narrow", scatter_dimension=0, tiled=True)
    hidden, slope = gelu_parts(mm(normed_low, ffn_in))
    branch = mm(low(hidden), ffn_out)
    placed = lax.dynamic_slice_in_dim(branch, block_start, block_size, 0) + 4.0 * adapted.astype(jnp.float32)
    branch = lax.dynamic_update_slice_in_dim(branch, placed, block_start, 0)
    third_sum = low(own_columns(normed_two) + spread(branch))
    gathered_three = collect(third_sum)
    output = low(own_columns(normalize(gathered_three.astype(jnp.float32))[0] * gains[2]))
    grad_three = norm_grad(gathered_three, gains[2], collect(cotangent).astype(jnp.float32))
    grad_branch = low(grad_three)
    grad_pre = low(mm_nt(grad_branch, ffn_out) * slope)
    grad_normed = mm_nt(grad_pre, ffn_in)
    grad_adapted = low(4.0 * lax.dynamic_slice_in_dim(grad_branch, block_start, block_size, 0).astype(jnp.float32))
    grad_adapted = lax.all_gather(grad_adapted, "narrow", axis=0, tiled=True)
    bottle_grad = low(mm_nt(grad_adapted, adapter_up) * bottle_slope)
    grad_in = lax.psum_scatter(low(mm_nt(bottle_grad, adapter_down)), "narrow", scatter_dimension=0, tiled=True)
    placed = lax.dynamic_slice_in_dim(grad_normed, block_start, block_size, 0) + grad_in.astype(jnp.float32)
    grad_normed = lax.dynamic_update_slice_in_dim(grad_normed, placed, block_start, 0)
    grad_down, grad_up = lax.psum(
        (mm_tn(adapter_rows, bottle_grad), mm_tn(bottle, grad_adapted)), ("dp", "wide")
    )
    grad_two = collect(low(own_columns(grad_three) + spread(grad_normed))).astype(jnp.float32)
    grad_second = norm_grad(gathered_two, gains[1], grad_two)
    grad_cross = low(mm_nt(low(grad_second), cross_out))
    (cdq,), (cdkv,), cross_dp = attend_bwd(
        cross_qp, cross_k, cross_v, [(grad_cross, 0)], columns, cross_ot, cross_lt,
        cross_masks, cross_pre, cross_lo, cross_hi, False,
    )
    spread_one = spread(low(mm_nt(cdq, cross_q))).astype(jnp.float32)
    grad_memory = spread(low(mm_nt(cdkv[0], cross_kv[0]) + mm_nt(cdkv[1], cross_kv[1]))).astype(jnp.float32)
    grad_one = collect(low(own_columns(grad_second) + spread_one)).astype(jnp.float32)
    grad_first = norm_grad(gathered_one, gains[0], grad_one)
    grad_self = low(mm_nt(low(grad_first), self_out))
    (sdq,), (sdkv,), self_dp = attend_bwd(
        self_q, self_k, self_v, [(grad_self, 0)], columns, self_ot, self_lt,
        self_masks, self_pre, self_lo, self_hi, True,
    )
    grad_input = mm_nt(sdq, self_qkv[0]) + mm_nt(sdkv[0], self_qkv[1]) + mm_nt(sdkv[1], self_qkv[2])
    grad_tokens = own_columns(grad_first) + spread(grad_input)
    totals = lax.psum((low(self_dp), low(cross_dp)), ("dp", "narrow"))
    grad_self_prefix, grad_cross_prefix = (t.astype(jnp.float32)[:, :prefix_count] for t in totals)
    return (output, grad_tokens, grad_memory, grad_self_prefix, grad_cross_prefix, grad_down, grad_up)


def solution(mesh):
    dp, wide, narrow = (mesh.shape[name] for name in ("dp", "wide", "narrow"))
    if wide == 2 and narrow % 2 == 0:
        zl = 2 if dp % 2 == 0 else 1
        parts = Mesh(mesh.devices.reshape(dp // zl, zl, wide, narrow // 2, 2), ("zh", "zl", "x", "y", "c"))
        device, used = paired_device, parts
        rows, split, thin = ("zh", "zl", "y", "c"), "x", ("y", "c")
    else:
        device, used = wide_device, mesh
        rows, split, thin = ("dp", "narrow"), "wide", "narrow"
    return jax.shard_map(
        device,
        mesh=used,
        in_specs=(
            P(rows, split),
            P(rows, split),
            P(rows, None),
            P(rows, None),
            P(None, None, split),
            P(split, None),
            P(None, split),
            P(None, None, split),
            P(split, None),
            P(None, split),
            P(split, None),
            P(None, thin),
            P(thin, None),
            P(None, None, split),
            P(None, None, split),
            P(),
            P(rows, split),
        ),
        out_specs=(
            P(rows, split),
            P(rows, split),
            P(rows, split),
            P(None, None, split),
            P(None, None, split),
            P(None, thin),
            P(thin, None),
        ),
        check_vma=False,
    )
```

```python
import functools
import math
from functools import partial

import jax
import jax.numpy as jnp
from jax import lax
from jax.experimental import pallas as pl
from jax.experimental.pallas import tpu as pltpu
from jax.sharding import Mesh
from jax.sharding import PartitionSpec as P

HEAD_DIM = 64
DOCS = 4
NEG = -1e30
BQ = 256
BK = 256
PP = 32
BT = 256
HEADS_FWD = 8
HEADS_BWD = 4
SWAP = [(0, 1), (1, 0)]
MIB = 2**20


def mm(a, b):
    return jnp.dot(a, b, preferred_element_type=jnp.float32)


def mm_nt(a, b):
    return lax.dot_general(a, b, (((1,), (1,)), ((), ())), preferred_element_type=jnp.float32)


def mm_tn(a, b):
    return lax.dot_general(a, b, (((0,), (0,)), ((), ())), preferred_element_type=jnp.float32)


def pair_rows(t):
    zero = jnp.zeros((HEAD_DIM, t.shape[1]), t.dtype)
    return [
        jnp.concatenate([t[:HEAD_DIM], zero], axis=0),
        jnp.concatenate([zero, t[HEAD_DIM:]], axis=0),
    ]


def part_offsets(n_parts, part_len):
    if n_parts == 1:
        return [0]
    core = lax.axis_index("c")
    return [pl.multiple_of(core * part_len, part_len), pl.multiple_of((1 - core) * part_len, part_len)]


def fwd_kernel(causal, n_parts, lo_ref, hi_ref, *refs):
    q_parts, k_parts, v_parts = refs[:n_parts], refs[n_parts:2 * n_parts], refs[2 * n_parts:3 * n_parts]
    ek_ref, eq_ref, pre_ref, ep_ref = refs[3 * n_parts:3 * n_parts + 4]
    o_parts = refs[3 * n_parts + 4:4 * n_parts + 4]
    ot_ref, lt_ref, qt, vt, ke = refs[4 * n_parts + 4:]
    seq = qt.shape[1]
    q_len, m_len = q_parts[0].shape[0], k_parts[0].shape[0]
    width = q_parts[0].shape[1]
    n_pairs = width // 128
    heads_here = width // HEAD_DIM
    n_q = seq // BQ

    for q_ref, at in zip(q_parts, part_offsets(n_parts, q_len)):
        qt[:, pl.ds(at, q_len)] = (q_ref[...] * jnp.bfloat16(0.125)).T
    for k_ref, v_ref, at in zip(k_parts, v_parts, part_offsets(n_parts, m_len)):
        vt[:, pl.ds(at, m_len)] = v_ref[...].T
        for p in range(n_pairs):
            ke[p, pl.ds(at, m_len), :128] = k_ref[:, p * 128:(p + 1) * 128]
    for p in range(n_pairs):
        ke[p, :, 128:] = ek_ref[...]
    vpt = pre_ref[1].T
    ones = jnp.ones((16, BK), jnp.bfloat16)

    def q_step(i, _):
        qs = pl.ds(pl.multiple_of(i * BQ, BQ), BQ)
        eq = eq_ref[:, qs]
        heads = []
        for p in range(n_pairs):
            heads += [jnp.concatenate([r, eq], axis=0) for r in pair_rows(qt[p * 128:(p + 1) * 128, qs])]

        def block(j, carry, diag):
            ks = pl.ds(pl.multiple_of(j * BK, BK), BK)
            out = []
            scores = [mm(ke[h // 2, ks, :], heads[h]) for h in range(heads_here)]
            for h in range(heads_here):
                m, acc = carry[h]
                s = scores[h]
                if diag:
                    kk = lax.broadcasted_iota(jnp.int32, (BK, BQ), 0)
                    qq = lax.broadcasted_iota(jnp.int32, (BK, BQ), 1)
                    s = jnp.where(kk <= qq, s, NEG)
                m_new = jnp.maximum(m, jnp.max(s, axis=0, keepdims=True))
                p = jnp.exp(s - m_new).astype(jnp.bfloat16)
                vb = jnp.concatenate([vt[h * HEAD_DIM:(h + 1) * HEAD_DIM, ks], ones], axis=0)
                acc = acc * jnp.exp(m - m_new) + mm(vb, p)
                out.append((m_new, acc))
            return tuple(out)

        carry = []
        for h in range(heads_here):
            kp = jnp.concatenate([pre_ref[0, :, (h // 2) * 128:(h // 2 + 1) * 128], ep_ref[...]], axis=1)
            s = mm(kp, heads[h])
            m = jnp.max(s, axis=0, keepdims=True)
            p = jnp.exp(s - m).astype(jnp.bfloat16)
            vb = jnp.concatenate([vpt[h * HEAD_DIM:(h + 1) * HEAD_DIM], ones[:, :PP]], axis=0)
            carry.append((m, mm(vb, p)))
        carry = tuple(carry)
        if causal:
            carry = block(i, carry, True)
        carry = lax.fori_loop(lo_ref[i], hi_ref[i], lambda j, c: block(j, c, False), carry)
        outs = []
        for h in range(heads_here):
            m, acc = carry[h]
            total = acc[HEAD_DIM:HEAD_DIM + 1]
            lt_ref[h // 2, h % 2:h % 2 + 1, qs] = m + jnp.log(total)
            outs.append(acc[:HEAD_DIM] / total)
        ot = jnp.concatenate(outs, axis=0)
        ot_ref[:, qs] = ot.astype(jnp.bfloat16)
        o = ot.T.astype(jnp.bfloat16)
        store_part(o_parts, i, o)
        return 0

    lax.fori_loop(0, n_q, q_step, 0)


def store_part(parts, i, value):
    per_part = parts[0].shape[0] // BQ
    at = pl.ds(pl.multiple_of((i % per_part) * BQ, BQ), BQ)
    if len(parts) == 1:
        parts[0][at, :] = value
        return
    own = i // per_part == lax.axis_index("c")

    @pl.when(own)
    def _():
        parts[0][at, :] = value

    @pl.when(jnp.logical_not(own))
    def _():
        parts[1][at, :] = value


def attend_fwd(qs, ks, vs, cols, masks, prefix, lo, hi, causal):
    ek, eq, ep = masks
    n = len(qs)
    q_len, m_len = qs[0][0].shape[0], ks[0][0].shape[0]
    seq, mem = q_len * n, m_len * n
    wd = min(HEAD_DIM * HEADS_FWD, cols)
    steps = cols // wd
    in_specs, operands = [], []
    for group, length in ((qs, q_len), (ks, m_len), (vs, m_len)):
        for array, at in group:
            in_specs.append(pl.BlockSpec((length, wd), partial(lambda at, p, *_: (0, at * steps + p), at)))
            operands.append(array)
    in_specs += [
        pl.BlockSpec((mem, 128), lambda p, *_: (0, 0)),
        pl.BlockSpec((128, seq), lambda p, *_: (0, 0)),
        pl.BlockSpec((2, PP, wd), lambda p, *_: (0, 0, p)),
        pl.BlockSpec((PP, 128), lambda p, *_: (0, 0)),
    ]
    grid_spec = pltpu.PrefetchScalarGridSpec(
        num_scalar_prefetch=2,
        grid=(steps,),
        in_specs=in_specs,
        out_specs=[pl.BlockSpec((q_len, wd), lambda p, *_: (0, p))] * n
        + [
            pl.BlockSpec((wd, seq), lambda p, *_: (p, 0)),
            pl.BlockSpec((wd // 128, 2, seq), lambda p, *_: (p, 0, 0)),
        ],
        scratch_shapes=[
            pltpu.VMEM((wd, seq), jnp.bfloat16),
            pltpu.VMEM((wd, mem), jnp.bfloat16),
            pltpu.VMEM((wd // 128, mem, 256), jnp.bfloat16),
        ],
    )
    result = pl.pallas_call(
        functools.partial(fwd_kernel, causal, n),
        grid_spec=grid_spec,
        out_shape=[jax.ShapeDtypeStruct((q_len, cols), jnp.bfloat16)] * n
        + [
            jax.ShapeDtypeStruct((cols, seq), jnp.bfloat16),
            jax.ShapeDtypeStruct((cols // 128, 2, seq), jnp.float32),
        ],
        compiler_params=pltpu.CompilerParams(vmem_limit_bytes=58 * MIB),
        cost_estimate=pl.CostEstimate(
            flops=8 * seq * mem * cols, bytes_accessed=12 * MIB, transcendentals=seq * mem * cols // 256
        ),
        name="attend_fwd_self" if causal else "attend_fwd_cross",
    )(lo, hi, *operands, ek, eq, prefix, ep)
    return result[:n], result[n], result[n + 1]


def bwd_kernel(causal, n_parts, lo_ref, hi_ref, *refs):
    q_parts, k_parts, v_parts, g_parts = (refs[t * n_parts:(t + 1) * n_parts] for t in range(4))
    ot_ref, lt_ref, ek_ref, eq_ref, pre_ref, ep_ref = refs[4 * n_parts:4 * n_parts + 6]
    dq_parts = refs[4 * n_parts + 6:5 * n_parts + 6]
    dkv_parts = refs[5 * n_parts + 6:6 * n_parts + 6]
    dp_ref, qt, gt, kt, ke, vv, qm, gm, dk, dv, delta = refs[6 * n_parts + 6:]
    seq = qt.shape[1]
    q_len, m_len = q_parts[0].shape[0], k_parts[0].shape[0]
    width = q_parts[0].shape[1]
    n_pairs = width // 128
    heads_here = width // HEAD_DIM
    n_q = seq // BQ
    lane = lax.broadcasted_iota(jnp.int32, (1, width), 1)
    first = lane % 128 < HEAD_DIM
    zero = jnp.zeros((), jnp.bfloat16)

    for q_ref, g_ref, at in zip(q_parts, g_parts, part_offsets(n_parts, q_len)):
        here = pl.ds(at, q_len)
        q_all = q_ref[...] * jnp.bfloat16(0.125)
        g_all = g_ref[...]
        qt[:, here] = q_all.T
        g_turned = g_all.T
        gt[:, here] = g_turned
        qm[0, here, :] = jnp.where(first, q_all, zero)
        qm[1, here, :] = jnp.where(first, zero, q_all)
        gm[0, here, :] = jnp.where(first, g_all, zero)
        gm[1, here, :] = jnp.where(first, zero, g_all)
        prod = g_turned.astype(jnp.float32) * ot_ref[:, here].astype(jnp.float32)
        for h in range(heads_here):
            delta[h:h + 1, here] = jnp.sum(prod[h * HEAD_DIM:(h + 1) * HEAD_DIM], axis=0, keepdims=True)
    for k_ref, v_ref, at in zip(k_parts, v_parts, part_offsets(n_parts, m_len)):
        here = pl.ds(at, m_len)
        kt[:, here] = k_ref[...].T
        vv[here, :] = v_ref[...]
        for p in range(n_pairs):
            ke[p, here, :128] = k_ref[:, p * 128:(p + 1) * 128]
    for p in range(n_pairs):
        ke[p, :, 128:] = ek_ref[...]
    dk[...] = jnp.zeros_like(dk)
    dv[...] = jnp.zeros_like(dv)
    dp_ref[...] = jnp.zeros_like(dp_ref)
    kpt = pre_ref[0].T

    def q_step(i, _):
        qs = pl.ds(pl.multiple_of(i * BQ, BQ), BQ)
        eq = eq_ref[:, qs]
        q_heads, g_heads = [], []
        for p in range(n_pairs):
            q_heads += [jnp.concatenate([r, eq], axis=0) for r in pair_rows(qt[p * 128:(p + 1) * 128, qs])]
            g_heads += pair_rows(gt[p * 128:(p + 1) * 128, qs])
        lts = [lt_ref[h // 2, h % 2:h % 2 + 1, qs] for h in range(heads_here)]
        dls = [delta[h:h + 1, qs] for h in range(heads_here)]

        def grads(s, dp, h, diag):
            if diag:
                kk = lax.broadcasted_iota(jnp.int32, s.shape, 0)
                qq = lax.broadcasted_iota(jnp.int32, s.shape, 1)
                s = jnp.where(kk <= qq, s, NEG)
            p = jnp.exp(s - lts[h])
            ds = (p * (dp - dls[h])).astype(jnp.bfloat16)
            return p.astype(jnp.bfloat16), ds

        def block(j, carry, diag):
            ks = pl.ds(pl.multiple_of(j * BK, BK), BK)
            out, both = [], []
            for h in range(heads_here):
                c = (h // 2) * 128
                both.append((mm(ke[h // 2, ks, :], q_heads[h]), mm(vv[ks, c:c + 128], g_heads[h])))
            for pr in range(n_pairs):
                c = pr * 128
                dkb = dk[ks, c:c + 128]
                dvb = dv[ks, c:c + 128]
                for h in (2 * pr, 2 * pr + 1):
                    p, ds = grads(*both[h], h, diag)
                    dvb += mm(p, gm[h % 2, qs, c:c + 128])
                    dkb += mm(ds, qm[h % 2, qs, c:c + 128])
                    out.append(carry[h] + mm(kt[h * HEAD_DIM:(h + 1) * HEAD_DIM, ks], ds))
                dk[ks, c:c + 128] = dkb
                dv[ks, c:c + 128] = dvb
            return tuple(out)

        carry = []
        for h in range(heads_here):
            c = (h // 2) * 128
            kp = jnp.concatenate([pre_ref[0, :, c:c + 128], ep_ref[...]], axis=1)
            p, ds = grads(mm(kp, q_heads[h]), mm(pre_ref[1, :, c:c + 128], g_heads[h]), h, False)
            dp_ref[0, :, c:c + 128] += mm(ds, qm[h % 2, qs, c:c + 128])
            dp_ref[1, :, c:c + 128] += mm(p, gm[h % 2, qs, c:c + 128])
            carry.append(mm(kpt[h * HEAD_DIM:(h + 1) * HEAD_DIM], ds))
        carry = tuple(carry)
        if causal:
            carry = block(i, carry, True)
        carry = lax.fori_loop(lo_ref[i], hi_ref[i], lambda j, c: block(j, c, False), carry)
        dq = jnp.concatenate(carry, axis=0) * 0.125
        store_part(dq_parts, i, dq.T.astype(jnp.bfloat16))
        return 0

    lax.fori_loop(0, n_q, q_step, 0)
    for dkv_ref, at in zip(dkv_parts, part_offsets(n_parts, m_len)):
        here = pl.ds(at, m_len)
        dkv_ref[0] = dk[here, :].astype(jnp.bfloat16)
        dkv_ref[1] = dv[here, :].astype(jnp.bfloat16)


def attend_bwd(qs, ks, vs, gs, cols, ot, lt, masks, prefix, lo, hi, causal):
    ek, eq, ep = masks
    n = len(qs)
    q_len, m_len = qs[0][0].shape[0], ks[0][0].shape[0]
    seq, mem = q_len * n, m_len * n
    wd = min(HEAD_DIM * HEADS_BWD, cols)
    steps = cols // wd
    in_specs, operands = [], []
    for group, length in ((qs, q_len), (ks, m_len), (vs, m_len), (gs, q_len)):
        for array, at in group:
            in_specs.append(pl.BlockSpec((length, wd), partial(lambda at, p, *_: (0, at * steps + p), at)))
            operands.append(array)
    in_specs += [
        pl.BlockSpec((wd, seq), lambda p, *_: (p, 0)),
        pl.BlockSpec((wd // 128, 2, seq), lambda p, *_: (p, 0, 0)),
        pl.BlockSpec((mem, 128), lambda p, *_: (0, 0)),
        pl.BlockSpec((128, seq), lambda p, *_: (0, 0)),
        pl.BlockSpec((2, PP, wd), lambda p, *_: (0, 0, p)),
        pl.BlockSpec((PP, 128), lambda p, *_: (0, 0)),
    ]
    grid_spec = pltpu.PrefetchScalarGridSpec(
        num_scalar_prefetch=2,
        grid=(steps,),
        in_specs=in_specs,
        out_specs=[pl.BlockSpec((q_len, wd), lambda p, *_: (0, p))] * n
        + [pl.BlockSpec((2, m_len, wd), lambda p, *_: (0, 0, p))] * n
        + [pl.BlockSpec((2, PP, wd), lambda p, *_: (0, 0, p))],
        scratch_shapes=[
            pltpu.VMEM((wd, seq), jnp.bfloat16),
            pltpu.VMEM((wd, seq), jnp.bfloat16),
            pltpu.VMEM((wd, mem), jnp.bfloat16),
            pltpu.VMEM((wd // 128, mem, 256), jnp.bfloat16),
            pltpu.VMEM((mem, wd), jnp.bfloat16),
            pltpu.VMEM((2, seq, wd), jnp.bfloat16),
            pltpu.VMEM((2, seq, wd), jnp.bfloat16),
            pltpu.VMEM((mem, wd), jnp.float32),
            pltpu.VMEM((mem, wd), jnp.float32),
            pltpu.VMEM((8, seq), jnp.float32),
        ],
    )
    result = pl.pallas_call(
        functools.partial(bwd_kernel, causal, n),
        grid_spec=grid_spec,
        out_shape=[jax.ShapeDtypeStruct((q_len, cols), jnp.bfloat16)] * n
        + [jax.ShapeDtypeStruct((2, m_len, cols), jnp.bfloat16)] * n
        + [jax.ShapeDtypeStruct((2, PP, cols), jnp.float32)],
        compiler_params=pltpu.CompilerParams(vmem_limit_bytes=58 * MIB),
        cost_estimate=pl.CostEstimate(
            flops=12 * seq * mem * cols, bytes_accessed=20 * MIB, transcendentals=seq * mem * cols // 256
        ),
        name="attend_bwd_self" if causal else "attend_bwd_cross",
    )(lo, hi, *operands, ot, lt, ek, eq, prefix, ep)
    return result[:n], result[n:2 * n], result[2 * n]


def ranges(dec_seg, mem_seg, causal):
    seq = dec_seg.shape[0]
    blocks = dec_seg.reshape(seq // BQ, BQ)
    low, high = blocks[:, 0], blocks[:, -1]
    lo = jnp.sum((mem_seg[None, :] < low[:, None]).astype(jnp.int32), axis=1) // BK
    if causal:
        hi = jnp.arange(seq // BQ, dtype=jnp.int32)
    else:
        hi = (jnp.sum((mem_seg[None, :] <= high[:, None]).astype(jnp.int32), axis=1) + BK - 1) // BK
    return lo, hi


def mask_columns(dec_seg, mem_seg, prefix_count):
    lane = jnp.arange(128, dtype=jnp.int32)
    row = lane[:, None]
    ek = (mem_seg[:, None] == lane[None, :]).astype(jnp.bfloat16)
    differ = jnp.logical_and(row < DOCS, row != dec_seg[None, :])
    eq = jnp.where(jnp.logical_or(differ, row == DOCS), NEG, 0.0).astype(jnp.bfloat16)
    padding = jnp.arange(PP, dtype=jnp.int32)[:, None] >= prefix_count
    ep = jnp.logical_and(padding, lane[None, :] == DOCS).astype(jnp.bfloat16)
    return ek, eq, ep


def normalize(v):
    centered = v - jnp.mean(v, axis=-1, keepdims=True)
    r = lax.rsqrt(jnp.mean(centered * centered, axis=-1, keepdims=True) + 1e-05)
    return centered * r, r


def norm_back(n, r, gain, upstream):
    u = upstream * gain
    return r * (u - jnp.mean(u, axis=-1, keepdims=True) - n * jnp.mean(u * n, axis=-1, keepdims=True))


def gelu_parts(v):
    chance = 0.5 * (1.0 + lax.erf(v * math.sqrt(0.5)))
    slope = chance + v * (jnp.exp(-0.5 * v * v) * (1.0 / math.sqrt(2.0 * math.pi)))
    return v * chance, slope


def low(v):
    return v.astype(jnp.bfloat16)


def place_halves(own, other, held, sems, at):
    x = lax.axis_index("x")
    return [
        pltpu.make_async_copy(own, held.at[x], sems.at[at]),
        pltpu.make_async_copy(other, held.at[1 - x], sems.at[at + 1]),
    ]


def on_first(copies, act):
    @pl.when(pl.program_id(0) == 0)
    def _():
        for copy in copies:
            getattr(copy, act)()


def after_self_kernel(own_ref, par_ref, tok_ref, gains_ref, so_own, so_oth, cq_own, cq_oth,
                      first_ref, q_own_ref, q_par_ref, so, cq, sems):
    core = lax.axis_index("c")
    so_copies = place_halves(so_own, so_oth, so, sems, 0)
    cq_copies = place_halves(cq_own, cq_oth, cq, sems, 2)
    on_first(so_copies + cq_copies, "start")
    on_first(so_copies, "wait")
    total = tok_ref[...].astype(jnp.float32) + (mm(own_ref[...], so[core]) + mm(par_ref[...], so[1 - core]))
    first = low(total)
    first_ref[...] = first
    n, _ = normalize(first.astype(jnp.float32))
    normed = low(n * gains_ref[0:1, :])
    on_first(cq_copies, "wait")
    q_own_ref[...] = low(mm(normed, cq[core]))
    q_par_ref[...] = low(mm(normed, cq[1 - core]))


def rows_spec(width):
    return pl.BlockSpec((BT, width), lambda i: (i, 0))


ANY = pl.BlockSpec(memory_space=pl.ANY)


def after_self(own, par, tokens, gains, so_own, so_oth, cq_own, cq_oth):
    rows, d = tokens.shape
    half = d // 2
    return pl.pallas_call(
        after_self_kernel,
        grid=(rows // BT,),
        in_specs=[rows_spec(half), rows_spec(half), rows_spec(d), pl.BlockSpec((3, d), lambda i: (0, 0)), ANY, ANY, ANY, ANY],
        out_specs=[rows_spec(d), rows_spec(half), rows_spec(half)],
        out_shape=[
            jax.ShapeDtypeStruct((rows, d), jnp.bfloat16),
            jax.ShapeDtypeStruct((rows, half), jnp.bfloat16),
            jax.ShapeDtypeStruct((rows, half), jnp.bfloat16),
        ],
        scratch_shapes=[
            pltpu.VMEM((2, half, d), jnp.bfloat16),
            pltpu.VMEM((2, d, half), jnp.bfloat16),
            pltpu.SemaphoreType.DMA((4,)),
        ],
        compiler_params=pltpu.CompilerParams(vmem_limit_bytes=58 * MIB),
        cost_estimate=pl.CostEstimate(flops=4 * rows * d * d, bytes_accessed=12 * MIB, transcendentals=0),
        name="after_self",
    )(own, par, tokens, gains, so_own, so_oth, cq_own, cq_oth)


CHUNK = 512


def ffn_kernel(own_ref, par_ref, first_ref, cot_mine_ref, cot_got_ref, gains_ref, down_ref, up_ref,
               co_own, co_oth, in_own, out_own, ffn_other,
               keep_ref, send_ref, gsec_ref, g_own_ref, g_par_ref, adapt_ref,
               co, w_in, w_out, slopes, acc, full, sems):
    core = lax.axis_index("c")
    x = lax.axis_index("x")
    half = keep_ref.shape[1]
    hidden_half = w_in.shape[3]
    d = full.shape[1]
    chunks = 2 * hidden_half // CHUNK
    co_copies = place_halves(co_own, co_oth, co, sems, 0)
    in_copies = [pltpu.make_async_copy(in_own, w_in.at[x], sems.at[2])]
    out_copies = [pltpu.make_async_copy(out_own, w_out.at[x], sems.at[3])]
    at = 0
    for held, copies in ((w_in, in_copies), (w_out, out_copies)):
        tall, wide = held.shape[2:]
        for j in range(wide // half):
            copies.append(
                pltpu.make_async_copy(
                    ffn_other.at[:, pl.ds(at, tall)], held.at[1 - x, :, :, pl.ds(j * half, half)], sems.at[4 + len(copies) + 4 * (held is w_out)]
                )
            )
            at += tall
    on_first(co_copies + in_copies + out_copies, "start")

    @pl.when(pl.program_id(0) == 0)
    def _():
        adapt_ref[...] = jnp.zeros_like(adapt_ref)

    n_one, _ = normalize(first_ref[...].astype(jnp.float32))
    on_first(co_copies, "wait")
    cross = mm(own_ref[...], co[core]) + mm(par_ref[...], co[1 - core])
    second = low(n_one * gains_ref[0:1, :] + cross)
    n_two, r_two = normalize(second.astype(jnp.float32))
    normed_two = n_two * gains_ref[1:2, :]
    normed_low = low(normed_two)
    bottle_pre = mm(normed_low, down_ref[...])
    bottle, bottle_slope = gelu_parts(bottle_pre)
    bottle = low(bottle)
    acc[...] = normed_two + 4.0 * mm(bottle, up_ref[...])
    on_first(in_copies, "wait")
    on_first(out_copies, "wait")

    tall_out = w_out.shape[2]

    def tall_at(t):
        return (t % (hidden_half // CHUNK)) * (CHUNK // tall_out)

    def up_step(t, _):
        which = t // (hidden_half // CHUNK)
        at = pl.ds(pl.multiple_of((t % (hidden_half // CHUNK)) * CHUNK, CHUNK), CHUNK)
        pre = mm(normed_low, w_in[which, :, :, at].reshape(d, CHUNK))
        hidden, slope = gelu_parts(pre)
        slopes[t] = slope
        acc[...] += mm(low(hidden), w_out[which, pl.ds(tall_at(t), CHUNK // tall_out)].reshape(CHUNK, d))
        return 0

    lax.fori_loop(0, chunks, up_step, 0, unroll=2)
    third = low(acc[...])
    n_three, r_three = normalize(third.astype(jnp.float32))
    gain_three = gains_ref[2:3, :]
    full[...] = low(n_three * gain_three)
    keep_ref[...] = full[:, pl.ds(pl.multiple_of(x * half, half), half)]
    send_ref[...] = full[:, pl.ds(pl.multiple_of((1 - x) * half, half), half)]

    full[:, pl.ds(pl.multiple_of(x * half, half), half)] = cot_mine_ref[...]
    full[:, pl.ds(pl.multiple_of((1 - x) * half, half), half)] = cot_got_ref[...]
    grad_three = norm_back(n_three, r_three, gain_three, full[...].astype(jnp.float32))
    branch = low(grad_three)
    adapted = low(4.0 * branch.astype(jnp.float32))
    bottle_grad = low(mm_nt(adapted, up_ref[...]) * bottle_slope)
    adapt_ref[0] += mm_tn(bottle_grad, normed_low)
    adapt_ref[1] += mm_tn(bottle, adapted)
    acc[...] = grad_three + mm_nt(bottle_grad, down_ref[...])

    def down_step(t, _):
        which = t // (hidden_half // CHUNK)
        at = pl.ds(pl.multiple_of((t % (hidden_half // CHUNK)) * CHUNK, CHUNK), CHUNK)
        grad_pre = low(mm_nt(branch, w_out[which, pl.ds(tall_at(t), CHUNK // tall_out)].reshape(CHUNK, d)) * slopes[t])
        acc[...] += mm_nt(grad_pre, w_in[which, :, :, at].reshape(d, CHUNK))
        return 0

    lax.fori_loop(0, chunks, down_step, 0, unroll=2)
    grad_two = low(acc[...]).astype(jnp.float32)
    grad_second = norm_back(n_two, r_two, gains_ref[1:2, :], grad_two)
    gsec_ref[...] = grad_second
    second_low = low(grad_second)
    g_own_ref[...] = low(mm_nt(second_low, co[core]))
    g_par_ref[...] = low(mm_nt(second_low, co[1 - core]))


def ffn_both_ways(own, par, first, cot_mine, cot_got, gains, down, up, co_own, co_oth, in_own, out_own, ffn_other):
    rows, d = first.shape
    half = d // 2
    hidden_half = in_own.shape[1]
    in_own = in_own.reshape(8, d // 8, hidden_half)
    out_own = out_own.reshape(8, hidden_half // 8, d)
    bottleneck = down.shape[1]
    whole = lambda shape: pl.BlockSpec(shape, lambda i: (0,) * len(shape))
    flops = 2 * rows * d * (8 * hidden_half + 6 * bottleneck + 2 * d)
    return pl.pallas_call(
        ffn_kernel,
        grid=(rows // BT,),
        in_specs=[
            rows_spec(half), rows_spec(half), rows_spec(d), rows_spec(half), rows_spec(half),
            whole((3, d)), whole((d, bottleneck)), whole((bottleneck, d)),
            ANY, ANY, ANY, ANY, ANY,
        ],
        out_specs=[
            rows_spec(half), rows_spec(half), rows_spec(d), rows_spec(half), rows_spec(half),
            whole((2, bottleneck, d)),
        ],
        out_shape=[
            jax.ShapeDtypeStruct((rows, half), jnp.bfloat16),
            jax.ShapeDtypeStruct((rows, half), jnp.bfloat16),
            jax.ShapeDtypeStruct((rows, d), jnp.float32),
            jax.ShapeDtypeStruct((rows, half), jnp.bfloat16),
            jax.ShapeDtypeStruct((rows, half), jnp.bfloat16),
            jax.ShapeDtypeStruct((2, bottleneck, d), jnp.float32),
        ],
        scratch_shapes=[
            pltpu.VMEM((2, half, d), jnp.bfloat16),
            pltpu.VMEM((2, *in_own.shape), jnp.bfloat16),
            pltpu.VMEM((2, *out_own.shape), jnp.bfloat16),
            pltpu.VMEM((2 * hidden_half // CHUNK, BT, CHUNK), jnp.float32),
            pltpu.VMEM((BT, d), jnp.float32),
            pltpu.VMEM((BT, d), jnp.bfloat16),
            pltpu.SemaphoreType.DMA((16,)),
        ],
        compiler_params=pltpu.CompilerParams(vmem_limit_bytes=58 * MIB),
        cost_estimate=pl.CostEstimate(flops=flops, bytes_accessed=48 * MIB, transcendentals=0),
        name="ffn_both_ways",
    )(own, par, first, cot_mine, cot_got, gains, down, up, co_own, co_oth, in_own, out_own, ffn_other)


def before_self_kernel(gsec_ref, own_ref, par_ref, first_ref, gains_ref, so_own, so_oth, cq_own, cq_oth,
                       gfirst_ref, g_own_ref, g_par_ref, so, cq, sems):
    core = lax.axis_index("c")
    so_copies = place_halves(so_own, so_oth, so, sems, 0)
    cq_copies = place_halves(cq_own, cq_oth, cq, sems, 2)
    on_first(cq_copies + so_copies, "start")
    on_first(cq_copies, "wait")
    grad_one = low(gsec_ref[...] + (mm_nt(own_ref[...], cq[core]) + mm_nt(par_ref[...], cq[1 - core])))
    n, r = normalize(first_ref[...].astype(jnp.float32))
    grad_first = norm_back(n, r, gains_ref[0:1, :], grad_one.astype(jnp.float32))
    gfirst_ref[...] = grad_first
    first_low = low(grad_first)
    on_first(so_copies, "wait")
    g_own_ref[...] = low(mm_nt(first_low, so[core]))
    g_par_ref[...] = low(mm_nt(first_low, so[1 - core]))


def before_self(gsec, own, par, first, gains, so_own, so_oth, cq_own, cq_oth):
    rows, d = first.shape
    half = d // 2
    return pl.pallas_call(
        before_self_kernel,
        grid=(rows // BT,),
        in_specs=[
            rows_spec(d), rows_spec(half), rows_spec(half), rows_spec(d), pl.BlockSpec((3, d), lambda i: (0, 0)),
            ANY, ANY, ANY, ANY,
        ],
        out_specs=[rows_spec(d), rows_spec(half), rows_spec(half)],
        out_shape=[
            jax.ShapeDtypeStruct((rows, d), jnp.float32),
            jax.ShapeDtypeStruct((rows, half), jnp.bfloat16),
            jax.ShapeDtypeStruct((rows, half), jnp.bfloat16),
        ],
        scratch_shapes=[
            pltpu.VMEM((2, half, d), jnp.bfloat16),
            pltpu.VMEM((2, d, half), jnp.bfloat16),
            pltpu.SemaphoreType.DMA((4,)),
        ],
        compiler_params=pltpu.CompilerParams(vmem_limit_bytes=58 * MIB),
        cost_estimate=pl.CostEstimate(flops=4 * rows * d * d, bytes_accessed=16 * MIB, transcendentals=0),
        name="before_self",
    )(gsec, own, par, first, gains, so_own, so_oth, cq_own, cq_oth)


MESH_ID = pl.DeviceIdType.MESH
PARTS_IN = 4


def greet(targets):
    barrier = pltpu.get_barrier_semaphore()
    for target in targets:
        pl.semaphore_signal(barrier, inc=1, device_id=target, device_id_type=MESH_ID)
    pl.semaphore_wait(barrier, len(targets))


def remote(src, dst, send, recv, target):
    return pltpu.make_async_remote_copy(
        src_ref=src, dst_ref=dst, send_sem=send, recv_sem=recv, device_id=target, device_id_type=MESH_ID
    )


def eighth_index():
    return (lax.axis_index("zl") * 2 + lax.axis_index("y")) * 2 + lax.axis_index("c")


def piece_copies(wholes, pieces, send, recv, at):
    index = eighth_index()
    copies = []
    for n, (whole, piece) in enumerate(zip(wholes, pieces)):
        rows = piece.shape[0]
        source = whole.at[pl.ds(pl.multiple_of(index * rows, rows), rows)]
        copies.append(remote(source, piece, send.at[at + n], recv.at[at + n], {"x": 1 - lax.axis_index("x")}))
    return copies


def piece_shapes(weights):
    return [jax.ShapeDtypeStruct((w.shape[0] // 8, w.shape[1]), w.dtype) for w in weights]


def bring_kernel(tok, mem, cot, qkv, prefix, segs, w_in, w_out, *refs):
    wholes, pieces = refs[:2], refs[11:13]
    rows_own, rows_par, mem_mine, packed, cot_mine, cot_send, qkv_oth, prefix_got, segs_got = refs[2:11]
    stage, send, recv, load = refs[13:]
    x, y, zl, core = (lax.axis_index(name) for name in ("x", "y", "zl", "c"))
    half = rows_own.shape[0]
    cols = tok.shape[1]
    chunk = half // PARTS_IN
    piece = qkv.shape[0] // 8
    stays = x == core
    partner = {"c": 1 - core}
    across = {"x": 1 - x}

    def token_half(which):
        return pl.ds(pl.multiple_of(which * half, half), half)

    loads = [
        pltpu.make_async_copy(source.at[token_half(which)], stage.at[n], load.at[n])
        for n, (source, which) in enumerate(((tok, core), (tok, 1 - core), (mem, core), (cot, core)))
    ]
    at = 0
    for whole in (w_in, w_out):
        tall, wide = whole.shape[0] // 8, whole.shape[1]
        source = pl.ds(pl.multiple_of(eighth_index() * tall, tall), tall)
        for j in range(wide // cols):
            n = len(loads)
            loads.append(
                pltpu.make_async_copy(
                    whole.at[source, pl.ds(j * cols, cols)], stage.at[4, pl.ds(at, tall)], load.at[n]
                )
            )
            at += tall
    pack = pltpu.make_async_copy(stage.at[4], packed.at[pl.ds(half, half)], load.at[len(loads)])
    mem_send = packed.at[pl.ds(0, half)]
    for copy in loads:
        copy.start()
    greet([across, {"x": 1 - x, "c": 1 - core}, {"y": 1 - y}, {"zl": 1 - zl}, partner])

    def features(which):
        return pl.ds(pl.multiple_of(which * cols, cols), cols)

    def part(k):
        return pl.ds(k * chunk, chunk)

    def eighth(a, b, c):
        return pl.ds(pl.multiple_of(((a * 2 + b) * 2 + c) * piece, piece), piece)

    def weight(at, slot, target, source=None):
        return remote((qkv_oth if source is None else source).at[at], qkv_oth.at[at], send.at[slot], recv.at[slot], target)

    mine = eighth(zl, y, core)
    w_x = weight(mine, 0, across, qkv)
    w_x.start()
    at_small = 14 + 3 * PARTS_IN
    small = [
        remote(prefix, prefix_got, send.at[at_small], recv.at[at_small], across),
        remote(segs, segs_got, send.at[at_small + 1], recv.at[at_small + 1], partner),
    ]
    for copy in small:
        copy.start()
    others = small + piece_copies(wholes, pieces, send, recv, at_small + 2)

    at_own, at_par = 8, 8 + PARTS_IN
    at_here = 8 + 2 * PARTS_IN

    def token_sends():
        copies = []
        for t in range(2):
            for k in range(PARTS_IN):
                slot = at_own + k
                copies.append(
                    remote(
                        tok.at[pl.ds(t * half + k * chunk, chunk)],
                        rows_own.at[part(k), features(x)],
                        send.at[slot + t * PARTS_IN],
                        recv.at[slot],
                        {"x": 1 - x, "c": t},
                    )
                )
        return copies

    def here_copies():
        own = tok.at[token_half(core)]
        other = tok.at[token_half(1 - core)]
        return [
            remote(other, rows_own.at[:, features(x)], send.at[at_here], recv.at[at_here], partner),
            remote(own, rows_par.at[:, features(x)], send.at[at_here + 1], recv.at[at_here + 1], partner),
        ]

    def row_copy(source, to, slot):
        return remote(source.at[token_half(1 - core)], to, send.at[slot], recv.at[slot], partner)

    @pl.when(jnp.logical_not(stays))
    def _():
        for copy in token_sends():
            copy.start()
        row_copy(mem, mem_send, at_here + 3).start()
        row_copy(cot, cot_send, at_here + 5).start()
        for n, to, slot in ((2, mem_send, at_here + 3), (3, cot_send, at_here + 5)):
            loads[n].wait()
            pltpu.make_async_copy(stage.at[n], to, recv.at[slot]).start()
        loads[0].wait()
        loads[1].wait()

    @pl.when(stays)
    def _():
        for copy in here_copies():
            copy.start()
        row_copy(mem, mem_mine, at_here + 2).start()
        row_copy(cot, cot_mine, at_here + 4).start()
        for n, to, slot in (
            (0, rows_own.at[:, features(x)], at_here),
            (1, rows_par.at[:, features(x)], at_here + 1),
            (2, mem_mine, at_here + 2),
            (3, cot_mine, at_here + 4),
        ):
            loads[n].wait()
            pltpu.make_async_copy(stage.at[n], to, recv.at[slot]).start()

    for copy in others[2:]:
        copy.start()

    for copy in loads[4:]:
        copy.wait()
    pack.start()

    w_x.wait_recv()
    w_y = weight(mine, 1, {"y": 1 - y})
    w_z = weight(mine, 2, {"zl": 1 - zl})
    w_c = weight(mine, 4, partner)
    for copy in (w_y, w_z, w_c):
        copy.start()

    forwards = []

    def forward(k):
        here = rows_own.at[part(k), features(1 - x)]
        remote(here, here, send.at[at_own + k], recv.at[at_own + k], across).wait_recv()
        copy = remote(here, rows_par.at[part(k), features(1 - x)], send.at[at_here + 6 + k], recv.at[at_par + k], partner)
        copy.start()
        forwards.append(copy)

    forward(0)
    w_y.wait_recv()
    from_y = eighth(zl, 1 - y, core)
    w_yz = weight(from_y, 3, {"zl": 1 - zl})
    w_yc = weight(from_y, 5, partner)
    w_yz.start()
    w_yc.start()
    forward(1)
    w_z.wait_recv()
    w_zc = weight(eighth(1 - zl, y, core), 6, partner)
    w_zc.start()
    for k in range(2, PARTS_IN):
        forward(k)
    w_yz.wait_recv()
    w_yzc = weight(eighth(1 - zl, 1 - y, core), 7, partner)
    w_yzc.start()

    for copy in (w_c, w_yc, w_zc, w_yzc, *others):
        copy.wait_recv()
    for k, copy in enumerate(forwards):
        copy.wait_recv()
    for to, slot in (
        (rows_own.at[:, features(x)], at_here),
        (rows_par.at[:, features(x)], at_here + 1),
        (mem_mine, at_here + 2),
        (mem_send, at_here + 3),
        (cot_mine, at_here + 4),
        (cot_send, at_here + 5),
    ):
        remote(to, to, send.at[slot], recv.at[slot], partner).wait_recv()

    pack.wait()

    for copy in (w_x, w_y, w_z, w_c, w_yz, w_yc, w_zc, w_yzc, *forwards, *others):
        copy.wait_send()

    @pl.when(jnp.logical_not(stays))
    def _():
        for copy in token_sends():
            copy.wait_send()
        row_copy(mem, mem_send, at_here + 3).wait_send()
        row_copy(cot, cot_send, at_here + 5).wait_send()

    @pl.when(stays)
    def _():
        for copy in here_copies():
            copy.wait_send()
        row_copy(mem, mem_mine, at_here + 2).wait_send()
        row_copy(cot, cot_mine, at_here + 4).wait_send()


def bring_rows(tokens, memory, cotangent, qkv_flat, prefixes, segs, ffn_in, ffn_out, weights):
    rows, cols = tokens.shape
    half = rows // 2
    wide_rows = jax.ShapeDtypeStruct((half, 2 * cols), jnp.bfloat16)
    thin_rows = jax.ShapeDtypeStruct((half, cols), jnp.bfloat16)
    slots = 16 + 3 * PARTS_IN + len(weights)
    return pl.pallas_call(
        bring_kernel,
        in_specs=[ANY] * 10,
        out_specs=[ANY] * 11,
        out_shape=[wide_rows, wide_rows, thin_rows, jax.ShapeDtypeStruct((rows, cols), jnp.bfloat16), thin_rows, thin_rows,
                   jax.ShapeDtypeStruct(qkv_flat.shape, jnp.bfloat16),
                   jax.ShapeDtypeStruct(prefixes.shape, prefixes.dtype),
                   jax.ShapeDtypeStruct(segs.shape, segs.dtype)] + piece_shapes(weights),
        scratch_shapes=[
            pltpu.VMEM((5, half, cols), jnp.bfloat16),
            pltpu.SemaphoreType.DMA((slots,)),
            pltpu.SemaphoreType.DMA((slots,)),
            pltpu.SemaphoreType.DMA((16,)),
        ],
        compiler_params=pltpu.CompilerParams(collective_id=0, has_side_effects=True, vmem_limit_bytes=58 * MIB),
        cost_estimate=pl.CostEstimate(flops=0, bytes_accessed=64 * MIB, transcendentals=0),
        name="bring_rows",
    )(tokens, memory, cotangent, qkv_flat, prefixes, segs, ffn_in, ffn_out, *weights)


def project_kernel(n_weights, n_pieces, n_passed, *refs):
    own, par = refs[:n_pieces], refs[n_pieces:2 * n_pieces]
    refs = refs[2 * n_pieces:]
    w_own, w_oth, wholes = refs[0], refs[1], refs[2:2 + n_passed]
    out_own, out_par, passed = refs[2 + n_passed], refs[3 + n_passed], refs[4 + n_passed:4 + 2 * n_passed]
    held, sems = refs[4 + 2 * n_passed:6 + 2 * n_passed]
    x, core = lax.axis_index("x"), lax.axis_index("c")
    d = held.shape[0] // n_weights
    cols = held.shape[1]

    def copies(source):
        return [
            pltpu.make_async_copy(source.at[pl.ds(t * d, d)], held.at[pl.ds(t * d, d)], sems.at[t])
            for t in range(n_weights)
        ]

    first = pl.program_id(0) == 0

    @pl.when(jnp.logical_and(first, x == core))
    def _():
        for copy in copies(w_own):
            copy.start()

    @pl.when(jnp.logical_and(first, x != core))
    def _():
        for copy in copies(w_oth):
            copy.start()

    if n_passed:
        send, recv = refs[6 + 2 * n_passed:]

        @pl.when(first)
        def _():
            greet([{"x": 1 - x}])
            for copy in piece_copies(wholes, passed, send, recv, 0):
                copy.start()

    offsets = [0] if n_pieces == 1 else [x * (d // 2), (1 - x) * (d // 2)]
    for t in range(n_weights):
        @pl.when(first)
        def _(t=t):
            copies(w_own)[t].wait()

        for pieces, out in ((own, out_own), (par, out_par)):
            total = None
            for piece, at in zip(pieces, offsets):
                rows = pl.ds(pl.multiple_of(t * d + at, d // 2), piece.shape[1])
                term = mm(piece[...], held[rows, :])
                total = term if total is None else total + term
            out[:, t * cols:(t + 1) * cols] = low(total)

    if n_passed:
        @pl.when(pl.program_id(0) == pl.num_programs(0) - 1)
        def _():
            for copy in piece_copies(wholes, passed, send, recv, 0):
                copy.wait()


def project(own, par, w_own, w_oth, n_weights, passed=()):
    rows = own[0].shape[0]
    cols = w_own.shape[1]
    d = w_own.shape[0] // n_weights
    n = len(passed)
    reach = [pltpu.SemaphoreType.DMA((n,))] * 2 if n else []
    extra = dict(collective_id=2, has_side_effects=True) if n else {}
    return pl.pallas_call(
        functools.partial(project_kernel, n_weights, len(own), n),
        grid=(rows // BT,),
        in_specs=[rows_spec(piece.shape[1]) for piece in (*own, *par)] + [ANY] * (2 + n),
        out_specs=[rows_spec(n_weights * cols)] * 2 + [ANY] * n,
        out_shape=[jax.ShapeDtypeStruct((rows, n_weights * cols), jnp.bfloat16)] * 2 + piece_shapes(passed),
        scratch_shapes=[pltpu.VMEM(w_own.shape, jnp.bfloat16), pltpu.SemaphoreType.DMA((n_weights,))] + reach,
        compiler_params=pltpu.CompilerParams(vmem_limit_bytes=58 * MIB, **extra),
        cost_estimate=pl.CostEstimate(flops=4 * rows * d * cols * n_weights, bytes_accessed=16 * MIB, transcendentals=0),
        name="project",
    )(*own, *par, w_own, w_oth, *passed)


PREFIX_STEPS = ("zl", "y", "zh", "x")


def finish_kernel(dq_own, dq_got, dkv_own, dkv_got, gfirst, w_own, w_oth, pre_ref,
                  out_ref, pre_out_ref,
                  lhs, first, held, boxes, land, sums, arrived, local, send, recv):
    x, core = lax.axis_index("x"), lax.axis_index("c")
    here = {name: lax.axis_index(name) for name in PREFIX_STEPS}
    partner, across = {"c": 1 - core}, {"x": 1 - x}
    stays = x == core
    blocks = lhs.shape[0]
    half = blocks * BT
    cols = out_ref.shape[1]
    d = held.shape[1] // 3

    def loads(b):
        rows = pl.ds(b * BT, BT)
        pairs = [(dq_own.at[rows], lhs.at[b, 0]), (dkv_own.at[0, rows], lhs.at[b, 1]), (dkv_own.at[1, rows], lhs.at[b, 2]),
                 (dq_got.at[rows], lhs.at[b, 3]), (dkv_got.at[0, rows], lhs.at[b, 4]), (dkv_got.at[1, rows], lhs.at[b, 5]),
                 (gfirst.at[rows], first.at[b])]
        return [pltpu.make_async_copy(src, dst, local.at[b, n]) for n, (src, dst) in enumerate(pairs)]

    def weights(agree):
        pair = (w_own, w_oth) if agree else (w_oth, w_own)
        return [pltpu.make_async_copy(src, held.at[n], local.at[blocks, n]) for n, src in enumerate(pair)]

    for copy in loads(0):
        copy.start()

    @pl.when(stays)
    def _():
        for copy in weights(True):
            copy.start()

    @pl.when(jnp.logical_not(stays))
    def _():
        for copy in weights(False):
            copy.start()

    for b in range(1, blocks):
        for copy in loads(b):
            copy.start()
    greet([across, {"x": 1 - x, "c": 1 - core}, partner] + [{name: 1 - here[name]} for name in PREFIX_STEPS[:3]])

    def landing(b):
        return pl.ds(pl.multiple_of(core * half + b * BT, BT), BT)

    def over(b):
        return remote(boxes.at[b, 0], land.at[landing(b)], send.at[0, b], recv.at[landing_slot(b)], {"x": 1 - x, "c": x})

    def beside(b):
        return remote(boxes.at[b, 1], land.at[landing(b)], send.at[1, b], recv.at[landing_slot(b)], partner)

    def landing_slot(b):
        return core * blocks + b

    def compute(b, which):
        at = pl.ds(pl.multiple_of(which * cols, cols), cols)
        total = first[b, :, at]
        for n in range(6):
            rows = pl.ds(pl.multiple_of((n % 3) * d + which * cols, cols), cols)
            total += mm_nt(lhs[b, n], held[n // 3, rows, :])
        return low(total)

    steps = len(PREFIX_STEPS) + 1

    def prefix_copy(s):
        target = {PREFIX_STEPS[s]: 1 - here[PREFIX_STEPS[s]]} if s < steps - 1 else partner
        return remote(sums.at[s], arrived.at[s], send.at[2, s], recv.at[2 * blocks + s], target)

    sums[0] = pre_ref[...]
    prefix_copy(0).start()
    for copy in weights(True):
        copy.wait()
    for b in range(blocks):
        for copy in loads(b):
            copy.wait()
        boxes[b, 0] = compute(b, 1 - x)
        over(b).start()
        kept = compute(b, x)

        @pl.when(stays)
        def _(b=b, kept=kept):
            land[landing(b), :] = kept

        @pl.when(jnp.logical_not(stays))
        def _(b=b, kept=kept):
            boxes[b, 1] = kept
            beside(b).start()

        if b < steps - 1:
            prefix_copy(b).wait()
            sums[b + 1] = sums[b] + arrived[b]
            prefix_copy(b + 1).start()
    for b in range(blocks, steps - 1):
        prefix_copy(b).wait()
        sums[b + 1] = sums[b] + arrived[b]
        prefix_copy(b + 1).start()

    def deliver(t, b):
        rows = pl.ds(pl.multiple_of(t * half + b * BT, BT), BT)
        out_ref[rows, :] = land[rows, :].astype(jnp.float32)

    def wait_for(t, b):
        rows = land.at[pl.ds(pl.multiple_of(t * half + b * BT, BT), BT)]
        remote(rows, rows, send.at[0, b], recv.at[t * blocks + b], across).wait_recv()

    for b in range(blocks):
        @pl.when(stays)
        def _(b=b):
            deliver(core, b)
            wait_for(1 - core, b)
            deliver(1 - core, b)

        @pl.when(jnp.logical_not(stays))
        def _(b=b):
            for t in range(2):
                wait_for(t, b)
                deliver(t, b)

    prefix_copy(steps - 1).wait()
    pre_out_ref[...] = jnp.where(stays, sums[steps - 1], arrived[steps - 1])
    for b in range(blocks):
        over(b).wait_send()

        @pl.when(jnp.logical_not(stays))
        def _(b=b):
            beside(b).wait_send()


def finish_tokens(dq_own, dq_got, dkv_own, dkv_got, gfirst, w_own, w_oth, prefix):
    half, cols = dq_own.shape
    blocks = half // BT
    steps = len(PREFIX_STEPS) + 1
    vmem = pl.BlockSpec(memory_space=pltpu.VMEM)
    return pl.pallas_call(
        finish_kernel,
        in_specs=[ANY] * 7 + [vmem],
        out_specs=[vmem, vmem],
        out_shape=[jax.ShapeDtypeStruct((2 * half, cols), jnp.float32), jax.ShapeDtypeStruct(prefix.shape, jnp.float32)],
        scratch_shapes=[
            pltpu.VMEM((blocks, 6, BT, cols), jnp.bfloat16),
            pltpu.VMEM((blocks, BT, 2 * cols), jnp.float32),
            pltpu.VMEM((2, *w_own.shape), jnp.bfloat16),
            pltpu.VMEM((blocks, 2, BT, cols), jnp.bfloat16),
            pltpu.VMEM((2 * half, cols), jnp.bfloat16),
            pltpu.VMEM((steps, *prefix.shape), jnp.float32),
            pltpu.VMEM((steps, *prefix.shape), jnp.float32),
            pltpu.SemaphoreType.DMA((blocks + 1, 7)),
            pltpu.SemaphoreType.DMA((3, max(blocks, steps))),
            pltpu.SemaphoreType.DMA((2 * blocks + steps,)),
        ],
        compiler_params=pltpu.CompilerParams(collective_id=1, has_side_effects=True, vmem_limit_bytes=58 * MIB),
        cost_estimate=pl.CostEstimate(flops=12 * half * cols * 2 * cols, bytes_accessed=64 * MIB, transcendentals=0),
        name="finish_tokens",
    )(dq_own, dq_got, dkv_own, dkv_got, gfirst, w_own, w_oth, prefix)


def swap(value, axis):
    return lax.ppermute(value, axis, SWAP)


def after(value, *others):
    return lax.optimization_barrier((value, *others))[0]


def gather_half(piece):
    return lax.all_gather(piece, ("zl", "y", "c"), axis=0, tiled=True)


def in_order(first_here, mine, others, axis):
    left = jnp.where(first_here, mine, others)
    right = jnp.where(first_here, others, mine)
    return jnp.concatenate([left, right], axis=axis)


def send_out(keep, send, agree):
    got = swap(send, "x")
    mine = jnp.where(agree, keep, got)
    passed = swap(jnp.where(agree, got, keep), "c")
    return in_order(lax.axis_index("c") == 0, mine, passed, 0)


def feature_halves(value):
    half = value.shape[1] // 2
    x = lax.axis_index("x")
    return lax.dynamic_slice_in_dim(value, x * half, half, 1), lax.dynamic_slice_in_dim(value, (1 - x) * half, half, 1)


def paired_device(
    tokens, memory, dec_segments, mem_segments, self_qkv, self_out, cross_q, cross_kv, cross_out, ffn_in, ffn_out,
    adapter_down, adapter_up, self_prefix, cross_prefix, gains, cotangent,
):
    x, core = lax.axis_index("x"), lax.axis_index("c")
    agree = x == core
    columns = tokens.shape[1]
    prefix_count = self_prefix.shape[1]

    qkv_flat = self_qkv.reshape(-1, columns)
    ckv_flat = cross_kv.reshape(-1, columns)
    segs = jnp.concatenate([dec_segments, mem_segments], axis=0)
    prefixes = jnp.concatenate([self_prefix, cross_prefix], axis=0)
    prefixes = jnp.pad(prefixes, ((0, 0), (0, PP - prefix_count), (0, 0)))
    (
        rows_own, rows_par, mem_mine, packed, cot_mine, cot_send, qkv_other, prefixes_got, segs_got, *pieces
    ) = bring_rows(
        tokens, memory, cotangent, qkv_flat, prefixes, segs, ffn_in, ffn_out, [self_out, cross_q]
    )
    segs = jnp.where(agree, segs, segs_got)
    dec_seg, mem_seg = segs[0], segs[1]
    prefixes = jnp.where(agree, prefixes, prefixes_got)
    self_pre, cross_pre = prefixes[:2], prefixes[2:]
    self_masks = mask_columns(dec_seg, dec_seg, prefix_count)
    self_lo, self_hi = ranges(dec_seg, dec_seg, True)
    cross_masks = mask_columns(dec_seg, mem_seg, prefix_count)
    cross_lo, cross_hi = ranges(dec_seg, mem_seg, False)

    so_other, cq_other = (gather_half(piece) for piece in pieces)
    own, par, *pieces = project([rows_own], [rows_par], qkv_flat, qkv_other, 3, [ckv_flat, cross_out])
    ckv_other, co_other = (gather_half(piece) for piece in pieces)
    got = swap(after(packed, own), "x")
    self_q, self_k, self_v = ([(own, t), (par, t)] for t in range(3))
    self_o, self_ot, self_lt = attend_fwd(
        self_q, self_k, self_v, columns, self_masks, self_pre, self_lo, self_hi, True
    )
    heads_got = swap(self_o[1], "c")

    mem_got = got[:mem_mine.shape[0]]
    ffn_other = gather_half(after(got, heads_got)[mem_mine.shape[0]:])
    ffn_other = ffn_other.reshape(8, -1, columns)
    down_full = lax.all_gather(adapter_down.T, ("y", "c"), axis=0, tiled=True).T
    up_full = lax.all_gather(adapter_up, ("y", "c"), axis=0, tiled=True)

    cot_got = swap(after(cot_send, got), "x")
    mem_par, mem_par_got = swap(mem_mine, "c"), swap(mem_got, "c")
    first_sum, cq_own, cq_send = after_self(
        self_o[0], heads_got, rows_own, gains, self_out, so_other, cross_q, cq_other
    )
    cq_par = swap(cq_send, "c")
    own, par = project([mem_mine, mem_got], [mem_par, mem_par_got], ckv_flat, ckv_other, 2)
    cross_qp = [(cq_own, 0), (cq_par, 0)]
    cross_k, cross_v = ([(own, t), (par, t)] for t in range(2))
    cross_o, cross_ot, cross_lt = attend_fwd(
        cross_qp, cross_k, cross_v, columns, cross_masks, cross_pre, cross_lo, cross_hi, False
    )
    cross_got = swap(cross_o[1], "c")
    out_keep, out_send, grad_second, g_own, g_send, grad_adapt = ffn_both_ways(
        cross_o[0], cross_got, first_sum, cot_mine, cot_got, gains, down_full, up_full,
        cross_out, co_other, ffn_in, ffn_out, ffn_other,
    )
    g_par = swap(g_send, "c")
    output = send_out(out_keep, out_send, agree)

    blocks = grad_adapt.reshape(2, 2, 2, grad_adapt.shape[1] // 4, -1)
    part = lax.dynamic_index_in_dim(blocks, core, 2, False) + swap(
        lax.dynamic_index_in_dim(blocks, 1 - core, 2, False), "c"
    )
    y = lax.axis_index("y")
    part = lax.dynamic_index_in_dim(part, y, 1, False) + swap(
        low(lax.dynamic_index_in_dim(part, 1 - y, 1, False)), "y"
    ).astype(jnp.float32)
    for name in ("zl", "zh", "x"):
        part = low(part)
        part = part.astype(jnp.float32) + swap(part, name).astype(jnp.float32)
    grad_down, grad_up = part[0].T, part[1]

    cdq, cdkv, cross_dp = attend_bwd(
        cross_qp, cross_k, cross_v, [(g_own, 0), (g_par, 0)], columns, cross_ot, cross_lt,
        cross_masks, cross_pre, cross_lo, cross_hi, False,
    )
    cdq_got = swap(cdq[1], "c")
    cdkv_got = swap(cdkv[1], "c")
    grad_first, g_own, g_send = before_self(
        grad_second, cdq[0], cdq_got, first_sum, gains, self_out, so_other, cross_q, cq_other
    )
    g_par = swap(g_send, "c")

    def back(own, got, here, there):
        total = None
        for t in range(here.shape[0]):
            for rows, weight in ((own[t], here[t]), (got[t], there[t])):
                term = mm_nt(rows, weight)
                total = term if total is None else total + term
        return total

    ckv_here = jnp.where(agree, ckv_flat, ckv_other).reshape(cross_kv.shape)
    ckv_there = jnp.where(agree, ckv_other, ckv_flat).reshape(cross_kv.shape)
    grad_mem = low(back(cdkv[0], cdkv_got, ckv_here, ckv_there))
    mem_keep, mem_out = feature_halves(grad_mem)
    grad_memory = send_out(mem_keep, mem_out, agree).astype(jnp.float32)

    sdq, sdkv, self_dp = attend_bwd(
        self_q, self_k, self_v, [(g_own, 0), (g_par, 0)], columns, self_ot, self_lt,
        self_masks, self_pre, self_lo, self_hi, True,
    )
    sdq_got = swap(sdq[1], "c")
    sdkv_got = swap(sdkv[1], "c")
    grad_tokens, prefix_sums = finish_tokens(
        sdq[0], sdq_got, sdkv[0], sdkv_got, grad_first, qkv_flat, qkv_other,
        jnp.concatenate([self_dp, cross_dp], axis=0),
    )
    prefix_sums = prefix_sums[:, :prefix_count]

    return (output, grad_tokens, grad_memory, prefix_sums[:2], prefix_sums[2:], grad_down, grad_up)


def norm_grad(gathered, gain, upstream):
    n, r = normalize(gathered.astype(jnp.float32))
    return norm_back(n, r, gain, upstream)


def wide_device(
    tokens, memory, dec_segments, mem_segments, self_qkv, self_out, cross_q, cross_kv, cross_out, ffn_in, ffn_out,
    adapter_down, adapter_up, self_prefix, cross_prefix, gains, cotangent,
):
    n_wide = lax.axis_size("wide")
    row_count, columns = tokens.shape
    own_start = lax.axis_index("wide") * columns
    block_size = row_count // n_wide
    block_start = lax.axis_index("wide") * block_size
    prefix_count = self_prefix.shape[1]
    dec_seg, mem_seg = dec_segments[0], mem_segments[0]

    def collect(values):
        return lax.all_gather(values, "wide", axis=1, tiled=True)

    def spread(term):
        return lax.psum_scatter(term, "wide", scatter_dimension=1, tiled=True)

    def own_columns(values):
        return lax.dynamic_slice_in_dim(values, own_start, columns, 1)

    def padded(prefix):
        return jnp.pad(prefix, ((0, 0), (0, PP - prefix_count), (0, 0)))

    self_masks = mask_columns(dec_seg, dec_seg, prefix_count)
    self_lo, self_hi = ranges(dec_seg, dec_seg, True)
    cross_masks = mask_columns(dec_seg, mem_seg, prefix_count)
    cross_lo, cross_hi = ranges(dec_seg, mem_seg, False)
    self_pre, cross_pre = padded(self_prefix), padded(cross_prefix)

    all_tokens, all_memory = collect(tokens), collect(memory)
    self_q, self_k, self_v = ([(low(mm(all_tokens, self_qkv[t])), 0)] for t in range(3))
    (self_heads,), self_ot, self_lt = attend_fwd(
        self_q, self_k, self_v, columns, self_masks, self_pre, self_lo, self_hi, True
    )
    first_sum = low(tokens.astype(jnp.float32) + spread(mm(self_heads, self_out)))
    gathered_one = collect(first_sum)
    normed_one = normalize(gathered_one.astype(jnp.float32))[0] * gains[0]
    cross_qp = [(low(mm(low(normed_one), cross_q)), 0)]
    cross_k, cross_v = ([(low(mm(all_memory, cross_kv[t])), 0)] for t in range(2))
    (cross_heads,), cross_ot, cross_lt = attend_fwd(
        cross_qp, cross_k, cross_v, columns, cross_masks, cross_pre, cross_lo, cross_hi, False
    )
    second_sum = low(own_columns(normed_one) + spread(mm(cross_heads, cross_out)))
    gathered_two = collect(second_sum)
    normed_two = normalize(gathered_two.astype(jnp.float32))[0] * gains[1]
    normed_low = low(normed_two)
    adapter_in = lax.dynamic_slice_in_dim(normed_low, block_start, block_size, 0)
    adapter_rows = lax.all_gather(adapter_in, "narrow", axis=0, tiled=True)
    bottle, bottle_slope = gelu_parts(mm(adapter_rows, adapter_down))
    bottle = low(bottle)
    adapted = lax.psum_scatter(low(mm(bottle, adapter_up)), "narrow", scatter_dimension=0, tiled=True)
    hidden, slope = gelu_parts(mm(normed_low, ffn_in))
    branch = mm(low(hidden), ffn_out)
    placed = lax.dynamic_slice_in_dim(branch, block_start, block_size, 0) + 4.0 * adapted.astype(jnp.float32)
    branch = lax.dynamic_update_slice_in_dim(branch, placed, block_start, 0)
    third_sum = low(own_columns(normed_two) + spread(branch))
    gathered_three = collect(third_sum)
    output = low(own_columns(normalize(gathered_three.astype(jnp.float32))[0] * gains[2]))
    grad_three = norm_grad(gathered_three, gains[2], collect(cotangent).astype(jnp.float32))
    grad_branch = low(grad_three)
    grad_pre = low(mm_nt(grad_branch, ffn_out) * slope)
    grad_normed = mm_nt(grad_pre, ffn_in)
    grad_adapted = low(4.0 * lax.dynamic_slice_in_dim(grad_branch, block_start, block_size, 0).astype(jnp.float32))
    grad_adapted = lax.all_gather(grad_adapted, "narrow", axis=0, tiled=True)
    bottle_grad = low(mm_nt(grad_adapted, adapter_up) * bottle_slope)
    grad_in = lax.psum_scatter(low(mm_nt(bottle_grad, adapter_down)), "narrow", scatter_dimension=0, tiled=True)
    placed = lax.dynamic_slice_in_dim(grad_normed, block_start, block_size, 0) + grad_in.astype(jnp.float32)
    grad_normed = lax.dynamic_update_slice_in_dim(grad_normed, placed, block_start, 0)
    grad_down, grad_up = lax.psum(
        (mm_tn(adapter_rows, bottle_grad), mm_tn(bottle, grad_adapted)), ("dp", "wide")
    )
    grad_two = collect(low(own_columns(grad_three) + spread(grad_normed))).astype(jnp.float32)
    grad_second = norm_grad(gathered_two, gains[1], grad_two)
    grad_cross = low(mm_nt(low(grad_second), cross_out))
    (cdq,), (cdkv,), cross_dp = attend_bwd(
        cross_qp, cross_k, cross_v, [(grad_cross, 0)], columns, cross_ot, cross_lt,
        cross_masks, cross_pre, cross_lo, cross_hi, False,
    )
    spread_one = spread(low(mm_nt(cdq, cross_q))).astype(jnp.float32)
    grad_memory = spread(low(mm_nt(cdkv[0], cross_kv[0]) + mm_nt(cdkv[1], cross_kv[1]))).astype(jnp.float32)
    grad_one = collect(low(own_columns(grad_second) + spread_one)).astype(jnp.float32)
    grad_first = norm_grad(gathered_one, gains[0], grad_one)
    grad_self = low(mm_nt(low(grad_first), self_out))
    (sdq,), (sdkv,), self_dp = attend_bwd(
        self_q, self_k, self_v, [(grad_self, 0)], columns, self_ot, self_lt,
        self_masks, self_pre, self_lo, self_hi, True,
    )
    grad_input = mm_nt(sdq, self_qkv[0]) + mm_nt(sdkv[0], self_qkv[1]) + mm_nt(sdkv[1], self_qkv[2])
    grad_tokens = own_columns(grad_first) + spread(grad_input)
    totals = lax.psum((low(self_dp), low(cross_dp)), ("dp", "narrow"))
    grad_self_prefix, grad_cross_prefix = (t.astype(jnp.float32)[:, :prefix_count] for t in totals)
    return (output, grad_tokens, grad_memory, grad_self_prefix, grad_cross_prefix, grad_down, grad_up)


def solution(mesh):
    dp, wide, narrow = (mesh.shape[name] for name in ("dp", "wide", "narrow"))
    if (dp, wide, narrow) == (4, 2, 4):
        parts = Mesh(mesh.devices.reshape(2, 2, 2, 2, 2), ("zh", "zl", "x", "y", "c"))
        device, used = paired_device, parts
        rows, split, thin = ("zh", "zl", "y", "c"), "x", ("y", "c")
    else:
        device, used = wide_device, mesh
        rows, split, thin = ("dp", "narrow"), "wide", "narrow"
    return jax.shard_map(
        device,
        mesh=used,
        in_specs=(
            P(rows, split),
            P(rows, split),
            P(rows, None),
            P(rows, None),
            P(None, None, split),
            P(split, None),
            P(None, split),
            P(None, None, split),
            P(split, None),
            P(None, split),
            P(split, None),
            P(None, thin),
            P(thin, None),
            P(None, None, split),
            P(None, None, split),
            P(),
            P(rows, split),
        ),
        out_specs=(
            P(rows, split),
            P(rows, split),
            P(rows, split),
            P(None, None, split),
            P(None, None, split),
            P(None, thin),
            P(thin, None),
        ),
        check_vma=False,
    )
```

```python
import functools
import math
from functools import partial

import jax
import jax.numpy as jnp
from jax import lax
from jax.experimental import pallas as pl
from jax.experimental.pallas import tpu as pltpu
from jax.sharding import Mesh
from jax.sharding import PartitionSpec as P

HEAD_DIM = 64
DOCS = 4
NEG = -1e30
BQ = 256
BK = 256
BP = 1024
FWD_KEYS = 2
BWD_KEYS = 2
PP = 32
BT = 256
BR = 512
HEADS_FWD = 8
HEADS_BWD = 4
SWAP = [(0, 1), (1, 0)]
MIB = 2**20


def mm(a, b):
    return jnp.dot(a, b, preferred_element_type=jnp.float32)


def mm_nt(a, b):
    return lax.dot_general(a, b, (((1,), (1,)), ((), ())), preferred_element_type=jnp.float32)


def mm_tn(a, b):
    return lax.dot_general(a, b, (((0,), (0,)), ((), ())), preferred_element_type=jnp.float32)


def part_offsets(n_parts, part_len):
    if n_parts == 1:
        return [0]
    core = lax.axis_index("c")
    return [pl.multiple_of(core * part_len, part_len), pl.multiple_of((1 - core) * part_len, part_len)]


def block_at(i, size):
    return pl.ds(pl.multiple_of(i * size, size), size)


def key_blocks(j, count):
    return pl.ds(pl.multiple_of(j * BK, BK), count * BK)


def for_key_blocks(lo, hi, most, act):
    rounds = (hi - lo) // most

    def many(t, _):
        act(lo + t * most, most)
        return 0

    def single(j, _):
        act(j, 1)
        return 0

    if most > 1:
        lax.fori_loop(0, rounds, many, 0)
        lax.fori_loop(lo + rounds * most, hi, single, 0)
    else:
        lax.fori_loop(lo, hi, single, 0)


def head_rows(h):
    return pl.ds(h * HEAD_DIM, HEAD_DIM)


def later_keys(shape):
    return lax.broadcasted_iota(jnp.int32, shape, 0) > lax.broadcasted_iota(jnp.int32, shape, 1)


def by_head(prefix, heads_here):
    shape = (heads_here * PP, heads_here * HEAD_DIM)
    rows = lax.broadcasted_iota(jnp.int32, shape, 0) // PP
    columns = lax.broadcasted_iota(jnp.int32, shape, 1) // HEAD_DIM
    tall = jnp.concatenate([prefix] * heads_here, axis=0)
    return jnp.where(rows == columns, tall, jnp.zeros((), prefix.dtype))


def padding_rows(shape, prefix_count):
    return lax.broadcasted_iota(jnp.int32, shape, 0) % PP >= prefix_count


def load_queries(q_turned, h, eq, qx, here):
    zero = jnp.zeros((HEAD_DIM, q_turned.shape[1]), q_turned.dtype)
    mine = (h % 2) * HEAD_DIM
    qx[h, pl.ds(mine, HEAD_DIM), here] = q_turned[h * HEAD_DIM:(h + 1) * HEAD_DIM]
    qx[h, pl.ds(HEAD_DIM - mine, HEAD_DIM), here] = zero
    if eq is not None:
        qx[h, pl.ds(2 * HEAD_DIM, 2 * HEAD_DIM), here] = eq


def fwd_kernel(causal, n_parts, prefix_count, lo_ref, hi_ref, *refs):
    q_parts, k_parts, v_parts = refs[:n_parts], refs[n_parts:2 * n_parts], refs[2 * n_parts:3 * n_parts]
    ek_ref, eq_ref, pre_ref = refs[3 * n_parts:3 * n_parts + 3]
    o_parts = refs[3 * n_parts + 3:4 * n_parts + 3]
    ot_ref, lt_ref, qt, qx, vx, ke, acc, top = refs[4 * n_parts + 3:]
    seq = qt.shape[1]
    q_len, m_len = q_parts[0].shape[0], k_parts[0].shape[0]
    heads_here = qt.shape[0] // HEAD_DIM
    n_pairs = heads_here // 2
    n_q = seq // BQ
    ones_rows = vx.shape[1] - HEAD_DIM

    for q_ref, at in zip(q_parts, part_offsets(n_parts, q_len)):
        here = pl.ds(at, q_len)
        q_turned = (q_ref[...] * jnp.bfloat16(0.125)).T
        qt[:, here] = q_turned
        for h in range(heads_here):
            load_queries(q_turned, h, eq_ref[:, here], qx, here)
    for k_ref, v_ref, at in zip(k_parts, v_parts, part_offsets(n_parts, m_len)):
        here = pl.ds(at, m_len)
        v_turned = v_ref[...].T
        for h in range(heads_here):
            vx[h, :HEAD_DIM, here] = v_turned[h * HEAD_DIM:(h + 1) * HEAD_DIM]
        for p in range(n_pairs):
            ke[p, here, :128] = k_ref[:, p * 128:(p + 1) * 128]
    for h in range(heads_here):
        vx[h, HEAD_DIM:, :] = jnp.ones((ones_rows, vx.shape[2]), jnp.bfloat16)
    for p in range(n_pairs):
        ke[p, :, 128:] = ek_ref[...]
    keys_p = by_head(pre_ref[0], heads_here)
    values_p = by_head(pre_ref[1], heads_here).T

    wide = min(BP, seq)

    def prefix_step(find_top):
        def step(i, _):
            qs = block_at(i, wide)
            scores = mm(keys_p, qt[:, qs])
            scores = jnp.where(padding_rows(scores.shape, prefix_count), NEG, scores)
            chances = []
            for h in range(heads_here):
                s = scores[h * PP:(h + 1) * PP]
                if find_top:
                    top[h:h + 1, qs] = jnp.max(s, axis=0, keepdims=True)
                p = jnp.exp(s - top[h:h + 1, qs])
                acc[h, HEAD_DIM:, qs] = jnp.broadcast_to(jnp.sum(p, axis=0, keepdims=True), (ones_rows, wide))
                chances.append(low(p))
            out = mm(values_p, jnp.concatenate(chances, axis=0))
            for h in range(heads_here):
                acc[h, :HEAD_DIM, qs] = out[h * HEAD_DIM:(h + 1) * HEAD_DIM]
            return 0

        lax.fori_loop(0, seq // wide, step, 0)

    def scores_of(i, j, count, diag):
        qs, ks = block_at(i, BQ), key_blocks(j, count)
        scores = [mm(ke[h // 2, ks, :], qx[h, :, qs]) for h in range(heads_here)]
        if diag:
            scores = [jnp.where(later_keys(s.shape), NEG, s) for s in scores]
        return scores

    def add_block(i, j, count, diag):
        qs, ks = block_at(i, BQ), key_blocks(j, count)
        scores = scores_of(i, j, count, diag)
        for h in range(heads_here):
            p = low(jnp.exp(scores[h] - top[h:h + 1, qs]))
            acc[h, :, qs] += mm(vx[h, :, ks], p)

    def raise_top(i, j, count, diag):
        qs = block_at(i, BQ)
        for h, s in enumerate(scores_of(i, j, count, diag)):
            top[h:h + 1, qs] = jnp.maximum(top[h:h + 1, qs], jnp.max(s, axis=0, keepdims=True))

    def all_blocks(act):
        def step(i, _):
            if causal:
                act(i, i, 1, True)
            for_key_blocks(lo_ref[i], hi_ref[i], FWD_KEYS, lambda j, count: act(i, j, count, False))
            return 0

        lax.fori_loop(0, n_q, step, 0)

    prefix_step(True)
    all_blocks(add_block)
    largest = jnp.max(jnp.where(acc[0, HEAD_DIM:HEAD_DIM + 8, :] < 1e30, 0.0, 1.0))
    for h in range(1, heads_here):
        largest = jnp.maximum(largest, jnp.max(jnp.where(acc[h, HEAD_DIM:HEAD_DIM + 8, :] < 1e30, 0.0, 1.0)))

    @pl.when(largest > 0.5)
    def _():
        all_blocks(raise_top)
        prefix_step(False)
        all_blocks(add_block)

    def finish(i, _):
        qs = block_at(i, BQ)
        outs = []
        for h in range(heads_here):
            total = acc[h, HEAD_DIM:HEAD_DIM + 1, qs]
            lt_ref[h // 2, h % 2:h % 2 + 1, qs] = top[h:h + 1, qs] + jnp.log(total)
            outs.append(acc[h, :HEAD_DIM, qs] / total)
        ot = jnp.concatenate(outs, axis=0)
        ot_ref[:, qs] = low(ot)
        store_part(o_parts, i, low(ot.T))
        return 0

    lax.fori_loop(0, n_q, finish, 0)


def store_part(parts, i, value):
    per_part = parts[0].shape[0] // BQ
    at = pl.ds(pl.multiple_of((i % per_part) * BQ, BQ), BQ)
    if len(parts) == 1:
        parts[0][at, :] = value
        return
    own = i // per_part == lax.axis_index("c")

    @pl.when(own)
    def _():
        parts[0][at, :] = value

    @pl.when(jnp.logical_not(own))
    def _():
        parts[1][at, :] = value


def attend_fwd(qs, ks, vs, cols, masks, prefix, lo, hi, causal):
    ek, eq, prefix_count = masks
    n = len(qs)
    q_len, m_len = qs[0][0].shape[0], ks[0][0].shape[0]
    seq, mem = q_len * n, m_len * n
    wd = min(HEAD_DIM * HEADS_FWD, cols)
    heads_here = wd // HEAD_DIM
    steps = cols // wd
    in_specs, operands = [], []
    for group, length in ((qs, q_len), (ks, m_len), (vs, m_len)):
        for array, at in group:
            in_specs.append(pl.BlockSpec((length, wd), partial(lambda at, p, *_: (0, at * steps + p), at)))
            operands.append(array)
    in_specs += [
        pl.BlockSpec((mem, 128), lambda p, *_: (0, 0)),
        pl.BlockSpec((128, seq), lambda p, *_: (0, 0)),
        pl.BlockSpec((2, PP, wd), lambda p, *_: (0, 0, p)),
    ]
    grid_spec = pltpu.PrefetchScalarGridSpec(
        num_scalar_prefetch=2,
        grid=(steps,),
        in_specs=in_specs,
        out_specs=[pl.BlockSpec((q_len, wd), lambda p, *_: (0, p))] * n
        + [
            pl.BlockSpec((wd, seq), lambda p, *_: (p, 0)),
            pl.BlockSpec((wd // 128, 2, seq), lambda p, *_: (p, 0, 0)),
        ],
        scratch_shapes=[
            pltpu.VMEM((wd, seq), jnp.bfloat16),
            pltpu.VMEM((heads_here, 256, seq), jnp.bfloat16),
            pltpu.VMEM((heads_here, HEAD_DIM + 16, mem), jnp.bfloat16),
            pltpu.VMEM((wd // 128, mem, 256), jnp.bfloat16),
            pltpu.VMEM((heads_here, HEAD_DIM + 16, seq), jnp.float32),
            pltpu.VMEM((8, seq), jnp.float32),
        ],
    )
    result = pl.pallas_call(
        functools.partial(fwd_kernel, causal, n, prefix_count),
        grid_spec=grid_spec,
        out_shape=[jax.ShapeDtypeStruct((q_len, cols), jnp.bfloat16)] * n
        + [
            jax.ShapeDtypeStruct((cols, seq), jnp.bfloat16),
            jax.ShapeDtypeStruct((cols // 128, 2, seq), jnp.float32),
        ],
        compiler_params=pltpu.CompilerParams(vmem_limit_bytes=60 * MIB),
        cost_estimate=pl.CostEstimate(
            flops=8 * seq * mem * cols, bytes_accessed=12 * MIB, transcendentals=seq * mem * cols // 256
        ),
        name="attend_fwd_self" if causal else "attend_fwd_cross",
    )(lo, hi, *operands, ek, eq, prefix)
    return result[:n], result[n], result[n + 1]


def bwd_kernel(causal, n_parts, prefix_count, lo_ref, hi_ref, *refs):
    q_parts, k_parts, v_parts, g_parts = (refs[t * n_parts:(t + 1) * n_parts] for t in range(4))
    ot_ref, lt_ref, ek_ref, eq_ref, pre_ref = refs[4 * n_parts:4 * n_parts + 5]
    dq_parts = refs[4 * n_parts + 5:5 * n_parts + 5]
    dkv_parts = refs[5 * n_parts + 5:6 * n_parts + 5]
    dp_ref, qt, gt, qx, gx, kt, ke, vv, qm, gm, dq, dk, dv, delta = refs[6 * n_parts + 5:]
    seq = qt.shape[1]
    q_len, m_len = q_parts[0].shape[0], k_parts[0].shape[0]
    width = qt.shape[0]
    heads_here = width // HEAD_DIM
    n_pairs = heads_here // 2
    n_q = seq // BQ
    lane = lax.broadcasted_iota(jnp.int32, (1, width), 1)
    first = lane % 128 < HEAD_DIM
    zero = jnp.zeros((), jnp.bfloat16)

    for q_ref, g_ref, at in zip(q_parts, g_parts, part_offsets(n_parts, q_len)):
        here = pl.ds(at, q_len)
        q_all = q_ref[...] * jnp.bfloat16(0.125)
        g_all = g_ref[...]
        q_turned, g_turned = q_all.T, g_all.T
        qt[:, here] = q_turned
        gt[:, here] = g_turned
        for h in range(heads_here):
            load_queries(q_turned, h, eq_ref[:, here], qx, here)
            load_queries(g_turned, h, None, gx, here)
        qm[0, here, :] = jnp.where(first, q_all, zero)
        qm[1, here, :] = jnp.where(first, zero, q_all)
        gm[0, here, :] = jnp.where(first, g_all, zero)
        gm[1, here, :] = jnp.where(first, zero, g_all)
        prod = g_turned.astype(jnp.float32) * ot_ref[:, here].astype(jnp.float32)
        for h in range(heads_here):
            delta[h:h + 1, here] = jnp.sum(prod[h * HEAD_DIM:(h + 1) * HEAD_DIM], axis=0, keepdims=True)
    for k_ref, v_ref, at in zip(k_parts, v_parts, part_offsets(n_parts, m_len)):
        here = pl.ds(at, m_len)
        kt[:, here] = k_ref[...].T
        vv[here, :] = v_ref[...]
        for p in range(n_pairs):
            ke[p, here, :128] = k_ref[:, p * 128:(p + 1) * 128]
    for p in range(n_pairs):
        ke[p, :, 128:] = ek_ref[...]
    dk[...] = jnp.zeros_like(dk)
    dv[...] = jnp.zeros_like(dv)
    keys_p = by_head(pre_ref[0], heads_here)
    values_p = by_head(pre_ref[1], heads_here)
    keys_turned = keys_p.T

    def grads(s, dp, h, qs):
        p = jnp.exp(s - lt_ref[h // 2, h % 2:h % 2 + 1, qs])
        ds = low(p * (dp - delta[h:h + 1, qs]))
        return low(p), ds

    wide = min(BP, seq)

    def prefix_step(i, totals):
        qs = block_at(i, wide)
        scores = mm(keys_p, qt[:, qs])
        scores = jnp.where(padding_rows(scores.shape, prefix_count), NEG, scores)
        dps = mm(values_p, gt[:, qs])
        chances, slopes = [], []
        for h in range(heads_here):
            rows = slice(h * PP, (h + 1) * PP)
            p, ds = grads(scores[rows], dps[rows], h, qs)
            chances.append(p)
            slopes.append(ds)
        p, ds = jnp.concatenate(chances, axis=0), jnp.concatenate(slopes, axis=0)
        dq[:, qs] = mm(keys_turned, ds)
        dkp = totals[0] + mm(ds, qm[0, qs, :] + qm[1, qs, :])
        dvp = totals[1] + mm(p, gm[0, qs, :] + gm[1, qs, :])
        return dkp, dvp

    zeros = jnp.zeros((heads_here * PP, width), jnp.float32)
    totals = lax.fori_loop(0, seq // wide, prefix_step, (zeros, zeros))
    for n, total in enumerate(totals):
        rows = lax.broadcasted_iota(jnp.int32, total.shape, 0) // PP
        columns = lax.broadcasted_iota(jnp.int32, total.shape, 1) // HEAD_DIM
        total = jnp.where(rows == columns, total, 0.0)
        folded = total[:PP]
        for h in range(1, heads_here):
            folded += total[h * PP:(h + 1) * PP]
        dp_ref[n] = folded

    def add_block(i, j, count, diag):
        qs, ks = block_at(i, BQ), key_blocks(j, count)
        both = []
        for h in range(heads_here):
            c = (h // 2) * 128
            both.append((mm(ke[h // 2, ks, :], qx[h, :, qs]), mm(vv[ks, c:c + 128], gx[h, :, qs])))
        for pr in range(n_pairs):
            c = pr * 128
            dkb = dk[ks, c:c + 128]
            dvb = dv[ks, c:c + 128]
            for h in (2 * pr, 2 * pr + 1):
                s, dp = both[h]
                if diag:
                    s = jnp.where(later_keys(s.shape), NEG, s)
                p, ds = grads(s, dp, h, qs)
                dvb += mm(p, gm[h % 2, qs, c:c + 128])
                dkb += mm(ds, qm[h % 2, qs, c:c + 128])
                dq[head_rows(h), qs] += mm(kt[h * HEAD_DIM:(h + 1) * HEAD_DIM, ks], ds)
            dk[ks, c:c + 128] = dkb
            dv[ks, c:c + 128] = dvb

    def q_step(i, _):
        if causal:
            add_block(i, i, 1, True)
        for_key_blocks(lo_ref[i], hi_ref[i], BWD_KEYS, lambda j, count: add_block(i, j, count, False))
        return 0

    lax.fori_loop(0, n_q, q_step, 0)

    def finish(i, _):
        store_part(dq_parts, i, low((dq[:, block_at(i, BQ)] * 0.125).T))
        return 0

    lax.fori_loop(0, n_q, finish, 0)
    for dkv_ref, at in zip(dkv_parts, part_offsets(n_parts, m_len)):
        here = pl.ds(at, m_len)
        dkv_ref[0] = low(dk[here, :])
        dkv_ref[1] = low(dv[here, :])


def attend_bwd(qs, ks, vs, gs, cols, ot, lt, masks, prefix, lo, hi, causal):
    ek, eq, prefix_count = masks
    n = len(qs)
    q_len, m_len = qs[0][0].shape[0], ks[0][0].shape[0]
    seq, mem = q_len * n, m_len * n
    wd = min(HEAD_DIM * HEADS_BWD, cols)
    heads_here = wd // HEAD_DIM
    steps = cols // wd
    in_specs, operands = [], []
    for group, length in ((qs, q_len), (ks, m_len), (vs, m_len), (gs, q_len)):
        for array, at in group:
            in_specs.append(pl.BlockSpec((length, wd), partial(lambda at, p, *_: (0, at * steps + p), at)))
            operands.append(array)
    in_specs += [
        pl.BlockSpec((wd, seq), lambda p, *_: (p, 0)),
        pl.BlockSpec((wd // 128, 2, seq), lambda p, *_: (p, 0, 0)),
        pl.BlockSpec((mem, 128), lambda p, *_: (0, 0)),
        pl.BlockSpec((128, seq), lambda p, *_: (0, 0)),
        pl.BlockSpec((2, PP, wd), lambda p, *_: (0, 0, p)),
    ]
    grid_spec = pltpu.PrefetchScalarGridSpec(
        num_scalar_prefetch=2,
        grid=(steps,),
        in_specs=in_specs,
        out_specs=[pl.BlockSpec((q_len, wd), lambda p, *_: (0, p))] * n
        + [pl.BlockSpec((2, m_len, wd), lambda p, *_: (0, 0, p))] * n
        + [pl.BlockSpec((2, PP, wd), lambda p, *_: (0, 0, p))],
        scratch_shapes=[
            pltpu.VMEM((wd, seq), jnp.bfloat16),
            pltpu.VMEM((wd, seq), jnp.bfloat16),
            pltpu.VMEM((heads_here, 256, seq), jnp.bfloat16),
            pltpu.VMEM((heads_here, 128, seq), jnp.bfloat16),
            pltpu.VMEM((wd, mem), jnp.bfloat16),
            pltpu.VMEM((wd // 128, mem, 256), jnp.bfloat16),
            pltpu.VMEM((mem, wd), jnp.bfloat16),
            pltpu.VMEM((2, seq, wd), jnp.bfloat16),
            pltpu.VMEM((2, seq, wd), jnp.bfloat16),
            pltpu.VMEM((wd, seq), jnp.float32),
            pltpu.VMEM((mem, wd), jnp.float32),
            pltpu.VMEM((mem, wd), jnp.float32),
            pltpu.VMEM((8, seq), jnp.float32),
        ],
    )
    result = pl.pallas_call(
        functools.partial(bwd_kernel, causal, n, prefix_count),
        grid_spec=grid_spec,
        out_shape=[jax.ShapeDtypeStruct((q_len, cols), jnp.bfloat16)] * n
        + [jax.ShapeDtypeStruct((2, m_len, cols), jnp.bfloat16)] * n
        + [jax.ShapeDtypeStruct((2, PP, cols), jnp.float32)],
        compiler_params=pltpu.CompilerParams(vmem_limit_bytes=60 * MIB),
        cost_estimate=pl.CostEstimate(
            flops=12 * seq * mem * cols, bytes_accessed=20 * MIB, transcendentals=seq * mem * cols // 256
        ),
        name="attend_bwd_self" if causal else "attend_bwd_cross",
    )(lo, hi, *operands, ot, lt, ek, eq, prefix)
    return result[:n], result[n:2 * n], result[2 * n]


def ranges(dec_seg, mem_seg, causal):
    seq = dec_seg.shape[0]
    blocks = dec_seg.reshape(seq // BQ, BQ)
    low, high = blocks[:, 0], blocks[:, -1]
    lo = jnp.sum((mem_seg[None, :] < low[:, None]).astype(jnp.int32), axis=1) // BK
    if causal:
        hi = jnp.arange(seq // BQ, dtype=jnp.int32)
    else:
        hi = (jnp.sum((mem_seg[None, :] <= high[:, None]).astype(jnp.int32), axis=1) + BK - 1) // BK
    return lo, hi


def mask_columns(dec_seg, mem_seg, prefix_count):
    lane = jnp.arange(128, dtype=jnp.int32)
    row = lane[:, None]
    ek = (mem_seg[:, None] == lane[None, :]).astype(jnp.bfloat16)
    eq = jnp.where(jnp.logical_and(row < DOCS, row != dec_seg[None, :]), NEG, 0.0).astype(jnp.bfloat16)
    return ek, eq, prefix_count


def normalize(v):
    centered = v - jnp.mean(v, axis=-1, keepdims=True)
    r = lax.rsqrt(jnp.mean(centered * centered, axis=-1, keepdims=True) + 1e-05)
    return centered * r, r


def norm_back(n, r, gain, upstream):
    u = upstream * gain
    return r * (u - jnp.mean(u, axis=-1, keepdims=True) - n * jnp.mean(u * n, axis=-1, keepdims=True))


def gelu_parts(v):
    chance = 0.5 * (1.0 + lax.erf(v * math.sqrt(0.5)))
    slope = chance + v * (jnp.exp(-0.5 * v * v) * (1.0 / math.sqrt(2.0 * math.pi)))
    return v * chance, slope


def low(v):
    return v.astype(jnp.bfloat16)


def place_halves(own, packed, row, held, sems, at):
    x = lax.axis_index("x")
    tall, wide = held.shape[2:]
    cols = packed.shape[2]
    copies = [pltpu.make_async_copy(own, held.at[x], sems.at[at])]
    for j in range(wide // cols):
        copies.append(
            pltpu.make_async_copy(
                packed.at[:, pl.ds(row + j * tall, tall)],
                held.at[1 - x, :, :, pl.ds(j * cols, cols)],
                sems.at[at + 1 + j],
            )
        )
    return copies


def half_of(held, which):
    return held[which].reshape(-1, held.shape[3])


def eighths(weight):
    return weight.reshape(8, weight.shape[0] // 8, weight.shape[1])


def on_first(copies, act):
    @pl.when(pl.program_id(0) == 0)
    def _():
        for copy in copies:
            getattr(copy, act)()


def after_self_kernel(own_ref, par_ref, tok_ref, gains_ref, so_own, cq_own, packed,
                      first_ref, q_own_ref, q_par_ref, so, cq, sems):
    core = lax.axis_index("c")
    so_copies = place_halves(so_own, packed, 0, so, sems, 0)
    cq_copies = place_halves(cq_own, packed, 2 * so.shape[2], cq, sems, 4)
    on_first(so_copies + cq_copies, "start")
    on_first(so_copies, "wait")
    total = tok_ref[...].astype(jnp.float32) + (mm(own_ref[...], half_of(so, core)) + mm(par_ref[...], half_of(so, 1 - core)))
    first = low(total)
    first_ref[...] = first
    n, _ = normalize(first.astype(jnp.float32))
    normed = low(n * gains_ref[0:1, :])
    on_first(cq_copies, "wait")
    q_own_ref[...] = low(mm(normed, half_of(cq, core)))
    q_par_ref[...] = low(mm(normed, half_of(cq, 1 - core)))


def rows_spec(width):
    return pl.BlockSpec((BR, width), lambda i: (i, 0))


ANY = pl.BlockSpec(memory_space=pl.ANY)


def after_self(own, par, tokens, gains, so_own, cq_own, packed):
    rows, d = tokens.shape
    half = d // 2
    return pl.pallas_call(
        after_self_kernel,
        grid=(rows // BR,),
        in_specs=[rows_spec(half), rows_spec(half), rows_spec(d), pl.BlockSpec((3, d), lambda i: (0, 0)), ANY, ANY, ANY],
        out_specs=[rows_spec(d), rows_spec(half), rows_spec(half)],
        out_shape=[
            jax.ShapeDtypeStruct((rows, d), jnp.bfloat16),
            jax.ShapeDtypeStruct((rows, half), jnp.bfloat16),
            jax.ShapeDtypeStruct((rows, half), jnp.bfloat16),
        ],
        scratch_shapes=[
            pltpu.VMEM((2, 8, half // 8, d), jnp.bfloat16),
            pltpu.VMEM((2, 8, d // 8, half), jnp.bfloat16),
            pltpu.SemaphoreType.DMA((8,)),
        ],
        compiler_params=pltpu.CompilerParams(vmem_limit_bytes=58 * MIB),
        cost_estimate=pl.CostEstimate(flops=4 * rows * d * d, bytes_accessed=12 * MIB, transcendentals=0),
        name="after_self",
    )(own, par, tokens, gains, eighths(so_own), eighths(cq_own), packed)


def before_self_kernel(gsec_ref, own_ref, par_ref, first_ref, gains_ref, so_own, cq_own, packed,
                       gfirst_ref, g_own_ref, g_par_ref, so, cq, sems):
    core = lax.axis_index("c")
    so_copies = place_halves(so_own, packed, 0, so, sems, 0)
    cq_copies = place_halves(cq_own, packed, 2 * so.shape[2], cq, sems, 4)
    on_first(cq_copies + so_copies, "start")
    on_first(cq_copies, "wait")
    grad_one = low(gsec_ref[...] + (mm_nt(own_ref[...], half_of(cq, core)) + mm_nt(par_ref[...], half_of(cq, 1 - core))))
    n, r = normalize(first_ref[...].astype(jnp.float32))
    grad_first = norm_back(n, r, gains_ref[0:1, :], grad_one.astype(jnp.float32))
    gfirst_ref[...] = grad_first
    first_low = low(grad_first)
    on_first(so_copies, "wait")
    g_own_ref[...] = low(mm_nt(first_low, half_of(so, core)))
    g_par_ref[...] = low(mm_nt(first_low, half_of(so, 1 - core)))


def before_self(gsec, own, par, first, gains, so_own, cq_own, packed):
    rows, d = first.shape
    half = d // 2
    return pl.pallas_call(
        before_self_kernel,
        grid=(rows // BR,),
        in_specs=[
            rows_spec(d), rows_spec(half), rows_spec(half), rows_spec(d), pl.BlockSpec((3, d), lambda i: (0, 0)),
            ANY, ANY, ANY,
        ],
        out_specs=[rows_spec(d), rows_spec(half), rows_spec(half)],
        out_shape=[
            jax.ShapeDtypeStruct((rows, d), jnp.float32),
            jax.ShapeDtypeStruct((rows, half), jnp.bfloat16),
            jax.ShapeDtypeStruct((rows, half), jnp.bfloat16),
        ],
        scratch_shapes=[
            pltpu.VMEM((2, 8, half // 8, d), jnp.bfloat16),
            pltpu.VMEM((2, 8, d // 8, half), jnp.bfloat16),
            pltpu.SemaphoreType.DMA((8,)),
        ],
        compiler_params=pltpu.CompilerParams(vmem_limit_bytes=58 * MIB),
        cost_estimate=pl.CostEstimate(flops=4 * rows * d * d, bytes_accessed=16 * MIB, transcendentals=0),
        name="before_self",
    )(gsec, own, par, first, gains, eighths(so_own), eighths(cq_own), packed)


MESH_ID = pl.DeviceIdType.MESH
PARTS_IN = 4


def greet(targets):
    barrier = pltpu.get_barrier_semaphore()
    for target in targets:
        pl.semaphore_signal(barrier, inc=1, device_id=target, device_id_type=MESH_ID)
    pl.semaphore_wait(barrier, len(targets))


def remote(src, dst, send, recv, target):
    return pltpu.make_async_remote_copy(
        src_ref=src, dst_ref=dst, send_sem=send, recv_sem=recv, device_id=target, device_id_type=MESH_ID
    )


def eighth_index():
    return (lax.axis_index("zl") * 2 + lax.axis_index("y")) * 2 + lax.axis_index("c")


def piece_copies(wholes, packed, send, recv):
    cols = packed.shape[1]
    copies, at = [], 0
    for whole in wholes:
        tall = whole.shape[0] // 8
        source = pl.ds(pl.multiple_of(eighth_index() * tall, tall), tall)
        for j in range(whole.shape[1] // cols):
            n = len(copies)
            copies.append(
                remote(
                    whole.at[source, pl.ds(j * cols, cols)], packed.at[pl.ds(at, tall)], send.at[n], recv.at[n],
                    {"x": 1 - lax.axis_index("x")},
                )
            )
            at += tall
    return copies


def bring_kernel(tok, mem, cot, qkv, prefix, segs, w_in, w_out, down, up,
                 rows_own, rows_par, mem_mine, packed, cot_mine, cot_send, qkv_oth, prefix_got, segs_got, down_all, up_all,
                 stage, stage_down, stage_up, send, recv, load):
    x, y, zl, core = (lax.axis_index(name) for name in ("x", "y", "zl", "c"))
    half = rows_own.shape[0]
    cols = tok.shape[1]
    chunk = half // PARTS_IN
    piece = qkv.shape[0] // 8
    stays = x == core
    partner = {"c": 1 - core}
    across = {"x": 1 - x}

    def token_half(which):
        return pl.ds(pl.multiple_of(which * half, half), half)

    loads = [
        pltpu.make_async_copy(source.at[token_half(which)], stage.at[n], load.at[n])
        for n, (source, which) in enumerate(((tok, core), (tok, 1 - core), (mem, core), (cot, core)))
    ]
    at = 0
    for whole in (w_in, w_out):
        tall, wide = whole.shape[0] // 8, whole.shape[1]
        source = pl.ds(pl.multiple_of(eighth_index() * tall, tall), tall)
        for j in range(wide // cols):
            n = len(loads)
            loads.append(
                pltpu.make_async_copy(
                    whole.at[source, pl.ds(j * cols, cols)], stage.at[4, pl.ds(at, tall)], load.at[n]
                )
            )
            at += tall
    pack = pltpu.make_async_copy(stage.at[4], packed.at[pl.ds(half, half)], load.at[len(loads)])
    mem_send = packed.at[pl.ds(0, half)]
    for copy in loads:
        copy.start()
    greet([across, {"x": 1 - x, "c": 1 - core}, {"y": 1 - y}, {"zl": 1 - zl}, partner])

    def features(which):
        return pl.ds(pl.multiple_of(which * cols, cols), cols)

    def part(k):
        return pl.ds(k * chunk, chunk)

    def eighth(a, b, c):
        return pl.ds(pl.multiple_of(((a * 2 + b) * 2 + c) * piece, piece), piece)

    def weight(at, slot, target, source=None):
        return remote((qkv_oth if source is None else source).at[at], qkv_oth.at[at], send.at[slot], recv.at[slot], target)

    mine = eighth(zl, y, core)
    w_x = weight(mine, 0, across, qkv)
    w_x.start()
    at_small = 14 + 3 * PARTS_IN
    small = [
        remote(prefix, prefix_got, send.at[at_small], recv.at[at_small], across),
        remote(segs, segs_got, send.at[at_small + 1], recv.at[at_small + 1], partner),
    ]
    for copy in small:
        copy.start()
    others = small

    units = up.shape[0]

    def adapt_places(a, b):
        at = pl.ds(pl.multiple_of((a * 2 + b) * units, units), units)
        return down_all.at[:, at], up_all.at[at]

    def adapt_copies(sources, a, b, n, target):
        return [
            remote(source, place, send.at[at_small + 2 + n + m], recv.at[at_small + 2 + n + m], target)
            for m, (source, place) in enumerate(zip(sources, adapt_places(a, b)))
        ]

    adapt_y = adapt_copies((down, up), y, core, 0, {"y": 1 - y})
    adapt_c = adapt_copies((down, up), y, core, 2, partner)
    adapt_in = [
        pltpu.make_async_copy(down, stage_down, load.at[14]),
        pltpu.make_async_copy(up, stage_up, load.at[15]),
    ]
    for copy in adapt_y + adapt_c + adapt_in:
        copy.start()

    at_own, at_par = 8, 8 + PARTS_IN
    at_here = 8 + 2 * PARTS_IN

    def token_sends():
        copies = []
        for t in range(2):
            for k in range(PARTS_IN):
                slot = at_own + k
                copies.append(
                    remote(
                        tok.at[pl.ds(t * half + k * chunk, chunk)],
                        rows_own.at[part(k), features(x)],
                        send.at[slot + t * PARTS_IN],
                        recv.at[slot],
                        {"x": 1 - x, "c": t},
                    )
                )
        return copies

    def here_copies():
        own = tok.at[token_half(core)]
        other = tok.at[token_half(1 - core)]
        return [
            remote(other, rows_own.at[:, features(x)], send.at[at_here], recv.at[at_here], partner),
            remote(own, rows_par.at[:, features(x)], send.at[at_here + 1], recv.at[at_here + 1], partner),
        ]

    def row_copy(source, to, slot):
        return remote(source.at[token_half(1 - core)], to, send.at[slot], recv.at[slot], partner)

    @pl.when(jnp.logical_not(stays))
    def _():
        for copy in token_sends():
            copy.start()
        row_copy(mem, mem_send, at_here + 3).start()
        row_copy(cot, cot_send, at_here + 5).start()
        for n, to, slot in ((2, mem_send, at_here + 3), (3, cot_send, at_here + 5)):
            loads[n].wait()
            pltpu.make_async_copy(stage.at[n], to, recv.at[slot]).start()
        loads[0].wait()
        loads[1].wait()

    @pl.when(stays)
    def _():
        for copy in here_copies():
            copy.start()
        row_copy(mem, mem_mine, at_here + 2).start()
        row_copy(cot, cot_mine, at_here + 4).start()
        for n, to, slot in (
            (0, rows_own.at[:, features(x)], at_here),
            (1, rows_par.at[:, features(x)], at_here + 1),
            (2, mem_mine, at_here + 2),
            (3, cot_mine, at_here + 4),
        ):
            loads[n].wait()
            pltpu.make_async_copy(stage.at[n], to, recv.at[slot]).start()

    for copy in loads[4:]:
        copy.wait()
    pack.start()
    adapt_here = [
        pltpu.make_async_copy(source, place, load.at[14 + m])
        for m, (source, place) in enumerate(zip((stage_down, stage_up), adapt_places(y, core)))
    ]
    for came, placed in zip(adapt_in, adapt_here):
        came.wait()
        placed.start()

    for copy in adapt_y:
        copy.wait_recv()
    adapt_yc = adapt_copies(adapt_places(1 - y, core), 1 - y, core, 4, partner)
    for copy in adapt_yc:
        copy.start()
    w_x.wait_recv()
    w_y = weight(mine, 1, {"y": 1 - y})
    w_z = weight(mine, 2, {"zl": 1 - zl})
    w_c = weight(mine, 4, partner)
    for copy in (w_y, w_z, w_c):
        copy.start()

    forwards = []

    def forward(k):
        here = rows_own.at[part(k), features(1 - x)]
        remote(here, here, send.at[at_own + k], recv.at[at_own + k], across).wait_recv()
        copy = remote(here, rows_par.at[part(k), features(1 - x)], send.at[at_here + 6 + k], recv.at[at_par + k], partner)
        copy.start()
        forwards.append(copy)

    forward(0)
    w_y.wait_recv()
    from_y = eighth(zl, 1 - y, core)
    w_yz = weight(from_y, 3, {"zl": 1 - zl})
    w_yc = weight(from_y, 5, partner)
    w_yz.start()
    w_yc.start()
    forward(1)
    w_z.wait_recv()
    w_zc = weight(eighth(1 - zl, y, core), 6, partner)
    w_zc.start()
    for k in range(2, PARTS_IN):
        forward(k)
    w_yz.wait_recv()
    w_yzc = weight(eighth(1 - zl, 1 - y, core), 7, partner)
    w_yzc.start()

    for copy in (w_c, w_yc, w_zc, w_yzc, *adapt_c, *adapt_yc, *others):
        copy.wait_recv()
    for k, copy in enumerate(forwards):
        copy.wait_recv()
    for to, slot in (
        (rows_own.at[:, features(x)], at_here),
        (rows_par.at[:, features(x)], at_here + 1),
        (mem_mine, at_here + 2),
        (mem_send, at_here + 3),
        (cot_mine, at_here + 4),
        (cot_send, at_here + 5),
    ):
        remote(to, to, send.at[slot], recv.at[slot], partner).wait_recv()

    pack.wait()
    for copy in adapt_here:
        copy.wait()

    for copy in (w_x, w_y, w_z, w_c, w_yz, w_yc, w_zc, w_yzc, *adapt_y, *adapt_c, *adapt_yc, *forwards, *others):
        copy.wait_send()

    @pl.when(jnp.logical_not(stays))
    def _():
        for copy in token_sends():
            copy.wait_send()
        row_copy(mem, mem_send, at_here + 3).wait_send()
        row_copy(cot, cot_send, at_here + 5).wait_send()

    @pl.when(stays)
    def _():
        for copy in here_copies():
            copy.wait_send()
        row_copy(mem, mem_mine, at_here + 2).wait_send()
        row_copy(cot, cot_mine, at_here + 4).wait_send()


def bring_rows(tokens, memory, cotangent, qkv_flat, prefixes, segs, ffn_in, ffn_out, down, up):
    rows, cols = tokens.shape
    half = rows // 2
    wide_rows = jax.ShapeDtypeStruct((half, 2 * cols), jnp.bfloat16)
    thin_rows = jax.ShapeDtypeStruct((half, cols), jnp.bfloat16)
    slots = 22 + 3 * PARTS_IN
    return pl.pallas_call(
        bring_kernel,
        in_specs=[ANY] * 10,
        out_specs=[ANY] * 11,
        out_shape=[wide_rows, wide_rows, thin_rows, jax.ShapeDtypeStruct((rows, cols), jnp.bfloat16), thin_rows, thin_rows,
                   jax.ShapeDtypeStruct(qkv_flat.shape, jnp.bfloat16),
                   jax.ShapeDtypeStruct(prefixes.shape, prefixes.dtype),
                   jax.ShapeDtypeStruct(segs.shape, segs.dtype),
                   jax.ShapeDtypeStruct((down.shape[0], 4 * down.shape[1]), down.dtype),
                   jax.ShapeDtypeStruct((4 * up.shape[0], up.shape[1]), up.dtype)],
        scratch_shapes=[
            pltpu.VMEM((5, half, cols), jnp.bfloat16),
            pltpu.VMEM(down.shape, jnp.bfloat16),
            pltpu.VMEM(up.shape, jnp.bfloat16),
            pltpu.SemaphoreType.DMA((slots,)),
            pltpu.SemaphoreType.DMA((slots,)),
            pltpu.SemaphoreType.DMA((16,)),
        ],
        compiler_params=pltpu.CompilerParams(collective_id=0, has_side_effects=True, vmem_limit_bytes=58 * MIB),
        cost_estimate=pl.CostEstimate(flops=0, bytes_accessed=64 * MIB, transcendentals=0),
        name="bring_rows",
    )(tokens, memory, cotangent, qkv_flat, prefixes, segs, ffn_in, ffn_out, down, up)


def project_kernel(n_weights, n_pieces, wholes_count, *refs):
    own, par = refs[:n_pieces], refs[n_pieces:2 * n_pieces]
    refs = refs[2 * n_pieces:]
    w_own, w_oth, wholes = refs[0], refs[1], refs[2:2 + wholes_count]
    refs = refs[2 + wholes_count:]
    if wholes_count:
        out_own, out_par, packed, held, sems, send, recv = refs
    else:
        out_own, out_par, held, sems = refs
    x, core = lax.axis_index("x"), lax.axis_index("c")
    d = held.shape[0] // n_weights
    cols = held.shape[1]

    def copies(source):
        if len(source.shape) == 2:
            tall = held.shape[0] // n_weights
            parts = [source.at[pl.ds(t * tall, tall)] for t in range(n_weights)]
        else:
            tall = held.shape[0] // 8
            parts = [source.at[e, pl.ds(0, tall)] for e in range(8)]
        return [
            pltpu.make_async_copy(part, held.at[pl.ds(t * tall, tall)], sems.at[t]) for t, part in enumerate(parts)
        ]

    first = pl.program_id(0) == 0

    def weights(act, t=None):
        for source, chosen in ((w_own, x == core), (w_oth, x != core)):
            @pl.when(jnp.logical_and(first, chosen))
            def _(source=source):
                group = copies(source)
                if t is not None:
                    share = len(group) // n_weights
                    group = group[t * share:(t + 1) * share]
                for copy in group:
                    getattr(copy, act)()

    weights("start")
    if wholes_count:
        @pl.when(first)
        def _():
            greet([{"x": 1 - x}])
            for copy in piece_copies(wholes, packed, send, recv):
                copy.start()

    offsets = [0] if n_pieces == 1 else [x * (d // 2), (1 - x) * (d // 2)]
    for t in range(n_weights):
        weights("wait", t)
        for pieces, out in ((own, out_own), (par, out_par)):
            total = None
            for piece, at in zip(pieces, offsets):
                rows = pl.ds(pl.multiple_of(t * d + at, d // 2), piece.shape[1])
                term = mm(piece[...], held[rows, :])
                total = term if total is None else total + term
            out[:, t * cols:(t + 1) * cols] = low(total)

    if wholes_count:
        @pl.when(pl.program_id(0) == pl.num_programs(0) - 1)
        def _():
            for copy in piece_copies(wholes, packed, send, recv):
                copy.wait()


def project(own, par, w_own, w_oth, n_weights, wholes=()):
    rows = own[0].shape[0]
    cols = w_own.shape[1]
    d = w_own.shape[0] // n_weights
    n = len(wholes)
    held = pltpu.VMEM(w_own.shape, jnp.bfloat16)
    out_specs = [rows_spec(n_weights * cols)] * 2
    out_shape = [jax.ShapeDtypeStruct((rows, n_weights * cols), jnp.bfloat16)] * 2
    scratch = [held, pltpu.SemaphoreType.DMA((8,))]
    extra = {}
    if n:
        packed_rows = sum(w.shape[0] // 8 * (w.shape[1] // cols) for w in wholes)
        slots = sum(w.shape[1] // cols for w in wholes)
        out_specs = out_specs + [ANY]
        out_shape = out_shape + [jax.ShapeDtypeStruct((packed_rows, cols), jnp.bfloat16)]
        scratch = scratch + [pltpu.SemaphoreType.DMA((slots,))] * 2
        extra = dict(collective_id=2, has_side_effects=True)
    return pl.pallas_call(
        functools.partial(project_kernel, n_weights, len(own), n),
        grid=(rows // BR,),
        in_specs=[rows_spec(piece.shape[1]) for piece in (*own, *par)] + [ANY] * (2 + n),
        out_specs=out_specs,
        out_shape=out_shape,
        scratch_shapes=scratch,
        compiler_params=pltpu.CompilerParams(vmem_limit_bytes=58 * MIB, **extra),
        cost_estimate=pl.CostEstimate(flops=4 * rows * d * cols * n_weights, bytes_accessed=16 * MIB, transcendentals=0),
        name="project",
    )(*own, *par, w_own, w_oth, *wholes)


def back_memory_kernel(ckv_row, own_ref, got_ref, w_own, packed, keep_ref, send_ref, held, sems):
    x, core = lax.axis_index("x"), lax.axis_index("c")
    copies = place_halves(w_own, packed, ckv_row, held, sems, 0)
    on_first(copies, "start")
    on_first(copies, "wait")
    n_weights = own_ref.shape[0]
    share = 8 // (2 * n_weights)
    for out, which in ((send_ref, 1 - x), (keep_ref, x)):
        total = None
        for t in range(n_weights):
            for rows, heads in ((own_ref, core), (got_ref, 1 - core)):
                weight = held[heads, pl.ds(2 * share * t + share * which, share)]
                term = mm_nt(rows[t], weight.reshape(-1, weight.shape[2]))
                total = term if total is None else total + term
        out[...] = low(total)


def back_memory(own, got, w_own, packed, ckv_row):
    n, rows, cols = own.shape
    w_own = eighths(w_own)
    both = pl.BlockSpec((n, BR, cols), lambda i: (0, i, 0))
    return pl.pallas_call(
        functools.partial(back_memory_kernel, ckv_row),
        grid=(rows // BR,),
        in_specs=[both, both, ANY, ANY],
        out_specs=[rows_spec(cols)] * 2,
        out_shape=[jax.ShapeDtypeStruct((rows, cols), jnp.bfloat16)] * 2,
        scratch_shapes=[pltpu.VMEM((2, *w_own.shape), jnp.bfloat16), pltpu.SemaphoreType.DMA((2,))],
        compiler_params=pltpu.CompilerParams(vmem_limit_bytes=58 * MIB),
        cost_estimate=pl.CostEstimate(flops=8 * n * rows * cols * cols, bytes_accessed=12 * MIB, transcendentals=0),
        name="back_memory",
    )(own, got, w_own, packed)


CHUNK = 512
ROWS = 256


def ffn_kernel(co_row, own_ref, par_ref, first_hbm, cot_mine, cot_got, gains_ref, down, up,
               co_own, packed, in_own, out_own, ffn_other,
               keep_ref, send_ref, gsec_ref, g_own_ref, g_par_ref, part_ref,
               first, cot, co, w_in, w_out, normed, second, branch, full, acc, slopes,
               bottle, bottle_slope, bottle_grad, grads, got_c, part_out, part_got,
               co_sems, w_sems, sems, send, recv):
    x, y, core = (lax.axis_index(name) for name in ("x", "y", "c"))
    rows, d = normed.shape
    half = d // 2
    in_tall = ffn_other.shape[1] // 2
    chunks = 2 * in_own.shape[2] // CHUNK
    own_chunks = chunks // 2

    def columns(which):
        return pl.ds(pl.multiple_of(which * half, half), half)

    loads = [
        pltpu.make_async_copy(first_hbm, first, sems.at[0]),
        pltpu.make_async_copy(cot_mine, cot.at[:, columns(x)], sems.at[1]),
        pltpu.make_async_copy(cot_got, cot.at[:, columns(1 - x)], sems.at[2]),
    ]
    co_copies = place_halves(co_own, packed, co_row, co, co_sems, 0)

    def weight_copies(t, slot, own):
        if own:
            at = pl.ds(pl.multiple_of(t * CHUNK, CHUNK), CHUNK)
            source_in = in_own.at[:, :, at]
            sources = [out_own.at[pl.ds(2 * t, 2), :, pl.ds(j * half, half)] for j in range(2)]
        else:
            t = t - own_chunks
            tall = w_in.shape[2]
            source_in = ffn_other.at[:, pl.ds(pl.multiple_of(t * tall, tall), tall)]
            sources = [
                ffn_other.at[pl.ds(2 * t, 2), pl.ds(in_tall + j * (CHUNK // 2), CHUNK // 2)] for j in range(2)
            ]
        return [pltpu.make_async_copy(source_in, w_in.at[slot], w_sems.at[slot, 0])] + [
            pltpu.make_async_copy(source, w_out.at[slot, :, :, pl.ds(j * half, half)], w_sems.at[slot, 1 + j])
            for j, source in enumerate(sources)
        ]

    def fetch(t):
        slot = t % 2

        @pl.when(t < own_chunks)
        def _():
            for copy in weight_copies(t, slot, True):
                copy.start()

        @pl.when(jnp.logical_and(t >= own_chunks, t < chunks))
        def _():
            for copy in weight_copies(t, slot, False):
                copy.start()

    def arrive(t):
        slot = t % 2

        @pl.when(t < own_chunks)
        def _():
            for copy in weight_copies(t, slot, True):
                copy.wait()

        @pl.when(t >= own_chunks)
        def _():
            for copy in weight_copies(t, slot, False):
                copy.wait()

    for copy in co_copies + loads[:1]:
        copy.start()
    fetch(0)
    fetch(1)
    for copy in loads[1:]:
        copy.start()
    greet([{"c": 1 - core}, {"y": 1 - y}, {"x": 1 - x}])
    for copy in co_copies + loads[:1]:
        copy.wait()
    acc[...] = mm(own_ref[...], half_of(co, core)) + mm(par_ref[...], half_of(co, 1 - core))

    def by_rows(act):
        def step(i, _):
            act(pl.ds(pl.multiple_of(i * ROWS, ROWS), ROWS))
            return 0

        lax.fori_loop(0, rows // ROWS, step, 0)

    def norm_two(at):
        n_one, _ = normalize(first[at, :].astype(jnp.float32))
        summed = low(n_one * gains_ref[0:1, :] + acc[at, :])
        second[at, :] = summed
        n_two, _ = normalize(summed.astype(jnp.float32))
        normed_two = n_two * gains_ref[1:2, :]
        normed[at, :] = low(normed_two)
        acc[at, :] = normed_two

    by_rows(norm_two)
    value, slope = gelu_parts(mm(normed[...], down[...]))
    bottle[...] = low(value)
    bottle_slope[...] = slope
    acc[...] += 4.0 * mm(bottle[...], up[...])

    def up_step(t, _):
        arrive(t)
        slot = t % 2
        weight_in = w_in[slot].reshape(d, CHUNK)
        weight_out = w_out[slot].reshape(CHUNK, d)
        halves = (slice(0, rows // 2), slice(rows // 2, rows))
        products = [mm(normed[at, :], weight_in) for at in halves]
        for at, product in zip(halves, products):
            value, slope = gelu_parts(product)
            slopes[t, at, :] = low(slope)
            acc[at, :] += mm(low(value), weight_out)
        fetch(t + 2)
        return 0

    lax.fori_loop(0, chunks, up_step, 0)
    fetch(0)
    fetch(1)
    for copy in loads[1:]:
        copy.wait()

    def norm_three(at):
        third = low(acc[at, :])
        n_three, r_three = normalize(third.astype(jnp.float32))
        gain = gains_ref[2:3, :]
        full[at, :] = low(n_three * gain)
        grad_three = norm_back(n_three, r_three, gain, cot[at, :].astype(jnp.float32))
        branch[at, :] = low(grad_three)
        acc[at, :] = grad_three

    by_rows(norm_three)
    outs = [
        pltpu.make_async_copy(full.at[:, columns(x)], keep_ref, sems.at[0]),
        pltpu.make_async_copy(full.at[:, columns(1 - x)], send_ref, sems.at[1]),
    ]
    for copy in outs:
        copy.start()
    adapted = low(4.0 * branch[...].astype(jnp.float32))
    bottle_grad[...] = low(mm_nt(adapted, up[...]) * bottle_slope[...])
    tall = grads.shape[3]
    for which, grad in ((0, mm_tn(bottle_grad[...], normed[...])), (1, mm_tn(bottle[...], adapted))):
        for n in range(4):
            grads[n // 2, n % 2, which] = grad[n * tall:(n + 1) * tall]
    over_c = remote(grads.at[:, 1 - core], got_c, send.at[0], recv.at[0], {"c": 1 - core})
    over_y = remote(part_out.at[0], part_got.at[0], send.at[1], recv.at[1], {"y": 1 - y})
    over_x = remote(part_out.at[1], part_got.at[1], send.at[2], recv.at[2], {"x": 1 - x})
    over_c.start()
    acc[...] += mm_nt(bottle_grad[...], down[...])

    def down_step(t, _):
        arrive(t)
        slot = t % 2
        weight_in = w_in[slot].reshape(d, CHUNK)
        weight_out = w_out[slot].reshape(CHUNK, d)
        halves = (slice(0, rows // 2), slice(rows // 2, rows))
        products = [mm_nt(branch[at, :], weight_out) for at in halves]
        for at, product in zip(halves, products):
            grad_pre = low(product * slopes[t, at, :].astype(jnp.float32))
            acc[at, :] += mm_nt(grad_pre, weight_in)
        fetch(t + 2)

        @pl.when(t == 1)
        def _():
            over_c.wait()
            part_out[0] = low(grads[1 - y, core] + got_c[1 - y])
            over_y.start()

        @pl.when(t == 5)
        def _():
            over_y.wait()
            part_out[1] = low(grads[y, core] + got_c[y] + part_got[0].astype(jnp.float32))
            over_x.start()

        return 0

    lax.fori_loop(0, chunks, down_step, 0)
    for copy in outs:
        copy.wait()

    def norm_two_back(at):
        n_two, r_two = normalize(second[at, :].astype(jnp.float32))
        grad_two = low(acc[at, :]).astype(jnp.float32)
        grad_second = norm_back(n_two, r_two, gains_ref[1:2, :], grad_two)
        acc[at, :] = grad_second
        branch[at, :] = low(grad_second)

    by_rows(norm_two_back)
    out_acc = pltpu.make_async_copy(acc, gsec_ref, sems.at[0])
    out_acc.start()
    full[:, :half] = low(mm_nt(branch[...], half_of(co, core)))
    full[:, half:] = low(mm_nt(branch[...], half_of(co, 1 - core)))
    outs = [
        pltpu.make_async_copy(full.at[:, pl.ds(0, half)], g_own_ref, sems.at[1]),
        pltpu.make_async_copy(full.at[:, pl.ds(half, half)], g_par_ref, sems.at[2]),
    ]
    for copy in outs:
        copy.start()
    over_x.wait()
    part_ref[...] = low(part_out[1].astype(jnp.float32) + part_got[1].astype(jnp.float32))
    for copy in outs + [out_acc]:
        copy.wait()


def ffn_both_ways(own, par, first, cot_mine, cot_got, gains, down, up, co_own, packed, co_row, in_own, out_own, ffn_other):
    rows, d = first.shape
    half = d // 2
    hidden_half = in_own.shape[1]
    bottleneck = up.shape[0]
    co_own, in_own, out_own = eighths(co_own), eighths(in_own), eighths(out_own)
    vmem = pl.BlockSpec(memory_space=pltpu.VMEM)
    thin = jax.ShapeDtypeStruct((rows, half), jnp.bfloat16)
    part = (2, bottleneck // 4, d)
    flops = 2 * rows * d * (8 * hidden_half + 6 * bottleneck + 2 * d)
    return pl.pallas_call(
        functools.partial(ffn_kernel, co_row),
        in_specs=[vmem, vmem, ANY, ANY, ANY, vmem, vmem, vmem, ANY, ANY, ANY, ANY, ANY],
        out_specs=[ANY, ANY, ANY, ANY, ANY, vmem],
        out_shape=[thin, thin, jax.ShapeDtypeStruct((rows, d), jnp.float32), thin, thin,
                   jax.ShapeDtypeStruct(part, jnp.bfloat16)],
        scratch_shapes=[
            pltpu.VMEM((rows, d), jnp.bfloat16),
            pltpu.VMEM((rows, d), jnp.bfloat16),
            pltpu.VMEM((2, *co_own.shape), jnp.bfloat16),
            pltpu.VMEM((2, 8, d // 8, CHUNK), jnp.bfloat16),
            pltpu.VMEM((2, 2, CHUNK // 2, d), jnp.bfloat16),
            pltpu.VMEM((rows, d), jnp.bfloat16),
            pltpu.VMEM((rows, d), jnp.bfloat16),
            pltpu.VMEM((rows, d), jnp.bfloat16),
            pltpu.VMEM((rows, d), jnp.bfloat16),
            pltpu.VMEM((rows, d), jnp.float32),
            pltpu.VMEM((2 * hidden_half // CHUNK, rows, CHUNK), jnp.bfloat16),
            pltpu.VMEM((rows, bottleneck), jnp.bfloat16),
            pltpu.VMEM((rows, bottleneck), jnp.float32),
            pltpu.VMEM((rows, bottleneck), jnp.bfloat16),
            pltpu.VMEM((2, 2, *part), jnp.float32),
            pltpu.VMEM((2, *part), jnp.float32),
            pltpu.VMEM((2, *part), jnp.bfloat16),
            pltpu.VMEM((2, *part), jnp.bfloat16),
            pltpu.SemaphoreType.DMA((4,)),
            pltpu.SemaphoreType.DMA((2, 3)),
            pltpu.SemaphoreType.DMA((3,)),
            pltpu.SemaphoreType.DMA((3,)),
            pltpu.SemaphoreType.DMA((3,)),
        ],
        compiler_params=pltpu.CompilerParams(collective_id=3, has_side_effects=True, vmem_limit_bytes=63 * MIB),
        cost_estimate=pl.CostEstimate(flops=flops, bytes_accessed=48 * MIB, transcendentals=0),
        name="ffn_both_ways",
    )(own, par, first, cot_mine, cot_got, gains, down, up, co_own, packed, in_own, out_own, ffn_other)


PREFIX_STEPS = ("x", "zl", "y", "zh")


def finish_kernel(dq_own, dq_got, dkv_own, dkv_got, gfirst, w_own, w_oth, mem_keep, mem_got, o_keep, o_got, pre_ref, part_ref,
                  out_ref, mem_ref, o_ref, pre_out_ref, part_got_ref,
                  lhs, first, held, boxes, stage, sums, arrived, local, place, send, recv):
    x, core = lax.axis_index("x"), lax.axis_index("c")
    here = {name: lax.axis_index(name) for name in PREFIX_STEPS}
    partner, across = {"c": 1 - core}, {"x": 1 - x}
    stays = x == core
    blocks = lhs.shape[0]
    half = blocks * BT
    cols = out_ref.shape[1]
    d = held.shape[1] // 3
    steps = len(PREFIX_STEPS) + 1

    def loads(b):
        rows = pl.ds(b * BT, BT)
        pairs = [(dq_own.at[rows], lhs.at[b, 0]), (dkv_own.at[0, rows], lhs.at[b, 1]), (dkv_own.at[1, rows], lhs.at[b, 2]),
                 (dq_got.at[rows], lhs.at[b, 3]), (dkv_got.at[0, rows], lhs.at[b, 4]), (dkv_got.at[1, rows], lhs.at[b, 5]),
                 (gfirst.at[rows], first.at[b])]
        return [pltpu.make_async_copy(src, dst, local.at[b, n]) for n, (src, dst) in enumerate(pairs)]

    def weights(agree):
        pair = (w_own, w_oth) if agree else (w_oth, w_own)
        return [pltpu.make_async_copy(src, held.at[n], local.at[blocks, n]) for n, src in enumerate(pair)]

    ours = pl.ds(pl.multiple_of(core * half, half), half)

    def settled(agree):
        mine, passed = ((mem_keep, o_keep), (mem_got, o_got)) if agree else ((mem_got, o_got), (mem_keep, o_keep))
        return (
            [pltpu.make_async_copy(src, stage.at[n], local.at[blocks, 2 + n]) for n, src in enumerate(mine)],
            [pltpu.make_async_copy(stage.at[n], to.at[ours], local.at[blocks, 4 + n]) for n, to in enumerate((mem_ref, o_ref))],
            [
                remote(src, to.at[ours], send.at[0, blocks + n], recv.at[blocks + n, core], partner)
                for n, (src, to) in enumerate(zip(passed, (mem_ref, o_ref)))
            ],
        )

    def prefix_copy(s):
        target = {PREFIX_STEPS[s]: 1 - here[PREFIX_STEPS[s]]} if s < steps - 1 else partner
        return remote(sums.at[s], arrived.at[s], send.at[2, s], recv.at[blocks + 2 + s, 0], target)

    for copy in loads(0):
        copy.start()
    for agree, chosen in ((True, stays), (False, jnp.logical_not(stays))):
        @pl.when(chosen)
        def _(agree=agree):
            for copy in weights(agree):
                copy.start()

    for b in range(1, blocks):
        for copy in loads(b):
            copy.start()
    for agree, chosen in ((True, stays), (False, jnp.logical_not(stays))):
        @pl.when(chosen)
        def _(agree=agree):
            for copy in settled(agree)[0]:
                copy.start()

    sums[0] = low(pre_ref[...])
    greet([across, {"x": 1 - x, "c": 1 - core}, partner] + [{name: 1 - here[name]} for name in PREFIX_STEPS[1:]])
    prefix_copy(0).start()
    part_copy = remote(
        part_ref, part_got_ref, send.at[1, blocks], recv.at[blocks + 2, 1], {"zl": 1 - here["zl"]}
    )
    part_copy.start()

    def landing(b):
        return pl.ds(pl.multiple_of(core * half + b * BT, BT), BT)

    def over(b):
        return remote(boxes.at[b, 0], out_ref.at[landing(b)], send.at[0, b], recv.at[b, core], {"x": 1 - x, "c": x})

    def beside(b):
        return remote(boxes.at[b, 1], out_ref.at[landing(b)], send.at[1, b], recv.at[b, core], partner)

    def kept_here(b):
        return pltpu.make_async_copy(boxes.at[b, 1], out_ref.at[landing(b)], place.at[b])

    def compute(b, which):
        at = pl.ds(pl.multiple_of(which * cols, cols), cols)
        total = first[b, :, at]
        for n in range(6):
            rows = pl.ds(pl.multiple_of((n % 3) * d + which * cols, cols), cols)
            total += mm_nt(lhs[b, n], held[n // 3, rows, :])
        return low(total)

    def next_prefix(s):
        prefix_copy(s).wait()
        sums[s + 1] = low(sums[s].astype(jnp.float32) + arrived[s].astype(jnp.float32))
        prefix_copy(s + 1).start()

    for copy in weights(True):
        copy.wait()
    for b in range(blocks):
        for copy in loads(b):
            copy.wait()
        boxes[b, 0] = compute(b, 1 - x)
        over(b).start()
        if b == 1:
            next_prefix(0)
    for b in range(blocks):
        boxes[b, 1] = compute(b, x)

        @pl.when(stays)
        def _(b=b):
            kept_here(b).start()

        @pl.when(jnp.logical_not(stays))
        def _(b=b):
            beside(b).start()

        if b + 1 < steps - 1:
            next_prefix(b + 1)

    for agree, chosen in ((True, stays), (False, jnp.logical_not(stays))):
        @pl.when(chosen)
        def _(agree=agree):
            loaded, placed, passed = settled(agree)
            for copy in passed:
                copy.start()
            for copy in loaded:
                copy.wait()
            for copy in placed:
                copy.start()

    prefix_copy(steps - 1).wait()
    pre_out_ref[...] = jnp.where(stays, sums[steps - 1], arrived[steps - 1]).astype(jnp.float32)

    def wait_for(t, b):
        rows = out_ref.at[pl.ds(pl.multiple_of(t * half + b * BT, BT), BT)]
        remote(rows, rows, send.at[0, b], recv.at[b, t], across).wait_recv()

    part_copy.wait()
    theirs = pl.ds(pl.multiple_of((1 - core) * half, half), half)
    for n, to in enumerate((mem_ref, o_ref)):
        remote(to.at[theirs], to.at[theirs], send.at[0, 0], recv.at[blocks + n, 1 - core], partner).wait_recv()
    for agree, chosen in ((True, stays), (False, jnp.logical_not(stays))):
        @pl.when(chosen)
        def _(agree=agree):
            loaded, placed, passed = settled(agree)
            for copy in placed:
                copy.wait()
            for copy in passed:
                copy.wait_send()

    for b in range(blocks):
        over(b).wait_send()

        @pl.when(stays)
        def _(b=b):
            kept_here(b).wait()
            wait_for(1 - core, b)

        @pl.when(jnp.logical_not(stays))
        def _(b=b):
            beside(b).wait_send()
            for t in range(2):
                wait_for(t, b)


def finish_tokens(dq_own, dq_got, dkv_own, dkv_got, gfirst, w_own, w_oth, mem_keep, mem_got, o_keep, o_got, prefix, part):
    half, cols = dq_own.shape
    blocks = half // BT
    steps = len(PREFIX_STEPS) + 1
    vmem = pl.BlockSpec(memory_space=pltpu.VMEM)
    rows = jax.ShapeDtypeStruct((2 * half, cols), jnp.bfloat16)
    return pl.pallas_call(
        finish_kernel,
        in_specs=[ANY] * 11 + [vmem, vmem],
        out_specs=[ANY, ANY, ANY, vmem, vmem],
        out_shape=[rows, rows, rows, jax.ShapeDtypeStruct(prefix.shape, jnp.float32),
                   jax.ShapeDtypeStruct(part.shape, part.dtype)],
        scratch_shapes=[
            pltpu.VMEM((blocks, 6, BT, cols), jnp.bfloat16),
            pltpu.VMEM((blocks, BT, 2 * cols), jnp.float32),
            pltpu.VMEM((2, *w_own.shape), jnp.bfloat16),
            pltpu.VMEM((blocks, 2, BT, cols), jnp.bfloat16),
            pltpu.VMEM((2, half, cols), jnp.bfloat16),
            pltpu.VMEM((steps, *prefix.shape), jnp.bfloat16),
            pltpu.VMEM((steps, *prefix.shape), jnp.bfloat16),
            pltpu.SemaphoreType.DMA((blocks + 1, 7)),
            pltpu.SemaphoreType.DMA((blocks,)),
            pltpu.SemaphoreType.DMA((3, max(blocks + 2, steps))),
            pltpu.SemaphoreType.DMA((blocks + 2 + steps, 2)),
        ],
        compiler_params=pltpu.CompilerParams(collective_id=1, has_side_effects=True, vmem_limit_bytes=58 * MIB),
        cost_estimate=pl.CostEstimate(flops=12 * half * cols * 2 * cols, bytes_accessed=64 * MIB, transcendentals=0),
        name="finish_tokens",
    )(dq_own, dq_got, dkv_own, dkv_got, gfirst, w_own, w_oth, mem_keep, mem_got, o_keep, o_got, prefix, part)


def swap(value, axis):
    return lax.ppermute(value, axis, SWAP)


def after(value, *others):
    return lax.optimization_barrier((value, *others))[0]


def gather_half(piece):
    return lax.all_gather(piece, ("zl", "y", "c"), axis=0, tiled=True)


def paired_device(
    tokens, memory, dec_segments, mem_segments, self_qkv, self_out, cross_q, cross_kv, cross_out, ffn_in, ffn_out,
    adapter_down, adapter_up, self_prefix, cross_prefix, gains, cotangent,
):
    x, core = lax.axis_index("x"), lax.axis_index("c")
    agree = x == core
    columns = tokens.shape[1]
    prefix_count = self_prefix.shape[1]

    qkv_flat = self_qkv.reshape(-1, columns)
    ckv_flat = cross_kv.reshape(-1, columns)
    segs = jnp.concatenate([dec_segments, mem_segments], axis=0)
    prefixes = jnp.concatenate([self_prefix, cross_prefix], axis=0)
    prefixes = jnp.pad(prefixes, ((0, 0), (0, PP - prefix_count), (0, 0)))
    (
        rows_own, rows_par, mem_mine, packed, cot_mine, cot_send, qkv_other, prefixes_got, segs_got, down_full, up_full
    ) = bring_rows(
        tokens, memory, cotangent, qkv_flat, prefixes, segs, ffn_in, ffn_out,
        adapter_down, adapter_up,
    )
    segs = jnp.where(agree, segs, segs_got)
    dec_seg, mem_seg = segs[0], segs[1]
    prefixes = jnp.where(agree, prefixes, prefixes_got)
    self_pre, cross_pre = prefixes[:2], prefixes[2:]
    self_masks = mask_columns(dec_seg, dec_seg, prefix_count)
    self_lo, self_hi = ranges(dec_seg, dec_seg, True)
    cross_masks = mask_columns(dec_seg, mem_seg, prefix_count)
    cross_lo, cross_hi = ranges(dec_seg, mem_seg, False)

    own, par, piece = project(
        [rows_own], [rows_par], qkv_flat, qkv_other, 3, [self_out, cross_q, cross_out, ckv_flat]
    )
    others = gather_half(piece).reshape(8, *piece.shape)
    so_tall, cq_tall, ckv_tall = self_out.shape[0] // 8, cross_q.shape[0] // 8, ckv_flat.shape[0] // 8
    co_row = 2 * so_tall + cq_tall
    ckv_row = co_row + 2 * so_tall
    got = swap(after(packed, own), "x")
    self_q, self_k, self_v = ([(own, t), (par, t)] for t in range(3))
    self_o, self_ot, self_lt = attend_fwd(
        self_q, self_k, self_v, columns, self_masks, self_pre, self_lo, self_hi, True
    )
    heads_got = swap(self_o[1], "c")

    mem_got = got[:mem_mine.shape[0]]
    cot_got = swap(after(cot_send, got), "x")
    mem_par, mem_par_got = swap(mem_mine, "c"), swap(mem_got, "c")
    first_sum, cq_own, cq_send = after_self(
        self_o[0], heads_got, rows_own, gains, self_out, cross_q, others
    )
    ffn_other = gather_half(after(got, first_sum)[mem_mine.shape[0]:])
    ffn_other = ffn_other.reshape(8, -1, columns)
    cq_par = swap(cq_send, "c")
    own, par = project([mem_mine, mem_got], [mem_par, mem_par_got], ckv_flat, others[:, ckv_row:], 2)
    cross_qp = [(cq_own, 0), (cq_par, 0)]
    cross_k, cross_v = ([(own, t), (par, t)] for t in range(2))
    cross_o, cross_ot, cross_lt = attend_fwd(
        cross_qp, cross_k, cross_v, columns, cross_masks, cross_pre, cross_lo, cross_hi, False
    )
    cross_got = swap(cross_o[1], "c")
    out_keep, out_send, grad_second, g_own, g_send, part = ffn_both_ways(
        cross_o[0], cross_got, first_sum, cot_mine, cot_got, gains, down_full, up_full,
        cross_out, others, co_row, ffn_in, ffn_out, ffn_other,
    )
    g_par = swap(g_send, "c")
    out_got = swap(out_send, "x")

    part_got = swap(part, "zh")

    cdq, cdkv, cross_dp = attend_bwd(
        cross_qp, cross_k, cross_v, [(g_own, 0), (g_par, 0)], columns, cross_ot, cross_lt,
        cross_masks, cross_pre, cross_lo, cross_hi, False,
    )
    cdq_got = swap(after(cdq[1], out_got, part_got), "c")
    part = low(part.astype(jnp.float32) + part_got.astype(jnp.float32))
    cdkv_got = swap(cdkv[1], "c")
    grad_first, g_own, g_send = before_self(
        grad_second, cdq[0], cdq_got, first_sum, gains, self_out, cross_q, others
    )
    g_par = swap(g_send, "c")

    mem_keep, mem_out = back_memory(cdkv[0], cdkv_got, ckv_flat, others, ckv_row)
    mem_back = swap(mem_out, "x")
    g_par = after(g_par, mem_out)

    sdq, sdkv, self_dp = attend_bwd(
        self_q, self_k, self_v, [(g_own, 0), (g_par, 0)], columns, self_ot, self_lt,
        self_masks, self_pre, self_lo, self_hi, True,
    )
    sdq_got = swap(after(sdq[1], mem_back), "c")
    sdkv_got = swap(sdkv[1], "c")
    grad_tokens, grad_memory, output, prefix_sums, part_got = finish_tokens(
        sdq[0], sdq_got, sdkv[0], sdkv_got, grad_first, qkv_flat, qkv_other, mem_keep, mem_back, out_keep, out_got,
        jnp.concatenate([self_dp, cross_dp], axis=0), part,
    )
    part = part.astype(jnp.float32) + part_got.astype(jnp.float32)
    grad_down, grad_up = part[0].T, part[1]
    grad_tokens, grad_memory = grad_tokens.astype(jnp.float32), grad_memory.astype(jnp.float32)
    prefix_sums = prefix_sums[:, :prefix_count]

    return (output, grad_tokens, grad_memory, prefix_sums[:2], prefix_sums[2:], grad_down, grad_up)


def norm_grad(gathered, gain, upstream):
    n, r = normalize(gathered.astype(jnp.float32))
    return norm_back(n, r, gain, upstream)


def wide_device(
    tokens, memory, dec_segments, mem_segments, self_qkv, self_out, cross_q, cross_kv, cross_out, ffn_in, ffn_out,
    adapter_down, adapter_up, self_prefix, cross_prefix, gains, cotangent,
):
    n_wide = lax.axis_size("wide")
    row_count, columns = tokens.shape
    own_start = lax.axis_index("wide") * columns
    block_size = row_count // n_wide
    block_start = lax.axis_index("wide") * block_size
    prefix_count = self_prefix.shape[1]
    dec_seg, mem_seg = dec_segments[0], mem_segments[0]

    def collect(values):
        return lax.all_gather(values, "wide", axis=1, tiled=True)

    def spread(term):
        return lax.psum_scatter(term, "wide", scatter_dimension=1, tiled=True)

    def own_columns(values):
        return lax.dynamic_slice_in_dim(values, own_start, columns, 1)

    def padded(prefix):
        return jnp.pad(prefix, ((0, 0), (0, PP - prefix_count), (0, 0)))

    self_masks = mask_columns(dec_seg, dec_seg, prefix_count)
    self_lo, self_hi = ranges(dec_seg, dec_seg, True)
    cross_masks = mask_columns(dec_seg, mem_seg, prefix_count)
    cross_lo, cross_hi = ranges(dec_seg, mem_seg, False)
    self_pre, cross_pre = padded(self_prefix), padded(cross_prefix)

    all_tokens, all_memory = collect(tokens), collect(memory)
    self_q, self_k, self_v = ([(low(mm(all_tokens, self_qkv[t])), 0)] for t in range(3))
    (self_heads,), self_ot, self_lt = attend_fwd(
        self_q, self_k, self_v, columns, self_masks, self_pre, self_lo, self_hi, True
    )
    first_sum = low(tokens.astype(jnp.float32) + spread(mm(self_heads, self_out)))
    gathered_one = collect(first_sum)
    normed_one = normalize(gathered_one.astype(jnp.float32))[0] * gains[0]
    cross_qp = [(low(mm(low(normed_one), cross_q)), 0)]
    cross_k, cross_v = ([(low(mm(all_memory, cross_kv[t])), 0)] for t in range(2))
    (cross_heads,), cross_ot, cross_lt = attend_fwd(
        cross_qp, cross_k, cross_v, columns, cross_masks, cross_pre, cross_lo, cross_hi, False
    )
    second_sum = low(own_columns(normed_one) + spread(mm(cross_heads, cross_out)))
    gathered_two = collect(second_sum)
    normed_two = normalize(gathered_two.astype(jnp.float32))[0] * gains[1]
    normed_low = low(normed_two)
    adapter_in = lax.dynamic_slice_in_dim(normed_low, block_start, block_size, 0)
    adapter_rows = lax.all_gather(adapter_in, "narrow", axis=0, tiled=True)
    bottle, bottle_slope = gelu_parts(mm(adapter_rows, adapter_down))
    bottle = low(bottle)
    adapted = lax.psum_scatter(low(mm(bottle, adapter_up)), "narrow", scatter_dimension=0, tiled=True)
    hidden, slope = gelu_parts(mm(normed_low, ffn_in))
    branch = mm(low(hidden), ffn_out)
    placed = lax.dynamic_slice_in_dim(branch, block_start, block_size, 0) + 4.0 * adapted.astype(jnp.float32)
    branch = lax.dynamic_update_slice_in_dim(branch, placed, block_start, 0)
    third_sum = low(own_columns(normed_two) + spread(branch))
    gathered_three = collect(third_sum)
    output = low(own_columns(normalize(gathered_three.astype(jnp.float32))[0] * gains[2]))
    grad_three = norm_grad(gathered_three, gains[2], collect(cotangent).astype(jnp.float32))
    grad_branch = low(grad_three)
    grad_pre = low(mm_nt(grad_branch, ffn_out) * slope)
    grad_normed = mm_nt(grad_pre, ffn_in)
    grad_adapted = low(4.0 * lax.dynamic_slice_in_dim(grad_branch, block_start, block_size, 0).astype(jnp.float32))
    grad_adapted = lax.all_gather(grad_adapted, "narrow", axis=0, tiled=True)
    bottle_grad = low(mm_nt(grad_adapted, adapter_up) * bottle_slope)
    grad_in = lax.psum_scatter(low(mm_nt(bottle_grad, adapter_down)), "narrow", scatter_dimension=0, tiled=True)
    placed = lax.dynamic_slice_in_dim(grad_normed, block_start, block_size, 0) + grad_in.astype(jnp.float32)
    grad_normed = lax.dynamic_update_slice_in_dim(grad_normed, placed, block_start, 0)
    grad_down, grad_up = lax.psum(
        (mm_tn(adapter_rows, bottle_grad), mm_tn(bottle, grad_adapted)), ("dp", "wide")
    )
    grad_two = collect(low(own_columns(grad_three) + spread(grad_normed))).astype(jnp.float32)
    grad_second = norm_grad(gathered_two, gains[1], grad_two)
    grad_cross = low(mm_nt(low(grad_second), cross_out))
    (cdq,), (cdkv,), cross_dp = attend_bwd(
        cross_qp, cross_k, cross_v, [(grad_cross, 0)], columns, cross_ot, cross_lt,
        cross_masks, cross_pre, cross_lo, cross_hi, False,
    )
    spread_one = spread(low(mm_nt(cdq, cross_q))).astype(jnp.float32)
    grad_memory = spread(low(mm_nt(cdkv[0], cross_kv[0]) + mm_nt(cdkv[1], cross_kv[1]))).astype(jnp.float32)
    grad_one = collect(low(own_columns(grad_second) + spread_one)).astype(jnp.float32)
    grad_first = norm_grad(gathered_one, gains[0], grad_one)
    grad_self = low(mm_nt(low(grad_first), self_out))
    (sdq,), (sdkv,), self_dp = attend_bwd(
        self_q, self_k, self_v, [(grad_self, 0)], columns, self_ot, self_lt,
        self_masks, self_pre, self_lo, self_hi, True,
    )
    grad_input = mm_nt(sdq, self_qkv[0]) + mm_nt(sdkv[0], self_qkv[1]) + mm_nt(sdkv[1], self_qkv[2])
    grad_tokens = own_columns(grad_first) + spread(grad_input)
    totals = lax.psum((low(self_dp), low(cross_dp)), ("dp", "narrow"))
    grad_self_prefix, grad_cross_prefix = (t.astype(jnp.float32)[:, :prefix_count] for t in totals)
    return (output, grad_tokens, grad_memory, grad_self_prefix, grad_cross_prefix, grad_down, grad_up)


def solution(mesh):
    dp, wide, narrow = (mesh.shape[name] for name in ("dp", "wide", "narrow"))
    if (dp, wide, narrow) == (4, 2, 4):
        parts = Mesh(mesh.devices.reshape(2, 2, 2, 2, 2), ("zh", "zl", "x", "y", "c"))
        device, used = paired_device, parts
        rows, split, thin = ("zh", "zl", "y", "c"), "x", ("y", "c")
    else:
        device, used = wide_device, mesh
        rows, split, thin = ("dp", "narrow"), "wide", "narrow"
    return jax.shard_map(
        device,
        mesh=used,
        in_specs=(
            P(rows, split),
            P(rows, split),
            P(rows, None),
            P(rows, None),
            P(None, None, split),
            P(split, None),
            P(None, split),
            P(None, None, split),
            P(split, None),
            P(None, split),
            P(split, None),
            P(None, thin),
            P(thin, None),
            P(None, None, split),
            P(None, None, split),
            P(),
            P(rows, split),
        ),
        out_specs=(
            P(rows, split),
            P(rows, split),
            P(rows, split),
            P(None, None, split),
            P(None, None, split),
            P(None, thin),
            P(thin, None),
        ),
        check_vma=False,
    )
```

```python
import functools
import math
from functools import partial

import jax
import jax.numpy as jnp
from jax import lax
from jax.experimental import pallas as pl
from jax.experimental.pallas import tpu as pltpu
from jax.sharding import Mesh
from jax.sharding import PartitionSpec as P

HEAD_DIM = 64
DOCS = 4
NEG = -1e30
BQ = 256
BK = 256
BP = 1024
FWD_KEYS = 2
BWD_KEYS = 2
PP = 32
BT = 256
BR = 512
HEADS_FWD = 8
HEADS_BWD = 4
SWAP = [(0, 1), (1, 0)]
MIB = 2**20


def mm(a, b):
    return jnp.dot(a, b, preferred_element_type=jnp.float32)


def mm_nt(a, b):
    return lax.dot_general(a, b, (((1,), (1,)), ((), ())), preferred_element_type=jnp.float32)


def mm_tn(a, b):
    return lax.dot_general(a, b, (((0,), (0,)), ((), ())), preferred_element_type=jnp.float32)


def part_offsets(n_parts, part_len):
    if n_parts == 1:
        return [0]
    core = lax.axis_index("c")
    return [pl.multiple_of(core * part_len, part_len), pl.multiple_of((1 - core) * part_len, part_len)]


def block_at(i, size):
    return pl.ds(pl.multiple_of(i * size, size), size)


def key_blocks(j, count):
    return pl.ds(pl.multiple_of(j * BK, BK), count * BK)


def for_key_blocks(lo, hi, most, act):
    rounds = (hi - lo) // most

    def many(t, _):
        act(lo + t * most, most)
        return 0

    def single(j, _):
        act(j, 1)
        return 0

    if most > 1:
        lax.fori_loop(0, rounds, many, 0)
        lax.fori_loop(lo + rounds * most, hi, single, 0)
    else:
        lax.fori_loop(lo, hi, single, 0)


def head_rows(h):
    return pl.ds(h * HEAD_DIM, HEAD_DIM)


def later_keys(shape):
    return lax.broadcasted_iota(jnp.int32, shape, 0) > lax.broadcasted_iota(jnp.int32, shape, 1)


def by_head(prefix, heads_here):
    shape = (heads_here * PP, heads_here * HEAD_DIM)
    rows = lax.broadcasted_iota(jnp.int32, shape, 0) // PP
    columns = lax.broadcasted_iota(jnp.int32, shape, 1) // HEAD_DIM
    tall = jnp.concatenate([prefix] * heads_here, axis=0)
    return jnp.where(rows == columns, tall, jnp.zeros((), prefix.dtype))


def padding_rows(shape, prefix_count):
    return lax.broadcasted_iota(jnp.int32, shape, 0) % PP >= prefix_count


def load_queries(q_turned, h, eq, qx, here):
    zero = jnp.zeros((HEAD_DIM, q_turned.shape[1]), q_turned.dtype)
    mine = (h % 2) * HEAD_DIM
    qx[h, pl.ds(mine, HEAD_DIM), here] = q_turned[h * HEAD_DIM:(h + 1) * HEAD_DIM]
    qx[h, pl.ds(HEAD_DIM - mine, HEAD_DIM), here] = zero
    if eq is not None:
        qx[h, pl.ds(2 * HEAD_DIM, 2 * HEAD_DIM), here] = eq


def fwd_kernel(causal, n_parts, prefix_count, lo_ref, hi_ref, *refs):
    q_parts, k_parts, v_parts = refs[:n_parts], refs[n_parts:2 * n_parts], refs[2 * n_parts:3 * n_parts]
    ek_ref, eq_ref, pre_ref = refs[3 * n_parts:3 * n_parts + 3]
    o_parts = refs[3 * n_parts + 3:4 * n_parts + 3]
    ot_ref, lt_ref, qt, qx, vx, ke, acc, top = refs[4 * n_parts + 3:]
    seq = qt.shape[1]
    q_len, m_len = q_parts[0].shape[0], k_parts[0].shape[0]
    heads_here = qt.shape[0] // HEAD_DIM
    n_pairs = heads_here // 2
    n_q = seq // BQ
    ones_rows = vx.shape[1] - HEAD_DIM

    for q_ref, at in zip(q_parts, part_offsets(n_parts, q_len)):
        here = pl.ds(at, q_len)
        q_turned = (q_ref[...] * jnp.bfloat16(0.125)).T
        qt[:, here] = q_turned
        for h in range(heads_here):
            load_queries(q_turned, h, eq_ref[:, here], qx, here)
    for k_ref, v_ref, at in zip(k_parts, v_parts, part_offsets(n_parts, m_len)):
        here = pl.ds(at, m_len)
        v_turned = v_ref[...].T
        for h in range(heads_here):
            vx[h, :HEAD_DIM, here] = v_turned[h * HEAD_DIM:(h + 1) * HEAD_DIM]
        for p in range(n_pairs):
            ke[p, here, :128] = k_ref[:, p * 128:(p + 1) * 128]
    for h in range(heads_here):
        vx[h, HEAD_DIM:, :] = jnp.ones((ones_rows, vx.shape[2]), jnp.bfloat16)
    for p in range(n_pairs):
        ke[p, :, 128:] = ek_ref[...]
    keys_p = by_head(pre_ref[0], heads_here)
    values_p = by_head(pre_ref[1], heads_here).T

    wide = min(BP, seq)

    def prefix_step(find_top):
        def step(i, _):
            qs = block_at(i, wide)
            scores = mm(keys_p, qt[:, qs])
            scores = jnp.where(padding_rows(scores.shape, prefix_count), NEG, scores)
            chances = []
            for h in range(heads_here):
                s = scores[h * PP:(h + 1) * PP]
                if find_top:
                    top[h:h + 1, qs] = jnp.max(s, axis=0, keepdims=True)
                p = jnp.exp(s - top[h:h + 1, qs])
                acc[h, HEAD_DIM:, qs] = jnp.broadcast_to(jnp.sum(p, axis=0, keepdims=True), (ones_rows, wide))
                chances.append(low(p))
            out = mm(values_p, jnp.concatenate(chances, axis=0))
            for h in range(heads_here):
                acc[h, :HEAD_DIM, qs] = out[h * HEAD_DIM:(h + 1) * HEAD_DIM]
            return 0

        lax.fori_loop(0, seq // wide, step, 0)

    def scores_of(i, j, count, diag):
        qs, ks = block_at(i, BQ), key_blocks(j, count)
        scores = [mm(ke[h // 2, ks, :], qx[h, :, qs]) for h in range(heads_here)]
        if diag:
            scores = [jnp.where(later_keys(s.shape), NEG, s) for s in scores]
        return scores

    def add_block(i, j, count, diag):
        qs, ks = block_at(i, BQ), key_blocks(j, count)
        scores = scores_of(i, j, count, diag)
        for h in range(heads_here):
            p = low(jnp.exp(scores[h] - top[h:h + 1, qs]))
            acc[h, :, qs] += mm(vx[h, :, ks], p)

    def raise_top(i, j, count, diag):
        qs = block_at(i, BQ)
        for h, s in enumerate(scores_of(i, j, count, diag)):
            top[h:h + 1, qs] = jnp.maximum(top[h:h + 1, qs], jnp.max(s, axis=0, keepdims=True))

    def all_blocks(act):
        def step(i, _):
            if causal:
                act(i, i, 1, True)
            for_key_blocks(lo_ref[i], hi_ref[i], FWD_KEYS, lambda j, count: act(i, j, count, False))
            return 0

        lax.fori_loop(0, n_q, step, 0)

    prefix_step(True)
    all_blocks(add_block)
    largest = jnp.max(jnp.where(acc[0, HEAD_DIM:HEAD_DIM + 8, :] < 1e30, 0.0, 1.0))
    for h in range(1, heads_here):
        largest = jnp.maximum(largest, jnp.max(jnp.where(acc[h, HEAD_DIM:HEAD_DIM + 8, :] < 1e30, 0.0, 1.0)))

    @pl.when(largest > 0.5)
    def _():
        all_blocks(raise_top)
        prefix_step(False)
        all_blocks(add_block)

    def finish(i, _):
        qs = block_at(i, BQ)
        outs = []
        for h in range(heads_here):
            total = acc[h, HEAD_DIM:HEAD_DIM + 1, qs]
            lt_ref[h // 2, h % 2:h % 2 + 1, qs] = top[h:h + 1, qs] + jnp.log(total)
            outs.append(acc[h, :HEAD_DIM, qs] / total)
        ot = jnp.concatenate(outs, axis=0)
        ot_ref[:, qs] = low(ot)
        store_part(o_parts, i, low(ot.T))
        return 0

    lax.fori_loop(0, n_q, finish, 0)


def store_part(parts, i, value):
    per_part = parts[0].shape[0] // BQ
    at = pl.ds(pl.multiple_of((i % per_part) * BQ, BQ), BQ)
    if len(parts) == 1:
        parts[0][at, :] = value
        return
    own = i // per_part == lax.axis_index("c")

    @pl.when(own)
    def _():
        parts[0][at, :] = value

    @pl.when(jnp.logical_not(own))
    def _():
        parts[1][at, :] = value


def attend_fwd(qs, ks, vs, cols, masks, prefix, lo, hi, causal):
    ek, eq, prefix_count = masks
    n = len(qs)
    q_len, m_len = qs[0][0].shape[0], ks[0][0].shape[0]
    seq, mem = q_len * n, m_len * n
    wd = min(HEAD_DIM * HEADS_FWD, cols)
    heads_here = wd // HEAD_DIM
    steps = cols // wd
    in_specs, operands = [], []
    for group, length in ((qs, q_len), (ks, m_len), (vs, m_len)):
        for array, at in group:
            in_specs.append(pl.BlockSpec((length, wd), partial(lambda at, p, *_: (0, at * steps + p), at)))
            operands.append(array)
    in_specs += [
        pl.BlockSpec((mem, 128), lambda p, *_: (0, 0)),
        pl.BlockSpec((128, seq), lambda p, *_: (0, 0)),
        pl.BlockSpec((2, PP, wd), lambda p, *_: (0, 0, p)),
    ]
    grid_spec = pltpu.PrefetchScalarGridSpec(
        num_scalar_prefetch=2,
        grid=(steps,),
        in_specs=in_specs,
        out_specs=[pl.BlockSpec((q_len, wd), lambda p, *_: (0, p))] * n
        + [
            pl.BlockSpec((wd, seq), lambda p, *_: (p, 0)),
            pl.BlockSpec((wd // 128, 2, seq), lambda p, *_: (p, 0, 0)),
        ],
        scratch_shapes=[
            pltpu.VMEM((wd, seq), jnp.bfloat16),
            pltpu.VMEM((heads_here, 256, seq), jnp.bfloat16),
            pltpu.VMEM((heads_here, HEAD_DIM + 16, mem), jnp.bfloat16),
            pltpu.VMEM((wd // 128, mem, 256), jnp.bfloat16),
            pltpu.VMEM((heads_here, HEAD_DIM + 16, seq), jnp.float32),
            pltpu.VMEM((8, seq), jnp.float32),
        ],
    )
    result = pl.pallas_call(
        functools.partial(fwd_kernel, causal, n, prefix_count),
        grid_spec=grid_spec,
        out_shape=[jax.ShapeDtypeStruct((q_len, cols), jnp.bfloat16)] * n
        + [
            jax.ShapeDtypeStruct((cols, seq), jnp.bfloat16),
            jax.ShapeDtypeStruct((cols // 128, 2, seq), jnp.float32),
        ],
        compiler_params=pltpu.CompilerParams(vmem_limit_bytes=60 * MIB),
        cost_estimate=pl.CostEstimate(
            flops=8 * seq * mem * cols, bytes_accessed=12 * MIB, transcendentals=seq * mem * cols // 256
        ),
        name="attend_fwd_self" if causal else "attend_fwd_cross",
    )(lo, hi, *operands, ek, eq, prefix)
    return result[:n], result[n], result[n + 1]


def bwd_kernel(causal, n_parts, prefix_count, lo_ref, hi_ref, *refs):
    q_parts, k_parts, v_parts, g_parts = (refs[t * n_parts:(t + 1) * n_parts] for t in range(4))
    ot_ref, lt_ref, ek_ref, eq_ref, pre_ref = refs[4 * n_parts:4 * n_parts + 5]
    dq_parts = refs[4 * n_parts + 5:5 * n_parts + 5]
    dkv_parts = refs[5 * n_parts + 5:6 * n_parts + 5]
    dp_ref, qt, gt, qx, gx, kt, ke, vv, qm, gm, dq, dk, dv, delta = refs[6 * n_parts + 5:]
    seq = qt.shape[1]
    q_len, m_len = q_parts[0].shape[0], k_parts[0].shape[0]
    width = qt.shape[0]
    heads_here = width // HEAD_DIM
    n_pairs = heads_here // 2
    n_q = seq // BQ
    lane = lax.broadcasted_iota(jnp.int32, (1, width), 1)
    first = lane % 128 < HEAD_DIM
    zero = jnp.zeros((), jnp.bfloat16)

    for q_ref, g_ref, at in zip(q_parts, g_parts, part_offsets(n_parts, q_len)):
        here = pl.ds(at, q_len)
        q_all = q_ref[...] * jnp.bfloat16(0.125)
        g_all = g_ref[...]
        q_turned, g_turned = q_all.T, g_all.T
        qt[:, here] = q_turned
        gt[:, here] = g_turned
        for h in range(heads_here):
            load_queries(q_turned, h, eq_ref[:, here], qx, here)
            load_queries(g_turned, h, None, gx, here)
        qm[0, here, :] = jnp.where(first, q_all, zero)
        qm[1, here, :] = jnp.where(first, zero, q_all)
        gm[0, here, :] = jnp.where(first, g_all, zero)
        gm[1, here, :] = jnp.where(first, zero, g_all)
        prod = g_turned.astype(jnp.float32) * ot_ref[:, here].astype(jnp.float32)
        for h in range(heads_here):
            delta[h:h + 1, here] = jnp.sum(prod[h * HEAD_DIM:(h + 1) * HEAD_DIM], axis=0, keepdims=True)
    for k_ref, v_ref, at in zip(k_parts, v_parts, part_offsets(n_parts, m_len)):
        here = pl.ds(at, m_len)
        kt[:, here] = k_ref[...].T
        vv[here, :] = v_ref[...]
        for p in range(n_pairs):
            ke[p, here, :128] = k_ref[:, p * 128:(p + 1) * 128]
    for p in range(n_pairs):
        ke[p, :, 128:] = ek_ref[...]
    dk[...] = jnp.zeros_like(dk)
    dv[...] = jnp.zeros_like(dv)
    keys_p = by_head(pre_ref[0], heads_here)
    values_p = by_head(pre_ref[1], heads_here)
    keys_turned = keys_p.T

    def grads(s, dp, h, qs):
        p = jnp.exp(s - lt_ref[h // 2, h % 2:h % 2 + 1, qs])
        ds = low(p * (dp - delta[h:h + 1, qs]))
        return low(p), ds

    wide = min(BP, seq)

    def prefix_step(i, totals):
        qs = block_at(i, wide)
        scores = mm(keys_p, qt[:, qs])
        scores = jnp.where(padding_rows(scores.shape, prefix_count), NEG, scores)
        dps = mm(values_p, gt[:, qs])
        chances, slopes = [], []
        for h in range(heads_here):
            rows = slice(h * PP, (h + 1) * PP)
            p, ds = grads(scores[rows], dps[rows], h, qs)
            chances.append(p)
            slopes.append(ds)
        p, ds = jnp.concatenate(chances, axis=0), jnp.concatenate(slopes, axis=0)
        dq[:, qs] = mm(keys_turned, ds)
        dkp = totals[0] + mm(ds, qm[0, qs, :] + qm[1, qs, :])
        dvp = totals[1] + mm(p, gm[0, qs, :] + gm[1, qs, :])
        return dkp, dvp

    zeros = jnp.zeros((heads_here * PP, width), jnp.float32)
    totals = lax.fori_loop(0, seq // wide, prefix_step, (zeros, zeros))
    for n, total in enumerate(totals):
        rows = lax.broadcasted_iota(jnp.int32, total.shape, 0) // PP
        columns = lax.broadcasted_iota(jnp.int32, total.shape, 1) // HEAD_DIM
        total = jnp.where(rows == columns, total, 0.0)
        folded = total[:PP]
        for h in range(1, heads_here):
            folded += total[h * PP:(h + 1) * PP]
        dp_ref[n] = folded

    def add_block(i, j, count, diag):
        qs, ks = block_at(i, BQ), key_blocks(j, count)
        both = []
        for h in range(heads_here):
            c = (h // 2) * 128
            both.append((mm(ke[h // 2, ks, :], qx[h, :, qs]), mm(vv[ks, c:c + 128], gx[h, :, qs])))
        for pr in range(n_pairs):
            c = pr * 128
            dkb = dk[ks, c:c + 128]
            dvb = dv[ks, c:c + 128]
            for h in (2 * pr, 2 * pr + 1):
                s, dp = both[h]
                if diag:
                    s = jnp.where(later_keys(s.shape), NEG, s)
                p, ds = grads(s, dp, h, qs)
                dvb += mm(p, gm[h % 2, qs, c:c + 128])
                dkb += mm(ds, qm[h % 2, qs, c:c + 128])
                dq[head_rows(h), qs] += mm(kt[h * HEAD_DIM:(h + 1) * HEAD_DIM, ks], ds)
            dk[ks, c:c + 128] = dkb
            dv[ks, c:c + 128] = dvb

    def q_step(i, _):
        if causal:
            add_block(i, i, 1, True)
        for_key_blocks(lo_ref[i], hi_ref[i], BWD_KEYS, lambda j, count: add_block(i, j, count, False))
        return 0

    lax.fori_loop(0, n_q, q_step, 0)

    def finish(i, _):
        store_part(dq_parts, i, low((dq[:, block_at(i, BQ)] * 0.125).T))
        return 0

    lax.fori_loop(0, n_q, finish, 0)
    for dkv_ref, at in zip(dkv_parts, part_offsets(n_parts, m_len)):
        here = pl.ds(at, m_len)
        dkv_ref[0] = low(dk[here, :])
        dkv_ref[1] = low(dv[here, :])


def attend_bwd(qs, ks, vs, gs, cols, ot, lt, masks, prefix, lo, hi, causal):
    ek, eq, prefix_count = masks
    n = len(qs)
    q_len, m_len = qs[0][0].shape[0], ks[0][0].shape[0]
    seq, mem = q_len * n, m_len * n
    wd = min(HEAD_DIM * HEADS_BWD, cols)
    heads_here = wd // HEAD_DIM
    steps = cols // wd
    in_specs, operands = [], []
    for group, length in ((qs, q_len), (ks, m_len), (vs, m_len), (gs, q_len)):
        for array, at in group:
            in_specs.append(pl.BlockSpec((length, wd), partial(lambda at, p, *_: (0, at * steps + p), at)))
            operands.append(array)
    in_specs += [
        pl.BlockSpec((wd, seq), lambda p, *_: (p, 0)),
        pl.BlockSpec((wd // 128, 2, seq), lambda p, *_: (p, 0, 0)),
        pl.BlockSpec((mem, 128), lambda p, *_: (0, 0)),
        pl.BlockSpec((128, seq), lambda p, *_: (0, 0)),
        pl.BlockSpec((2, PP, wd), lambda p, *_: (0, 0, p)),
    ]
    grid_spec = pltpu.PrefetchScalarGridSpec(
        num_scalar_prefetch=2,
        grid=(steps,),
        in_specs=in_specs,
        out_specs=[pl.BlockSpec((q_len, wd), lambda p, *_: (0, p))] * n
        + [pl.BlockSpec((2, m_len, wd), lambda p, *_: (0, 0, p))] * n
        + [pl.BlockSpec((2, PP, wd), lambda p, *_: (0, 0, p))],
        scratch_shapes=[
            pltpu.VMEM((wd, seq), jnp.bfloat16),
            pltpu.VMEM((wd, seq), jnp.bfloat16),
            pltpu.VMEM((heads_here, 256, seq), jnp.bfloat16),
            pltpu.VMEM((heads_here, 128, seq), jnp.bfloat16),
            pltpu.VMEM((wd, mem), jnp.bfloat16),
            pltpu.VMEM((wd // 128, mem, 256), jnp.bfloat16),
            pltpu.VMEM((mem, wd), jnp.bfloat16),
            pltpu.VMEM((2, seq, wd), jnp.bfloat16),
            pltpu.VMEM((2, seq, wd), jnp.bfloat16),
            pltpu.VMEM((wd, seq), jnp.float32),
            pltpu.VMEM((mem, wd), jnp.float32),
            pltpu.VMEM((mem, wd), jnp.float32),
            pltpu.VMEM((8, seq), jnp.float32),
        ],
    )
    result = pl.pallas_call(
        functools.partial(bwd_kernel, causal, n, prefix_count),
        grid_spec=grid_spec,
        out_shape=[jax.ShapeDtypeStruct((q_len, cols), jnp.bfloat16)] * n
        + [jax.ShapeDtypeStruct((2, m_len, cols), jnp.bfloat16)] * n
        + [jax.ShapeDtypeStruct((2, PP, cols), jnp.float32)],
        compiler_params=pltpu.CompilerParams(vmem_limit_bytes=60 * MIB),
        cost_estimate=pl.CostEstimate(
            flops=12 * seq * mem * cols, bytes_accessed=20 * MIB, transcendentals=seq * mem * cols // 256
        ),
        name="attend_bwd_self" if causal else "attend_bwd_cross",
    )(lo, hi, *operands, ot, lt, ek, eq, prefix)
    return result[:n], result[n:2 * n], result[2 * n]


def ranges(dec_seg, mem_seg, causal):
    seq = dec_seg.shape[0]
    blocks = dec_seg.reshape(seq // BQ, BQ)
    low, high = blocks[:, 0], blocks[:, -1]
    lo = jnp.sum((mem_seg[None, :] < low[:, None]).astype(jnp.int32), axis=1) // BK
    if causal:
        hi = jnp.arange(seq // BQ, dtype=jnp.int32)
    else:
        hi = (jnp.sum((mem_seg[None, :] <= high[:, None]).astype(jnp.int32), axis=1) + BK - 1) // BK
    return lo, hi


def mask_columns(dec_seg, mem_seg, prefix_count):
    lane = jnp.arange(128, dtype=jnp.int32)
    row = lane[:, None]
    ek = (mem_seg[:, None] == lane[None, :]).astype(jnp.bfloat16)
    eq = jnp.where(jnp.logical_and(row < DOCS, row != dec_seg[None, :]), NEG, 0.0).astype(jnp.bfloat16)
    return ek, eq, prefix_count


def normalize(v):
    centered = v - jnp.mean(v, axis=-1, keepdims=True)
    r = lax.rsqrt(jnp.mean(centered * centered, axis=-1, keepdims=True) + 1e-05)
    return centered * r, r


def norm_back(n, r, gain, upstream):
    u = upstream * gain
    return r * (u - jnp.mean(u, axis=-1, keepdims=True) - n * jnp.mean(u * n, axis=-1, keepdims=True))


def gelu_parts(v):
    chance = 0.5 * (1.0 + lax.erf(v * math.sqrt(0.5)))
    slope = chance + v * (jnp.exp(-0.5 * v * v) * (1.0 / math.sqrt(2.0 * math.pi)))
    return v * chance, slope


def low(v):
    return v.astype(jnp.bfloat16)


def place_halves(own, packed, row, held, sems, at):
    x = lax.axis_index("x")
    tall, wide = held.shape[2:]
    cols = packed.shape[2]
    copies = [pltpu.make_async_copy(own, held.at[x], sems.at[at])]
    for j in range(wide // cols):
        copies.append(
            pltpu.make_async_copy(
                packed.at[:, pl.ds(row + j * tall, tall)],
                held.at[1 - x, :, :, pl.ds(j * cols, cols)],
                sems.at[at + 1 + j],
            )
        )
    return copies


def half_of(held, which):
    return held[which].reshape(-1, held.shape[3])


def eighths(weight):
    return weight.reshape(8, weight.shape[0] // 8, weight.shape[1])


def on_first(copies, act):
    @pl.when(pl.program_id(0) == 0)
    def _():
        for copy in copies:
            getattr(copy, act)()


def after_self_kernel(own_ref, par_ref, tok_ref, gains_ref, so_own, cq_own, packed,
                      first_ref, q_own_ref, q_par_ref, so, cq, sems):
    core = lax.axis_index("c")
    so_copies = place_halves(so_own, packed, 0, so, sems, 0)
    cq_copies = place_halves(cq_own, packed, 2 * so.shape[2], cq, sems, 4)
    on_first(so_copies + cq_copies, "start")
    on_first(so_copies, "wait")
    total = tok_ref[...].astype(jnp.float32) + (mm(own_ref[...], half_of(so, core)) + mm(par_ref[...], half_of(so, 1 - core)))
    first = low(total)
    first_ref[...] = first
    n, _ = normalize(first.astype(jnp.float32))
    normed = low(n * gains_ref[0:1, :])
    on_first(cq_copies, "wait")
    q_own_ref[...] = low(mm(normed, half_of(cq, core)))
    q_par_ref[...] = low(mm(normed, half_of(cq, 1 - core)))


def rows_spec(width):
    return pl.BlockSpec((BR, width), lambda i: (i, 0))


ANY = pl.BlockSpec(memory_space=pl.ANY)


def after_self(own, par, tokens, gains, so_own, cq_own, packed):
    rows, d = tokens.shape
    half = d // 2
    return pl.pallas_call(
        after_self_kernel,
        grid=(rows // BR,),
        in_specs=[rows_spec(half), rows_spec(half), rows_spec(d), pl.BlockSpec((3, d), lambda i: (0, 0)), ANY, ANY, ANY],
        out_specs=[rows_spec(d), rows_spec(half), rows_spec(half)],
        out_shape=[
            jax.ShapeDtypeStruct((rows, d), jnp.bfloat16),
            jax.ShapeDtypeStruct((rows, half), jnp.bfloat16),
            jax.ShapeDtypeStruct((rows, half), jnp.bfloat16),
        ],
        scratch_shapes=[
            pltpu.VMEM((2, 8, half // 8, d), jnp.bfloat16),
            pltpu.VMEM((2, 8, d // 8, half), jnp.bfloat16),
            pltpu.SemaphoreType.DMA((8,)),
        ],
        compiler_params=pltpu.CompilerParams(vmem_limit_bytes=58 * MIB),
        cost_estimate=pl.CostEstimate(flops=4 * rows * d * d, bytes_accessed=12 * MIB, transcendentals=0),
        name="after_self",
    )(own, par, tokens, gains, eighths(so_own), eighths(cq_own), packed)


def before_self_kernel(gsec_ref, own_ref, par_ref, first_ref, gains_ref, so_own, cq_own, packed,
                       gfirst_ref, g_own_ref, g_par_ref, so, cq, sems):
    core = lax.axis_index("c")
    so_copies = place_halves(so_own, packed, 0, so, sems, 0)
    cq_copies = place_halves(cq_own, packed, 2 * so.shape[2], cq, sems, 4)
    on_first(cq_copies + so_copies, "start")
    on_first(cq_copies, "wait")
    grad_one = low(gsec_ref[...] + (mm_nt(own_ref[...], half_of(cq, core)) + mm_nt(par_ref[...], half_of(cq, 1 - core))))
    n, r = normalize(first_ref[...].astype(jnp.float32))
    grad_first = norm_back(n, r, gains_ref[0:1, :], grad_one.astype(jnp.float32))
    gfirst_ref[...] = grad_first
    first_low = low(grad_first)
    on_first(so_copies, "wait")
    g_own_ref[...] = low(mm_nt(first_low, half_of(so, core)))
    g_par_ref[...] = low(mm_nt(first_low, half_of(so, 1 - core)))


def before_self(gsec, own, par, first, gains, so_own, cq_own, packed):
    rows, d = first.shape
    half = d // 2
    return pl.pallas_call(
        before_self_kernel,
        grid=(rows // BR,),
        in_specs=[
            rows_spec(d), rows_spec(half), rows_spec(half), rows_spec(d), pl.BlockSpec((3, d), lambda i: (0, 0)),
            ANY, ANY, ANY,
        ],
        out_specs=[rows_spec(d), rows_spec(half), rows_spec(half)],
        out_shape=[
            jax.ShapeDtypeStruct((rows, d), jnp.float32),
            jax.ShapeDtypeStruct((rows, half), jnp.bfloat16),
            jax.ShapeDtypeStruct((rows, half), jnp.bfloat16),
        ],
        scratch_shapes=[
            pltpu.VMEM((2, 8, half // 8, d), jnp.bfloat16),
            pltpu.VMEM((2, 8, d // 8, half), jnp.bfloat16),
            pltpu.SemaphoreType.DMA((8,)),
        ],
        compiler_params=pltpu.CompilerParams(vmem_limit_bytes=58 * MIB),
        cost_estimate=pl.CostEstimate(flops=4 * rows * d * d, bytes_accessed=16 * MIB, transcendentals=0),
        name="before_self",
    )(gsec, own, par, first, gains, eighths(so_own), eighths(cq_own), packed)


MESH_ID = pl.DeviceIdType.MESH
PARTS_IN = 4


def greet(targets):
    barrier = pltpu.get_barrier_semaphore()
    for target in targets:
        pl.semaphore_signal(barrier, inc=1, device_id=target, device_id_type=MESH_ID)
    pl.semaphore_wait(barrier, len(targets))


def remote(src, dst, send, recv, target):
    return pltpu.make_async_remote_copy(
        src_ref=src, dst_ref=dst, send_sem=send, recv_sem=recv, device_id=target, device_id_type=MESH_ID
    )


def eighth_index():
    return (lax.axis_index("zl") * 2 + lax.axis_index("y")) * 2 + lax.axis_index("c")


def piece_copies(wholes, packed, send, recv):
    cols = packed.shape[1]
    copies, at = [], 0
    for whole in wholes:
        tall = whole.shape[0] // 8
        source = pl.ds(pl.multiple_of(eighth_index() * tall, tall), tall)
        for j in range(whole.shape[1] // cols):
            n = len(copies)
            copies.append(
                remote(
                    whole.at[source, pl.ds(j * cols, cols)], packed.at[pl.ds(at, tall)], send.at[n], recv.at[n],
                    {"x": 1 - lax.axis_index("x")},
                )
            )
            at += tall
    return copies


def bring_kernel(tok, mem, cot, qkv, prefix, segs, w_in, w_out, down, up, so, cq, co, ckv,
                 rows_out, q_own, q_par, passed, mem_mine, packed, cot_mine, cot_send, qkv_oth, prefix_got, segs_got, down_all, up_all,
                 rows_own, rows_par, held, stage, stage_down, stage_up, send, recv, load, p_send, p_recv):
    x, y, zl, core = (lax.axis_index(name) for name in ("x", "y", "zl", "c"))
    half = rows_own.shape[0]
    cols = tok.shape[1]
    chunk = half // PARTS_IN
    piece = qkv.shape[0] // 8
    stays = x == core
    partner = {"c": 1 - core}
    across = {"x": 1 - x}

    def token_half(which):
        return pl.ds(pl.multiple_of(which * half, half), half)

    loads = [
        pltpu.make_async_copy(source.at[token_half(which)], stage.at[n], load.at[n])
        for n, (source, which) in enumerate(((mem, core), (cot, core)))
    ]
    at = 0
    for whole in (w_in, w_out):
        tall, wide = whole.shape[0] // 8, whole.shape[1]
        source = pl.ds(pl.multiple_of(eighth_index() * tall, tall), tall)
        for j in range(wide // cols):
            n = len(loads)
            loads.append(
                pltpu.make_async_copy(
                    whole.at[source, pl.ds(j * cols, cols)], stage.at[2, pl.ds(at, tall)], load.at[n]
                )
            )
            at += tall
    pack = pltpu.make_async_copy(stage.at[2], packed.at[pl.ds(half, half)], load.at[len(loads)])
    mem_send = packed.at[pl.ds(0, half)]
    for copy in loads:
        copy.start()
    greet([across, {"x": 1 - x, "c": 1 - core}, {"y": 1 - y}, {"zl": 1 - zl}, partner])

    def features(which):
        return pl.ds(pl.multiple_of(which * cols, cols), cols)

    def part(k):
        return pl.ds(k * chunk, chunk)

    def eighth(a, b, c):
        return pl.ds(pl.multiple_of(((a * 2 + b) * 2 + c) * piece, piece), piece)

    def weight(at, slot, target, source=None):
        return remote((qkv_oth if source is None else source).at[at], qkv_oth.at[at], send.at[slot], recv.at[slot], target)

    mine = eighth(zl, y, core)
    w_x = weight(mine, 0, across, qkv)
    w_x.start()
    at_small = 14 + 3 * PARTS_IN
    small = [
        remote(prefix, prefix_got, send.at[at_small], recv.at[at_small], across),
        remote(segs, segs_got, send.at[at_small + 1], recv.at[at_small + 1], partner),
    ]
    for copy in small:
        copy.start()
    others = small

    units = up.shape[0]

    def adapt_places(a, b):
        at = pl.ds(pl.multiple_of((a * 2 + b) * units, units), units)
        return down_all.at[:, at], up_all.at[at]

    def adapt_copies(sources, a, b, n, target):
        return [
            remote(source, place, send.at[at_small + 2 + n + m], recv.at[at_small + 2 + n + m], target)
            for m, (source, place) in enumerate(zip(sources, adapt_places(a, b)))
        ]

    adapt_y = adapt_copies((down, up), y, core, 0, {"y": 1 - y})
    adapt_c = adapt_copies((down, up), y, core, 2, partner)
    adapt_in = [
        pltpu.make_async_copy(down, stage_down, load.at[14]),
        pltpu.make_async_copy(up, stage_up, load.at[15]),
    ]
    for copy in adapt_y + adapt_c + adapt_in:
        copy.start()

    at_own, at_par = 8, 8 + PARTS_IN
    at_here = 8 + 2 * PARTS_IN

    def token_sends():
        copies = []
        for t in range(2):
            for k in range(PARTS_IN):
                slot = at_own + k
                copies.append(
                    remote(
                        tok.at[pl.ds(t * half + k * chunk, chunk)],
                        rows_own.at[part(k), features(x)],
                        send.at[slot + t * PARTS_IN],
                        recv.at[slot],
                        {"x": 1 - x, "c": t},
                    )
                )
        return copies

    def here_copies():
        own = tok.at[token_half(core)]
        other = tok.at[token_half(1 - core)]
        return [
            remote(other, rows_own.at[:, features(x)], send.at[at_here], recv.at[at_here], partner),
            remote(own, rows_par.at[:, features(x)], send.at[at_here + 1], recv.at[at_here + 1], partner),
        ]

    def weight_rows(source):
        tall = held.shape[0] // 3
        return [
            pltpu.make_async_copy(source.at[pl.ds(t * tall, tall)], held.at[pl.ds(t * tall, tall)], load.at[9 + t])
            for t in range(3)
        ]

    def own_weights():
        return weight_rows(qkv)

    def row_copy(source, to, slot):
        return remote(source.at[token_half(1 - core)], to, send.at[slot], recv.at[slot], partner)

    @pl.when(jnp.logical_not(stays))
    def _():
        for copy in token_sends():
            copy.start()
        row_copy(mem, mem_send, at_here + 3).start()
        row_copy(cot, cot_send, at_here + 5).start()
        for n, to, slot in ((0, mem_send, at_here + 3), (1, cot_send, at_here + 5)):
            loads[n].wait()
            pltpu.make_async_copy(stage.at[n], to, recv.at[slot]).start()

    @pl.when(stays)
    def _():
        for copy in here_copies():
            copy.start()
        row_copy(mem, mem_mine, at_here + 2).start()
        row_copy(cot, cot_mine, at_here + 4).start()
        for which, to, slot in ((core, rows_own, at_here), (1 - core, rows_par, at_here + 1)):
            pltpu.make_async_copy(tok.at[token_half(which)], to.at[:, features(x)], recv.at[slot]).start()
        for copy in own_weights():
            copy.start()
        for n, to, slot in ((0, mem_mine, at_here + 2), (1, cot_mine, at_here + 4)):
            loads[n].wait()
            pltpu.make_async_copy(stage.at[n], to, recv.at[slot]).start()

    for copy in loads[2:]:
        copy.wait()
    pack.start()
    adapt_here = [
        pltpu.make_async_copy(source, place, load.at[14 + m])
        for m, (source, place) in enumerate(zip((stage_down, stage_up), adapt_places(y, core)))
    ]
    for came, placed in zip(adapt_in, adapt_here):
        came.wait()
        placed.start()

    for copy in adapt_y:
        copy.wait_recv()
    adapt_yc = adapt_copies(adapt_places(1 - y, core), 1 - y, core, 4, partner)
    for copy in adapt_yc:
        copy.start()
    w_x.wait_recv()
    w_y = weight(mine, 1, {"y": 1 - y})
    w_z = weight(mine, 2, {"zl": 1 - zl})
    w_c = weight(mine, 4, partner)
    for copy in (w_y, w_z, w_c):
        copy.start()

    forwards = []

    def forward(k):
        here = rows_own.at[part(k), features(1 - x)]
        remote(here, here, send.at[at_own + k], recv.at[at_own + k], across).wait_recv()
        copy = remote(here, rows_par.at[part(k), features(1 - x)], send.at[at_here + 6 + k], recv.at[at_par + k], partner)
        copy.start()
        forwards.append(copy)

    forward(0)
    w_y.wait_recv()
    from_y = eighth(zl, 1 - y, core)
    w_yz = weight(from_y, 3, {"zl": 1 - zl})
    w_yc = weight(from_y, 5, partner)
    w_yz.start()
    w_yc.start()
    forward(1)
    w_z.wait_recv()
    w_zc = weight(eighth(1 - zl, y, core), 6, partner)
    w_zc.start()
    for k in range(2, PARTS_IN):
        forward(k)
    w_yz.wait_recv()
    w_yzc = weight(eighth(1 - zl, 1 - y, core), 7, partner)
    w_yzc.start()

    pieces = piece_copies((so, cq, co, ckv), passed, p_send, p_recv)
    for copy in pieces:
        copy.start()

    for copy in (w_c, w_yc, w_zc, w_yzc):
        copy.wait_recv()

    @pl.when(jnp.logical_not(stays))
    def _():
        for copy in weight_rows(qkv_oth):
            copy.start()

    for copy in weight_rows(qkv):
        copy.wait()
    for to, slot in ((rows_own.at[:, features(x)], at_here), (rows_par.at[:, features(x)], at_here + 1)):
        remote(to, to, send.at[slot], recv.at[slot], partner).wait_recv()
    tall = held.shape[0] // 3
    keep_rows = pltpu.make_async_copy(rows_own, rows_out, load.at[12])
    keep_rows.start()
    for t in range(3):
        q_own[:, t * cols:(t + 1) * cols] = low(mm(rows_own[...], held[t * tall:(t + 1) * tall, :]))
    for copy in forwards:
        copy.wait_recv()
    for t in range(3):
        q_par[:, t * cols:(t + 1) * cols] = low(mm(rows_par[...], held[t * tall:(t + 1) * tall, :]))
    keep_rows.wait()

    for copy in (*adapt_c, *adapt_yc, *others, *pieces):
        copy.wait_recv()
    for to, slot in (
        (mem_mine, at_here + 2),
        (mem_send, at_here + 3),
        (cot_mine, at_here + 4),
        (cot_send, at_here + 5),
    ):
        remote(to, to, send.at[slot], recv.at[slot], partner).wait_recv()

    pack.wait()
    for copy in adapt_here:
        copy.wait()

    for copy in (w_x, w_y, w_z, w_c, w_yz, w_yc, w_zc, w_yzc, *adapt_y, *adapt_c, *adapt_yc, *forwards, *others, *pieces):
        copy.wait_send()

    @pl.when(jnp.logical_not(stays))
    def _():
        for copy in token_sends():
            copy.wait_send()
        row_copy(mem, mem_send, at_here + 3).wait_send()
        row_copy(cot, cot_send, at_here + 5).wait_send()

    @pl.when(stays)
    def _():
        for copy in here_copies():
            copy.wait_send()
        row_copy(mem, mem_mine, at_here + 2).wait_send()
        row_copy(cot, cot_mine, at_here + 4).wait_send()


def bring_rows(tokens, memory, cotangent, qkv_flat, prefixes, segs, ffn_in, ffn_out, down, up, others):
    rows, cols = tokens.shape
    half = rows // 2
    wide_rows = jax.ShapeDtypeStruct((half, 2 * cols), jnp.bfloat16)
    thin_rows = jax.ShapeDtypeStruct((half, cols), jnp.bfloat16)
    slots = 22 + 3 * PARTS_IN
    packed_rows = sum(w.shape[0] // 8 * (w.shape[1] // cols) for w in others)
    pieces = sum(w.shape[1] // cols for w in others)
    vmem = pl.BlockSpec(memory_space=pltpu.VMEM)
    return pl.pallas_call(
        bring_kernel,
        in_specs=[ANY] * 14,
        out_specs=[ANY, vmem, vmem] + [ANY] * 10,
        out_shape=[wide_rows, jax.ShapeDtypeStruct((half, 3 * cols), jnp.bfloat16),
                   jax.ShapeDtypeStruct((half, 3 * cols), jnp.bfloat16),
                   jax.ShapeDtypeStruct((packed_rows, cols), jnp.bfloat16),
                   thin_rows, jax.ShapeDtypeStruct((rows, cols), jnp.bfloat16), thin_rows, thin_rows,
                   jax.ShapeDtypeStruct(qkv_flat.shape, jnp.bfloat16),
                   jax.ShapeDtypeStruct(prefixes.shape, prefixes.dtype),
                   jax.ShapeDtypeStruct(segs.shape, segs.dtype),
                   jax.ShapeDtypeStruct((down.shape[0], 4 * down.shape[1]), down.dtype),
                   jax.ShapeDtypeStruct((4 * up.shape[0], up.shape[1]), up.dtype)],
        scratch_shapes=[
            pltpu.VMEM((half, 2 * cols), jnp.bfloat16),
            pltpu.VMEM((half, 2 * cols), jnp.bfloat16),
            pltpu.VMEM(qkv_flat.shape, jnp.bfloat16),
            pltpu.VMEM((3, half, cols), jnp.bfloat16),
            pltpu.VMEM(down.shape, jnp.bfloat16),
            pltpu.VMEM(up.shape, jnp.bfloat16),
            pltpu.SemaphoreType.DMA((slots,)),
            pltpu.SemaphoreType.DMA((slots,)),
            pltpu.SemaphoreType.DMA((16,)),
            pltpu.SemaphoreType.DMA((pieces,)),
            pltpu.SemaphoreType.DMA((pieces,)),
        ],
        compiler_params=pltpu.CompilerParams(collective_id=0, has_side_effects=True, vmem_limit_bytes=58 * MIB),
        cost_estimate=pl.CostEstimate(flops=0, bytes_accessed=64 * MIB, transcendentals=0),
        name="bring_rows",
    )(tokens, memory, cotangent, qkv_flat, prefixes, segs, ffn_in, ffn_out, down, up, *others)


def project_kernel(n_weights, row, own_mine, own_got, par_mine, par_got, w_own, w_oth, out_own, out_par, held, sems):
    x, core = lax.axis_index("x"), lax.axis_index("c")
    d = held.shape[0] // n_weights
    cols = held.shape[1]

    def copies(agree):
        tall = held.shape[0] // 8
        parts = [w_own.at[pl.ds(e * tall, tall)] if agree else w_oth.at[e, pl.ds(row, tall)] for e in range(8)]
        return [
            pltpu.make_async_copy(part, held.at[pl.ds(e * tall, tall)], sems.at[e]) for e, part in enumerate(parts)
        ]

    for act in ("start", "wait"):
        for agree, chosen in ((True, x == core), (False, x != core)):
            @pl.when(jnp.logical_and(pl.program_id(0) == 0, chosen))
            def _(agree=agree, act=act):
                for copy in copies(agree):
                    getattr(copy, act)()

    for t in range(n_weights):
        for pieces, out in (((own_mine, own_got), out_own), ((par_mine, par_got), out_par)):
            total = None
            for piece, at in zip(pieces, (x * (d // 2), (1 - x) * (d // 2))):
                rows = pl.ds(pl.multiple_of(t * d + at, d // 2), d // 2)
                term = mm(piece[...], held[rows, :])
                total = term if total is None else total + term
            out[:, t * cols:(t + 1) * cols] = low(total)


def project(own, par, w_own, w_oth, row, n_weights):
    rows, cols = own[0].shape
    d = w_own.shape[0] // n_weights
    return pl.pallas_call(
        functools.partial(project_kernel, n_weights, row),
        grid=(rows // BR,),
        in_specs=[rows_spec(cols)] * 4 + [ANY, ANY],
        out_specs=[rows_spec(n_weights * cols)] * 2,
        out_shape=[jax.ShapeDtypeStruct((rows, n_weights * cols), jnp.bfloat16)] * 2,
        scratch_shapes=[pltpu.VMEM(w_own.shape, jnp.bfloat16), pltpu.SemaphoreType.DMA((8,))],
        compiler_params=pltpu.CompilerParams(vmem_limit_bytes=58 * MIB),
        cost_estimate=pl.CostEstimate(flops=4 * rows * d * cols * n_weights, bytes_accessed=16 * MIB, transcendentals=0),
        name="project",
    )(*own, *par, w_own, w_oth)


def back_memory_kernel(ckv_row, own_ref, got_ref, w_own, packed, keep_ref, send_ref, held, sems):
    x, core = lax.axis_index("x"), lax.axis_index("c")
    copies = place_halves(w_own, packed, ckv_row, held, sems, 0)
    on_first(copies, "start")
    on_first(copies, "wait")
    n_weights = own_ref.shape[0]
    share = 8 // (2 * n_weights)
    for out, which in ((send_ref, 1 - x), (keep_ref, x)):
        total = None
        for t in range(n_weights):
            for rows, heads in ((own_ref, core), (got_ref, 1 - core)):
                weight = held[heads, pl.ds(2 * share * t + share * which, share)]
                term = mm_nt(rows[t], weight.reshape(-1, weight.shape[2]))
                total = term if total is None else total + term
        out[...] = low(total)


def back_memory(own, got, w_own, packed, ckv_row):
    n, rows, cols = own.shape
    w_own = eighths(w_own)
    both = pl.BlockSpec((n, BR, cols), lambda i: (0, i, 0))
    return pl.pallas_call(
        functools.partial(back_memory_kernel, ckv_row),
        grid=(rows // BR,),
        in_specs=[both, both, ANY, ANY],
        out_specs=[rows_spec(cols)] * 2,
        out_shape=[jax.ShapeDtypeStruct((rows, cols), jnp.bfloat16)] * 2,
        scratch_shapes=[pltpu.VMEM((2, *w_own.shape), jnp.bfloat16), pltpu.SemaphoreType.DMA((2,))],
        compiler_params=pltpu.CompilerParams(vmem_limit_bytes=58 * MIB),
        cost_estimate=pl.CostEstimate(flops=8 * n * rows * cols * cols, bytes_accessed=12 * MIB, transcendentals=0),
        name="back_memory",
    )(own, got, w_own, packed)


CHUNK = 512
ROWS = 256


def ffn_kernel(co_row, own_ref, par_ref, first_hbm, cot_mine, cot_got, gains_ref, down, up,
               co_own, packed, in_own, out_own, ffn_other,
               keep_ref, send_ref, gsec_ref, g_own_ref, g_par_ref, part_ref,
               first, cot, co, w_in, w_out, normed, second, branch, full, acc, slopes,
               bottle, bottle_slope, bottle_grad, grads, got_c, part_out, part_got,
               co_sems, w_sems, sems, send, recv):
    x, y, core = (lax.axis_index(name) for name in ("x", "y", "c"))
    rows, d = normed.shape
    half = d // 2
    in_tall = ffn_other.shape[1] // 2
    chunks = 2 * in_own.shape[2] // CHUNK
    own_chunks = chunks // 2

    def columns(which):
        return pl.ds(pl.multiple_of(which * half, half), half)

    loads = [
        pltpu.make_async_copy(first_hbm, first, sems.at[0]),
        pltpu.make_async_copy(cot_mine, cot.at[:, columns(x)], sems.at[1]),
        pltpu.make_async_copy(cot_got, cot.at[:, columns(1 - x)], sems.at[2]),
    ]
    co_copies = place_halves(co_own, packed, co_row, co, co_sems, 0)

    def weight_copies(t, slot, own):
        if own:
            at = pl.ds(pl.multiple_of(t * CHUNK, CHUNK), CHUNK)
            source_in = in_own.at[:, :, at]
            sources = [out_own.at[pl.ds(2 * t, 2), :, pl.ds(j * half, half)] for j in range(2)]
        else:
            t = t - own_chunks
            tall = w_in.shape[2]
            source_in = ffn_other.at[:, pl.ds(pl.multiple_of(t * tall, tall), tall)]
            sources = [
                ffn_other.at[pl.ds(2 * t, 2), pl.ds(in_tall + j * (CHUNK // 2), CHUNK // 2)] for j in range(2)
            ]
        return [pltpu.make_async_copy(source_in, w_in.at[slot], w_sems.at[slot, 0])] + [
            pltpu.make_async_copy(source, w_out.at[slot, :, :, pl.ds(j * half, half)], w_sems.at[slot, 1 + j])
            for j, source in enumerate(sources)
        ]

    def fetch(t):
        slot = t % 2

        @pl.when(t < own_chunks)
        def _():
            for copy in weight_copies(t, slot, True):
                copy.start()

        @pl.when(jnp.logical_and(t >= own_chunks, t < chunks))
        def _():
            for copy in weight_copies(t, slot, False):
                copy.start()

    def arrive(t):
        slot = t % 2

        @pl.when(t < own_chunks)
        def _():
            for copy in weight_copies(t, slot, True):
                copy.wait()

        @pl.when(t >= own_chunks)
        def _():
            for copy in weight_copies(t, slot, False):
                copy.wait()

    for copy in co_copies + loads[:1]:
        copy.start()
    fetch(0)
    fetch(1)
    for copy in loads[1:]:
        copy.start()
    greet([{"c": 1 - core}, {"y": 1 - y}, {"x": 1 - x}])
    for copy in co_copies + loads[:1]:
        copy.wait()
    acc[...] = mm(own_ref[...], half_of(co, core)) + mm(par_ref[...], half_of(co, 1 - core))

    def by_rows(act):
        def step(i, _):
            act(pl.ds(pl.multiple_of(i * ROWS, ROWS), ROWS))
            return 0

        lax.fori_loop(0, rows // ROWS, step, 0)

    def norm_two(at):
        n_one, _ = normalize(first[at, :].astype(jnp.float32))
        summed = low(n_one * gains_ref[0:1, :] + acc[at, :])
        second[at, :] = summed
        n_two, _ = normalize(summed.astype(jnp.float32))
        normed_two = n_two * gains_ref[1:2, :]
        normed[at, :] = low(normed_two)
        acc[at, :] = normed_two

    by_rows(norm_two)
    value, slope = gelu_parts(mm(normed[...], down[...]))
    bottle[...] = low(value)
    bottle_slope[...] = slope
    acc[...] += 4.0 * mm(bottle[...], up[...])

    def up_step(t, _):
        arrive(t)
        slot = t % 2
        weight_in = w_in[slot].reshape(d, CHUNK)
        weight_out = w_out[slot].reshape(CHUNK, d)
        halves = (slice(0, rows // 2), slice(rows // 2, rows))
        products = [mm(normed[at, :], weight_in) for at in halves]
        for at, product in zip(halves, products):
            value, slope = gelu_parts(product)
            slopes[t, at, :] = low(slope)
            acc[at, :] += mm(low(value), weight_out)
        fetch(t + 2)
        return 0

    lax.fori_loop(0, chunks, up_step, 0)
    fetch(0)
    fetch(1)
    for copy in loads[1:]:
        copy.wait()

    def norm_three(at):
        third = low(acc[at, :])
        n_three, r_three = normalize(third.astype(jnp.float32))
        gain = gains_ref[2:3, :]
        full[at, :] = low(n_three * gain)
        grad_three = norm_back(n_three, r_three, gain, cot[at, :].astype(jnp.float32))
        branch[at, :] = low(grad_three)
        acc[at, :] = grad_three

    by_rows(norm_three)
    outs = [
        pltpu.make_async_copy(full.at[:, columns(x)], keep_ref, sems.at[0]),
        pltpu.make_async_copy(full.at[:, columns(1 - x)], send_ref, sems.at[1]),
    ]
    for copy in outs:
        copy.start()
    adapted = low(4.0 * branch[...].astype(jnp.float32))
    bottle_grad[...] = low(mm_nt(adapted, up[...]) * bottle_slope[...])
    tall = grads.shape[3]
    for which, grad in ((0, mm_tn(bottle_grad[...], normed[...])), (1, mm_tn(bottle[...], adapted))):
        for n in range(4):
            grads[n // 2, n % 2, which] = grad[n * tall:(n + 1) * tall]
    over_c = remote(grads.at[:, 1 - core], got_c, send.at[0], recv.at[0], {"c": 1 - core})
    over_y = remote(part_out.at[0], part_got.at[0], send.at[1], recv.at[1], {"y": 1 - y})
    over_x = remote(part_out.at[1], part_got.at[1], send.at[2], recv.at[2], {"x": 1 - x})
    over_c.start()
    acc[...] += mm_nt(bottle_grad[...], down[...])

    def down_step(t, _):
        arrive(t)
        slot = t % 2
        weight_in = w_in[slot].reshape(d, CHUNK)
        weight_out = w_out[slot].reshape(CHUNK, d)
        halves = (slice(0, rows // 2), slice(rows // 2, rows))
        products = [mm_nt(branch[at, :], weight_out) for at in halves]
        for at, product in zip(halves, products):
            grad_pre = low(product * slopes[t, at, :].astype(jnp.float32))
            acc[at, :] += mm_nt(grad_pre, weight_in)
        fetch(t + 2)

        @pl.when(t == 1)
        def _():
            over_c.wait()
            part_out[0] = low(grads[1 - y, core] + got_c[1 - y])
            over_y.start()

        @pl.when(t == 5)
        def _():
            over_y.wait()
            part_out[1] = low(grads[y, core] + got_c[y] + part_got[0].astype(jnp.float32))
            over_x.start()

        return 0

    lax.fori_loop(0, chunks, down_step, 0)
    for copy in outs:
        copy.wait()

    def norm_two_back(at):
        n_two, r_two = normalize(second[at, :].astype(jnp.float32))
        grad_two = low(acc[at, :]).astype(jnp.float32)
        grad_second = norm_back(n_two, r_two, gains_ref[1:2, :], grad_two)
        acc[at, :] = grad_second
        branch[at, :] = low(grad_second)

    by_rows(norm_two_back)
    out_acc = pltpu.make_async_copy(acc, gsec_ref, sems.at[0])
    out_acc.start()
    full[:, :half] = low(mm_nt(branch[...], half_of(co, core)))
    full[:, half:] = low(mm_nt(branch[...], half_of(co, 1 - core)))
    outs = [
        pltpu.make_async_copy(full.at[:, pl.ds(0, half)], g_own_ref, sems.at[1]),
        pltpu.make_async_copy(full.at[:, pl.ds(half, half)], g_par_ref, sems.at[2]),
    ]
    for copy in outs:
        copy.start()
    over_x.wait()
    part_ref[...] = low(part_out[1].astype(jnp.float32) + part_got[1].astype(jnp.float32))
    for copy in outs + [out_acc]:
        copy.wait()


def ffn_both_ways(own, par, first, cot_mine, cot_got, gains, down, up, co_own, packed, co_row, in_own, out_own, ffn_other):
    rows, d = first.shape
    half = d // 2
    hidden_half = in_own.shape[1]
    bottleneck = up.shape[0]
    co_own, in_own, out_own = eighths(co_own), eighths(in_own), eighths(out_own)
    vmem = pl.BlockSpec(memory_space=pltpu.VMEM)
    thin = jax.ShapeDtypeStruct((rows, half), jnp.bfloat16)
    part = (2, bottleneck // 4, d)
    flops = 2 * rows * d * (8 * hidden_half + 6 * bottleneck + 2 * d)
    return pl.pallas_call(
        functools.partial(ffn_kernel, co_row),
        in_specs=[vmem, vmem, ANY, ANY, ANY, vmem, vmem, vmem, ANY, ANY, ANY, ANY, ANY],
        out_specs=[ANY, ANY, ANY, ANY, ANY, vmem],
        out_shape=[thin, thin, jax.ShapeDtypeStruct((rows, d), jnp.float32), thin, thin,
                   jax.ShapeDtypeStruct(part, jnp.bfloat16)],
        scratch_shapes=[
            pltpu.VMEM((rows, d), jnp.bfloat16),
            pltpu.VMEM((rows, d), jnp.bfloat16),
            pltpu.VMEM((2, *co_own.shape), jnp.bfloat16),
            pltpu.VMEM((2, 8, d // 8, CHUNK), jnp.bfloat16),
            pltpu.VMEM((2, 2, CHUNK // 2, d), jnp.bfloat16),
            pltpu.VMEM((rows, d), jnp.bfloat16),
            pltpu.VMEM((rows, d), jnp.bfloat16),
            pltpu.VMEM((rows, d), jnp.bfloat16),
            pltpu.VMEM((rows, d), jnp.bfloat16),
            pltpu.VMEM((rows, d), jnp.float32),
            pltpu.VMEM((2 * hidden_half // CHUNK, rows, CHUNK), jnp.bfloat16),
            pltpu.VMEM((rows, bottleneck), jnp.bfloat16),
            pltpu.VMEM((rows, bottleneck), jnp.float32),
            pltpu.VMEM((rows, bottleneck), jnp.bfloat16),
            pltpu.VMEM((2, 2, *part), jnp.float32),
            pltpu.VMEM((2, *part), jnp.float32),
            pltpu.VMEM((2, *part), jnp.bfloat16),
            pltpu.VMEM((2, *part), jnp.bfloat16),
            pltpu.SemaphoreType.DMA((4,)),
            pltpu.SemaphoreType.DMA((2, 3)),
            pltpu.SemaphoreType.DMA((3,)),
            pltpu.SemaphoreType.DMA((3,)),
            pltpu.SemaphoreType.DMA((3,)),
        ],
        compiler_params=pltpu.CompilerParams(collective_id=3, has_side_effects=True, vmem_limit_bytes=63 * MIB),
        cost_estimate=pl.CostEstimate(flops=flops, bytes_accessed=48 * MIB, transcendentals=0),
        name="ffn_both_ways",
    )(own, par, first, cot_mine, cot_got, gains, down, up, co_own, packed, in_own, out_own, ffn_other)


PREFIX_STEPS = ("x", "zl", "y", "zh")


def finish_kernel(dq_own, dq_got, dkv_own, dkv_got, gfirst, w_own, w_oth, mem_keep, mem_got, o_keep, o_got, pre_ref, part_ref,
                  out_ref, mem_ref, o_ref, pre_out_ref, part_got_ref,
                  lhs, first, held, boxes, stage, sums, arrived, local, place, send, recv):
    x, core = lax.axis_index("x"), lax.axis_index("c")
    here = {name: lax.axis_index(name) for name in PREFIX_STEPS}
    partner, across = {"c": 1 - core}, {"x": 1 - x}
    stays = x == core
    blocks = lhs.shape[0]
    half = blocks * BT
    cols = out_ref.shape[1]
    d = held.shape[1] // 3
    steps = len(PREFIX_STEPS) + 1

    def loads(b):
        rows = pl.ds(b * BT, BT)
        pairs = [(dq_own.at[rows], lhs.at[b, 0]), (dkv_own.at[0, rows], lhs.at[b, 1]), (dkv_own.at[1, rows], lhs.at[b, 2]),
                 (dq_got.at[rows], lhs.at[b, 3]), (dkv_got.at[0, rows], lhs.at[b, 4]), (dkv_got.at[1, rows], lhs.at[b, 5]),
                 (gfirst.at[rows], first.at[b])]
        return [pltpu.make_async_copy(src, dst, local.at[b, n]) for n, (src, dst) in enumerate(pairs)]

    def weights(agree):
        pair = (w_own, w_oth) if agree else (w_oth, w_own)
        return [pltpu.make_async_copy(src, held.at[n], local.at[blocks, n]) for n, src in enumerate(pair)]

    ours = pl.ds(pl.multiple_of(core * half, half), half)

    def settled(agree):
        mine, passed = ((mem_keep, o_keep), (mem_got, o_got)) if agree else ((mem_got, o_got), (mem_keep, o_keep))
        return (
            [pltpu.make_async_copy(src, stage.at[n], local.at[blocks, 2 + n]) for n, src in enumerate(mine)],
            [pltpu.make_async_copy(stage.at[n], to.at[ours], local.at[blocks, 4 + n]) for n, to in enumerate((mem_ref, o_ref))],
            [
                remote(src, to.at[ours], send.at[0, blocks + n], recv.at[blocks + n, core], partner)
                for n, (src, to) in enumerate(zip(passed, (mem_ref, o_ref)))
            ],
        )

    def prefix_copy(s):
        target = {PREFIX_STEPS[s]: 1 - here[PREFIX_STEPS[s]]} if s < steps - 1 else partner
        return remote(sums.at[s], arrived.at[s], send.at[2, s], recv.at[blocks + 2 + s, 0], target)

    for copy in loads(0):
        copy.start()
    for agree, chosen in ((True, stays), (False, jnp.logical_not(stays))):
        @pl.when(chosen)
        def _(agree=agree):
            for copy in weights(agree):
                copy.start()

    for b in range(1, blocks):
        for copy in loads(b):
            copy.start()
    for agree, chosen in ((True, stays), (False, jnp.logical_not(stays))):
        @pl.when(chosen)
        def _(agree=agree):
            for copy in settled(agree)[0]:
                copy.start()

    sums[0] = low(pre_ref[...])
    greet([across, {"x": 1 - x, "c": 1 - core}, partner] + [{name: 1 - here[name]} for name in PREFIX_STEPS[1:]])
    prefix_copy(0).start()
    part_copy = remote(
        part_ref, part_got_ref, send.at[1, blocks], recv.at[blocks + 2, 1], {"zl": 1 - here["zl"]}
    )
    part_copy.start()

    def landing(b):
        return pl.ds(pl.multiple_of(core * half + b * BT, BT), BT)

    def over(b):
        return remote(boxes.at[b, 0], out_ref.at[landing(b)], send.at[0, b], recv.at[b, core], {"x": 1 - x, "c": x})

    def beside(b):
        return remote(boxes.at[b, 1], out_ref.at[landing(b)], send.at[1, b], recv.at[b, core], partner)

    def kept_here(b):
        return pltpu.make_async_copy(boxes.at[b, 1], out_ref.at[landing(b)], place.at[b])

    def compute(b, which):
        at = pl.ds(pl.multiple_of(which * cols, cols), cols)
        total = first[b, :, at]
        for n in range(6):
            rows = pl.ds(pl.multiple_of((n % 3) * d + which * cols, cols), cols)
            total += mm_nt(lhs[b, n], held[n // 3, rows, :])
        return low(total)

    def next_prefix(s):
        prefix_copy(s).wait()
        sums[s + 1] = low(sums[s].astype(jnp.float32) + arrived[s].astype(jnp.float32))
        prefix_copy(s + 1).start()

    for copy in weights(True):
        copy.wait()
    for b in range(blocks):
        for copy in loads(b):
            copy.wait()
        boxes[b, 0] = compute(b, 1 - x)
        over(b).start()
        if b == 1:
            next_prefix(0)
    for b in range(blocks):
        boxes[b, 1] = compute(b, x)

        @pl.when(stays)
        def _(b=b):
            kept_here(b).start()

        @pl.when(jnp.logical_not(stays))
        def _(b=b):
            beside(b).start()

        if b + 1 < steps - 1:
            next_prefix(b + 1)

    for agree, chosen in ((True, stays), (False, jnp.logical_not(stays))):
        @pl.when(chosen)
        def _(agree=agree):
            loaded, placed, passed = settled(agree)
            for copy in passed:
                copy.start()
            for copy in loaded:
                copy.wait()
            for copy in placed:
                copy.start()

    prefix_copy(steps - 1).wait()
    pre_out_ref[...] = jnp.where(stays, sums[steps - 1], arrived[steps - 1]).astype(jnp.float32)

    def wait_for(t, b):
        rows = out_ref.at[pl.ds(pl.multiple_of(t * half + b * BT, BT), BT)]
        remote(rows, rows, send.at[0, b], recv.at[b, t], across).wait_recv()

    part_copy.wait()
    theirs = pl.ds(pl.multiple_of((1 - core) * half, half), half)
    for n, to in enumerate((mem_ref, o_ref)):
        remote(to.at[theirs], to.at[theirs], send.at[0, 0], recv.at[blocks + n, 1 - core], partner).wait_recv()
    for agree, chosen in ((True, stays), (False, jnp.logical_not(stays))):
        @pl.when(chosen)
        def _(agree=agree):
            loaded, placed, passed = settled(agree)
            for copy in placed:
                copy.wait()
            for copy in passed:
                copy.wait_send()

    for b in range(blocks):
        over(b).wait_send()

        @pl.when(stays)
        def _(b=b):
            kept_here(b).wait()
            wait_for(1 - core, b)

        @pl.when(jnp.logical_not(stays))
        def _(b=b):
            beside(b).wait_send()
            for t in range(2):
                wait_for(t, b)


def finish_tokens(dq_own, dq_got, dkv_own, dkv_got, gfirst, w_own, w_oth, mem_keep, mem_got, o_keep, o_got, prefix, part):
    half, cols = dq_own.shape
    blocks = half // BT
    steps = len(PREFIX_STEPS) + 1
    vmem = pl.BlockSpec(memory_space=pltpu.VMEM)
    rows = jax.ShapeDtypeStruct((2 * half, cols), jnp.bfloat16)
    return pl.pallas_call(
        finish_kernel,
        in_specs=[ANY] * 11 + [vmem, vmem],
        out_specs=[ANY, ANY, ANY, vmem, vmem],
        out_shape=[rows, rows, rows, jax.ShapeDtypeStruct(prefix.shape, jnp.float32),
                   jax.ShapeDtypeStruct(part.shape, part.dtype)],
        scratch_shapes=[
            pltpu.VMEM((blocks, 6, BT, cols), jnp.bfloat16),
            pltpu.VMEM((blocks, BT, 2 * cols), jnp.float32),
            pltpu.VMEM((2, *w_own.shape), jnp.bfloat16),
            pltpu.VMEM((blocks, 2, BT, cols), jnp.bfloat16),
            pltpu.VMEM((2, half, cols), jnp.bfloat16),
            pltpu.VMEM((steps, *prefix.shape), jnp.bfloat16),
            pltpu.VMEM((steps, *prefix.shape), jnp.bfloat16),
            pltpu.SemaphoreType.DMA((blocks + 1, 7)),
            pltpu.SemaphoreType.DMA((blocks,)),
            pltpu.SemaphoreType.DMA((3, max(blocks + 2, steps))),
            pltpu.SemaphoreType.DMA((blocks + 2 + steps, 2)),
        ],
        compiler_params=pltpu.CompilerParams(collective_id=1, has_side_effects=True, vmem_limit_bytes=58 * MIB),
        cost_estimate=pl.CostEstimate(flops=12 * half * cols * 2 * cols, bytes_accessed=64 * MIB, transcendentals=0),
        name="finish_tokens",
    )(dq_own, dq_got, dkv_own, dkv_got, gfirst, w_own, w_oth, mem_keep, mem_got, o_keep, o_got, prefix, part)


def swap(value, axis):
    return lax.ppermute(value, axis, SWAP)


def after(value, *others):
    return lax.optimization_barrier((value, *others))[0]


def gather_half(piece):
    return lax.all_gather(piece, ("zl", "y", "c"), axis=0, tiled=True)


def paired_device(
    tokens, memory, dec_segments, mem_segments, self_qkv, self_out, cross_q, cross_kv, cross_out, ffn_in, ffn_out,
    adapter_down, adapter_up, self_prefix, cross_prefix, gains, cotangent,
):
    x, core = lax.axis_index("x"), lax.axis_index("c")
    agree = x == core
    columns = tokens.shape[1]
    prefix_count = self_prefix.shape[1]

    qkv_flat = self_qkv.reshape(-1, columns)
    ckv_flat = cross_kv.reshape(-1, columns)
    segs = jnp.concatenate([dec_segments, mem_segments], axis=0)
    prefixes = jnp.concatenate([self_prefix, cross_prefix], axis=0)
    prefixes = jnp.pad(prefixes, ((0, 0), (0, PP - prefix_count), (0, 0)))
    (
        rows_own, own, par, piece, mem_mine, packed, cot_mine, cot_send, qkv_other, prefixes_got, segs_got, down_full, up_full
    ) = bring_rows(
        tokens, memory, cotangent, qkv_flat, prefixes, segs, ffn_in, ffn_out,
        adapter_down, adapter_up, [self_out, cross_q, cross_out, ckv_flat],
    )
    segs = jnp.where(agree, segs, segs_got)
    dec_seg, mem_seg = segs[0], segs[1]
    prefixes = jnp.where(agree, prefixes, prefixes_got)
    self_pre, cross_pre = prefixes[:2], prefixes[2:]
    self_masks = mask_columns(dec_seg, dec_seg, prefix_count)
    self_lo, self_hi = ranges(dec_seg, dec_seg, True)
    cross_masks = mask_columns(dec_seg, mem_seg, prefix_count)
    cross_lo, cross_hi = ranges(dec_seg, mem_seg, False)

    others = gather_half(piece).reshape(8, *piece.shape)
    so_tall, cq_tall, ckv_tall = self_out.shape[0] // 8, cross_q.shape[0] // 8, ckv_flat.shape[0] // 8
    co_row = 2 * so_tall + cq_tall
    ckv_row = co_row + 2 * so_tall
    got = swap(after(packed, own), "x")
    self_q, self_k, self_v = ([(own, t), (par, t)] for t in range(3))
    self_o, self_ot, self_lt = attend_fwd(
        self_q, self_k, self_v, columns, self_masks, self_pre, self_lo, self_hi, True
    )
    heads_got = swap(self_o[1], "c")

    mem_got = got[:mem_mine.shape[0]]
    cot_got = swap(after(cot_send, got), "x")
    mem_par, mem_par_got = swap(mem_mine, "c"), swap(mem_got, "c")
    first_sum, cq_own, cq_send = after_self(
        self_o[0], heads_got, rows_own, gains, self_out, cross_q, others
    )
    ffn_other = gather_half(after(got, first_sum)[mem_mine.shape[0]:])
    ffn_other = ffn_other.reshape(8, -1, columns)
    cq_par = swap(cq_send, "c")
    own, par = project([mem_mine, mem_got], [mem_par, mem_par_got], ckv_flat, others, ckv_row, 2)
    cross_qp = [(cq_own, 0), (cq_par, 0)]
    cross_k, cross_v = ([(own, t), (par, t)] for t in range(2))
    cross_o, cross_ot, cross_lt = attend_fwd(
        cross_qp, cross_k, cross_v, columns, cross_masks, cross_pre, cross_lo, cross_hi, False
    )
    cross_got = swap(cross_o[1], "c")
    out_keep, out_send, grad_second, g_own, g_send, part = ffn_both_ways(
        cross_o[0], cross_got, first_sum, cot_mine, cot_got, gains, down_full, up_full,
        cross_out, others, co_row, ffn_in, ffn_out, ffn_other,
    )
    g_par = swap(g_send, "c")
    out_got = swap(out_send, "x")

    part_got = swap(part, "zh")

    cdq, cdkv, cross_dp = attend_bwd(
        cross_qp, cross_k, cross_v, [(g_own, 0), (g_par, 0)], columns, cross_ot, cross_lt,
        cross_masks, cross_pre, cross_lo, cross_hi, False,
    )
    cdq_got = swap(after(cdq[1], out_got, part_got), "c")
    part = low(part.astype(jnp.float32) + part_got.astype(jnp.float32))
    cdkv_got = swap(cdkv[1], "c")
    grad_first, g_own, g_send = before_self(
        grad_second, cdq[0], cdq_got, first_sum, gains, self_out, cross_q, others
    )
    g_par = swap(g_send, "c")

    mem_keep, mem_out = back_memory(cdkv[0], cdkv_got, ckv_flat, others, ckv_row)
    mem_back = swap(mem_out, "x")
    g_par = after(g_par, mem_out)

    sdq, sdkv, self_dp = attend_bwd(
        self_q, self_k, self_v, [(g_own, 0), (g_par, 0)], columns, self_ot, self_lt,
        self_masks, self_pre, self_lo, self_hi, True,
    )
    sdq_got = swap(after(sdq[1], mem_back), "c")
    sdkv_got = swap(sdkv[1], "c")
    grad_tokens, grad_memory, output, prefix_sums, part_got = finish_tokens(
        sdq[0], sdq_got, sdkv[0], sdkv_got, grad_first, qkv_flat, qkv_other, mem_keep, mem_back, out_keep, out_got,
        jnp.concatenate([self_dp, cross_dp], axis=0), part,
    )
    part = part.astype(jnp.float32) + part_got.astype(jnp.float32)
    grad_down, grad_up = part[0].T, part[1]
    grad_tokens, grad_memory = grad_tokens.astype(jnp.float32), grad_memory.astype(jnp.float32)
    prefix_sums = prefix_sums[:, :prefix_count]

    return (output, grad_tokens, grad_memory, prefix_sums[:2], prefix_sums[2:], grad_down, grad_up)


def norm_grad(gathered, gain, upstream):
    n, r = normalize(gathered.astype(jnp.float32))
    return norm_back(n, r, gain, upstream)


def wide_device(
    tokens, memory, dec_segments, mem_segments, self_qkv, self_out, cross_q, cross_kv, cross_out, ffn_in, ffn_out,
    adapter_down, adapter_up, self_prefix, cross_prefix, gains, cotangent,
):
    n_wide = lax.axis_size("wide")
    row_count, columns = tokens.shape
    own_start = lax.axis_index("wide") * columns
    block_size = row_count // n_wide
    block_start = lax.axis_index("wide") * block_size
    prefix_count = self_prefix.shape[1]
    dec_seg, mem_seg = dec_segments[0], mem_segments[0]

    def collect(values):
        return lax.all_gather(values, "wide", axis=1, tiled=True)

    def spread(term):
        return lax.psum_scatter(term, "wide", scatter_dimension=1, tiled=True)

    def own_columns(values):
        return lax.dynamic_slice_in_dim(values, own_start, columns, 1)

    def padded(prefix):
        return jnp.pad(prefix, ((0, 0), (0, PP - prefix_count), (0, 0)))

    self_masks = mask_columns(dec_seg, dec_seg, prefix_count)
    self_lo, self_hi = ranges(dec_seg, dec_seg, True)
    cross_masks = mask_columns(dec_seg, mem_seg, prefix_count)
    cross_lo, cross_hi = ranges(dec_seg, mem_seg, False)
    self_pre, cross_pre = padded(self_prefix), padded(cross_prefix)

    all_tokens, all_memory = collect(tokens), collect(memory)
    self_q, self_k, self_v = ([(low(mm(all_tokens, self_qkv[t])), 0)] for t in range(3))
    (self_heads,), self_ot, self_lt = attend_fwd(
        self_q, self_k, self_v, columns, self_masks, self_pre, self_lo, self_hi, True
    )
    first_sum = low(tokens.astype(jnp.float32) + spread(mm(self_heads, self_out)))
    gathered_one = collect(first_sum)
    normed_one = normalize(gathered_one.astype(jnp.float32))[0] * gains[0]
    cross_qp = [(low(mm(low(normed_one), cross_q)), 0)]
    cross_k, cross_v = ([(low(mm(all_memory, cross_kv[t])), 0)] for t in range(2))
    (cross_heads,), cross_ot, cross_lt = attend_fwd(
        cross_qp, cross_k, cross_v, columns, cross_masks, cross_pre, cross_lo, cross_hi, False
    )
    second_sum = low(own_columns(normed_one) + spread(mm(cross_heads, cross_out)))
    gathered_two = collect(second_sum)
    normed_two = normalize(gathered_two.astype(jnp.float32))[0] * gains[1]
    normed_low = low(normed_two)
    adapter_in = lax.dynamic_slice_in_dim(normed_low, block_start, block_size, 0)
    adapter_rows = lax.all_gather(adapter_in, "narrow", axis=0, tiled=True)
    bottle, bottle_slope = gelu_parts(mm(adapter_rows, adapter_down))
    bottle = low(bottle)
    adapted = lax.psum_scatter(low(mm(bottle, adapter_up)), "narrow", scatter_dimension=0, tiled=True)
    hidden, slope = gelu_parts(mm(normed_low, ffn_in))
    branch = mm(low(hidden), ffn_out)
    placed = lax.dynamic_slice_in_dim(branch, block_start, block_size, 0) + 4.0 * adapted.astype(jnp.float32)
    branch = lax.dynamic_update_slice_in_dim(branch, placed, block_start, 0)
    third_sum = low(own_columns(normed_two) + spread(branch))
    gathered_three = collect(third_sum)
    output = low(own_columns(normalize(gathered_three.astype(jnp.float32))[0] * gains[2]))
    grad_three = norm_grad(gathered_three, gains[2], collect(cotangent).astype(jnp.float32))
    grad_branch = low(grad_three)
    grad_pre = low(mm_nt(grad_branch, ffn_out) * slope)
    grad_normed = mm_nt(grad_pre, ffn_in)
    grad_adapted = low(4.0 * lax.dynamic_slice_in_dim(grad_branch, block_start, block_size, 0).astype(jnp.float32))
    grad_adapted = lax.all_gather(grad_adapted, "narrow", axis=0, tiled=True)
    bottle_grad = low(mm_nt(grad_adapted, adapter_up) * bottle_slope)
    grad_in = lax.psum_scatter(low(mm_nt(bottle_grad, adapter_down)), "narrow", scatter_dimension=0, tiled=True)
    placed = lax.dynamic_slice_in_dim(grad_normed, block_start, block_size, 0) + grad_in.astype(jnp.float32)
    grad_normed = lax.dynamic_update_slice_in_dim(grad_normed, placed, block_start, 0)
    grad_down, grad_up = lax.psum(
        (mm_tn(adapter_rows, bottle_grad), mm_tn(bottle, grad_adapted)), ("dp", "wide")
    )
    grad_two = collect(low(own_columns(grad_three) + spread(grad_normed))).astype(jnp.float32)
    grad_second = norm_grad(gathered_two, gains[1], grad_two)
    grad_cross = low(mm_nt(low(grad_second), cross_out))
    (cdq,), (cdkv,), cross_dp = attend_bwd(
        cross_qp, cross_k, cross_v, [(grad_cross, 0)], columns, cross_ot, cross_lt,
        cross_masks, cross_pre, cross_lo, cross_hi, False,
    )
    spread_one = spread(low(mm_nt(cdq, cross_q))).astype(jnp.float32)
    grad_memory = spread(low(mm_nt(cdkv[0], cross_kv[0]) + mm_nt(cdkv[1], cross_kv[1]))).astype(jnp.float32)
    grad_one = collect(low(own_columns(grad_second) + spread_one)).astype(jnp.float32)
    grad_first = norm_grad(gathered_one, gains[0], grad_one)
    grad_self = low(mm_nt(low(grad_first), self_out))
    (sdq,), (sdkv,), self_dp = attend_bwd(
        self_q, self_k, self_v, [(grad_self, 0)], columns, self_ot, self_lt,
        self_masks, self_pre, self_lo, self_hi, True,
    )
    grad_input = mm_nt(sdq, self_qkv[0]) + mm_nt(sdkv[0], self_qkv[1]) + mm_nt(sdkv[1], self_qkv[2])
    grad_tokens = own_columns(grad_first) + spread(grad_input)
    totals = lax.psum((low(self_dp), low(cross_dp)), ("dp", "narrow"))
    grad_self_prefix, grad_cross_prefix = (t.astype(jnp.float32)[:, :prefix_count] for t in totals)
    return (output, grad_tokens, grad_memory, grad_self_prefix, grad_cross_prefix, grad_down, grad_up)


def solution(mesh):
    dp, wide, narrow = (mesh.shape[name] for name in ("dp", "wide", "narrow"))
    if (dp, wide, narrow) == (4, 2, 4):
        parts = Mesh(mesh.devices.reshape(2, 2, 2, 2, 2), ("zh", "zl", "x", "y", "c"))
        device, used = paired_device, parts
        rows, split, thin = ("zh", "zl", "y", "c"), "x", ("y", "c")
    else:
        device, used = wide_device, mesh
        rows, split, thin = ("dp", "narrow"), "wide", "narrow"
    return jax.shard_map(
        device,
        mesh=used,
        in_specs=(
            P(rows, split),
            P(rows, split),
            P(rows, None),
            P(rows, None),
            P(None, None, split),
            P(split, None),
            P(None, split),
            P(None, None, split),
            P(split, None),
            P(None, split),
            P(split, None),
            P(None, thin),
            P(thin, None),
            P(None, None, split),
            P(None, None, split),
            P(),
            P(rows, split),
        ),
        out_specs=(
            P(rows, split),
            P(rows, split),
            P(rows, split),
            P(None, None, split),
            P(None, None, split),
            P(None, thin),
            P(thin, None),
        ),
        check_vma=False,
    )
```

```python
import functools
import math
from functools import partial

import jax
import jax.numpy as jnp
from jax import lax
from jax.experimental import pallas as pl
from jax.experimental.pallas import tpu as pltpu
from jax.sharding import Mesh
from jax.sharding import PartitionSpec as P

HEAD_DIM = 64
DOCS = 4
NEG = -1e30
BQ = 256
BK = 128
BP = 1024
PP = 32
BT = 256
BR = 512
HEADS_FWD = 8
HEADS_BWD = 4
SWAP = [(0, 1), (1, 0)]
MIB = 2**20


def mm(a, b):
    return jnp.dot(a, b, preferred_element_type=jnp.float32)


def mm_nt(a, b):
    return lax.dot_general(a, b, (((1,), (1,)), ((), ())), preferred_element_type=jnp.float32)


def mm_tn(a, b):
    return lax.dot_general(a, b, (((0,), (0,)), ((), ())), preferred_element_type=jnp.float32)


def part_offsets(n_parts, part_len):
    if n_parts == 1:
        return [0]
    core = lax.axis_index("c")
    return [pl.multiple_of(core * part_len, part_len), pl.multiple_of((1 - core) * part_len, part_len)]


def block_at(i, size):
    return pl.ds(pl.multiple_of(i * size, size), size)


def key_blocks(j, count):
    return pl.ds(pl.multiple_of(j * BK, BK), count * BK)


def for_key_blocks(lo, hi, act):
    rounds = (hi - lo) // 4

    def four(t, _):
        act(lo + t * 4, 4)
        return 0

    lax.fori_loop(0, rounds, four, 0)
    rest = lo + rounds * 4

    @pl.when(hi - rest >= 2)
    def _():
        act(rest, 2)

    @pl.when((hi - rest) % 2 == 1)
    def _():
        act(hi - 1, 1)


def head_rows(h):
    return pl.ds(h * HEAD_DIM, HEAD_DIM)


def later_keys(shape):
    return lax.broadcasted_iota(jnp.int32, shape, 0) > lax.broadcasted_iota(jnp.int32, shape, 1)


def by_head(prefix, heads_here):
    shape = (heads_here * PP, heads_here * HEAD_DIM)
    rows = lax.broadcasted_iota(jnp.int32, shape, 0) // PP
    columns = lax.broadcasted_iota(jnp.int32, shape, 1) // HEAD_DIM
    tall = jnp.concatenate([prefix] * heads_here, axis=0)
    return jnp.where(rows == columns, tall, jnp.zeros((), prefix.dtype))


def padding_rows(shape, prefix_count):
    return lax.broadcasted_iota(jnp.int32, shape, 0) % PP >= prefix_count


def document_rows(seg):
    row = lax.broadcasted_iota(jnp.int32, (2 * HEAD_DIM, seg.shape[1]), 0)
    differ = jnp.logical_and(row < DOCS, row != seg)
    return jnp.where(differ, NEG, 0.0).astype(jnp.bfloat16)


def document_columns(seg):
    row = lax.broadcasted_iota(jnp.int32, (2 * HEAD_DIM, seg.shape[1]), 0)
    return jnp.where(row == seg, 1.0, 0.0).astype(jnp.bfloat16).T


def load_queries(q_turned, h, eq, qx, here):
    zero = jnp.zeros((HEAD_DIM, q_turned.shape[1]), q_turned.dtype)
    mine = (h % 2) * HEAD_DIM
    qx[h, pl.ds(mine, HEAD_DIM), here] = q_turned[h * HEAD_DIM:(h + 1) * HEAD_DIM]
    qx[h, pl.ds(HEAD_DIM - mine, HEAD_DIM), here] = zero
    if eq is not None:
        qx[h, pl.ds(2 * HEAD_DIM, 2 * HEAD_DIM), here] = eq


def fwd_kernel(causal, n_parts, prefix_count, lo_ref, hi_ref, *refs):
    q_parts, k_parts, v_parts = refs[:n_parts], refs[n_parts:2 * n_parts], refs[2 * n_parts:3 * n_parts]
    key_seg, query_seg, pre_ref = refs[3 * n_parts:3 * n_parts + 3]
    o_parts = refs[3 * n_parts + 3:4 * n_parts + 3]
    ot_ref, lt_ref, qt, qx, vx, ke, acc, top = refs[4 * n_parts + 3:]
    seq = qt.shape[1]
    q_len, m_len = q_parts[0].shape[0], k_parts[0].shape[0]
    heads_here = qt.shape[0] // HEAD_DIM
    n_pairs = heads_here // 2
    n_q = seq // BQ
    ones_rows = vx.shape[1] - HEAD_DIM

    for q_ref, at in zip(q_parts, part_offsets(n_parts, q_len)):
        here = pl.ds(at, q_len)
        q_turned = (q_ref[...] * jnp.bfloat16(0.125)).T
        qt[:, here] = q_turned
        documents = document_rows(query_seg[:, here])
        for h in range(heads_here):
            load_queries(q_turned, h, documents, qx, here)
    for k_ref, v_ref, at in zip(k_parts, v_parts, part_offsets(n_parts, m_len)):
        here = pl.ds(at, m_len)
        v_turned = v_ref[...].T
        for h in range(heads_here):
            vx[h, :HEAD_DIM, here] = v_turned[h * HEAD_DIM:(h + 1) * HEAD_DIM]
        documents = document_columns(key_seg[:, here])
        for p in range(n_pairs):
            ke[p, here, :128] = k_ref[:, p * 128:(p + 1) * 128]
            ke[p, here, 128:] = documents
    for h in range(heads_here):
        vx[h, HEAD_DIM:, :] = jnp.ones((ones_rows, vx.shape[2]), jnp.bfloat16)
    keys_p = by_head(pre_ref[0], heads_here)
    values_p = by_head(pre_ref[1], heads_here).T

    wide = min(BP, seq)

    def prefix_step(find_top):
        def step(i, _):
            qs = block_at(i, wide)
            scores = mm(keys_p, qt[:, qs])
            scores = jnp.where(padding_rows(scores.shape, prefix_count), NEG, scores)
            chances = []
            for h in range(heads_here):
                s = scores[h * PP:(h + 1) * PP]
                if find_top:
                    top[h:h + 1, qs] = jnp.max(s, axis=0, keepdims=True)
                p = jnp.exp(s - top[h:h + 1, qs])
                acc[h, HEAD_DIM:, qs] = jnp.broadcast_to(jnp.sum(p, axis=0, keepdims=True), (ones_rows, wide))
                chances.append(low(p))
            out = mm(values_p, jnp.concatenate(chances, axis=0))
            for h in range(heads_here):
                acc[h, :HEAD_DIM, qs] = out[h * HEAD_DIM:(h + 1) * HEAD_DIM]
            return 0

        lax.fori_loop(0, seq // wide, step, 0)

    def scores_of(i, j, count, diag):
        qs, ks = block_at(i, BQ), key_blocks(j, count)
        scores = [mm(ke[h // 2, ks, :], qx[h, :, qs]) for h in range(heads_here)]
        if diag:
            scores = [jnp.where(later_keys(s.shape), NEG, s) for s in scores]
        return scores

    def add_block(i, j, count, diag):
        qs, ks = block_at(i, BQ), key_blocks(j, count)
        scores = scores_of(i, j, count, diag)
        for h in range(heads_here):
            p = low(jnp.exp(scores[h] - top[h:h + 1, qs]))
            acc[h, :, qs] += mm(vx[h, :, ks], p)

    def raise_top(i, j, count, diag):
        qs = block_at(i, BQ)
        for h, s in enumerate(scores_of(i, j, count, diag)):
            top[h:h + 1, qs] = jnp.maximum(top[h:h + 1, qs], jnp.max(s, axis=0, keepdims=True))

    def all_blocks(act):
        def step(i, _):
            if causal:
                act(i, i * (BQ // BK), BQ // BK, True)
            for_key_blocks(lo_ref[i], hi_ref[i], lambda j, count: act(i, j, count, False))
            return 0

        lax.fori_loop(0, n_q, step, 0)

    prefix_step(True)
    all_blocks(add_block)
    largest = jnp.max(jnp.where(acc[0, HEAD_DIM:HEAD_DIM + 8, :] < 1e30, 0.0, 1.0))
    for h in range(1, heads_here):
        largest = jnp.maximum(largest, jnp.max(jnp.where(acc[h, HEAD_DIM:HEAD_DIM + 8, :] < 1e30, 0.0, 1.0)))

    @pl.when(largest > 0.5)
    def _():
        all_blocks(raise_top)
        prefix_step(False)
        all_blocks(add_block)

    def finish(i, _):
        qs = block_at(i, BQ)
        outs = []
        for h in range(heads_here):
            total = acc[h, HEAD_DIM:HEAD_DIM + 1, qs]
            lt_ref[h // 2, h % 2:h % 2 + 1, qs] = top[h:h + 1, qs] + jnp.log(total)
            outs.append(acc[h, :HEAD_DIM, qs] / total)
        ot = jnp.concatenate(outs, axis=0)
        ot_ref[:, qs] = low(ot)
        store_part(o_parts, i, low(ot.T))
        return 0

    lax.fori_loop(0, n_q, finish, 0)


def store_part(parts, i, value):
    per_part = parts[0].shape[0] // BQ
    at = pl.ds(pl.multiple_of((i % per_part) * BQ, BQ), BQ)
    if len(parts) == 1:
        parts[0][at, :] = value
        return
    own = i // per_part == lax.axis_index("c")

    @pl.when(own)
    def _():
        parts[0][at, :] = value

    @pl.when(jnp.logical_not(own))
    def _():
        parts[1][at, :] = value


def attend_fwd(qs, ks, vs, cols, masks, prefix, lo, hi, causal):
    ek, eq, prefix_count = masks
    n = len(qs)
    q_len, m_len = qs[0][0].shape[0], ks[0][0].shape[0]
    seq, mem = q_len * n, m_len * n
    wd = min(HEAD_DIM * HEADS_FWD, cols)
    heads_here = wd // HEAD_DIM
    steps = cols // wd
    in_specs, operands = [], []
    for group, length in ((qs, q_len), (ks, m_len), (vs, m_len)):
        for array, at in group:
            in_specs.append(pl.BlockSpec((length, wd), partial(lambda at, p, *_: (0, at * steps + p), at)))
            operands.append(array)
    in_specs += [
        pl.BlockSpec((1, mem), lambda p, *_: (0, 0)),
        pl.BlockSpec((1, seq), lambda p, *_: (0, 0)),
        pl.BlockSpec((2, PP, wd), lambda p, *_: (0, 0, p)),
    ]
    grid_spec = pltpu.PrefetchScalarGridSpec(
        num_scalar_prefetch=2,
        grid=(steps,),
        in_specs=in_specs,
        out_specs=[pl.BlockSpec((q_len, wd), lambda p, *_: (0, p))] * n
        + [
            pl.BlockSpec((wd, seq), lambda p, *_: (p, 0)),
            pl.BlockSpec((wd // 128, 2, seq), lambda p, *_: (p, 0, 0)),
        ],
        scratch_shapes=[
            pltpu.VMEM((wd, seq), jnp.bfloat16),
            pltpu.VMEM((heads_here, 256, seq), jnp.bfloat16),
            pltpu.VMEM((heads_here, HEAD_DIM + 16, mem), jnp.bfloat16),
            pltpu.VMEM((wd // 128, mem, 256), jnp.bfloat16),
            pltpu.VMEM((heads_here, HEAD_DIM + 16, seq), jnp.float32),
            pltpu.VMEM((8, seq), jnp.float32),
        ],
    )
    result = pl.pallas_call(
        functools.partial(fwd_kernel, causal, n, prefix_count),
        grid_spec=grid_spec,
        out_shape=[jax.ShapeDtypeStruct((q_len, cols), jnp.bfloat16)] * n
        + [
            jax.ShapeDtypeStruct((cols, seq), jnp.bfloat16),
            jax.ShapeDtypeStruct((cols // 128, 2, seq), jnp.float32),
        ],
        compiler_params=pltpu.CompilerParams(vmem_limit_bytes=60 * MIB),
        cost_estimate=pl.CostEstimate(
            flops=8 * seq * mem * cols, bytes_accessed=12 * MIB, transcendentals=seq * mem * cols // 256
        ),
        name="attend_fwd_self" if causal else "attend_fwd_cross",
    )(lo, hi, *operands, ek, eq, prefix)
    return result[:n], result[n], result[n + 1]


def bwd_kernel(causal, n_parts, prefix_count, lo_ref, hi_ref, *refs):
    q_parts, k_parts, v_parts, g_parts = (refs[t * n_parts:(t + 1) * n_parts] for t in range(4))
    ot_ref, lt_ref, key_seg, query_seg, pre_ref = refs[4 * n_parts:4 * n_parts + 5]
    dq_parts = refs[4 * n_parts + 5:5 * n_parts + 5]
    dkv_parts = refs[5 * n_parts + 5:6 * n_parts + 5]
    dp_ref, qt, gt, qx, gx, kt, ke, vv, qm, gm, dq, dk, dv, delta = refs[6 * n_parts + 5:]
    seq = qt.shape[1]
    q_len, m_len = q_parts[0].shape[0], k_parts[0].shape[0]
    width = qt.shape[0]
    heads_here = width // HEAD_DIM
    n_pairs = heads_here // 2
    n_q = seq // BQ
    lane = lax.broadcasted_iota(jnp.int32, (1, width), 1)
    first = lane % 128 < HEAD_DIM
    zero = jnp.zeros((), jnp.bfloat16)

    for q_ref, g_ref, at in zip(q_parts, g_parts, part_offsets(n_parts, q_len)):
        here = pl.ds(at, q_len)
        q_all = q_ref[...] * jnp.bfloat16(0.125)
        g_all = g_ref[...]
        q_turned, g_turned = q_all.T, g_all.T
        qt[:, here] = q_turned
        gt[:, here] = g_turned
        documents = document_rows(query_seg[:, here])
        for h in range(heads_here):
            load_queries(q_turned, h, documents, qx, here)
            load_queries(g_turned, h, None, gx, here)
        qm[0, here, :] = jnp.where(first, q_all, zero)
        qm[1, here, :] = jnp.where(first, zero, q_all)
        gm[0, here, :] = jnp.where(first, g_all, zero)
        gm[1, here, :] = jnp.where(first, zero, g_all)
        prod = g_turned.astype(jnp.float32) * ot_ref[:, here].astype(jnp.float32)
        for h in range(heads_here):
            delta[h:h + 1, here] = jnp.sum(prod[h * HEAD_DIM:(h + 1) * HEAD_DIM], axis=0, keepdims=True)
    for k_ref, v_ref, at in zip(k_parts, v_parts, part_offsets(n_parts, m_len)):
        here = pl.ds(at, m_len)
        kt[:, here] = k_ref[...].T
        vv[here, :] = v_ref[...]
        documents = document_columns(key_seg[:, here])
        for p in range(n_pairs):
            ke[p, here, :128] = k_ref[:, p * 128:(p + 1) * 128]
            ke[p, here, 128:] = documents
    dk[...] = jnp.zeros_like(dk)
    dv[...] = jnp.zeros_like(dv)
    keys_p = by_head(pre_ref[0], heads_here)
    values_p = by_head(pre_ref[1], heads_here)
    keys_turned = keys_p.T

    def grads(s, dp, h, qs):
        p = jnp.exp(s - lt_ref[h // 2, h % 2:h % 2 + 1, qs])
        ds = low(p * (dp - delta[h:h + 1, qs]))
        return low(p), ds

    wide = min(BP, seq)

    def prefix_step(i, totals):
        qs = block_at(i, wide)
        scores = mm(keys_p, qt[:, qs])
        scores = jnp.where(padding_rows(scores.shape, prefix_count), NEG, scores)
        dps = mm(values_p, gt[:, qs])
        chances, slopes = [], []
        for h in range(heads_here):
            rows = slice(h * PP, (h + 1) * PP)
            p, ds = grads(scores[rows], dps[rows], h, qs)
            chances.append(p)
            slopes.append(ds)
        p, ds = jnp.concatenate(chances, axis=0), jnp.concatenate(slopes, axis=0)
        dq[:, qs] = mm(keys_turned, ds)
        dkp = totals[0] + mm(ds, qm[0, qs, :] + qm[1, qs, :])
        dvp = totals[1] + mm(p, gm[0, qs, :] + gm[1, qs, :])
        return dkp, dvp

    zeros = jnp.zeros((heads_here * PP, width), jnp.float32)
    totals = lax.fori_loop(0, seq // wide, prefix_step, (zeros, zeros))
    for n, total in enumerate(totals):
        rows = lax.broadcasted_iota(jnp.int32, total.shape, 0) // PP
        columns = lax.broadcasted_iota(jnp.int32, total.shape, 1) // HEAD_DIM
        total = jnp.where(rows == columns, total, 0.0)
        folded = total[:PP]
        for h in range(1, heads_here):
            folded += total[h * PP:(h + 1) * PP]
        dp_ref[n] = folded

    def add_block(i, j, count, diag):
        qs, ks = block_at(i, BQ), key_blocks(j, count)
        both = []
        for h in range(heads_here):
            c = (h // 2) * 128
            both.append((mm(ke[h // 2, ks, :], qx[h, :, qs]), mm(vv[ks, c:c + 128], gx[h, :, qs])))
        for pr in range(n_pairs):
            c = pr * 128
            dkb = dk[ks, c:c + 128]
            dvb = dv[ks, c:c + 128]
            for h in (2 * pr, 2 * pr + 1):
                s, dp = both[h]
                if diag:
                    s = jnp.where(later_keys(s.shape), NEG, s)
                p, ds = grads(s, dp, h, qs)
                dvb += mm(p, gm[h % 2, qs, c:c + 128])
                dkb += mm(ds, qm[h % 2, qs, c:c + 128])
                dq[head_rows(h), qs] += mm(kt[h * HEAD_DIM:(h + 1) * HEAD_DIM, ks], ds)
            dk[ks, c:c + 128] = dkb
            dv[ks, c:c + 128] = dvb

    def q_step(i, _):
        if causal:
            add_block(i, i * (BQ // BK), BQ // BK, True)
        for_key_blocks(lo_ref[i], hi_ref[i], lambda j, count: add_block(i, j, count, False))
        return 0

    lax.fori_loop(0, n_q, q_step, 0)

    def finish(i, _):
        store_part(dq_parts, i, low((dq[:, block_at(i, BQ)] * 0.125).T))
        return 0

    lax.fori_loop(0, n_q, finish, 0)
    for dkv_ref, at in zip(dkv_parts, part_offsets(n_parts, m_len)):
        here = pl.ds(at, m_len)
        dkv_ref[0] = low(dk[here, :])
        dkv_ref[1] = low(dv[here, :])


def attend_bwd(qs, ks, vs, gs, cols, ot, lt, masks, prefix, lo, hi, causal):
    ek, eq, prefix_count = masks
    n = len(qs)
    q_len, m_len = qs[0][0].shape[0], ks[0][0].shape[0]
    seq, mem = q_len * n, m_len * n
    wd = min(HEAD_DIM * HEADS_BWD, cols)
    heads_here = wd // HEAD_DIM
    steps = cols // wd
    in_specs, operands = [], []
    for group, length in ((qs, q_len), (ks, m_len), (vs, m_len), (gs, q_len)):
        for array, at in group:
            in_specs.append(pl.BlockSpec((length, wd), partial(lambda at, p, *_: (0, at * steps + p), at)))
            operands.append(array)
    in_specs += [
        pl.BlockSpec((wd, seq), lambda p, *_: (p, 0)),
        pl.BlockSpec((wd // 128, 2, seq), lambda p, *_: (p, 0, 0)),
        pl.BlockSpec((1, mem), lambda p, *_: (0, 0)),
        pl.BlockSpec((1, seq), lambda p, *_: (0, 0)),
        pl.BlockSpec((2, PP, wd), lambda p, *_: (0, 0, p)),
    ]
    grid_spec = pltpu.PrefetchScalarGridSpec(
        num_scalar_prefetch=2,
        grid=(steps,),
        in_specs=in_specs,
        out_specs=[pl.BlockSpec((q_len, wd), lambda p, *_: (0, p))] * n
        + [pl.BlockSpec((2, m_len, wd), lambda p, *_: (0, 0, p))] * n
        + [pl.BlockSpec((2, PP, wd), lambda p, *_: (0, 0, p))],
        scratch_shapes=[
            pltpu.VMEM((wd, seq), jnp.bfloat16),
            pltpu.VMEM((wd, seq), jnp.bfloat16),
            pltpu.VMEM((heads_here, 256, seq), jnp.bfloat16),
            pltpu.VMEM((heads_here, 128, seq), jnp.bfloat16),
            pltpu.VMEM((wd, mem), jnp.bfloat16),
            pltpu.VMEM((wd // 128, mem, 256), jnp.bfloat16),
            pltpu.VMEM((mem, wd), jnp.bfloat16),
            pltpu.VMEM((2, seq, wd), jnp.bfloat16),
            pltpu.VMEM((2, seq, wd), jnp.bfloat16),
            pltpu.VMEM((wd, seq), jnp.float32),
            pltpu.VMEM((mem, wd), jnp.float32),
            pltpu.VMEM((mem, wd), jnp.float32),
            pltpu.VMEM((8, seq), jnp.float32),
        ],
    )
    result = pl.pallas_call(
        functools.partial(bwd_kernel, causal, n, prefix_count),
        grid_spec=grid_spec,
        out_shape=[jax.ShapeDtypeStruct((q_len, cols), jnp.bfloat16)] * n
        + [jax.ShapeDtypeStruct((2, m_len, cols), jnp.bfloat16)] * n
        + [jax.ShapeDtypeStruct((2, PP, cols), jnp.float32)],
        compiler_params=pltpu.CompilerParams(vmem_limit_bytes=60 * MIB),
        cost_estimate=pl.CostEstimate(
            flops=12 * seq * mem * cols, bytes_accessed=20 * MIB, transcendentals=seq * mem * cols // 256
        ),
        name="attend_bwd_self" if causal else "attend_bwd_cross",
    )(lo, hi, *operands, ot, lt, ek, eq, prefix)
    return result[:n], result[n:2 * n], result[2 * n]


def ranges(dec_seg, mem_seg, causal):
    seq = dec_seg.shape[0]
    blocks = dec_seg.reshape(seq // BQ, BQ)
    low, high = blocks[:, 0], blocks[:, -1]
    lo = jnp.sum((mem_seg[None, :] < low[:, None]).astype(jnp.int32), axis=1) // BK
    if causal:
        hi = jnp.arange(seq // BQ, dtype=jnp.int32) * (BQ // BK)
    else:
        hi = (jnp.sum((mem_seg[None, :] <= high[:, None]).astype(jnp.int32), axis=1) + BK - 1) // BK
    return lo, hi


def documents(dec_seg, mem_seg, prefix_count):
    return mem_seg[None], dec_seg[None], prefix_count


def normalize(v):
    centered = v - jnp.mean(v, axis=-1, keepdims=True)
    r = lax.rsqrt(jnp.mean(centered * centered, axis=-1, keepdims=True) + 1e-05)
    return centered * r, r


def norm_back(n, r, gain, upstream):
    u = upstream * gain
    return r * (u - jnp.mean(u, axis=-1, keepdims=True) - n * jnp.mean(u * n, axis=-1, keepdims=True))


def gelu_parts(v):
    chance = 0.5 * (1.0 + lax.erf(v * math.sqrt(0.5)))
    slope = chance + v * (jnp.exp(-0.5 * v * v) * (1.0 / math.sqrt(2.0 * math.pi)))
    return v * chance, slope


def low(v):
    return v.astype(jnp.bfloat16)


def place_halves(own, packed, row, held, sems, at):
    x = lax.axis_index("x")
    tall, wide = held.shape[2:]
    cols = packed.shape[2]
    copies = [pltpu.make_async_copy(own, held.at[x], sems.at[at])]
    for j in range(wide // cols):
        copies.append(
            pltpu.make_async_copy(
                packed.at[:, pl.ds(row + j * tall, tall)],
                held.at[1 - x, :, :, pl.ds(j * cols, cols)],
                sems.at[at + 1 + j],
            )
        )
    return copies


def half_of(held, which):
    return held[which].reshape(-1, held.shape[3])


def eighths(weight):
    return weight.reshape(8, weight.shape[0] // 8, weight.shape[1])


def on_first(copies, act):
    @pl.when(pl.program_id(0) == 0)
    def _():
        for copy in copies:
            getattr(copy, act)()


def after_self_kernel(own_ref, par_ref, tok_ref, gains_ref, so_own, cq_own, packed,
                      first_ref, q_own_ref, q_par_ref, so, cq, sems):
    core = lax.axis_index("c")
    so_copies = place_halves(so_own, packed, 0, so, sems, 0)
    cq_copies = place_halves(cq_own, packed, 2 * so.shape[2], cq, sems, 4)
    on_first(so_copies + cq_copies, "start")
    on_first(so_copies, "wait")
    total = tok_ref[...].astype(jnp.float32) + (mm(own_ref[...], half_of(so, core)) + mm(par_ref[...], half_of(so, 1 - core)))
    first = low(total)
    first_ref[...] = first
    n, _ = normalize(first.astype(jnp.float32))
    normed = low(n * gains_ref[0:1, :])
    on_first(cq_copies, "wait")
    q_own_ref[...] = low(mm(normed, half_of(cq, core)))
    q_par_ref[...] = low(mm(normed, half_of(cq, 1 - core)))


def rows_spec(width):
    return pl.BlockSpec((BR, width), lambda i: (i, 0))


ANY = pl.BlockSpec(memory_space=pl.ANY)


def after_self(own, par, tokens, gains, so_own, cq_own, packed):
    rows, d = tokens.shape
    half = d // 2
    return pl.pallas_call(
        after_self_kernel,
        grid=(rows // BR,),
        in_specs=[rows_spec(half), rows_spec(half), rows_spec(d), pl.BlockSpec((3, d), lambda i: (0, 0)), ANY, ANY, ANY],
        out_specs=[rows_spec(d), rows_spec(half), rows_spec(half)],
        out_shape=[
            jax.ShapeDtypeStruct((rows, d), jnp.bfloat16),
            jax.ShapeDtypeStruct((rows, half), jnp.bfloat16),
            jax.ShapeDtypeStruct((rows, half), jnp.bfloat16),
        ],
        scratch_shapes=[
            pltpu.VMEM((2, 8, half // 8, d), jnp.bfloat16),
            pltpu.VMEM((2, 8, d // 8, half), jnp.bfloat16),
            pltpu.SemaphoreType.DMA((8,)),
        ],
        compiler_params=pltpu.CompilerParams(vmem_limit_bytes=58 * MIB),
        cost_estimate=pl.CostEstimate(flops=4 * rows * d * d, bytes_accessed=12 * MIB, transcendentals=0),
        name="after_self",
    )(own, par, tokens, gains, eighths(so_own), eighths(cq_own), packed)


def before_self_kernel(gsec_ref, own_ref, par_ref, first_ref, gains_ref, so_own, cq_own, packed,
                       gfirst_ref, g_own_ref, g_par_ref, so, cq, sems):
    core = lax.axis_index("c")
    so_copies = place_halves(so_own, packed, 0, so, sems, 0)
    cq_copies = place_halves(cq_own, packed, 2 * so.shape[2], cq, sems, 4)
    on_first(cq_copies + so_copies, "start")
    on_first(cq_copies, "wait")
    grad_one = low(gsec_ref[...] + (mm_nt(own_ref[...], half_of(cq, core)) + mm_nt(par_ref[...], half_of(cq, 1 - core))))
    n, r = normalize(first_ref[...].astype(jnp.float32))
    grad_first = norm_back(n, r, gains_ref[0:1, :], grad_one.astype(jnp.float32))
    gfirst_ref[...] = grad_first
    first_low = low(grad_first)
    on_first(so_copies, "wait")
    g_own_ref[...] = low(mm_nt(first_low, half_of(so, core)))
    g_par_ref[...] = low(mm_nt(first_low, half_of(so, 1 - core)))


def before_self(gsec, own, par, first, gains, so_own, cq_own, packed):
    rows, d = first.shape
    half = d // 2
    return pl.pallas_call(
        before_self_kernel,
        grid=(rows // BR,),
        in_specs=[
            rows_spec(d), rows_spec(half), rows_spec(half), rows_spec(d), pl.BlockSpec((3, d), lambda i: (0, 0)),
            ANY, ANY, ANY,
        ],
        out_specs=[rows_spec(d), rows_spec(half), rows_spec(half)],
        out_shape=[
            jax.ShapeDtypeStruct((rows, d), jnp.float32),
            jax.ShapeDtypeStruct((rows, half), jnp.bfloat16),
            jax.ShapeDtypeStruct((rows, half), jnp.bfloat16),
        ],
        scratch_shapes=[
            pltpu.VMEM((2, 8, half // 8, d), jnp.bfloat16),
            pltpu.VMEM((2, 8, d // 8, half), jnp.bfloat16),
            pltpu.SemaphoreType.DMA((8,)),
        ],
        compiler_params=pltpu.CompilerParams(vmem_limit_bytes=58 * MIB),
        cost_estimate=pl.CostEstimate(flops=4 * rows * d * d, bytes_accessed=16 * MIB, transcendentals=0),
        name="before_self",
    )(gsec, own, par, first, gains, eighths(so_own), eighths(cq_own), packed)


MESH_ID = pl.DeviceIdType.MESH
PARTS_IN = 4


def greet(targets):
    barrier = pltpu.get_barrier_semaphore()
    for target in targets:
        pl.semaphore_signal(barrier, inc=1, device_id=target, device_id_type=MESH_ID)
    pl.semaphore_wait(barrier, len(targets))


def remote(src, dst, send, recv, target):
    return pltpu.make_async_remote_copy(
        src_ref=src, dst_ref=dst, send_sem=send, recv_sem=recv, device_id=target, device_id_type=MESH_ID
    )


def eighth_index():
    return (lax.axis_index("zl") * 2 + lax.axis_index("y")) * 2 + lax.axis_index("c")


def piece_copies(wholes, packed, send, recv):
    cols = packed.shape[1]
    copies, at = [], 0
    for whole in wholes:
        tall = whole.shape[0] // 8
        source = pl.ds(pl.multiple_of(eighth_index() * tall, tall), tall)
        for j in range(whole.shape[1] // cols):
            n = len(copies)
            copies.append(
                remote(
                    whole.at[source, pl.ds(j * cols, cols)], packed.at[pl.ds(at, tall)], send.at[n], recv.at[n],
                    {"x": 1 - lax.axis_index("x")},
                )
            )
            at += tall
    return copies


def bring_kernel(tok, mem, cot, qkv, prefix, segs, w_in, w_out, down, up, so, cq, co, ckv,
                 rows_out, q_own, q_par, passed, mem_mine, packed, cot_mine, cot_send, qkv_oth, prefix_got, segs_got, down_all, up_all,
                 rows_own, rows_par, held, stage, stage_down, stage_up, send, recv, load, p_send, p_recv):
    x, y, zl, core = (lax.axis_index(name) for name in ("x", "y", "zl", "c"))
    half = rows_own.shape[0]
    cols = tok.shape[1]
    chunk = half // PARTS_IN
    piece = qkv.shape[0] // 8
    stays = x == core
    partner = {"c": 1 - core}
    across = {"x": 1 - x}

    def token_half(which):
        return pl.ds(pl.multiple_of(which * half, half), half)

    loads = [
        pltpu.make_async_copy(source.at[token_half(which)], stage.at[n], load.at[n])
        for n, (source, which) in enumerate(((mem, core), (cot, core)))
    ]
    at = 0
    for whole in (w_in, w_out):
        tall, wide = whole.shape[0] // 8, whole.shape[1]
        source = pl.ds(pl.multiple_of(eighth_index() * tall, tall), tall)
        for j in range(wide // cols):
            n = len(loads)
            loads.append(
                pltpu.make_async_copy(
                    whole.at[source, pl.ds(j * cols, cols)], stage.at[2, pl.ds(at, tall)], load.at[n]
                )
            )
            at += tall
    pack = pltpu.make_async_copy(stage.at[2], packed.at[pl.ds(half, half)], load.at[len(loads)])
    mem_send = packed.at[pl.ds(0, half)]
    for copy in loads:
        copy.start()
    greet([across, {"x": 1 - x, "c": 1 - core}, {"y": 1 - y}, {"zl": 1 - zl}, partner])

    def features(which):
        return pl.ds(pl.multiple_of(which * cols, cols), cols)

    def part(k):
        return pl.ds(k * chunk, chunk)

    def eighth(a, b, c):
        return pl.ds(pl.multiple_of(((a * 2 + b) * 2 + c) * piece, piece), piece)

    def weight(at, slot, target, source=None):
        return remote((qkv_oth if source is None else source).at[at], qkv_oth.at[at], send.at[slot], recv.at[slot], target)

    mine = eighth(zl, y, core)
    w_x = weight(mine, 0, across, qkv)
    w_x.start()
    at_small = 14 + 3 * PARTS_IN
    small = [
        remote(prefix, prefix_got, send.at[at_small], recv.at[at_small], across),
        remote(segs, segs_got, send.at[at_small + 1], recv.at[at_small + 1], partner),
    ]
    for copy in small:
        copy.start()
    others = small

    units = up.shape[0]

    def adapt_places(a, b):
        at = pl.ds(pl.multiple_of((a * 2 + b) * units, units), units)
        return down_all.at[:, at], up_all.at[at]

    def adapt_copies(sources, a, b, n, target):
        return [
            remote(source, place, send.at[at_small + 2 + n + m], recv.at[at_small + 2 + n + m], target)
            for m, (source, place) in enumerate(zip(sources, adapt_places(a, b)))
        ]

    adapt_y = adapt_copies((down, up), y, core, 0, {"y": 1 - y})
    adapt_c = adapt_copies((down, up), y, core, 2, partner)
    adapt_in = [
        pltpu.make_async_copy(down, stage_down, load.at[14]),
        pltpu.make_async_copy(up, stage_up, load.at[15]),
    ]
    for copy in adapt_y + adapt_c + adapt_in:
        copy.start()

    at_own, at_par = 8, 8 + PARTS_IN
    at_here = 8 + 2 * PARTS_IN

    def token_sends():
        copies = []
        for t in range(2):
            for k in range(PARTS_IN):
                slot = at_own + k
                copies.append(
                    remote(
                        tok.at[pl.ds(t * half + k * chunk, chunk)],
                        rows_own.at[part(k), features(x)],
                        send.at[slot + t * PARTS_IN],
                        recv.at[slot],
                        {"x": 1 - x, "c": t},
                    )
                )
        return copies

    def here_copies():
        own = tok.at[token_half(core)]
        other = tok.at[token_half(1 - core)]
        return [
            remote(other, rows_own.at[:, features(x)], send.at[at_here], recv.at[at_here], partner),
            remote(own, rows_par.at[:, features(x)], send.at[at_here + 1], recv.at[at_here + 1], partner),
        ]

    def weight_rows(source):
        tall = held.shape[0] // 3
        return [
            pltpu.make_async_copy(source.at[pl.ds(t * tall, tall)], held.at[pl.ds(t * tall, tall)], load.at[9 + t])
            for t in range(3)
        ]

    def own_weights():
        return weight_rows(qkv)

    def row_copy(source, to, slot):
        return remote(source.at[token_half(1 - core)], to, send.at[slot], recv.at[slot], partner)

    @pl.when(jnp.logical_not(stays))
    def _():
        for copy in token_sends():
            copy.start()
        row_copy(mem, mem_send, at_here + 3).start()
        row_copy(cot, cot_send, at_here + 5).start()
        for n, to, slot in ((0, mem_send, at_here + 3), (1, cot_send, at_here + 5)):
            loads[n].wait()
            pltpu.make_async_copy(stage.at[n], to, recv.at[slot]).start()

    @pl.when(stays)
    def _():
        for copy in here_copies():
            copy.start()
        row_copy(mem, mem_mine, at_here + 2).start()
        row_copy(cot, cot_mine, at_here + 4).start()
        for which, to, slot in ((core, rows_own, at_here), (1 - core, rows_par, at_here + 1)):
            pltpu.make_async_copy(tok.at[token_half(which)], to.at[:, features(x)], recv.at[slot]).start()
        for copy in own_weights():
            copy.start()
        for n, to, slot in ((0, mem_mine, at_here + 2), (1, cot_mine, at_here + 4)):
            loads[n].wait()
            pltpu.make_async_copy(stage.at[n], to, recv.at[slot]).start()

    for copy in loads[2:]:
        copy.wait()
    pack.start()
    adapt_here = [
        pltpu.make_async_copy(source, place, load.at[14 + m])
        for m, (source, place) in enumerate(zip((stage_down, stage_up), adapt_places(y, core)))
    ]
    for came, placed in zip(adapt_in, adapt_here):
        came.wait()
        placed.start()

    for copy in adapt_y:
        copy.wait_recv()
    adapt_yc = adapt_copies(adapt_places(1 - y, core), 1 - y, core, 4, partner)
    for copy in adapt_yc:
        copy.start()
    w_x.wait_recv()
    w_y = weight(mine, 1, {"y": 1 - y})
    w_z = weight(mine, 2, {"zl": 1 - zl})
    w_c = weight(mine, 4, partner)
    for copy in (w_y, w_z, w_c):
        copy.start()

    forwards = []

    def forward(k):
        here = rows_own.at[part(k), features(1 - x)]
        remote(here, here, send.at[at_own + k], recv.at[at_own + k], across).wait_recv()
        copy = remote(here, rows_par.at[part(k), features(1 - x)], send.at[at_here + 6 + k], recv.at[at_par + k], partner)
        copy.start()
        forwards.append(copy)

    forward(0)
    w_y.wait_recv()
    from_y = eighth(zl, 1 - y, core)
    w_yz = weight(from_y, 3, {"zl": 1 - zl})
    w_yc = weight(from_y, 5, partner)
    w_yz.start()
    w_yc.start()
    forward(1)
    w_z.wait_recv()
    w_zc = weight(eighth(1 - zl, y, core), 6, partner)
    w_zc.start()
    for k in range(2, PARTS_IN):
        forward(k)
    w_yz.wait_recv()
    w_yzc = weight(eighth(1 - zl, 1 - y, core), 7, partner)
    w_yzc.start()

    pieces = piece_copies((so, cq, co, ckv), passed, p_send, p_recv)
    for copy in pieces:
        copy.start()

    for copy in (w_c, w_yc, w_zc, w_yzc):
        copy.wait_recv()

    @pl.when(jnp.logical_not(stays))
    def _():
        for copy in weight_rows(qkv_oth):
            copy.start()

    for copy in weight_rows(qkv):
        copy.wait()
    for to, slot in ((rows_own.at[:, features(x)], at_here), (rows_par.at[:, features(x)], at_here + 1)):
        remote(to, to, send.at[slot], recv.at[slot], partner).wait_recv()
    tall = held.shape[0] // 3
    keep_rows = pltpu.make_async_copy(rows_own, rows_out, load.at[12])
    keep_rows.start()
    for t in range(3):
        q_own[:, t * cols:(t + 1) * cols] = low(mm(rows_own[...], held[t * tall:(t + 1) * tall, :]))
    for copy in forwards:
        copy.wait_recv()
    for t in range(3):
        q_par[:, t * cols:(t + 1) * cols] = low(mm(rows_par[...], held[t * tall:(t + 1) * tall, :]))
    keep_rows.wait()

    for copy in (*adapt_c, *adapt_yc, *others, *pieces):
        copy.wait_recv()
    for to, slot in (
        (mem_mine, at_here + 2),
        (mem_send, at_here + 3),
        (cot_mine, at_here + 4),
        (cot_send, at_here + 5),
    ):
        remote(to, to, send.at[slot], recv.at[slot], partner).wait_recv()

    pack.wait()
    for copy in adapt_here:
        copy.wait()

    for copy in (w_x, w_y, w_z, w_c, w_yz, w_yc, w_zc, w_yzc, *adapt_y, *adapt_c, *adapt_yc, *forwards, *others, *pieces):
        copy.wait_send()

    @pl.when(jnp.logical_not(stays))
    def _():
        for copy in token_sends():
            copy.wait_send()
        row_copy(mem, mem_send, at_here + 3).wait_send()
        row_copy(cot, cot_send, at_here + 5).wait_send()

    @pl.when(stays)
    def _():
        for copy in here_copies():
            copy.wait_send()
        row_copy(mem, mem_mine, at_here + 2).wait_send()
        row_copy(cot, cot_mine, at_here + 4).wait_send()


def bring_rows(tokens, memory, cotangent, qkv_flat, prefixes, segs, ffn_in, ffn_out, down, up, others):
    rows, cols = tokens.shape
    half = rows // 2
    wide_rows = jax.ShapeDtypeStruct((half, 2 * cols), jnp.bfloat16)
    thin_rows = jax.ShapeDtypeStruct((half, cols), jnp.bfloat16)
    slots = 22 + 3 * PARTS_IN
    packed_rows = sum(w.shape[0] // 8 * (w.shape[1] // cols) for w in others)
    pieces = sum(w.shape[1] // cols for w in others)
    vmem = pl.BlockSpec(memory_space=pltpu.VMEM)
    return pl.pallas_call(
        bring_kernel,
        in_specs=[ANY] * 14,
        out_specs=[ANY, vmem, vmem] + [ANY] * 10,
        out_shape=[wide_rows, jax.ShapeDtypeStruct((half, 3 * cols), jnp.bfloat16),
                   jax.ShapeDtypeStruct((half, 3 * cols), jnp.bfloat16),
                   jax.ShapeDtypeStruct((packed_rows, cols), jnp.bfloat16),
                   thin_rows, jax.ShapeDtypeStruct((rows, cols), jnp.bfloat16), thin_rows, thin_rows,
                   jax.ShapeDtypeStruct(qkv_flat.shape, jnp.bfloat16),
                   jax.ShapeDtypeStruct(prefixes.shape, prefixes.dtype),
                   jax.ShapeDtypeStruct(segs.shape, segs.dtype),
                   jax.ShapeDtypeStruct((down.shape[0], 4 * down.shape[1]), down.dtype),
                   jax.ShapeDtypeStruct((4 * up.shape[0], up.shape[1]), up.dtype)],
        scratch_shapes=[
            pltpu.VMEM((half, 2 * cols), jnp.bfloat16),
            pltpu.VMEM((half, 2 * cols), jnp.bfloat16),
            pltpu.VMEM(qkv_flat.shape, jnp.bfloat16),
            pltpu.VMEM((3, half, cols), jnp.bfloat16),
            pltpu.VMEM(down.shape, jnp.bfloat16),
            pltpu.VMEM(up.shape, jnp.bfloat16),
            pltpu.SemaphoreType.DMA((slots,)),
            pltpu.SemaphoreType.DMA((slots,)),
            pltpu.SemaphoreType.DMA((16,)),
            pltpu.SemaphoreType.DMA((pieces,)),
            pltpu.SemaphoreType.DMA((pieces,)),
        ],
        compiler_params=pltpu.CompilerParams(collective_id=0, has_side_effects=True, vmem_limit_bytes=58 * MIB),
        cost_estimate=pl.CostEstimate(flops=0, bytes_accessed=64 * MIB, transcendentals=0),
        name="bring_rows",
    )(tokens, memory, cotangent, qkv_flat, prefixes, segs, ffn_in, ffn_out, down, up, *others)


def project_kernel(n_weights, row, own_mine, own_got, par_mine, par_got, w_own, w_oth, out_own, out_par, held, sems):
    x, core = lax.axis_index("x"), lax.axis_index("c")
    d = held.shape[0] // n_weights
    cols = held.shape[1]

    def copies(agree):
        tall = held.shape[0] // 8
        parts = [w_own.at[pl.ds(e * tall, tall)] if agree else w_oth.at[e, pl.ds(row, tall)] for e in range(8)]
        return [
            pltpu.make_async_copy(part, held.at[pl.ds(e * tall, tall)], sems.at[e]) for e, part in enumerate(parts)
        ]

    for act in ("start", "wait"):
        for agree, chosen in ((True, x == core), (False, x != core)):
            @pl.when(jnp.logical_and(pl.program_id(0) == 0, chosen))
            def _(agree=agree, act=act):
                for copy in copies(agree):
                    getattr(copy, act)()

    for t in range(n_weights):
        for pieces, out in (((own_mine, own_got), out_own), ((par_mine, par_got), out_par)):
            total = None
            for piece, at in zip(pieces, (x * (d // 2), (1 - x) * (d // 2))):
                rows = pl.ds(pl.multiple_of(t * d + at, d // 2), d // 2)
                term = mm(piece[...], held[rows, :])
                total = term if total is None else total + term
            out[:, t * cols:(t + 1) * cols] = low(total)


def project(own, par, w_own, w_oth, row, n_weights):
    rows, cols = own[0].shape
    d = w_own.shape[0] // n_weights
    return pl.pallas_call(
        functools.partial(project_kernel, n_weights, row),
        grid=(rows // BR,),
        in_specs=[rows_spec(cols)] * 4 + [ANY, ANY],
        out_specs=[rows_spec(n_weights * cols)] * 2,
        out_shape=[jax.ShapeDtypeStruct((rows, n_weights * cols), jnp.bfloat16)] * 2,
        scratch_shapes=[pltpu.VMEM(w_own.shape, jnp.bfloat16), pltpu.SemaphoreType.DMA((8,))],
        compiler_params=pltpu.CompilerParams(vmem_limit_bytes=58 * MIB),
        cost_estimate=pl.CostEstimate(flops=4 * rows * d * cols * n_weights, bytes_accessed=16 * MIB, transcendentals=0),
        name="project",
    )(*own, *par, w_own, w_oth)


def back_memory_kernel(ckv_row, own_ref, got_ref, w_own, packed, keep_ref, send_ref, held, sems):
    x, core = lax.axis_index("x"), lax.axis_index("c")
    copies = place_halves(w_own, packed, ckv_row, held, sems, 0)
    on_first(copies, "start")
    on_first(copies, "wait")
    n_weights = own_ref.shape[0]
    share = 8 // (2 * n_weights)
    for out, which in ((send_ref, 1 - x), (keep_ref, x)):
        total = None
        for t in range(n_weights):
            for rows, heads in ((own_ref, core), (got_ref, 1 - core)):
                weight = held[heads, pl.ds(2 * share * t + share * which, share)]
                term = mm_nt(rows[t], weight.reshape(-1, weight.shape[2]))
                total = term if total is None else total + term
        out[...] = low(total)


def back_memory(own, got, w_own, packed, ckv_row):
    n, rows, cols = own.shape
    w_own = eighths(w_own)
    both = pl.BlockSpec((n, BR, cols), lambda i: (0, i, 0))
    return pl.pallas_call(
        functools.partial(back_memory_kernel, ckv_row),
        grid=(rows // BR,),
        in_specs=[both, both, ANY, ANY],
        out_specs=[rows_spec(cols)] * 2,
        out_shape=[jax.ShapeDtypeStruct((rows, cols), jnp.bfloat16)] * 2,
        scratch_shapes=[pltpu.VMEM((2, *w_own.shape), jnp.bfloat16), pltpu.SemaphoreType.DMA((2,))],
        compiler_params=pltpu.CompilerParams(vmem_limit_bytes=58 * MIB),
        cost_estimate=pl.CostEstimate(flops=8 * n * rows * cols * cols, bytes_accessed=12 * MIB, transcendentals=0),
        name="back_memory",
    )(own, got, w_own, packed)


CHUNK = 512
ROWS = 256


def ffn_kernel(co_row, own_ref, par_ref, first_hbm, cot_mine, cot_got, gains_ref, down, up,
               co_own, packed, in_own, out_own, ffn_other,
               keep_ref, send_ref, gsec_ref, g_own_ref, g_par_ref, part_ref,
               first, cot, co, w_in, w_out, normed, second, branch, full, acc, slopes,
               bottle, bottle_slope, bottle_grad, grads, got_c, part_out, part_got,
               co_sems, w_sems, sems, send, recv):
    x, y, core = (lax.axis_index(name) for name in ("x", "y", "c"))
    rows, d = normed.shape
    half = d // 2
    in_tall = ffn_other.shape[1] // 2
    chunks = 2 * in_own.shape[2] // CHUNK
    own_chunks = chunks // 2
    out_tall = w_out.shape[2]
    pieces = CHUNK // out_tall

    def columns(which):
        return pl.ds(pl.multiple_of(which * half, half), half)

    loads = [
        pltpu.make_async_copy(first_hbm, first, sems.at[0]),
        pltpu.make_async_copy(cot_mine, cot.at[:, columns(x)], sems.at[1]),
        pltpu.make_async_copy(cot_got, cot.at[:, columns(1 - x)], sems.at[2]),
    ]
    co_copies = place_halves(co_own, packed, co_row, co, co_sems, 0)

    def weight_copies(t, slot, own):
        if own:
            at = pl.ds(pl.multiple_of(t * CHUNK, CHUNK), CHUNK)
            sources_in = [(in_own.at[:, :, at], w_in.at[slot])]
            sources = [out_own.at[pl.ds(pieces * t, pieces), :, pl.ds(j * half, half)] for j in range(2)]
        else:
            t = t - own_chunks
            tall = w_in.shape[2]
            blocks = CHUNK // half
            sources_in = [
                (
                    ffn_other.at[:, pl.ds(pl.multiple_of((t * blocks + j) * tall, tall), tall)],
                    w_in.at[slot, :, :, pl.ds(j * half, half)],
                )
                for j in range(blocks)
            ]
            sources = [
                ffn_other.at[pl.ds(pieces * t, pieces), pl.ds(in_tall + j * out_tall, out_tall)] for j in range(2)
            ]
        return [
            pltpu.make_async_copy(source, to, w_sems.at[slot, 2 + j]) for j, (source, to) in enumerate(sources_in)
        ] + [
            pltpu.make_async_copy(source, w_out.at[slot, :, :, pl.ds(j * half, half)], w_sems.at[slot, j])
            for j, source in enumerate(sources)
        ]

    def fetch(t):
        slot = t % 2

        @pl.when(t < own_chunks)
        def _():
            for copy in weight_copies(t, slot, True):
                copy.start()

        @pl.when(jnp.logical_and(t >= own_chunks, t < chunks))
        def _():
            for copy in weight_copies(t, slot, False):
                copy.start()

    def arrive(t):
        slot = t % 2

        @pl.when(t < own_chunks)
        def _():
            for copy in weight_copies(t, slot, True):
                copy.wait()

        @pl.when(t >= own_chunks)
        def _():
            for copy in weight_copies(t, slot, False):
                copy.wait()

    for copy in co_copies + loads[:1]:
        copy.start()
    fetch(0)
    fetch(1)
    for copy in loads[1:]:
        copy.start()
    greet([{"c": 1 - core}, {"y": 1 - y}, {"x": 1 - x}])
    for copy in co_copies + loads[:1]:
        copy.wait()
    acc[...] = mm(own_ref[...], half_of(co, core)) + mm(par_ref[...], half_of(co, 1 - core))

    def by_rows(act):
        def step(i, _):
            act(pl.ds(pl.multiple_of(i * ROWS, ROWS), ROWS))
            return 0

        lax.fori_loop(0, rows // ROWS, step, 0)

    def norm_two(at):
        n_one, _ = normalize(first[at, :].astype(jnp.float32))
        summed = low(n_one * gains_ref[0:1, :] + acc[at, :])
        second[at, :] = summed
        n_two, _ = normalize(summed.astype(jnp.float32))
        normed_two = n_two * gains_ref[1:2, :]
        normed[at, :] = low(normed_two)
        acc[at, :] = normed_two

    by_rows(norm_two)
    value, slope = gelu_parts(mm(normed[...], down[...]))
    bottle[...] = low(value)
    bottle_slope[...] = slope
    acc[...] += 4.0 * mm(bottle[...], up[...])

    def up_step(t, _):
        arrive(t)
        slot = t % 2
        weight_in = w_in[slot].reshape(d, CHUNK)
        weight_out = w_out[slot].reshape(CHUNK, d)
        halves = (slice(0, rows // 2), slice(rows // 2, rows))
        products = [mm(normed[at, :], weight_in) for at in halves]
        for at, product in zip(halves, products):
            value, slope = gelu_parts(product)
            slopes[t, at, :] = low(slope)
            acc[at, :] += mm(low(value), weight_out)
        fetch(t + 2)
        return 0

    lax.fori_loop(0, chunks, up_step, 0)
    fetch(0)
    fetch(1)
    for copy in loads[1:]:
        copy.wait()

    def norm_three(at):
        third = low(acc[at, :])
        n_three, r_three = normalize(third.astype(jnp.float32))
        gain = gains_ref[2:3, :]
        full[at, :] = low(n_three * gain)
        grad_three = norm_back(n_three, r_three, gain, cot[at, :].astype(jnp.float32))
        branch[at, :] = low(grad_three)
        acc[at, :] = grad_three

    by_rows(norm_three)
    outs = [
        pltpu.make_async_copy(full.at[:, columns(x)], keep_ref, sems.at[0]),
        pltpu.make_async_copy(full.at[:, columns(1 - x)], send_ref, sems.at[1]),
    ]
    for copy in outs:
        copy.start()
    adapted = low(4.0 * branch[...].astype(jnp.float32))
    bottle_grad[...] = low(mm_nt(adapted, up[...]) * bottle_slope[...])
    tall = grads.shape[3]
    for which, grad in ((0, mm_tn(bottle_grad[...], normed[...])), (1, mm_tn(bottle[...], adapted))):
        for n in range(4):
            grads[n // 2, n % 2, which] = grad[n * tall:(n + 1) * tall]
    over_c = remote(grads.at[:, 1 - core], got_c, send.at[0], recv.at[0], {"c": 1 - core})
    over_y = remote(part_out.at[0], part_got.at[0], send.at[1], recv.at[1], {"y": 1 - y})
    over_x = remote(part_out.at[1], part_got.at[1], send.at[2], recv.at[2], {"x": 1 - x})
    over_c.start()
    acc[...] += mm_nt(bottle_grad[...], down[...])

    def down_step(t, _):
        arrive(t)
        slot = t % 2
        weight_in = w_in[slot].reshape(d, CHUNK)
        weight_out = w_out[slot].reshape(CHUNK, d)
        halves = (slice(0, rows // 2), slice(rows // 2, rows))
        products = [mm_nt(branch[at, :], weight_out) for at in halves]
        for at, product in zip(halves, products):
            grad_pre = low(product * slopes[t, at, :].astype(jnp.float32))
            acc[at, :] += mm_nt(grad_pre, weight_in)
        fetch(t + 2)

        @pl.when(t == chunks // 4 - 1)
        def _():
            over_c.wait()
            part_out[0] = low(grads[1 - y, core] + got_c[1 - y])
            over_y.start()

        @pl.when(t == chunks * 5 // 8)
        def _():
            over_y.wait()
            part_out[1] = low(grads[y, core] + got_c[y] + part_got[0].astype(jnp.float32))
            over_x.start()

        return 0

    lax.fori_loop(0, chunks, down_step, 0)
    for copy in outs:
        copy.wait()

    def norm_two_back(at):
        n_two, r_two = normalize(second[at, :].astype(jnp.float32))
        grad_two = low(acc[at, :]).astype(jnp.float32)
        grad_second = norm_back(n_two, r_two, gains_ref[1:2, :], grad_two)
        acc[at, :] = grad_second
        branch[at, :] = low(grad_second)

    by_rows(norm_two_back)
    out_acc = pltpu.make_async_copy(acc, gsec_ref, sems.at[0])
    out_acc.start()
    full[:, :half] = low(mm_nt(branch[...], half_of(co, core)))
    full[:, half:] = low(mm_nt(branch[...], half_of(co, 1 - core)))
    outs = [
        pltpu.make_async_copy(full.at[:, pl.ds(0, half)], g_own_ref, sems.at[1]),
        pltpu.make_async_copy(full.at[:, pl.ds(half, half)], g_par_ref, sems.at[2]),
    ]
    for copy in outs:
        copy.start()
    over_x.wait()
    part_ref[...] = low(part_out[1].astype(jnp.float32) + part_got[1].astype(jnp.float32))
    for copy in outs + [out_acc]:
        copy.wait()


def ffn_both_ways(own, par, first, cot_mine, cot_got, gains, down, up, co_own, packed, co_row, in_own, out_own, ffn_other):
    rows, d = first.shape
    half = d // 2
    hidden_half = in_own.shape[1]
    bottleneck = up.shape[0]
    co_own, in_own, out_own = eighths(co_own), eighths(in_own), eighths(out_own)
    vmem = pl.BlockSpec(memory_space=pltpu.VMEM)
    thin = jax.ShapeDtypeStruct((rows, half), jnp.bfloat16)
    part = (2, bottleneck // 4, d)
    flops = 2 * rows * d * (8 * hidden_half + 6 * bottleneck + 2 * d)
    return pl.pallas_call(
        functools.partial(ffn_kernel, co_row),
        in_specs=[vmem, vmem, ANY, ANY, ANY, vmem, vmem, vmem, ANY, ANY, ANY, ANY, ANY],
        out_specs=[ANY, ANY, ANY, ANY, ANY, vmem],
        out_shape=[thin, thin, jax.ShapeDtypeStruct((rows, d), jnp.float32), thin, thin,
                   jax.ShapeDtypeStruct(part, jnp.bfloat16)],
        scratch_shapes=[
            pltpu.VMEM((rows, d), jnp.bfloat16),
            pltpu.VMEM((rows, d), jnp.bfloat16),
            pltpu.VMEM((2, *co_own.shape), jnp.bfloat16),
            pltpu.VMEM((2, 8, d // 8, CHUNK), jnp.bfloat16),
            pltpu.VMEM((2, CHUNK // out_own.shape[1], out_own.shape[1], d), jnp.bfloat16),
            pltpu.VMEM((rows, d), jnp.bfloat16),
            pltpu.VMEM((rows, d), jnp.bfloat16),
            pltpu.VMEM((rows, d), jnp.bfloat16),
            pltpu.VMEM((rows, d), jnp.bfloat16),
            pltpu.VMEM((rows, d), jnp.float32),
            pltpu.VMEM((2 * hidden_half // CHUNK, rows, CHUNK), jnp.bfloat16),
            pltpu.VMEM((rows, bottleneck), jnp.bfloat16),
            pltpu.VMEM((rows, bottleneck), jnp.float32),
            pltpu.VMEM((rows, bottleneck), jnp.bfloat16),
            pltpu.VMEM((2, 2, *part), jnp.float32),
            pltpu.VMEM((2, *part), jnp.float32),
            pltpu.VMEM((2, *part), jnp.bfloat16),
            pltpu.VMEM((2, *part), jnp.bfloat16),
            pltpu.SemaphoreType.DMA((4,)),
            pltpu.SemaphoreType.DMA((2, 2 + CHUNK // half)),
            pltpu.SemaphoreType.DMA((3,)),
            pltpu.SemaphoreType.DMA((3,)),
            pltpu.SemaphoreType.DMA((3,)),
        ],
        compiler_params=pltpu.CompilerParams(collective_id=3, has_side_effects=True, vmem_limit_bytes=63 * MIB),
        cost_estimate=pl.CostEstimate(flops=flops, bytes_accessed=48 * MIB, transcendentals=0),
        name="ffn_both_ways",
    )(own, par, first, cot_mine, cot_got, gains, down, up, co_own, packed, in_own, out_own, ffn_other)


PREFIX_STEPS = ("x", "zl", "y", "zh")


def finish_kernel(dq_own, dq_got, dkv_own, dkv_got, gfirst, w_own, w_oth, mem_keep, mem_got, o_keep, o_got, pre_ref, part_ref,
                  out_ref, mem_ref, o_ref, pre_out_ref, part_got_ref,
                  lhs, first, held, boxes, stage, sums, arrived, local, place, send, recv):
    x, core = lax.axis_index("x"), lax.axis_index("c")
    here = {name: lax.axis_index(name) for name in PREFIX_STEPS}
    partner, across = {"c": 1 - core}, {"x": 1 - x}
    stays = x == core
    blocks = lhs.shape[0]
    half = blocks * BT
    cols = out_ref.shape[1]
    d = held.shape[1] // 3
    steps = len(PREFIX_STEPS) + 1

    def loads(b):
        rows = pl.ds(b * BT, BT)
        pairs = [(dq_own.at[rows], lhs.at[b, 0]), (dkv_own.at[0, rows], lhs.at[b, 1]), (dkv_own.at[1, rows], lhs.at[b, 2]),
                 (dq_got.at[rows], lhs.at[b, 3]), (dkv_got.at[0, rows], lhs.at[b, 4]), (dkv_got.at[1, rows], lhs.at[b, 5]),
                 (gfirst.at[rows], first.at[b])]
        return [pltpu.make_async_copy(src, dst, local.at[b, n]) for n, (src, dst) in enumerate(pairs)]

    def weights(agree):
        pair = (w_own, w_oth) if agree else (w_oth, w_own)
        return [pltpu.make_async_copy(src, held.at[n], local.at[blocks, n]) for n, src in enumerate(pair)]

    ours = pl.ds(pl.multiple_of(core * half, half), half)

    def settled(agree):
        mine, passed = ((mem_keep, o_keep), (mem_got, o_got)) if agree else ((mem_got, o_got), (mem_keep, o_keep))
        return (
            [pltpu.make_async_copy(src, stage.at[n], local.at[blocks, 2 + n]) for n, src in enumerate(mine)],
            [pltpu.make_async_copy(stage.at[n], to.at[ours], local.at[blocks, 4 + n]) for n, to in enumerate((mem_ref, o_ref))],
            [
                remote(src, to.at[ours], send.at[0, blocks + n], recv.at[blocks + n, core], partner)
                for n, (src, to) in enumerate(zip(passed, (mem_ref, o_ref)))
            ],
        )

    def prefix_copy(s):
        target = {PREFIX_STEPS[s]: 1 - here[PREFIX_STEPS[s]]} if s < steps - 1 else partner
        return remote(sums.at[s], arrived.at[s], send.at[2, s], recv.at[blocks + 2 + s, 0], target)

    for copy in loads(0):
        copy.start()
    for agree, chosen in ((True, stays), (False, jnp.logical_not(stays))):
        @pl.when(chosen)
        def _(agree=agree):
            for copy in weights(agree):
                copy.start()

    for b in range(1, blocks):
        for copy in loads(b):
            copy.start()
    for agree, chosen in ((True, stays), (False, jnp.logical_not(stays))):
        @pl.when(chosen)
        def _(agree=agree):
            for copy in settled(agree)[0]:
                copy.start()

    sums[0] = low(pre_ref[...])
    greet([across, {"x": 1 - x, "c": 1 - core}, partner] + [{name: 1 - here[name]} for name in PREFIX_STEPS[1:]])
    prefix_copy(0).start()
    part_copy = remote(
        part_ref, part_got_ref, send.at[1, blocks], recv.at[blocks + 2, 1], {"zl": 1 - here["zl"]}
    )
    part_copy.start()

    def landing(b):
        return pl.ds(pl.multiple_of(core * half + b * BT, BT), BT)

    def over(b):
        return remote(boxes.at[b, 0], out_ref.at[landing(b)], send.at[0, b], recv.at[b, core], {"x": 1 - x, "c": x})

    def beside(b):
        return remote(boxes.at[b, 1], out_ref.at[landing(b)], send.at[1, b], recv.at[b, core], partner)

    def kept_here(b):
        return pltpu.make_async_copy(boxes.at[b, 1], out_ref.at[landing(b)], place.at[b])

    def compute(b, which):
        at = pl.ds(pl.multiple_of(which * cols, cols), cols)
        total = first[b, :, at]
        for n in range(6):
            rows = pl.ds(pl.multiple_of((n % 3) * d + which * cols, cols), cols)
            total += mm_nt(lhs[b, n], held[n // 3, rows, :])
        return low(total)

    def next_prefix(s):
        prefix_copy(s).wait()
        sums[s + 1] = low(sums[s].astype(jnp.float32) + arrived[s].astype(jnp.float32))
        prefix_copy(s + 1).start()

    for copy in weights(True):
        copy.wait()
    for b in range(blocks):
        for copy in loads(b):
            copy.wait()
        boxes[b, 0] = compute(b, 1 - x)
        over(b).start()
        if b == 1:
            next_prefix(0)
    for b in range(blocks):
        boxes[b, 1] = compute(b, x)

        @pl.when(stays)
        def _(b=b):
            kept_here(b).start()

        @pl.when(jnp.logical_not(stays))
        def _(b=b):
            beside(b).start()

        if b + 1 < steps - 1:
            next_prefix(b + 1)

    for agree, chosen in ((True, stays), (False, jnp.logical_not(stays))):
        @pl.when(chosen)
        def _(agree=agree):
            loaded, placed, passed = settled(agree)
            for copy in passed:
                copy.start()
            for copy in loaded:
                copy.wait()
            for copy in placed:
                copy.start()

    prefix_copy(steps - 1).wait()
    pre_out_ref[...] = jnp.where(stays, sums[steps - 1], arrived[steps - 1]).astype(jnp.float32)

    def wait_for(t, b):
        rows = out_ref.at[pl.ds(pl.multiple_of(t * half + b * BT, BT), BT)]
        remote(rows, rows, send.at[0, b], recv.at[b, t], across).wait_recv()

    part_copy.wait()
    theirs = pl.ds(pl.multiple_of((1 - core) * half, half), half)
    for n, to in enumerate((mem_ref, o_ref)):
        remote(to.at[theirs], to.at[theirs], send.at[0, 0], recv.at[blocks + n, 1 - core], partner).wait_recv()
    for agree, chosen in ((True, stays), (False, jnp.logical_not(stays))):
        @pl.when(chosen)
        def _(agree=agree):
            loaded, placed, passed = settled(agree)
            for copy in placed:
                copy.wait()
            for copy in passed:
                copy.wait_send()

    for b in range(blocks):
        over(b).wait_send()

        @pl.when(stays)
        def _(b=b):
            kept_here(b).wait()
            wait_for(1 - core, b)

        @pl.when(jnp.logical_not(stays))
        def _(b=b):
            beside(b).wait_send()
            for t in range(2):
                wait_for(t, b)


def finish_tokens(dq_own, dq_got, dkv_own, dkv_got, gfirst, w_own, w_oth, mem_keep, mem_got, o_keep, o_got, prefix, part):
    half, cols = dq_own.shape
    blocks = half // BT
    steps = len(PREFIX_STEPS) + 1
    vmem = pl.BlockSpec(memory_space=pltpu.VMEM)
    rows = jax.ShapeDtypeStruct((2 * half, cols), jnp.bfloat16)
    return pl.pallas_call(
        finish_kernel,
        in_specs=[ANY] * 11 + [vmem, vmem],
        out_specs=[ANY, ANY, ANY, vmem, vmem],
        out_shape=[rows, rows, rows, jax.ShapeDtypeStruct(prefix.shape, jnp.float32),
                   jax.ShapeDtypeStruct(part.shape, part.dtype)],
        scratch_shapes=[
            pltpu.VMEM((blocks, 6, BT, cols), jnp.bfloat16),
            pltpu.VMEM((blocks, BT, 2 * cols), jnp.float32),
            pltpu.VMEM((2, *w_own.shape), jnp.bfloat16),
            pltpu.VMEM((blocks, 2, BT, cols), jnp.bfloat16),
            pltpu.VMEM((2, half, cols), jnp.bfloat16),
            pltpu.VMEM((steps, *prefix.shape), jnp.bfloat16),
            pltpu.VMEM((steps, *prefix.shape), jnp.bfloat16),
            pltpu.SemaphoreType.DMA((blocks + 1, 7)),
            pltpu.SemaphoreType.DMA((blocks,)),
            pltpu.SemaphoreType.DMA((3, max(blocks + 2, steps))),
            pltpu.SemaphoreType.DMA((blocks + 2 + steps, 2)),
        ],
        compiler_params=pltpu.CompilerParams(collective_id=1, has_side_effects=True, vmem_limit_bytes=58 * MIB),
        cost_estimate=pl.CostEstimate(flops=12 * half * cols * 2 * cols, bytes_accessed=64 * MIB, transcendentals=0),
        name="finish_tokens",
    )(dq_own, dq_got, dkv_own, dkv_got, gfirst, w_own, w_oth, mem_keep, mem_got, o_keep, o_got, prefix, part)


def swap(value, axis):
    return lax.ppermute(value, axis, SWAP)


def after(value, *others):
    return lax.optimization_barrier((value, *others))[0]


def gather_half(piece):
    return lax.all_gather(piece, ("zl", "y", "c"), axis=0, tiled=True)


def paired_device(
    tokens, memory, dec_segments, mem_segments, self_qkv, self_out, cross_q, cross_kv, cross_out, ffn_in, ffn_out,
    adapter_down, adapter_up, self_prefix, cross_prefix, gains, cotangent,
):
    x, core = lax.axis_index("x"), lax.axis_index("c")
    agree = x == core
    columns = tokens.shape[1]
    prefix_count = self_prefix.shape[1]

    qkv_flat = self_qkv.reshape(-1, columns)
    ckv_flat = cross_kv.reshape(-1, columns)
    segs = jnp.concatenate([dec_segments, mem_segments], axis=0)
    prefixes = jnp.concatenate([self_prefix, cross_prefix], axis=0)
    prefixes = jnp.pad(prefixes, ((0, 0), (0, PP - prefix_count), (0, 0)))
    (
        rows_own, own, par, piece, mem_mine, packed, cot_mine, cot_send, qkv_other, prefixes_got, segs_got, down_full, up_full
    ) = bring_rows(
        tokens, memory, cotangent, qkv_flat, prefixes, segs, ffn_in, ffn_out,
        adapter_down, adapter_up, [self_out, cross_q, cross_out, ckv_flat],
    )
    segs = jnp.where(agree, segs, segs_got)
    dec_seg, mem_seg = segs[0], segs[1]
    prefixes = jnp.where(agree, prefixes, prefixes_got)
    self_pre, cross_pre = prefixes[:2], prefixes[2:]
    self_masks = documents(dec_seg, dec_seg, prefix_count)
    self_lo, self_hi = ranges(dec_seg, dec_seg, True)
    cross_masks = documents(dec_seg, mem_seg, prefix_count)
    cross_lo, cross_hi = ranges(dec_seg, mem_seg, False)

    others = gather_half(piece).reshape(8, *piece.shape)
    so_tall, cq_tall, ckv_tall = self_out.shape[0] // 8, cross_q.shape[0] // 8, ckv_flat.shape[0] // 8
    co_row = 2 * so_tall + cq_tall
    ckv_row = co_row + 2 * so_tall
    got = swap(after(packed, own), "x")
    self_q, self_k, self_v = ([(own, t), (par, t)] for t in range(3))
    self_o, self_ot, self_lt = attend_fwd(
        self_q, self_k, self_v, columns, self_masks, self_pre, self_lo, self_hi, True
    )
    heads_got = swap(self_o[1], "c")

    mem_got = got[:mem_mine.shape[0]]
    cot_got = swap(after(cot_send, got), "x")
    mem_par, mem_par_got = swap(mem_mine, "c"), swap(mem_got, "c")
    first_sum, cq_own, cq_send = after_self(
        self_o[0], heads_got, rows_own, gains, self_out, cross_q, others
    )
    ffn_other = gather_half(after(got, first_sum)[mem_mine.shape[0]:])
    ffn_other = ffn_other.reshape(8, -1, columns)
    cq_par = swap(cq_send, "c")
    own, par = project([mem_mine, mem_got], [mem_par, mem_par_got], ckv_flat, others, ckv_row, 2)
    cross_qp = [(cq_own, 0), (cq_par, 0)]
    cross_k, cross_v = ([(own, t), (par, t)] for t in range(2))
    cross_o, cross_ot, cross_lt = attend_fwd(
        cross_qp, cross_k, cross_v, columns, cross_masks, cross_pre, cross_lo, cross_hi, False
    )
    cross_got = swap(cross_o[1], "c")
    out_keep, out_send, grad_second, g_own, g_send, part = ffn_both_ways(
        cross_o[0], cross_got, first_sum, cot_mine, cot_got, gains, down_full, up_full,
        cross_out, others, co_row, ffn_in, ffn_out, ffn_other,
    )
    g_par = swap(g_send, "c")
    out_got = swap(out_send, "x")

    part_got = swap(part, "zh")

    cdq, cdkv, cross_dp = attend_bwd(
        cross_qp, cross_k, cross_v, [(g_own, 0), (g_par, 0)], columns, cross_ot, cross_lt,
        cross_masks, cross_pre, cross_lo, cross_hi, False,
    )
    cdq_got = swap(after(cdq[1], out_got, part_got), "c")
    part = low(part.astype(jnp.float32) + part_got.astype(jnp.float32))
    cdkv_got = swap(after(cdkv[1], cdq_got), "c")
    grad_first, g_own, g_send = before_self(
        grad_second, cdq[0], cdq_got, first_sum, gains, self_out, cross_q, others
    )
    g_par = swap(g_send, "c")

    mem_keep, mem_out = back_memory(cdkv[0], cdkv_got, ckv_flat, others, ckv_row)
    mem_back = swap(mem_out, "x")
    g_par = after(g_par, mem_out)

    sdq, sdkv, self_dp = attend_bwd(
        self_q, self_k, self_v, [(g_own, 0), (g_par, 0)], columns, self_ot, self_lt,
        self_masks, self_pre, self_lo, self_hi, True,
    )
    sdq_got = swap(after(sdq[1], mem_back), "c")
    sdkv_got = swap(sdkv[1], "c")
    grad_tokens, grad_memory, output, prefix_sums, part_got = finish_tokens(
        sdq[0], sdq_got, sdkv[0], sdkv_got, grad_first, qkv_flat, qkv_other, mem_keep, mem_back, out_keep, out_got,
        jnp.concatenate([self_dp, cross_dp], axis=0), part,
    )
    part = part.astype(jnp.float32) + part_got.astype(jnp.float32)
    grad_down, grad_up = part[0].T, part[1]
    grad_tokens, grad_memory = grad_tokens.astype(jnp.float32), grad_memory.astype(jnp.float32)
    prefix_sums = prefix_sums[:, :prefix_count]

    return (output, grad_tokens, grad_memory, prefix_sums[:2], prefix_sums[2:], grad_down, grad_up)


def norm_grad(gathered, gain, upstream):
    n, r = normalize(gathered.astype(jnp.float32))
    return norm_back(n, r, gain, upstream)


def wide_device(
    tokens, memory, dec_segments, mem_segments, self_qkv, self_out, cross_q, cross_kv, cross_out, ffn_in, ffn_out,
    adapter_down, adapter_up, self_prefix, cross_prefix, gains, cotangent,
):
    n_wide = lax.axis_size("wide")
    row_count, columns = tokens.shape
    own_start = lax.axis_index("wide") * columns
    block_size = row_count // n_wide
    block_start = lax.axis_index("wide") * block_size
    prefix_count = self_prefix.shape[1]
    dec_seg, mem_seg = dec_segments[0], mem_segments[0]

    def collect(values):
        return lax.all_gather(values, "wide", axis=1, tiled=True)

    def spread(term):
        return lax.psum_scatter(term, "wide", scatter_dimension=1, tiled=True)

    def own_columns(values):
        return lax.dynamic_slice_in_dim(values, own_start, columns, 1)

    def padded(prefix):
        return jnp.pad(prefix, ((0, 0), (0, PP - prefix_count), (0, 0)))

    self_masks = documents(dec_seg, dec_seg, prefix_count)
    self_lo, self_hi = ranges(dec_seg, dec_seg, True)
    cross_masks = documents(dec_seg, mem_seg, prefix_count)
    cross_lo, cross_hi = ranges(dec_seg, mem_seg, False)
    self_pre, cross_pre = padded(self_prefix), padded(cross_prefix)

    all_tokens, all_memory = collect(tokens), collect(memory)
    self_q, self_k, self_v = ([(low(mm(all_tokens, self_qkv[t])), 0)] for t in range(3))
    (self_heads,), self_ot, self_lt = attend_fwd(
        self_q, self_k, self_v, columns, self_masks, self_pre, self_lo, self_hi, True
    )
    first_sum = low(tokens.astype(jnp.float32) + spread(mm(self_heads, self_out)))
    gathered_one = collect(first_sum)
    normed_one = normalize(gathered_one.astype(jnp.float32))[0] * gains[0]
    cross_qp = [(low(mm(low(normed_one), cross_q)), 0)]
    cross_k, cross_v = ([(low(mm(all_memory, cross_kv[t])), 0)] for t in range(2))
    (cross_heads,), cross_ot, cross_lt = attend_fwd(
        cross_qp, cross_k, cross_v, columns, cross_masks, cross_pre, cross_lo, cross_hi, False
    )
    second_sum = low(own_columns(normed_one) + spread(mm(cross_heads, cross_out)))
    gathered_two = collect(second_sum)
    normed_two = normalize(gathered_two.astype(jnp.float32))[0] * gains[1]
    normed_low = low(normed_two)
    adapter_in = lax.dynamic_slice_in_dim(normed_low, block_start, block_size, 0)
    adapter_rows = lax.all_gather(adapter_in, "narrow", axis=0, tiled=True)
    bottle, bottle_slope = gelu_parts(mm(adapter_rows, adapter_down))
    bottle = low(bottle)
    adapted = lax.psum_scatter(low(mm(bottle, adapter_up)), "narrow", scatter_dimension=0, tiled=True)
    hidden, slope = gelu_parts(mm(normed_low, ffn_in))
    branch = mm(low(hidden), ffn_out)
    placed = lax.dynamic_slice_in_dim(branch, block_start, block_size, 0) + 4.0 * adapted.astype(jnp.float32)
    branch = lax.dynamic_update_slice_in_dim(branch, placed, block_start, 0)
    third_sum = low(own_columns(normed_two) + spread(branch))
    gathered_three = collect(third_sum)
    output = low(own_columns(normalize(gathered_three.astype(jnp.float32))[0] * gains[2]))
    grad_three = norm_grad(gathered_three, gains[2], collect(cotangent).astype(jnp.float32))
    grad_branch = low(grad_three)
    grad_pre = low(mm_nt(grad_branch, ffn_out) * slope)
    grad_normed = mm_nt(grad_pre, ffn_in)
    grad_adapted = low(4.0 * lax.dynamic_slice_in_dim(grad_branch, block_start, block_size, 0).astype(jnp.float32))
    grad_adapted = lax.all_gather(grad_adapted, "narrow", axis=0, tiled=True)
    bottle_grad = low(mm_nt(grad_adapted, adapter_up) * bottle_slope)
    grad_in = lax.psum_scatter(low(mm_nt(bottle_grad, adapter_down)), "narrow", scatter_dimension=0, tiled=True)
    placed = lax.dynamic_slice_in_dim(grad_normed, block_start, block_size, 0) + grad_in.astype(jnp.float32)
    grad_normed = lax.dynamic_update_slice_in_dim(grad_normed, placed, block_start, 0)
    grad_down, grad_up = lax.psum(
        (mm_tn(adapter_rows, bottle_grad), mm_tn(bottle, grad_adapted)), ("dp", "wide")
    )
    grad_two = collect(low(own_columns(grad_three) + spread(grad_normed))).astype(jnp.float32)
    grad_second = norm_grad(gathered_two, gains[1], grad_two)
    grad_cross = low(mm_nt(low(grad_second), cross_out))
    (cdq,), (cdkv,), cross_dp = attend_bwd(
        cross_qp, cross_k, cross_v, [(grad_cross, 0)], columns, cross_ot, cross_lt,
        cross_masks, cross_pre, cross_lo, cross_hi, False,
    )
    spread_one = spread(low(mm_nt(cdq, cross_q))).astype(jnp.float32)
    grad_memory = spread(low(mm_nt(cdkv[0], cross_kv[0]) + mm_nt(cdkv[1], cross_kv[1]))).astype(jnp.float32)
    grad_one = collect(low(own_columns(grad_second) + spread_one)).astype(jnp.float32)
    grad_first = norm_grad(gathered_one, gains[0], grad_one)
    grad_self = low(mm_nt(low(grad_first), self_out))
    (sdq,), (sdkv,), self_dp = attend_bwd(
        self_q, self_k, self_v, [(grad_self, 0)], columns, self_ot, self_lt,
        self_masks, self_pre, self_lo, self_hi, True,
    )
    grad_input = mm_nt(sdq, self_qkv[0]) + mm_nt(sdkv[0], self_qkv[1]) + mm_nt(sdkv[1], self_qkv[2])
    grad_tokens = own_columns(grad_first) + spread(grad_input)
    totals = lax.psum((low(self_dp), low(cross_dp)), ("dp", "narrow"))
    grad_self_prefix, grad_cross_prefix = (t.astype(jnp.float32)[:, :prefix_count] for t in totals)
    return (output, grad_tokens, grad_memory, grad_self_prefix, grad_cross_prefix, grad_down, grad_up)


def solution(mesh):
    dp, wide, narrow = (mesh.shape[name] for name in ("dp", "wide", "narrow"))
    if (dp, wide, narrow) == (4, 2, 4):
        parts = Mesh(mesh.devices.reshape(2, 2, 2, 2, 2), ("zh", "zl", "x", "y", "c"))
        device, used = paired_device, parts
        rows, split, thin = ("zh", "zl", "y", "c"), "x", ("y", "c")
    else:
        device, used = wide_device, mesh
        rows, split, thin = ("dp", "narrow"), "wide", "narrow"
    return jax.shard_map(
        device,
        mesh=used,
        in_specs=(
            P(rows, split),
            P(rows, split),
            P(rows, None),
            P(rows, None),
            P(None, None, split),
            P(split, None),
            P(None, split),
            P(None, None, split),
            P(split, None),
            P(None, split),
            P(split, None),
            P(None, thin),
            P(thin, None),
            P(None, None, split),
            P(None, None, split),
            P(),
            P(rows, split),
        ),
        out_specs=(
            P(rows, split),
            P(rows, split),
            P(rows, split),
            P(None, None, split),
            P(None, None, split),
            P(None, thin),
            P(thin, None),
        ),
        check_vma=False,
    )
```

```python
import functools
import math
from functools import partial

import jax
import jax.numpy as jnp
from jax import lax
from jax.experimental import pallas as pl
from jax.experimental.pallas import tpu as pltpu
from jax.sharding import Mesh
from jax.sharding import PartitionSpec as P

HEAD_DIM = 64
DOCS = 4
NEG = -1e30
BQ = 256
BK = 128
BP = 1024
PP = 32
BT = 256
BR = 512
HEADS_FWD = 8
HEADS_BWD = 4
SWAP = [(0, 1), (1, 0)]
MIB = 2**20


def mm(a, b):
    return jnp.dot(a, b, preferred_element_type=jnp.float32)


def mm_nt(a, b):
    return lax.dot_general(a, b, (((1,), (1,)), ((), ())), preferred_element_type=jnp.float32)


def mm_tn(a, b):
    return lax.dot_general(a, b, (((0,), (0,)), ((), ())), preferred_element_type=jnp.float32)


def part_offsets(n_parts, part_len):
    if n_parts == 1:
        return [0]
    core = lax.axis_index("c")
    return [pl.multiple_of(core * part_len, part_len), pl.multiple_of((1 - core) * part_len, part_len)]


def block_at(i, size):
    return pl.ds(pl.multiple_of(i * size, size), size)


def key_blocks(j, count):
    return pl.ds(pl.multiple_of(j * BK, BK), count * BK)


def for_key_blocks(lo, hi, act):
    rounds = (hi - lo) // 4

    def four(t, _):
        act(lo + t * 4, 4)
        return 0

    lax.fori_loop(0, rounds, four, 0)
    rest = lo + rounds * 4

    @pl.when(hi - rest >= 2)
    def _():
        act(rest, 2)

    @pl.when((hi - rest) % 2 == 1)
    def _():
        act(hi - 1, 1)


def head_rows(h):
    return pl.ds(h * HEAD_DIM, HEAD_DIM)


def later_keys(shape):
    return lax.broadcasted_iota(jnp.int32, shape, 0) > lax.broadcasted_iota(jnp.int32, shape, 1)


def by_head(prefix, heads_here):
    shape = (heads_here * PP, heads_here * HEAD_DIM)
    rows = lax.broadcasted_iota(jnp.int32, shape, 0) // PP
    columns = lax.broadcasted_iota(jnp.int32, shape, 1) // HEAD_DIM
    tall = jnp.concatenate([prefix] * heads_here, axis=0)
    return jnp.where(rows == columns, tall, jnp.zeros((), prefix.dtype))


def padding_rows(shape, prefix_count):
    return lax.broadcasted_iota(jnp.int32, shape, 0) % PP >= prefix_count


def document_rows(seg):
    row = lax.broadcasted_iota(jnp.int32, (2 * HEAD_DIM, seg.shape[1]), 0)
    differ = jnp.logical_and(row < DOCS, row != seg)
    return jnp.where(differ, NEG, 0.0).astype(jnp.bfloat16)


def document_columns(seg):
    row = lax.broadcasted_iota(jnp.int32, (2 * HEAD_DIM, seg.shape[1]), 0)
    return jnp.where(row == seg, 1.0, 0.0).astype(jnp.bfloat16).T


def load_queries(q_turned, h, eq, qx, here):
    zero = jnp.zeros((HEAD_DIM, q_turned.shape[1]), q_turned.dtype)
    mine = (h % 2) * HEAD_DIM
    qx[h, pl.ds(mine, HEAD_DIM), here] = q_turned[h * HEAD_DIM:(h + 1) * HEAD_DIM]
    qx[h, pl.ds(HEAD_DIM - mine, HEAD_DIM), here] = zero
    if eq is not None:
        qx[h, pl.ds(2 * HEAD_DIM, 2 * HEAD_DIM), here] = eq


def fwd_kernel(causal, n_parts, prefix_count, lo_ref, hi_ref, *refs):
    q_parts, k_parts, v_parts = refs[:n_parts], refs[n_parts:2 * n_parts], refs[2 * n_parts:3 * n_parts]
    key_seg, query_seg, pre_ref = refs[3 * n_parts:3 * n_parts + 3]
    o_parts = refs[3 * n_parts + 3:4 * n_parts + 3]
    ot_ref, lt_ref, qt, qx, vx, ke, acc, top = refs[4 * n_parts + 3:]
    seq = qt.shape[1]
    q_len, m_len = q_parts[0].shape[0], k_parts[0].shape[0]
    heads_here = qt.shape[0] // HEAD_DIM
    n_pairs = heads_here // 2
    n_q = seq // BQ
    ones_rows = vx.shape[1] - HEAD_DIM

    for q_ref, at in zip(q_parts, part_offsets(n_parts, q_len)):
        here = pl.ds(at, q_len)
        q_turned = (q_ref[...] * jnp.bfloat16(0.125)).T
        qt[:, here] = q_turned
        documents = document_rows(query_seg[:, here])
        for h in range(heads_here):
            load_queries(q_turned, h, documents, qx, here)
    for k_ref, v_ref, at in zip(k_parts, v_parts, part_offsets(n_parts, m_len)):
        here = pl.ds(at, m_len)
        v_turned = v_ref[...].T
        for h in range(heads_here):
            vx[h, :HEAD_DIM, here] = v_turned[h * HEAD_DIM:(h + 1) * HEAD_DIM]
        documents = document_columns(key_seg[:, here])
        for p in range(n_pairs):
            ke[p, here, :128] = k_ref[:, p * 128:(p + 1) * 128]
            ke[p, here, 128:] = documents
    for h in range(heads_here):
        vx[h, HEAD_DIM:, :] = jnp.ones((ones_rows, vx.shape[2]), jnp.bfloat16)
    keys_p = by_head(pre_ref[0], heads_here)
    values_p = by_head(pre_ref[1], heads_here).T

    wide = min(BP, seq)

    def prefix_step(find_top):
        def step(i, _):
            qs = block_at(i, wide)
            scores = mm(keys_p, qt[:, qs])
            scores = jnp.where(padding_rows(scores.shape, prefix_count), NEG, scores)
            chances = []
            for h in range(heads_here):
                s = scores[h * PP:(h + 1) * PP]
                if find_top:
                    top[h:h + 1, qs] = jnp.max(s, axis=0, keepdims=True)
                p = jnp.exp(s - top[h:h + 1, qs])
                acc[h, HEAD_DIM:, qs] = jnp.broadcast_to(jnp.sum(p, axis=0, keepdims=True), (ones_rows, wide))
                chances.append(low(p))
            out = mm(values_p, jnp.concatenate(chances, axis=0))
            for h in range(heads_here):
                acc[h, :HEAD_DIM, qs] = out[h * HEAD_DIM:(h + 1) * HEAD_DIM]
            return 0

        lax.fori_loop(0, seq // wide, step, 0)

    def scores_of(i, j, count, diag):
        qs, ks = block_at(i, BQ), key_blocks(j, count)
        scores = [mm(ke[h // 2, ks, :], qx[h, :, qs]) for h in range(heads_here)]
        if diag:
            scores = [jnp.where(later_keys(s.shape), NEG, s) for s in scores]
        return scores

    def add_block(i, j, count, diag):
        qs, ks = block_at(i, BQ), key_blocks(j, count)
        scores = scores_of(i, j, count, diag)
        for h in range(heads_here):
            p = low(jnp.exp(scores[h] - top[h:h + 1, qs]))
            acc[h, :, qs] += mm(vx[h, :, ks], p)

    def raise_top(i, j, count, diag):
        qs = block_at(i, BQ)
        for h, s in enumerate(scores_of(i, j, count, diag)):
            top[h:h + 1, qs] = jnp.maximum(top[h:h + 1, qs], jnp.max(s, axis=0, keepdims=True))

    def all_blocks(act):
        def step(i, _):
            if causal:
                act(i, i * (BQ // BK), BQ // BK, True)
            for_key_blocks(lo_ref[i], hi_ref[i], lambda j, count: act(i, j, count, False))
            return 0

        lax.fori_loop(0, n_q, step, 0)

    prefix_step(True)
    all_blocks(add_block)
    largest = jnp.max(jnp.where(acc[0, HEAD_DIM:HEAD_DIM + 8, :] < 1e30, 0.0, 1.0))
    for h in range(1, heads_here):
        largest = jnp.maximum(largest, jnp.max(jnp.where(acc[h, HEAD_DIM:HEAD_DIM + 8, :] < 1e30, 0.0, 1.0)))

    @pl.when(largest > 0.5)
    def _():
        all_blocks(raise_top)
        prefix_step(False)
        all_blocks(add_block)

    def finish(i, _):
        qs = block_at(i, BQ)
        outs = []
        for h in range(heads_here):
            total = acc[h, HEAD_DIM:HEAD_DIM + 1, qs]
            lt_ref[h // 2, h % 2:h % 2 + 1, qs] = top[h:h + 1, qs] + jnp.log(total)
            outs.append(acc[h, :HEAD_DIM, qs] / total)
        ot = jnp.concatenate(outs, axis=0)
        ot_ref[:, qs] = low(ot)
        store_part(o_parts, i, low(ot.T))
        return 0

    lax.fori_loop(0, n_q, finish, 0)


def store_part(parts, i, value):
    per_part = parts[0].shape[0] // BQ
    at = pl.ds(pl.multiple_of((i % per_part) * BQ, BQ), BQ)
    if len(parts) == 1:
        parts[0][at, :] = value
        return
    own = i // per_part == lax.axis_index("c")

    @pl.when(own)
    def _():
        parts[0][at, :] = value

    @pl.when(jnp.logical_not(own))
    def _():
        parts[1][at, :] = value


def attend_fwd(qs, ks, vs, cols, masks, prefix, lo, hi, causal):
    ek, eq, prefix_count = masks
    n = len(qs)
    q_len, m_len = qs[0][0].shape[0], ks[0][0].shape[0]
    seq, mem = q_len * n, m_len * n
    wd = min(HEAD_DIM * HEADS_FWD, cols)
    heads_here = wd // HEAD_DIM
    steps = cols // wd
    in_specs, operands = [], []
    for group, length in ((qs, q_len), (ks, m_len), (vs, m_len)):
        for array, at in group:
            in_specs.append(pl.BlockSpec((length, wd), partial(lambda at, p, *_: (0, at * steps + p), at)))
            operands.append(array)
    in_specs += [
        pl.BlockSpec((1, mem), lambda p, *_: (0, 0)),
        pl.BlockSpec((1, seq), lambda p, *_: (0, 0)),
        pl.BlockSpec((2, PP, wd), lambda p, *_: (0, 0, p)),
    ]
    grid_spec = pltpu.PrefetchScalarGridSpec(
        num_scalar_prefetch=2,
        grid=(steps,),
        in_specs=in_specs,
        out_specs=[pl.BlockSpec((q_len, wd), lambda p, *_: (0, p))] * n
        + [
            pl.BlockSpec((wd, seq), lambda p, *_: (p, 0)),
            pl.BlockSpec((wd // 128, 2, seq), lambda p, *_: (p, 0, 0)),
        ],
        scratch_shapes=[
            pltpu.VMEM((wd, seq), jnp.bfloat16),
            pltpu.VMEM((heads_here, 256, seq), jnp.bfloat16),
            pltpu.VMEM((heads_here, HEAD_DIM + 16, mem), jnp.bfloat16),
            pltpu.VMEM((wd // 128, mem, 256), jnp.bfloat16),
            pltpu.VMEM((heads_here, HEAD_DIM + 16, seq), jnp.float32),
            pltpu.VMEM((8, seq), jnp.float32),
        ],
    )
    result = pl.pallas_call(
        functools.partial(fwd_kernel, causal, n, prefix_count),
        grid_spec=grid_spec,
        out_shape=[jax.ShapeDtypeStruct((q_len, cols), jnp.bfloat16)] * n
        + [
            jax.ShapeDtypeStruct((cols, seq), jnp.bfloat16),
            jax.ShapeDtypeStruct((cols // 128, 2, seq), jnp.float32),
        ],
        compiler_params=pltpu.CompilerParams(vmem_limit_bytes=60 * MIB),
        cost_estimate=pl.CostEstimate(
            flops=8 * seq * mem * cols, bytes_accessed=12 * MIB, transcendentals=seq * mem * cols // 256
        ),
        name="attend_fwd_self" if causal else "attend_fwd_cross",
    )(lo, hi, *operands, ek, eq, prefix)
    return result[:n], result[n], result[n + 1]


def bwd_kernel(causal, n_parts, prefix_count, lo_ref, hi_ref, *refs):
    q_parts, k_parts, v_parts, g_parts = (refs[t * n_parts:(t + 1) * n_parts] for t in range(4))
    ot_ref, lt_ref, key_seg, query_seg, pre_ref = refs[4 * n_parts:4 * n_parts + 5]
    dq_parts = refs[4 * n_parts + 5:5 * n_parts + 5]
    dkv_parts = refs[5 * n_parts + 5:6 * n_parts + 5]
    dp_ref, qt, gt, qx, gx, kt, ke, vv, qm, gm, dq, dk, dv, delta = refs[6 * n_parts + 5:]
    seq = qt.shape[1]
    q_len, m_len = q_parts[0].shape[0], k_parts[0].shape[0]
    width = qt.shape[0]
    heads_here = width // HEAD_DIM
    n_pairs = heads_here // 2
    n_q = seq // BQ
    lane = lax.broadcasted_iota(jnp.int32, (1, width), 1)
    first = lane % 128 < HEAD_DIM
    zero = jnp.zeros((), jnp.bfloat16)

    for q_ref, g_ref, at in zip(q_parts, g_parts, part_offsets(n_parts, q_len)):
        here = pl.ds(at, q_len)
        q_all = q_ref[...] * jnp.bfloat16(0.125)
        g_all = g_ref[...]
        q_turned, g_turned = q_all.T, g_all.T
        qt[:, here] = q_turned
        gt[:, here] = g_turned
        documents = document_rows(query_seg[:, here])
        for h in range(heads_here):
            load_queries(q_turned, h, documents, qx, here)
            load_queries(g_turned, h, None, gx, here)
        qm[0, here, :] = jnp.where(first, q_all, zero)
        qm[1, here, :] = jnp.where(first, zero, q_all)
        gm[0, here, :] = jnp.where(first, g_all, zero)
        gm[1, here, :] = jnp.where(first, zero, g_all)
        prod = g_turned.astype(jnp.float32) * ot_ref[:, here].astype(jnp.float32)
        for h in range(heads_here):
            delta[h:h + 1, here] = jnp.sum(prod[h * HEAD_DIM:(h + 1) * HEAD_DIM], axis=0, keepdims=True)
    for k_ref, v_ref, at in zip(k_parts, v_parts, part_offsets(n_parts, m_len)):
        here = pl.ds(at, m_len)
        kt[:, here] = k_ref[...].T
        vv[here, :] = v_ref[...]
        documents = document_columns(key_seg[:, here])
        for p in range(n_pairs):
            ke[p, here, :128] = k_ref[:, p * 128:(p + 1) * 128]
            ke[p, here, 128:] = documents
    dk[...] = jnp.zeros_like(dk)
    dv[...] = jnp.zeros_like(dv)
    keys_p = by_head(pre_ref[0], heads_here)
    values_p = by_head(pre_ref[1], heads_here)
    keys_turned = keys_p.T

    def grads(s, dp, h, qs):
        p = jnp.exp(s - lt_ref[h // 2, h % 2:h % 2 + 1, qs])
        ds = low(p * (dp - delta[h:h + 1, qs]))
        return low(p), ds

    wide = min(BP, seq)

    def prefix_step(i, totals):
        qs = block_at(i, wide)
        scores = mm(keys_p, qt[:, qs])
        scores = jnp.where(padding_rows(scores.shape, prefix_count), NEG, scores)
        dps = mm(values_p, gt[:, qs])
        chances, slopes = [], []
        for h in range(heads_here):
            rows = slice(h * PP, (h + 1) * PP)
            p, ds = grads(scores[rows], dps[rows], h, qs)
            chances.append(p)
            slopes.append(ds)
        p, ds = jnp.concatenate(chances, axis=0), jnp.concatenate(slopes, axis=0)
        dq[:, qs] = mm(keys_turned, ds)
        dkp = totals[0] + mm(ds, qm[0, qs, :] + qm[1, qs, :])
        dvp = totals[1] + mm(p, gm[0, qs, :] + gm[1, qs, :])
        return dkp, dvp

    zeros = jnp.zeros((heads_here * PP, width), jnp.float32)
    totals = lax.fori_loop(0, seq // wide, prefix_step, (zeros, zeros))
    for n, total in enumerate(totals):
        rows = lax.broadcasted_iota(jnp.int32, total.shape, 0) // PP
        columns = lax.broadcasted_iota(jnp.int32, total.shape, 1) // HEAD_DIM
        total = jnp.where(rows == columns, total, 0.0)
        folded = total[:PP]
        for h in range(1, heads_here):
            folded += total[h * PP:(h + 1) * PP]
        dp_ref[n] = folded

    def add_block(i, j, count, diag):
        qs, ks = block_at(i, BQ), key_blocks(j, count)
        both = []
        for h in range(heads_here):
            c = (h // 2) * 128
            both.append((mm(ke[h // 2, ks, :], qx[h, :, qs]), mm(vv[ks, c:c + 128], gx[h, :, qs])))
        for pr in range(n_pairs):
            c = pr * 128
            dkb = dk[ks, c:c + 128]
            dvb = dv[ks, c:c + 128]
            for h in (2 * pr, 2 * pr + 1):
                s, dp = both[h]
                if diag:
                    s = jnp.where(later_keys(s.shape), NEG, s)
                p, ds = grads(s, dp, h, qs)
                dvb += mm(p, gm[h % 2, qs, c:c + 128])
                dkb += mm(ds, qm[h % 2, qs, c:c + 128])
                dq[head_rows(h), qs] += mm(kt[h * HEAD_DIM:(h + 1) * HEAD_DIM, ks], ds)
            dk[ks, c:c + 128] = dkb
            dv[ks, c:c + 128] = dvb

    def q_step(i, _):
        if causal:
            add_block(i, i * (BQ // BK), BQ // BK, True)
        for_key_blocks(lo_ref[i], hi_ref[i], lambda j, count: add_block(i, j, count, False))
        return 0

    lax.fori_loop(0, n_q, q_step, 0)

    def finish(i, _):
        store_part(dq_parts, i, low((dq[:, block_at(i, BQ)] * 0.125).T))
        return 0

    lax.fori_loop(0, n_q, finish, 0)
    for dkv_ref, at in zip(dkv_parts, part_offsets(n_parts, m_len)):
        here = pl.ds(at, m_len)
        dkv_ref[0] = low(dk[here, :])
        dkv_ref[1] = low(dv[here, :])


def attend_bwd(qs, ks, vs, gs, cols, ot, lt, masks, prefix, lo, hi, causal):
    ek, eq, prefix_count = masks
    n = len(qs)
    q_len, m_len = qs[0][0].shape[0], ks[0][0].shape[0]
    seq, mem = q_len * n, m_len * n
    wd = min(HEAD_DIM * HEADS_BWD, cols)
    heads_here = wd // HEAD_DIM
    steps = cols // wd
    in_specs, operands = [], []
    for group, length in ((qs, q_len), (ks, m_len), (vs, m_len), (gs, q_len)):
        for array, at in group:
            in_specs.append(pl.BlockSpec((length, wd), partial(lambda at, p, *_: (0, at * steps + p), at)))
            operands.append(array)
    in_specs += [
        pl.BlockSpec((wd, seq), lambda p, *_: (p, 0)),
        pl.BlockSpec((wd // 128, 2, seq), lambda p, *_: (p, 0, 0)),
        pl.BlockSpec((1, mem), lambda p, *_: (0, 0)),
        pl.BlockSpec((1, seq), lambda p, *_: (0, 0)),
        pl.BlockSpec((2, PP, wd), lambda p, *_: (0, 0, p)),
    ]
    grid_spec = pltpu.PrefetchScalarGridSpec(
        num_scalar_prefetch=2,
        grid=(steps,),
        in_specs=in_specs,
        out_specs=[pl.BlockSpec((q_len, wd), lambda p, *_: (0, p))] * n
        + [pl.BlockSpec((2, m_len, wd), lambda p, *_: (0, 0, p))] * n
        + [pl.BlockSpec((2, PP, wd), lambda p, *_: (0, 0, p))],
        scratch_shapes=[
            pltpu.VMEM((wd, seq), jnp.bfloat16),
            pltpu.VMEM((wd, seq), jnp.bfloat16),
            pltpu.VMEM((heads_here, 256, seq), jnp.bfloat16),
            pltpu.VMEM((heads_here, 128, seq), jnp.bfloat16),
            pltpu.VMEM((wd, mem), jnp.bfloat16),
            pltpu.VMEM((wd // 128, mem, 256), jnp.bfloat16),
            pltpu.VMEM((mem, wd), jnp.bfloat16),
            pltpu.VMEM((2, seq, wd), jnp.bfloat16),
            pltpu.VMEM((2, seq, wd), jnp.bfloat16),
            pltpu.VMEM((wd, seq), jnp.float32),
            pltpu.VMEM((mem, wd), jnp.float32),
            pltpu.VMEM((mem, wd), jnp.float32),
            pltpu.VMEM((8, seq), jnp.float32),
        ],
    )
    result = pl.pallas_call(
        functools.partial(bwd_kernel, causal, n, prefix_count),
        grid_spec=grid_spec,
        out_shape=[jax.ShapeDtypeStruct((q_len, cols), jnp.bfloat16)] * n
        + [jax.ShapeDtypeStruct((2, m_len, cols), jnp.bfloat16)] * n
        + [jax.ShapeDtypeStruct((2, PP, cols), jnp.float32)],
        compiler_params=pltpu.CompilerParams(vmem_limit_bytes=60 * MIB),
        cost_estimate=pl.CostEstimate(
            flops=12 * seq * mem * cols, bytes_accessed=20 * MIB, transcendentals=seq * mem * cols // 256
        ),
        name="attend_bwd_self" if causal else "attend_bwd_cross",
    )(lo, hi, *operands, ot, lt, ek, eq, prefix)
    return result[:n], result[n:2 * n], result[2 * n]


def ranges(dec_seg, mem_seg, causal):
    seq = dec_seg.shape[0]
    blocks = dec_seg.reshape(seq // BQ, BQ)
    low, high = blocks[:, 0], blocks[:, -1]
    lo = jnp.sum((mem_seg[None, :] < low[:, None]).astype(jnp.int32), axis=1) // BK
    if causal:
        hi = jnp.arange(seq // BQ, dtype=jnp.int32) * (BQ // BK)
    else:
        hi = (jnp.sum((mem_seg[None, :] <= high[:, None]).astype(jnp.int32), axis=1) + BK - 1) // BK
    return lo, hi


def documents(dec_seg, mem_seg, prefix_count):
    return mem_seg[None], dec_seg[None], prefix_count


def normalize(v):
    centered = v - jnp.mean(v, axis=-1, keepdims=True)
    r = lax.rsqrt(jnp.mean(centered * centered, axis=-1, keepdims=True) + 1e-05)
    return centered * r, r


def norm_back(n, r, gain, upstream):
    u = upstream * gain
    return r * (u - jnp.mean(u, axis=-1, keepdims=True) - n * jnp.mean(u * n, axis=-1, keepdims=True))


def gelu_parts(v):
    chance = 0.5 * (1.0 + lax.erf(v * math.sqrt(0.5)))
    slope = chance + v * (jnp.exp(-0.5 * v * v) * (1.0 / math.sqrt(2.0 * math.pi)))
    return v * chance, slope


def low(v):
    return v.astype(jnp.bfloat16)


def place_halves(own, packed, row, held, sems, at):
    x = lax.axis_index("x")
    tall, wide = held.shape[2:]
    cols = packed.shape[2]
    copies = [pltpu.make_async_copy(own, held.at[x], sems.at[at])]
    for j in range(wide // cols):
        copies.append(
            pltpu.make_async_copy(
                packed.at[:, pl.ds(row + j * tall, tall)],
                held.at[1 - x, :, :, pl.ds(j * cols, cols)],
                sems.at[at + 1 + j],
            )
        )
    return copies


def half_of(held, which):
    return held[which].reshape(-1, held.shape[3])


def eighths(weight):
    return weight.reshape(8, weight.shape[0] // 8, weight.shape[1])


def on_first(copies, act):
    @pl.when(pl.program_id(0) == 0)
    def _():
        for copy in copies:
            getattr(copy, act)()


def after_self_kernel(own_ref, par_ref, tok_ref, gains_ref, so_own, cq_own, packed,
                      first_ref, q_own_ref, q_par_ref, so, cq, sems):
    core = lax.axis_index("c")
    so_copies = place_halves(so_own, packed, 0, so, sems, 0)
    cq_copies = place_halves(cq_own, packed, 2 * so.shape[2], cq, sems, 4)
    on_first(so_copies + cq_copies, "start")
    on_first(so_copies, "wait")
    total = tok_ref[...].astype(jnp.float32) + (mm(own_ref[...], half_of(so, core)) + mm(par_ref[...], half_of(so, 1 - core)))
    first = low(total)
    first_ref[...] = first
    n, _ = normalize(first.astype(jnp.float32))
    normed = low(n * gains_ref[0:1, :])
    on_first(cq_copies, "wait")
    q_own_ref[...] = low(mm(normed, half_of(cq, core)))
    q_par_ref[...] = low(mm(normed, half_of(cq, 1 - core)))


def rows_spec(width):
    return pl.BlockSpec((BR, width), lambda i: (i, 0))


ANY = pl.BlockSpec(memory_space=pl.ANY)


def after_self(own, par, tokens, gains, so_own, cq_own, packed):
    rows, d = tokens.shape
    half = d // 2
    return pl.pallas_call(
        after_self_kernel,
        grid=(rows // BR,),
        in_specs=[rows_spec(half), rows_spec(half), rows_spec(d), pl.BlockSpec((3, d), lambda i: (0, 0)), ANY, ANY, ANY],
        out_specs=[rows_spec(d), rows_spec(half), rows_spec(half)],
        out_shape=[
            jax.ShapeDtypeStruct((rows, d), jnp.bfloat16),
            jax.ShapeDtypeStruct((rows, half), jnp.bfloat16),
            jax.ShapeDtypeStruct((rows, half), jnp.bfloat16),
        ],
        scratch_shapes=[
            pltpu.VMEM((2, 8, half // 8, d), jnp.bfloat16),
            pltpu.VMEM((2, 8, d // 8, half), jnp.bfloat16),
            pltpu.SemaphoreType.DMA((8,)),
        ],
        compiler_params=pltpu.CompilerParams(vmem_limit_bytes=58 * MIB),
        cost_estimate=pl.CostEstimate(flops=4 * rows * d * d, bytes_accessed=12 * MIB, transcendentals=0),
        name="after_self",
    )(own, par, tokens, gains, eighths(so_own), eighths(cq_own), packed)


def before_self_kernel(gsec_ref, own_ref, par_ref, first_ref, gains_ref, so_own, cq_own, packed,
                       gfirst_ref, g_own_ref, g_par_ref, so, cq, sems):
    core = lax.axis_index("c")
    so_copies = place_halves(so_own, packed, 0, so, sems, 0)
    cq_copies = place_halves(cq_own, packed, 2 * so.shape[2], cq, sems, 4)
    on_first(cq_copies + so_copies, "start")
    on_first(cq_copies, "wait")
    grad_one = low(gsec_ref[...] + (mm_nt(own_ref[...], half_of(cq, core)) + mm_nt(par_ref[...], half_of(cq, 1 - core))))
    n, r = normalize(first_ref[...].astype(jnp.float32))
    grad_first = norm_back(n, r, gains_ref[0:1, :], grad_one.astype(jnp.float32))
    gfirst_ref[...] = grad_first
    first_low = low(grad_first)
    on_first(so_copies, "wait")
    g_own_ref[...] = low(mm_nt(first_low, half_of(so, core)))
    g_par_ref[...] = low(mm_nt(first_low, half_of(so, 1 - core)))


def before_self(gsec, own, par, first, gains, so_own, cq_own, packed):
    rows, d = first.shape
    half = d // 2
    return pl.pallas_call(
        before_self_kernel,
        grid=(rows // BR,),
        in_specs=[
            rows_spec(d), rows_spec(half), rows_spec(half), rows_spec(d), pl.BlockSpec((3, d), lambda i: (0, 0)),
            ANY, ANY, ANY,
        ],
        out_specs=[rows_spec(d), rows_spec(half), rows_spec(half)],
        out_shape=[
            jax.ShapeDtypeStruct((rows, d), jnp.float32),
            jax.ShapeDtypeStruct((rows, half), jnp.bfloat16),
            jax.ShapeDtypeStruct((rows, half), jnp.bfloat16),
        ],
        scratch_shapes=[
            pltpu.VMEM((2, 8, half // 8, d), jnp.bfloat16),
            pltpu.VMEM((2, 8, d // 8, half), jnp.bfloat16),
            pltpu.SemaphoreType.DMA((8,)),
        ],
        compiler_params=pltpu.CompilerParams(vmem_limit_bytes=58 * MIB),
        cost_estimate=pl.CostEstimate(flops=4 * rows * d * d, bytes_accessed=16 * MIB, transcendentals=0),
        name="before_self",
    )(gsec, own, par, first, gains, eighths(so_own), eighths(cq_own), packed)


MESH_ID = pl.DeviceIdType.MESH
PARTS_IN = 4


def greet(targets):
    barrier = pltpu.get_barrier_semaphore()
    for target in targets:
        pl.semaphore_signal(barrier, inc=1, device_id=target, device_id_type=MESH_ID)
    pl.semaphore_wait(barrier, len(targets))


def remote(src, dst, send, recv, target):
    return pltpu.make_async_remote_copy(
        src_ref=src, dst_ref=dst, send_sem=send, recv_sem=recv, device_id=target, device_id_type=MESH_ID
    )


def eighth_index():
    return (lax.axis_index("zl") * 2 + lax.axis_index("y")) * 2 + lax.axis_index("c")


def piece_copies(wholes, packed, send, recv):
    cols = packed.shape[1]
    copies, at = [], 0
    for whole in wholes:
        tall = whole.shape[0] // 8
        source = pl.ds(pl.multiple_of(eighth_index() * tall, tall), tall)
        for j in range(whole.shape[1] // cols):
            n = len(copies)
            copies.append(
                remote(
                    whole.at[source, pl.ds(j * cols, cols)], packed.at[pl.ds(at, tall)], send.at[n], recv.at[n],
                    {"x": 1 - lax.axis_index("x")},
                )
            )
            at += tall
    return copies


def bring_kernel(tok, mem, cot, qkv, prefix, segs, w_in, w_out, down, up, so, cq, co, ckv,
                 rows_out, q_own, q_par, passed, mem_mine, packed, cot_mine, cot_send, qkv_oth, prefix_got, segs_got, down_all, up_all,
                 rows_own, rows_par, held, stage, stage_down, stage_up, send, recv, load, p_send, p_recv):
    x, y, zl, core = (lax.axis_index(name) for name in ("x", "y", "zl", "c"))
    half = rows_own.shape[0]
    cols = tok.shape[1]
    chunk = half // PARTS_IN
    piece = qkv.shape[0] // 8
    stays = x == core
    partner = {"c": 1 - core}
    across = {"x": 1 - x}

    def token_half(which):
        return pl.ds(pl.multiple_of(which * half, half), half)

    loads = [
        pltpu.make_async_copy(source.at[token_half(which)], stage.at[n], load.at[n])
        for n, (source, which) in enumerate(((mem, core), (cot, core)))
    ]
    at = 0
    for whole in (w_in, w_out):
        tall, wide = whole.shape[0] // 8, whole.shape[1]
        source = pl.ds(pl.multiple_of(eighth_index() * tall, tall), tall)
        for j in range(wide // cols):
            n = len(loads)
            loads.append(
                pltpu.make_async_copy(
                    whole.at[source, pl.ds(j * cols, cols)], stage.at[2, pl.ds(at, tall)], load.at[n]
                )
            )
            at += tall
    pack = pltpu.make_async_copy(stage.at[2], packed.at[pl.ds(half, half)], load.at[len(loads)])
    mem_send = packed.at[pl.ds(0, half)]
    for copy in loads:
        copy.start()
    greet([across, {"x": 1 - x, "c": 1 - core}, {"y": 1 - y}, {"zl": 1 - zl}, partner])

    def features(which):
        return pl.ds(pl.multiple_of(which * cols, cols), cols)

    def part(k):
        return pl.ds(k * chunk, chunk)

    def eighth(a, b, c):
        return pl.ds(pl.multiple_of(((a * 2 + b) * 2 + c) * piece, piece), piece)

    def weight(at, slot, target, source=None):
        return remote((qkv_oth if source is None else source).at[at], qkv_oth.at[at], send.at[slot], recv.at[slot], target)

    mine = eighth(zl, y, core)
    w_x = weight(mine, 0, across, qkv)
    w_x.start()
    at_small = 14 + 3 * PARTS_IN
    small = [
        remote(prefix, prefix_got, send.at[at_small], recv.at[at_small], across),
        remote(segs, segs_got, send.at[at_small + 1], recv.at[at_small + 1], partner),
    ]
    for copy in small:
        copy.start()
    others = small

    units = up.shape[0]

    def adapt_places(a, b):
        at = pl.ds(pl.multiple_of((a * 2 + b) * units, units), units)
        return down_all.at[:, at], up_all.at[at]

    def adapt_copies(sources, a, b, n, target):
        return [
            remote(source, place, send.at[at_small + 2 + n + m], recv.at[at_small + 2 + n + m], target)
            for m, (source, place) in enumerate(zip(sources, adapt_places(a, b)))
        ]

    adapt_y = adapt_copies((down, up), y, core, 0, {"y": 1 - y})
    adapt_c = adapt_copies((down, up), y, core, 2, partner)
    adapt_in = [
        pltpu.make_async_copy(down, stage_down, load.at[14]),
        pltpu.make_async_copy(up, stage_up, load.at[15]),
    ]
    for copy in adapt_y + adapt_c + adapt_in:
        copy.start()

    at_own, at_par = 8, 8 + PARTS_IN
    at_here = 8 + 2 * PARTS_IN

    def token_sends():
        copies = []
        for t in range(2):
            for k in range(PARTS_IN):
                slot = at_own + k
                copies.append(
                    remote(
                        tok.at[pl.ds(t * half + k * chunk, chunk)],
                        rows_own.at[part(k), features(x)],
                        send.at[slot + t * PARTS_IN],
                        recv.at[slot],
                        {"x": 1 - x, "c": t},
                    )
                )
        return copies

    def here_copies():
        own = tok.at[token_half(core)]
        other = tok.at[token_half(1 - core)]
        return [
            remote(other, rows_own.at[:, features(x)], send.at[at_here], recv.at[at_here], partner),
            remote(own, rows_par.at[:, features(x)], send.at[at_here + 1], recv.at[at_here + 1], partner),
        ]

    def weight_rows(source):
        tall = held.shape[0] // 3
        return [
            pltpu.make_async_copy(source.at[pl.ds(t * tall, tall)], held.at[pl.ds(t * tall, tall)], load.at[9 + t])
            for t in range(3)
        ]

    def own_weights():
        return weight_rows(qkv)

    def row_copy(source, to, slot):
        return remote(source.at[token_half(1 - core)], to, send.at[slot], recv.at[slot], partner)

    @pl.when(jnp.logical_not(stays))
    def _():
        for copy in token_sends():
            copy.start()
        row_copy(mem, mem_send, at_here + 3).start()
        row_copy(cot, cot_send, at_here + 5).start()
        for n, to, slot in ((0, mem_send, at_here + 3), (1, cot_send, at_here + 5)):
            loads[n].wait()
            pltpu.make_async_copy(stage.at[n], to, recv.at[slot]).start()

    @pl.when(stays)
    def _():
        for copy in here_copies():
            copy.start()
        row_copy(mem, mem_mine, at_here + 2).start()
        row_copy(cot, cot_mine, at_here + 4).start()
        for which, to, slot in ((core, rows_own, at_here), (1 - core, rows_par, at_here + 1)):
            pltpu.make_async_copy(tok.at[token_half(which)], to.at[:, features(x)], recv.at[slot]).start()
        for copy in own_weights():
            copy.start()
        for n, to, slot in ((0, mem_mine, at_here + 2), (1, cot_mine, at_here + 4)):
            loads[n].wait()
            pltpu.make_async_copy(stage.at[n], to, recv.at[slot]).start()

    for copy in loads[2:]:
        copy.wait()
    pack.start()
    adapt_here = [
        pltpu.make_async_copy(source, place, load.at[14 + m])
        for m, (source, place) in enumerate(zip((stage_down, stage_up), adapt_places(y, core)))
    ]
    for came, placed in zip(adapt_in, adapt_here):
        came.wait()
        placed.start()

    for copy in adapt_y:
        copy.wait_recv()
    adapt_yc = adapt_copies(adapt_places(1 - y, core), 1 - y, core, 4, partner)
    for copy in adapt_yc:
        copy.start()
    w_x.wait_recv()
    w_y = weight(mine, 1, {"y": 1 - y})
    w_z = weight(mine, 2, {"zl": 1 - zl})
    w_c = weight(mine, 4, partner)
    for copy in (w_y, w_z, w_c):
        copy.start()

    forwards = []

    def forward(k):
        here = rows_own.at[part(k), features(1 - x)]
        remote(here, here, send.at[at_own + k], recv.at[at_own + k], across).wait_recv()
        copy = remote(here, rows_par.at[part(k), features(1 - x)], send.at[at_here + 6 + k], recv.at[at_par + k], partner)
        copy.start()
        forwards.append(copy)

    forward(0)
    w_y.wait_recv()
    from_y = eighth(zl, 1 - y, core)
    w_yz = weight(from_y, 3, {"zl": 1 - zl})
    w_yc = weight(from_y, 5, partner)
    w_yz.start()
    w_yc.start()
    forward(1)
    w_z.wait_recv()
    w_zc = weight(eighth(1 - zl, y, core), 6, partner)
    w_zc.start()
    for k in range(2, PARTS_IN):
        forward(k)
    w_yz.wait_recv()
    w_yzc = weight(eighth(1 - zl, 1 - y, core), 7, partner)
    w_yzc.start()

    pieces = piece_copies((so, cq, co, ckv), passed, p_send, p_recv)
    for copy in pieces:
        copy.start()

    for copy in (w_c, w_yc, w_zc, w_yzc):
        copy.wait_recv()

    @pl.when(jnp.logical_not(stays))
    def _():
        for copy in weight_rows(qkv_oth):
            copy.start()

    for copy in weight_rows(qkv):
        copy.wait()
    for to, slot in ((rows_own.at[:, features(x)], at_here), (rows_par.at[:, features(x)], at_here + 1)):
        remote(to, to, send.at[slot], recv.at[slot], partner).wait_recv()
    tall = held.shape[0] // 3
    keep_rows = pltpu.make_async_copy(rows_own, rows_out, load.at[12])
    keep_rows.start()
    for t in range(3):
        q_own[:, t * cols:(t + 1) * cols] = low(mm(rows_own[...], held[t * tall:(t + 1) * tall, :]))
    for copy in forwards:
        copy.wait_recv()
    for t in range(3):
        q_par[:, t * cols:(t + 1) * cols] = low(mm(rows_par[...], held[t * tall:(t + 1) * tall, :]))
    keep_rows.wait()

    for copy in (*adapt_c, *adapt_yc, *others, *pieces):
        copy.wait_recv()
    for to, slot in (
        (mem_mine, at_here + 2),
        (mem_send, at_here + 3),
        (cot_mine, at_here + 4),
        (cot_send, at_here + 5),
    ):
        remote(to, to, send.at[slot], recv.at[slot], partner).wait_recv()

    pack.wait()
    for copy in adapt_here:
        copy.wait()

    for copy in (w_x, w_y, w_z, w_c, w_yz, w_yc, w_zc, w_yzc, *adapt_y, *adapt_c, *adapt_yc, *forwards, *others, *pieces):
        copy.wait_send()

    @pl.when(jnp.logical_not(stays))
    def _():
        for copy in token_sends():
            copy.wait_send()
        row_copy(mem, mem_send, at_here + 3).wait_send()
        row_copy(cot, cot_send, at_here + 5).wait_send()

    @pl.when(stays)
    def _():
        for copy in here_copies():
            copy.wait_send()
        row_copy(mem, mem_mine, at_here + 2).wait_send()
        row_copy(cot, cot_mine, at_here + 4).wait_send()


def bring_rows(tokens, memory, cotangent, qkv_flat, prefixes, segs, ffn_in, ffn_out, down, up, others):
    rows, cols = tokens.shape
    half = rows // 2
    wide_rows = jax.ShapeDtypeStruct((half, 2 * cols), jnp.bfloat16)
    thin_rows = jax.ShapeDtypeStruct((half, cols), jnp.bfloat16)
    slots = 22 + 3 * PARTS_IN
    packed_rows = sum(w.shape[0] // 8 * (w.shape[1] // cols) for w in others)
    pieces = sum(w.shape[1] // cols for w in others)
    vmem = pl.BlockSpec(memory_space=pltpu.VMEM)
    return pl.pallas_call(
        bring_kernel,
        in_specs=[ANY] * 14,
        out_specs=[ANY, vmem, vmem] + [ANY] * 10,
        out_shape=[wide_rows, jax.ShapeDtypeStruct((half, 3 * cols), jnp.bfloat16),
                   jax.ShapeDtypeStruct((half, 3 * cols), jnp.bfloat16),
                   jax.ShapeDtypeStruct((packed_rows, cols), jnp.bfloat16),
                   thin_rows, jax.ShapeDtypeStruct((rows, cols), jnp.bfloat16), thin_rows, thin_rows,
                   jax.ShapeDtypeStruct(qkv_flat.shape, jnp.bfloat16),
                   jax.ShapeDtypeStruct(prefixes.shape, prefixes.dtype),
                   jax.ShapeDtypeStruct(segs.shape, segs.dtype),
                   jax.ShapeDtypeStruct((down.shape[0], 4 * down.shape[1]), down.dtype),
                   jax.ShapeDtypeStruct((4 * up.shape[0], up.shape[1]), up.dtype)],
        scratch_shapes=[
            pltpu.VMEM((half, 2 * cols), jnp.bfloat16),
            pltpu.VMEM((half, 2 * cols), jnp.bfloat16),
            pltpu.VMEM(qkv_flat.shape, jnp.bfloat16),
            pltpu.VMEM((3, half, cols), jnp.bfloat16),
            pltpu.VMEM(down.shape, jnp.bfloat16),
            pltpu.VMEM(up.shape, jnp.bfloat16),
            pltpu.SemaphoreType.DMA((slots,)),
            pltpu.SemaphoreType.DMA((slots,)),
            pltpu.SemaphoreType.DMA((16,)),
            pltpu.SemaphoreType.DMA((pieces,)),
            pltpu.SemaphoreType.DMA((pieces,)),
        ],
        compiler_params=pltpu.CompilerParams(collective_id=0, has_side_effects=True, vmem_limit_bytes=58 * MIB),
        cost_estimate=pl.CostEstimate(flops=0, bytes_accessed=64 * MIB, transcendentals=0),
        name="bring_rows",
    )(tokens, memory, cotangent, qkv_flat, prefixes, segs, ffn_in, ffn_out, down, up, *others)


def project_kernel(n_weights, row, own_mine, own_got, par_mine, par_got, w_own, w_oth, out_own, out_par, held, sems):
    x, core = lax.axis_index("x"), lax.axis_index("c")
    d = held.shape[0] // n_weights
    cols = held.shape[1]

    def copies(agree):
        tall = held.shape[0] // 8
        parts = [w_own.at[pl.ds(e * tall, tall)] if agree else w_oth.at[e, pl.ds(row, tall)] for e in range(8)]
        return [
            pltpu.make_async_copy(part, held.at[pl.ds(e * tall, tall)], sems.at[e]) for e, part in enumerate(parts)
        ]

    for act in ("start", "wait"):
        for agree, chosen in ((True, x == core), (False, x != core)):
            @pl.when(jnp.logical_and(pl.program_id(0) == 0, chosen))
            def _(agree=agree, act=act):
                for copy in copies(agree):
                    getattr(copy, act)()

    for t in range(n_weights):
        for pieces, out in (((own_mine, own_got), out_own), ((par_mine, par_got), out_par)):
            total = None
            for piece, at in zip(pieces, (x * (d // 2), (1 - x) * (d // 2))):
                rows = pl.ds(pl.multiple_of(t * d + at, d // 2), d // 2)
                term = mm(piece[...], held[rows, :])
                total = term if total is None else total + term
            out[:, t * cols:(t + 1) * cols] = low(total)


def project(own, par, w_own, w_oth, row, n_weights):
    rows, cols = own[0].shape
    d = w_own.shape[0] // n_weights
    return pl.pallas_call(
        functools.partial(project_kernel, n_weights, row),
        grid=(rows // BR,),
        in_specs=[rows_spec(cols)] * 4 + [ANY, ANY],
        out_specs=[rows_spec(n_weights * cols)] * 2,
        out_shape=[jax.ShapeDtypeStruct((rows, n_weights * cols), jnp.bfloat16)] * 2,
        scratch_shapes=[pltpu.VMEM(w_own.shape, jnp.bfloat16), pltpu.SemaphoreType.DMA((8,))],
        compiler_params=pltpu.CompilerParams(vmem_limit_bytes=58 * MIB),
        cost_estimate=pl.CostEstimate(flops=4 * rows * d * cols * n_weights, bytes_accessed=16 * MIB, transcendentals=0),
        name="project",
    )(*own, *par, w_own, w_oth)


def back_memory_kernel(ckv_row, own_ref, got_ref, w_own, packed, keep_ref, send_ref, held, sems):
    x, core = lax.axis_index("x"), lax.axis_index("c")
    copies = place_halves(w_own, packed, ckv_row, held, sems, 0)
    on_first(copies, "start")
    on_first(copies, "wait")
    n_weights = own_ref.shape[0]
    share = 8 // (2 * n_weights)
    for out, which in ((send_ref, 1 - x), (keep_ref, x)):
        total = None
        for t in range(n_weights):
            for rows, heads in ((own_ref, core), (got_ref, 1 - core)):
                weight = held[heads, pl.ds(2 * share * t + share * which, share)]
                term = mm_nt(rows[t], weight.reshape(-1, weight.shape[2]))
                total = term if total is None else total + term
        out[...] = low(total)


def back_memory(own, got, w_own, packed, ckv_row):
    n, rows, cols = own.shape
    w_own = eighths(w_own)
    both = pl.BlockSpec((n, BR, cols), lambda i: (0, i, 0))
    return pl.pallas_call(
        functools.partial(back_memory_kernel, ckv_row),
        grid=(rows // BR,),
        in_specs=[both, both, ANY, ANY],
        out_specs=[rows_spec(cols)] * 2,
        out_shape=[jax.ShapeDtypeStruct((rows, cols), jnp.bfloat16)] * 2,
        scratch_shapes=[pltpu.VMEM((2, *w_own.shape), jnp.bfloat16), pltpu.SemaphoreType.DMA((2,))],
        compiler_params=pltpu.CompilerParams(vmem_limit_bytes=58 * MIB),
        cost_estimate=pl.CostEstimate(flops=8 * n * rows * cols * cols, bytes_accessed=12 * MIB, transcendentals=0),
        name="back_memory",
    )(own, got, w_own, packed)


CHUNK = 512
ROWS = 256


def ffn_kernel(co_row, own_ref, par_ref, first_hbm, cot_mine, cot_got, gains_ref, down, up,
               co_own, packed, in_own, out_own, ffn_other,
               keep_ref, send_ref, gsec_ref, g_own_ref, g_par_ref, part_ref,
               first, cot, co, w_in, w_out, normed, second, branch, full, acc, slopes,
               bottle, bottle_slope, bottle_grad, grads, got_c, part_out, part_got,
               co_sems, w_sems, sems, send, recv):
    x, y, core = (lax.axis_index(name) for name in ("x", "y", "c"))
    rows, d = normed.shape
    half = d // 2
    in_tall = ffn_other.shape[1] // 2
    chunks = 2 * in_own.shape[2] // CHUNK
    own_chunks = chunks // 2
    out_tall = w_out.shape[2]
    pieces = CHUNK // out_tall

    def columns(which):
        return pl.ds(pl.multiple_of(which * half, half), half)

    loads = [
        pltpu.make_async_copy(first_hbm, first, sems.at[0]),
        pltpu.make_async_copy(cot_mine, cot.at[:, columns(x)], sems.at[1]),
        pltpu.make_async_copy(cot_got, cot.at[:, columns(1 - x)], sems.at[2]),
    ]
    co_copies = place_halves(co_own, packed, co_row, co, co_sems, 0)

    def weight_copies(t, slot, own):
        if own:
            at = pl.ds(pl.multiple_of(t * CHUNK, CHUNK), CHUNK)
            sources_in = [(in_own.at[:, :, at], w_in.at[slot])]
            sources = [out_own.at[pl.ds(pieces * t, pieces), :, pl.ds(j * half, half)] for j in range(2)]
        else:
            t = t - own_chunks
            tall = w_in.shape[2]
            blocks = CHUNK // half
            sources_in = [
                (
                    ffn_other.at[:, pl.ds(pl.multiple_of((t * blocks + j) * tall, tall), tall)],
                    w_in.at[slot, :, :, pl.ds(j * half, half)],
                )
                for j in range(blocks)
            ]
            sources = [
                ffn_other.at[pl.ds(pieces * t, pieces), pl.ds(in_tall + j * out_tall, out_tall)] for j in range(2)
            ]
        return [
            pltpu.make_async_copy(source, to, w_sems.at[slot, 2 + j]) for j, (source, to) in enumerate(sources_in)
        ] + [
            pltpu.make_async_copy(source, w_out.at[slot, :, :, pl.ds(j * half, half)], w_sems.at[slot, j])
            for j, source in enumerate(sources)
        ]

    def fetch(t):
        slot = t % 2

        @pl.when(t < own_chunks)
        def _():
            for copy in weight_copies(t, slot, True):
                copy.start()

        @pl.when(jnp.logical_and(t >= own_chunks, t < chunks))
        def _():
            for copy in weight_copies(t, slot, False):
                copy.start()

    def arrive(t):
        slot = t % 2

        @pl.when(t < own_chunks)
        def _():
            for copy in weight_copies(t, slot, True):
                copy.wait()

        @pl.when(t >= own_chunks)
        def _():
            for copy in weight_copies(t, slot, False):
                copy.wait()

    for copy in co_copies + loads[:1]:
        copy.start()
    fetch(0)
    fetch(1)
    for copy in loads[1:]:
        copy.start()
    greet([{"c": 1 - core}, {"y": 1 - y}, {"x": 1 - x}])
    for copy in co_copies + loads[:1]:
        copy.wait()
    acc[...] = mm(own_ref[...], half_of(co, core)) + mm(par_ref[...], half_of(co, 1 - core))

    def by_rows(act):
        def step(i, _):
            act(pl.ds(pl.multiple_of(i * ROWS, ROWS), ROWS))
            return 0

        lax.fori_loop(0, rows // ROWS, step, 0)

    def norm_two(at):
        n_one, _ = normalize(first[at, :].astype(jnp.float32))
        summed = low(n_one * gains_ref[0:1, :] + acc[at, :])
        second[at, :] = summed
        n_two, _ = normalize(summed.astype(jnp.float32))
        normed_two = n_two * gains_ref[1:2, :]
        normed[at, :] = low(normed_two)
        acc[at, :] = normed_two

    by_rows(norm_two)
    value, slope = gelu_parts(mm(normed[...], down[...]))
    bottle[...] = low(value)
    bottle_slope[...] = slope
    acc[...] += 4.0 * mm(bottle[...], up[...])

    def up_step(t, _):
        arrive(t)
        slot = t % 2
        weight_in = w_in[slot].reshape(d, CHUNK)
        weight_out = w_out[slot].reshape(CHUNK, d)
        halves = (slice(0, rows // 2), slice(rows // 2, rows))
        products = [mm(normed[at, :], weight_in) for at in halves]
        for at, product in zip(halves, products):
            value, slope = gelu_parts(product)
            slopes[t, at, :] = low(slope)
            acc[at, :] += mm(low(value), weight_out)
        fetch(t + 2)
        return 0

    lax.fori_loop(0, chunks, up_step, 0)
    fetch(0)
    fetch(1)
    for copy in loads[1:]:
        copy.wait()

    def norm_three(at):
        third = low(acc[at, :])
        n_three, r_three = normalize(third.astype(jnp.float32))
        gain = gains_ref[2:3, :]
        full[at, :] = low(n_three * gain)
        grad_three = norm_back(n_three, r_three, gain, cot[at, :].astype(jnp.float32))
        branch[at, :] = low(grad_three)
        acc[at, :] = grad_three

    by_rows(norm_three)
    outs = [
        pltpu.make_async_copy(full.at[:, columns(x)], keep_ref, sems.at[0]),
        pltpu.make_async_copy(full.at[:, columns(1 - x)], send_ref, sems.at[1]),
    ]
    for copy in outs:
        copy.start()
    adapted = low(4.0 * branch[...].astype(jnp.float32))
    bottle_grad[...] = low(mm_nt(adapted, up[...]) * bottle_slope[...])
    tall = grads.shape[3]
    for which, grad in ((0, mm_tn(bottle_grad[...], normed[...])), (1, mm_tn(bottle[...], adapted))):
        for n in range(4):
            grads[n // 2, n % 2, which] = grad[n * tall:(n + 1) * tall]
    over_c = remote(grads.at[:, 1 - core], got_c, send.at[0], recv.at[0], {"c": 1 - core})
    over_y = remote(part_out.at[0], part_got.at[0], send.at[1], recv.at[1], {"y": 1 - y})
    over_x = remote(part_out.at[1], part_got.at[1], send.at[2], recv.at[2], {"x": 1 - x})
    over_c.start()
    acc[...] += mm_nt(bottle_grad[...], down[...])

    def down_step(t, _):
        arrive(t)
        slot = t % 2
        weight_in = w_in[slot].reshape(d, CHUNK)
        weight_out = w_out[slot].reshape(CHUNK, d)
        halves = (slice(0, rows // 2), slice(rows // 2, rows))
        products = [mm_nt(branch[at, :], weight_out) for at in halves]
        for at, product in zip(halves, products):
            grad_pre = low(product * slopes[t, at, :].astype(jnp.float32))
            acc[at, :] += mm_nt(grad_pre, weight_in)
        fetch(t + 2)

        @pl.when(t == chunks // 4 - 1)
        def _():
            over_c.wait()
            part_out[0] = low(grads[1 - y, core] + got_c[1 - y])
            over_y.start()

        @pl.when(t == chunks * 5 // 8)
        def _():
            over_y.wait()
            part_out[1] = low(grads[y, core] + got_c[y] + part_got[0].astype(jnp.float32))
            over_x.start()

        return 0

    lax.fori_loop(0, chunks, down_step, 0)
    for copy in outs:
        copy.wait()

    def norm_two_back(at):
        n_two, r_two = normalize(second[at, :].astype(jnp.float32))
        grad_two = low(acc[at, :]).astype(jnp.float32)
        grad_second = norm_back(n_two, r_two, gains_ref[1:2, :], grad_two)
        acc[at, :] = grad_second
        branch[at, :] = low(grad_second)

    by_rows(norm_two_back)
    out_acc = pltpu.make_async_copy(acc, gsec_ref, sems.at[0])
    out_acc.start()
    full[:, :half] = low(mm_nt(branch[...], half_of(co, core)))
    full[:, half:] = low(mm_nt(branch[...], half_of(co, 1 - core)))
    outs = [
        pltpu.make_async_copy(full.at[:, pl.ds(0, half)], g_own_ref, sems.at[1]),
        pltpu.make_async_copy(full.at[:, pl.ds(half, half)], g_par_ref, sems.at[2]),
    ]
    for copy in outs:
        copy.start()
    over_x.wait()
    part_ref[...] = low(part_out[1].astype(jnp.float32) + part_got[1].astype(jnp.float32))
    for copy in outs + [out_acc]:
        copy.wait()


def ffn_both_ways(own, par, first, cot_mine, cot_got, gains, down, up, co_own, packed, co_row, in_own, out_own, ffn_other):
    rows, d = first.shape
    half = d // 2
    hidden_half = in_own.shape[1]
    bottleneck = up.shape[0]
    co_own, in_own, out_own = eighths(co_own), eighths(in_own), eighths(out_own)
    vmem = pl.BlockSpec(memory_space=pltpu.VMEM)
    thin = jax.ShapeDtypeStruct((rows, half), jnp.bfloat16)
    part = (2, bottleneck // 4, d)
    flops = 2 * rows * d * (8 * hidden_half + 6 * bottleneck + 2 * d)
    return pl.pallas_call(
        functools.partial(ffn_kernel, co_row),
        in_specs=[vmem, vmem, ANY, ANY, ANY, vmem, vmem, vmem, ANY, ANY, ANY, ANY, ANY],
        out_specs=[ANY, ANY, ANY, ANY, ANY, vmem],
        out_shape=[thin, thin, jax.ShapeDtypeStruct((rows, d), jnp.float32), thin, thin,
                   jax.ShapeDtypeStruct(part, jnp.bfloat16)],
        scratch_shapes=[
            pltpu.VMEM((rows, d), jnp.bfloat16),
            pltpu.VMEM((rows, d), jnp.bfloat16),
            pltpu.VMEM((2, *co_own.shape), jnp.bfloat16),
            pltpu.VMEM((2, 8, d // 8, CHUNK), jnp.bfloat16),
            pltpu.VMEM((2, CHUNK // out_own.shape[1], out_own.shape[1], d), jnp.bfloat16),
            pltpu.VMEM((rows, d), jnp.bfloat16),
            pltpu.VMEM((rows, d), jnp.bfloat16),
            pltpu.VMEM((rows, d), jnp.bfloat16),
            pltpu.VMEM((rows, d), jnp.bfloat16),
            pltpu.VMEM((rows, d), jnp.float32),
            pltpu.VMEM((2 * hidden_half // CHUNK, rows, CHUNK), jnp.bfloat16),
            pltpu.VMEM((rows, bottleneck), jnp.bfloat16),
            pltpu.VMEM((rows, bottleneck), jnp.float32),
            pltpu.VMEM((rows, bottleneck), jnp.bfloat16),
            pltpu.VMEM((2, 2, *part), jnp.float32),
            pltpu.VMEM((2, *part), jnp.float32),
            pltpu.VMEM((2, *part), jnp.bfloat16),
            pltpu.VMEM((2, *part), jnp.bfloat16),
            pltpu.SemaphoreType.DMA((4,)),
            pltpu.SemaphoreType.DMA((2, 2 + CHUNK // half)),
            pltpu.SemaphoreType.DMA((3,)),
            pltpu.SemaphoreType.DMA((3,)),
            pltpu.SemaphoreType.DMA((3,)),
        ],
        compiler_params=pltpu.CompilerParams(collective_id=3, has_side_effects=True, vmem_limit_bytes=63 * MIB),
        cost_estimate=pl.CostEstimate(flops=flops, bytes_accessed=48 * MIB, transcendentals=0),
        name="ffn_both_ways",
    )(own, par, first, cot_mine, cot_got, gains, down, up, co_own, packed, in_own, out_own, ffn_other)


PREFIX_STEPS = ("x", "zl", "y", "zh")


def finish_kernel(dq_own, dq_send, dkv_own, dkv_send, gfirst, w_own, w_oth, mem_keep, mem_got, o_keep, o_got, pre_ref, part_ref,
                  out_ref, mem_ref, o_ref, pre_out_ref, part_got_ref,
                  lhs, first, held, boxes, stage, sums, arrived, local, place, send, recv, push_send, push_recv):
    x, core = lax.axis_index("x"), lax.axis_index("c")
    here = {name: lax.axis_index(name) for name in PREFIX_STEPS}
    partner, across = {"c": 1 - core}, {"x": 1 - x}
    stays = x == core
    blocks = lhs.shape[0]
    half = blocks * BT
    cols = out_ref.shape[1]
    d = held.shape[1] // 3
    steps = len(PREFIX_STEPS) + 1

    def loads(b):
        rows = pl.ds(b * BT, BT)
        pairs = [(dq_own.at[rows], lhs.at[b, 0]), (dkv_own.at[0, rows], lhs.at[b, 1]), (dkv_own.at[1, rows], lhs.at[b, 2]),
                 (gfirst.at[rows], first.at[b])]
        return [pltpu.make_async_copy(src, dst, local.at[b, n]) for n, (src, dst) in enumerate(pairs)]

    def pushes(b):
        rows = pl.ds(b * BT, BT)
        sources = (dq_send.at[rows], dkv_send.at[0, rows], dkv_send.at[1, rows])
        return [
            remote(source, lhs.at[b, 3 + n], push_send.at[b, n], push_recv.at[b, n], partner)
            for n, source in enumerate(sources)
        ]

    def weights(agree):
        pair = (w_own, w_oth) if agree else (w_oth, w_own)
        return [pltpu.make_async_copy(src, held.at[n], local.at[blocks, n]) for n, src in enumerate(pair)]

    ours = pl.ds(pl.multiple_of(core * half, half), half)

    def settled(agree):
        mine, passed = ((mem_keep, o_keep), (mem_got, o_got)) if agree else ((mem_got, o_got), (mem_keep, o_keep))
        return (
            [pltpu.make_async_copy(src, stage.at[n], local.at[blocks, 2 + n]) for n, src in enumerate(mine)],
            [pltpu.make_async_copy(stage.at[n], to.at[ours], local.at[blocks, 4 + n]) for n, to in enumerate((mem_ref, o_ref))],
            [
                remote(src, to.at[ours], send.at[0, blocks + n], recv.at[blocks + n, core], partner)
                for n, (src, to) in enumerate(zip(passed, (mem_ref, o_ref)))
            ],
        )

    def prefix_copy(s):
        target = {PREFIX_STEPS[s]: 1 - here[PREFIX_STEPS[s]]} if s < steps - 1 else partner
        return remote(sums.at[s], arrived.at[s], send.at[2, s], recv.at[blocks + 2 + s, 0], target)

    for copy in loads(0):
        copy.start()
    for agree, chosen in ((True, stays), (False, jnp.logical_not(stays))):
        @pl.when(chosen)
        def _(agree=agree):
            for copy in weights(agree):
                copy.start()

    for b in range(1, blocks):
        for copy in loads(b):
            copy.start()
    for agree, chosen in ((True, stays), (False, jnp.logical_not(stays))):
        @pl.when(chosen)
        def _(agree=agree):
            for copy in settled(agree)[0]:
                copy.start()

    sums[0] = low(pre_ref[...])
    greet([across, {"x": 1 - x, "c": 1 - core}, partner] + [{name: 1 - here[name]} for name in PREFIX_STEPS[1:]])
    for b in range(blocks):
        for copy in pushes(b):
            copy.start()
    prefix_copy(0).start()
    part_copy = remote(
        part_ref, part_got_ref, send.at[1, blocks], recv.at[blocks + 2, 1], {"zl": 1 - here["zl"]}
    )
    part_copy.start()

    def landing(b):
        return pl.ds(pl.multiple_of(core * half + b * BT, BT), BT)

    def over(b):
        return remote(boxes.at[b, 0], out_ref.at[landing(b)], send.at[0, b], recv.at[b, core], {"x": 1 - x, "c": x})

    def beside(b):
        return remote(boxes.at[b, 1], out_ref.at[landing(b)], send.at[1, b], recv.at[b, core], partner)

    def kept_here(b):
        return pltpu.make_async_copy(boxes.at[b, 1], out_ref.at[landing(b)], place.at[b])

    def compute(b, which):
        at = pl.ds(pl.multiple_of(which * cols, cols), cols)
        total = first[b, :, at]
        for n in range(6):
            rows = pl.ds(pl.multiple_of((n % 3) * d + which * cols, cols), cols)
            total += mm_nt(lhs[b, n], held[n // 3, rows, :])
        return low(total)

    def next_prefix(s):
        prefix_copy(s).wait()
        sums[s + 1] = low(sums[s].astype(jnp.float32) + arrived[s].astype(jnp.float32))
        prefix_copy(s + 1).start()

    for copy in weights(True):
        copy.wait()
    for b in range(blocks):
        for copy in loads(b):
            copy.wait()
        for copy in pushes(b):
            copy.wait_recv()
        boxes[b, 0] = compute(b, 1 - x)
        over(b).start()
        if b == 1:
            next_prefix(0)
    for b in range(blocks):
        boxes[b, 1] = compute(b, x)

        @pl.when(stays)
        def _(b=b):
            kept_here(b).start()

        @pl.when(jnp.logical_not(stays))
        def _(b=b):
            beside(b).start()

        if b + 1 < steps - 1:
            next_prefix(b + 1)

    for agree, chosen in ((True, stays), (False, jnp.logical_not(stays))):
        @pl.when(chosen)
        def _(agree=agree):
            loaded, placed, passed = settled(agree)
            for copy in passed:
                copy.start()
            for copy in loaded:
                copy.wait()
            for copy in placed:
                copy.start()

    prefix_copy(steps - 1).wait()
    pre_out_ref[...] = jnp.where(stays, sums[steps - 1], arrived[steps - 1]).astype(jnp.float32)

    def wait_for(t, b):
        rows = out_ref.at[pl.ds(pl.multiple_of(t * half + b * BT, BT), BT)]
        remote(rows, rows, send.at[0, b], recv.at[b, t], across).wait_recv()

    part_copy.wait()
    theirs = pl.ds(pl.multiple_of((1 - core) * half, half), half)
    for n, to in enumerate((mem_ref, o_ref)):
        remote(to.at[theirs], to.at[theirs], send.at[0, 0], recv.at[blocks + n, 1 - core], partner).wait_recv()
    for agree, chosen in ((True, stays), (False, jnp.logical_not(stays))):
        @pl.when(chosen)
        def _(agree=agree):
            loaded, placed, passed = settled(agree)
            for copy in placed:
                copy.wait()
            for copy in passed:
                copy.wait_send()

    for b in range(blocks):
        over(b).wait_send()
        for copy in pushes(b):
            copy.wait_send()

        @pl.when(stays)
        def _(b=b):
            kept_here(b).wait()
            wait_for(1 - core, b)

        @pl.when(jnp.logical_not(stays))
        def _(b=b):
            beside(b).wait_send()
            for t in range(2):
                wait_for(t, b)


def finish_tokens(dq_own, dq_send, dkv_own, dkv_send, gfirst, w_own, w_oth, mem_keep, mem_got, o_keep, o_got, prefix, part):
    half, cols = dq_own.shape
    blocks = half // BT
    steps = len(PREFIX_STEPS) + 1
    vmem = pl.BlockSpec(memory_space=pltpu.VMEM)
    rows = jax.ShapeDtypeStruct((2 * half, cols), jnp.bfloat16)
    return pl.pallas_call(
        finish_kernel,
        in_specs=[ANY] * 11 + [vmem, vmem],
        out_specs=[ANY, ANY, ANY, vmem, vmem],
        out_shape=[rows, rows, rows, jax.ShapeDtypeStruct(prefix.shape, jnp.float32),
                   jax.ShapeDtypeStruct(part.shape, part.dtype)],
        scratch_shapes=[
            pltpu.VMEM((blocks, 6, BT, cols), jnp.bfloat16),
            pltpu.VMEM((blocks, BT, 2 * cols), jnp.float32),
            pltpu.VMEM((2, *w_own.shape), jnp.bfloat16),
            pltpu.VMEM((blocks, 2, BT, cols), jnp.bfloat16),
            pltpu.VMEM((2, half, cols), jnp.bfloat16),
            pltpu.VMEM((steps, *prefix.shape), jnp.bfloat16),
            pltpu.VMEM((steps, *prefix.shape), jnp.bfloat16),
            pltpu.SemaphoreType.DMA((blocks + 1, 7)),
            pltpu.SemaphoreType.DMA((blocks,)),
            pltpu.SemaphoreType.DMA((3, max(blocks + 2, steps))),
            pltpu.SemaphoreType.DMA((blocks + 2 + steps, 2)),
            pltpu.SemaphoreType.DMA((blocks, 3)),
            pltpu.SemaphoreType.DMA((blocks, 3)),
        ],
        compiler_params=pltpu.CompilerParams(collective_id=1, has_side_effects=True, vmem_limit_bytes=58 * MIB),
        cost_estimate=pl.CostEstimate(flops=12 * half * cols * 2 * cols, bytes_accessed=64 * MIB, transcendentals=0),
        name="finish_tokens",
    )(dq_own, dq_send, dkv_own, dkv_send, gfirst, w_own, w_oth, mem_keep, mem_got, o_keep, o_got, prefix, part)


def swap(value, axis):
    return lax.ppermute(value, axis, SWAP)


def after(value, *others):
    return lax.optimization_barrier((value, *others))[0]


def gather_half(piece):
    return lax.all_gather(piece, ("zl", "y", "c"), axis=0, tiled=True)


def paired_device(
    tokens, memory, dec_segments, mem_segments, self_qkv, self_out, cross_q, cross_kv, cross_out, ffn_in, ffn_out,
    adapter_down, adapter_up, self_prefix, cross_prefix, gains, cotangent,
):
    x, core = lax.axis_index("x"), lax.axis_index("c")
    agree = x == core
    columns = tokens.shape[1]
    prefix_count = self_prefix.shape[1]

    qkv_flat = self_qkv.reshape(-1, columns)
    ckv_flat = cross_kv.reshape(-1, columns)
    segs = jnp.concatenate([dec_segments, mem_segments], axis=0)
    prefixes = jnp.concatenate([self_prefix, cross_prefix], axis=0)
    prefixes = jnp.pad(prefixes, ((0, 0), (0, PP - prefix_count), (0, 0)))
    (
        rows_own, own, par, piece, mem_mine, packed, cot_mine, cot_send, qkv_other, prefixes_got, segs_got, down_full, up_full
    ) = bring_rows(
        tokens, memory, cotangent, qkv_flat, prefixes, segs, ffn_in, ffn_out,
        adapter_down, adapter_up, [self_out, cross_q, cross_out, ckv_flat],
    )
    segs = jnp.where(agree, segs, segs_got)
    dec_seg, mem_seg = segs[0], segs[1]
    prefixes = jnp.where(agree, prefixes, prefixes_got)
    self_pre, cross_pre = prefixes[:2], prefixes[2:]
    self_masks = documents(dec_seg, dec_seg, prefix_count)
    self_lo, self_hi = ranges(dec_seg, dec_seg, True)
    cross_masks = documents(dec_seg, mem_seg, prefix_count)
    cross_lo, cross_hi = ranges(dec_seg, mem_seg, False)

    others = gather_half(piece).reshape(8, *piece.shape)
    so_tall, cq_tall, ckv_tall = self_out.shape[0] // 8, cross_q.shape[0] // 8, ckv_flat.shape[0] // 8
    co_row = 2 * so_tall + cq_tall
    ckv_row = co_row + 2 * so_tall
    got = swap(after(packed, own), "x")
    self_q, self_k, self_v = ([(own, t), (par, t)] for t in range(3))
    self_o, self_ot, self_lt = attend_fwd(
        self_q, self_k, self_v, columns, self_masks, self_pre, self_lo, self_hi, True
    )
    heads_got = swap(self_o[1], "c")

    mem_got = got[:mem_mine.shape[0]]
    cot_got = swap(after(cot_send, got), "x")
    mem_par, mem_par_got = swap(mem_mine, "c"), swap(mem_got, "c")
    first_sum, cq_own, cq_send = after_self(
        self_o[0], heads_got, rows_own, gains, self_out, cross_q, others
    )
    ffn_other = gather_half(after(got, first_sum)[mem_mine.shape[0]:])
    ffn_other = ffn_other.reshape(8, -1, columns)
    cq_par = swap(cq_send, "c")
    own, par = project([mem_mine, mem_got], [mem_par, mem_par_got], ckv_flat, others, ckv_row, 2)
    cross_qp = [(cq_own, 0), (cq_par, 0)]
    cross_k, cross_v = ([(own, t), (par, t)] for t in range(2))
    cross_o, cross_ot, cross_lt = attend_fwd(
        cross_qp, cross_k, cross_v, columns, cross_masks, cross_pre, cross_lo, cross_hi, False
    )
    cross_got = swap(cross_o[1], "c")
    out_keep, out_send, grad_second, g_own, g_send, part = ffn_both_ways(
        cross_o[0], cross_got, first_sum, cot_mine, cot_got, gains, down_full, up_full,
        cross_out, others, co_row, ffn_in, ffn_out, ffn_other,
    )
    g_par = swap(g_send, "c")
    out_got = swap(out_send, "x")

    part_got = swap(part, "zh")

    cdq, cdkv, cross_dp = attend_bwd(
        cross_qp, cross_k, cross_v, [(g_own, 0), (g_par, 0)], columns, cross_ot, cross_lt,
        cross_masks, cross_pre, cross_lo, cross_hi, False,
    )
    cdq_got = swap(after(cdq[1], out_got, part_got), "c")
    part = low(part.astype(jnp.float32) + part_got.astype(jnp.float32))
    cdkv_got = swap(after(cdkv[1], cdq_got), "c")
    grad_first, g_own, g_send = before_self(
        grad_second, cdq[0], cdq_got, first_sum, gains, self_out, cross_q, others
    )
    g_par = swap(g_send, "c")

    mem_keep, mem_out = back_memory(cdkv[0], cdkv_got, ckv_flat, others, ckv_row)
    mem_back = swap(mem_out, "x")
    g_par = after(g_par, mem_out)

    sdq, sdkv, self_dp = attend_bwd(
        self_q, self_k, self_v, [(g_own, 0), (g_par, 0)], columns, self_ot, self_lt,
        self_masks, self_pre, self_lo, self_hi, True,
    )
    grad_tokens, grad_memory, output, prefix_sums, part_got = finish_tokens(
        sdq[0], sdq[1], sdkv[0], sdkv[1], grad_first, qkv_flat, qkv_other, mem_keep, mem_back, out_keep, out_got,
        jnp.concatenate([self_dp, cross_dp], axis=0), part,
    )
    part = part.astype(jnp.float32) + part_got.astype(jnp.float32)
    grad_down, grad_up = part[0].T, part[1]
    grad_tokens, grad_memory = grad_tokens.astype(jnp.float32), grad_memory.astype(jnp.float32)
    prefix_sums = prefix_sums[:, :prefix_count]

    return (output, grad_tokens, grad_memory, prefix_sums[:2], prefix_sums[2:], grad_down, grad_up)


def norm_grad(gathered, gain, upstream):
    n, r = normalize(gathered.astype(jnp.float32))
    return norm_back(n, r, gain, upstream)


def wide_device(
    tokens, memory, dec_segments, mem_segments, self_qkv, self_out, cross_q, cross_kv, cross_out, ffn_in, ffn_out,
    adapter_down, adapter_up, self_prefix, cross_prefix, gains, cotangent,
):
    n_wide = lax.axis_size("wide")
    row_count, columns = tokens.shape
    own_start = lax.axis_index("wide") * columns
    block_size = row_count // n_wide
    block_start = lax.axis_index("wide") * block_size
    prefix_count = self_prefix.shape[1]
    dec_seg, mem_seg = dec_segments[0], mem_segments[0]

    def collect(values):
        return lax.all_gather(values, "wide", axis=1, tiled=True)

    def spread(term):
        return lax.psum_scatter(term, "wide", scatter_dimension=1, tiled=True)

    def own_columns(values):
        return lax.dynamic_slice_in_dim(values, own_start, columns, 1)

    def padded(prefix):
        return jnp.pad(prefix, ((0, 0), (0, PP - prefix_count), (0, 0)))

    self_masks = documents(dec_seg, dec_seg, prefix_count)
    self_lo, self_hi = ranges(dec_seg, dec_seg, True)
    cross_masks = documents(dec_seg, mem_seg, prefix_count)
    cross_lo, cross_hi = ranges(dec_seg, mem_seg, False)
    self_pre, cross_pre = padded(self_prefix), padded(cross_prefix)

    all_tokens, all_memory = collect(tokens), collect(memory)
    self_q, self_k, self_v = ([(low(mm(all_tokens, self_qkv[t])), 0)] for t in range(3))
    (self_heads,), self_ot, self_lt = attend_fwd(
        self_q, self_k, self_v, columns, self_masks, self_pre, self_lo, self_hi, True
    )
    first_sum = low(tokens.astype(jnp.float32) + spread(mm(self_heads, self_out)))
    gathered_one = collect(first_sum)
    normed_one = normalize(gathered_one.astype(jnp.float32))[0] * gains[0]
    cross_qp = [(low(mm(low(normed_one), cross_q)), 0)]
    cross_k, cross_v = ([(low(mm(all_memory, cross_kv[t])), 0)] for t in range(2))
    (cross_heads,), cross_ot, cross_lt = attend_fwd(
        cross_qp, cross_k, cross_v, columns, cross_masks, cross_pre, cross_lo, cross_hi, False
    )
    second_sum = low(own_columns(normed_one) + spread(mm(cross_heads, cross_out)))
    gathered_two = collect(second_sum)
    normed_two = normalize(gathered_two.astype(jnp.float32))[0] * gains[1]
    normed_low = low(normed_two)
    adapter_in = lax.dynamic_slice_in_dim(normed_low, block_start, block_size, 0)
    adapter_rows = lax.all_gather(adapter_in, "narrow", axis=0, tiled=True)
    bottle, bottle_slope = gelu_parts(mm(adapter_rows, adapter_down))
    bottle = low(bottle)
    adapted = lax.psum_scatter(low(mm(bottle, adapter_up)), "narrow", scatter_dimension=0, tiled=True)
    hidden, slope = gelu_parts(mm(normed_low, ffn_in))
    branch = mm(low(hidden), ffn_out)
    placed = lax.dynamic_slice_in_dim(branch, block_start, block_size, 0) + 4.0 * adapted.astype(jnp.float32)
    branch = lax.dynamic_update_slice_in_dim(branch, placed, block_start, 0)
    third_sum = low(own_columns(normed_two) + spread(branch))
    gathered_three = collect(third_sum)
    output = low(own_columns(normalize(gathered_three.astype(jnp.float32))[0] * gains[2]))
    grad_three = norm_grad(gathered_three, gains[2], collect(cotangent).astype(jnp.float32))
    grad_branch = low(grad_three)
    grad_pre = low(mm_nt(grad_branch, ffn_out) * slope)
    grad_normed = mm_nt(grad_pre, ffn_in)
    grad_adapted = low(4.0 * lax.dynamic_slice_in_dim(grad_branch, block_start, block_size, 0).astype(jnp.float32))
    grad_adapted = lax.all_gather(grad_adapted, "narrow", axis=0, tiled=True)
    bottle_grad = low(mm_nt(grad_adapted, adapter_up) * bottle_slope)
    grad_in = lax.psum_scatter(low(mm_nt(bottle_grad, adapter_down)), "narrow", scatter_dimension=0, tiled=True)
    placed = lax.dynamic_slice_in_dim(grad_normed, block_start, block_size, 0) + grad_in.astype(jnp.float32)
    grad_normed = lax.dynamic_update_slice_in_dim(grad_normed, placed, block_start, 0)
    grad_down, grad_up = lax.psum(
        (mm_tn(adapter_rows, bottle_grad), mm_tn(bottle, grad_adapted)), ("dp", "wide")
    )
    grad_two = collect(low(own_columns(grad_three) + spread(grad_normed))).astype(jnp.float32)
    grad_second = norm_grad(gathered_two, gains[1], grad_two)
    grad_cross = low(mm_nt(low(grad_second), cross_out))
    (cdq,), (cdkv,), cross_dp = attend_bwd(
        cross_qp, cross_k, cross_v, [(grad_cross, 0)], columns, cross_ot, cross_lt,
        cross_masks, cross_pre, cross_lo, cross_hi, False,
    )
    spread_one = spread(low(mm_nt(cdq, cross_q))).astype(jnp.float32)
    grad_memory = spread(low(mm_nt(cdkv[0], cross_kv[0]) + mm_nt(cdkv[1], cross_kv[1]))).astype(jnp.float32)
    grad_one = collect(low(own_columns(grad_second) + spread_one)).astype(jnp.float32)
    grad_first = norm_grad(gathered_one, gains[0], grad_one)
    grad_self = low(mm_nt(low(grad_first), self_out))
    (sdq,), (sdkv,), self_dp = attend_bwd(
        self_q, self_k, self_v, [(grad_self, 0)], columns, self_ot, self_lt,
        self_masks, self_pre, self_lo, self_hi, True,
    )
    grad_input = mm_nt(sdq, self_qkv[0]) + mm_nt(sdkv[0], self_qkv[1]) + mm_nt(sdkv[1], self_qkv[2])
    grad_tokens = own_columns(grad_first) + spread(grad_input)
    totals = lax.psum((low(self_dp), low(cross_dp)), ("dp", "narrow"))
    grad_self_prefix, grad_cross_prefix = (t.astype(jnp.float32)[:, :prefix_count] for t in totals)
    return (output, grad_tokens, grad_memory, grad_self_prefix, grad_cross_prefix, grad_down, grad_up)


def solution(mesh):
    dp, wide, narrow = (mesh.shape[name] for name in ("dp", "wide", "narrow"))
    if (dp, wide, narrow) == (4, 2, 4):
        parts = Mesh(mesh.devices.reshape(2, 2, 2, 2, 2), ("zh", "zl", "x", "y", "c"))
        device, used = paired_device, parts
        rows, split, thin = ("zh", "zl", "y", "c"), "x", ("y", "c")
    else:
        device, used = wide_device, mesh
        rows, split, thin = ("dp", "narrow"), "wide", "narrow"
    return jax.shard_map(
        device,
        mesh=used,
        in_specs=(
            P(rows, split),
            P(rows, split),
            P(rows, None),
            P(rows, None),
            P(None, None, split),
            P(split, None),
            P(None, split),
            P(None, None, split),
            P(split, None),
            P(None, split),
            P(split, None),
            P(None, thin),
            P(thin, None),
            P(None, None, split),
            P(None, None, split),
            P(),
            P(rows, split),
        ),
        out_specs=(
            P(rows, split),
            P(rows, split),
            P(rows, split),
            P(None, None, split),
            P(None, None, split),
            P(None, thin),
            P(thin, None),
        ),
        check_vma=False,
    )
```
